32 devices in a mesh: grp: 4 (over y, x), seq: 8 (over z, core).
Axes of the slice: x: 2, y: 2, z: 4, core: 2. Of those that a mesh axis runs over, the one named last changes fastest.
Arguments:
- tokens: bfloat16 [8, 4096, 1536], P('grp', 'seq'), may hold values from -6 to 6
- seg_ids: int32 [8, 4096], P('grp', 'seq'), may hold values from 0 to 7, never falling along the last dimension, each value on 1 to 2048 neighbouring positions
- cotangent: bfloat16 [8, 4096, 1536], P('grp', 'seq'), may hold values from -6 to 6
- first_gain: bfloat16 [1536], P('seq'), may hold values from 0.099609375 to 1.8984375
- in_proj: bfloat16 [1536, 4096], P('seq'), may hold values from -0.15625 to 0.15625
- conv_taps: bfloat16 [4, 2048], P(None, 'seq'), may hold values from -3 to 3
- decay_param: bfloat16 [2048], P('seq'), may hold values from 4 to 10
- gate_heads: bfloat16 [16, 128, 256], P('seq'), may hold values from -0.5 to 0.5
- out_proj: bfloat16 [2048, 1536], P('seq'), may hold values from -0.5 to 0.5
- second_gain: bfloat16 [1536], P('seq'), may hold values from 0.099609375 to 1.8984375
- up_proj: bfloat16 [1536, 9216], P('seq'), may hold values from -0.15625 to 0.15625
- down_proj: bfloat16 [4608, 1536], P('seq'), may hold values from -0.1875 to 0.1875
Outputs:
- block_out: bfloat16 [8, 4096, 1536], P('grp', 'seq')
- grad_tokens: bfloat16 [8, 4096, 1536], P('grp', 'seq')
- grad_first_gain: float32 [1536], P('seq')
- grad_in_proj: float32 [1536, 4096], P('seq')
- grad_conv_taps: float32 [4, 2048], P(None, 'seq')
- grad_decay_param: float32 [2048], P('seq')
- grad_gate_heads: float32 [16, 128, 256], P('seq')
- grad_out_proj: float32 [2048, 1536], P('seq')
- grad_second_gain: float32 [1536], P('seq')
- grad_up_proj: float32 [1536, 9216], P('seq')
- grad_down_proj: float32 [4608, 1536], P('seq')
The draws below stay inside these ranges and needn't reach their ends.
Inputs may be any that keep to these rules, and one draw needn't show every extreme that they name: `seg_ids`: along each sequence the ids never fall and each id covers one run of consecutive tokens; a run is 1 to 2048 tokens long, and one run in each sequence has exactly that length.
All inputs are finite; a program needn't handle non-finite values.
Results may differ from the reference program's by a relative error of at most 0.012.
Values may be sent and summed in bfloat16 or wider, within the bound.
No kernel may reach another device: no remote copies, remote signals or barrier semaphores. Data moves between devices by JAX's collectives and lax.ppermute only.
A program may use at most 448 MiB of HBM per device.

```python
import math
import jax
import jax.numpy as jnp
import numpy as np
from jax import lax

D = 1536
HEADS = 16
HS = 128
LRU = 2048
FF = 4608
CONV = 4
LEN = 4096
SEQS_ALL = 8


def block_levels(own_key, shape, pieces, low, largest):
    level = 1.0
    for position, shards_of in pieces:
        heights = jax.random.uniform(jax.random.fold_in(jax.random.fold_in(own_key, 6), position), (shards_of,), jnp.float32, low / len(pieces), largest / len(pieces))
        level = level * jnp.repeat(jnp.exp(heights), shape[position] // shards_of).reshape((-1,) + (1,) * (len(shape) - 1 - position))
    return level


def split_up(amount, total, bound, slope):
    weights = [(1 << 20) // math.isqrt(rank ** slope) + 1 for rank in range(2, amount + 1)]
    spare, given = total - bound - (amount - 1), [1] * (amount - 1)
    while spare > 0:
        movable = [i for i in range(amount - 1) if given[i] < bound]
        mass, left = sum([weights[i] for i in movable]), spare
        for i in movable:
            addition = min(bound - given[i], max(1, left * weights[i] // mass), spare)
            given[i] = given[i] + addition
            spare = spare - addition
    return np.array([bound] + given)


def ragged_sizes(stream_key, amount, total, bound, lean):
    if amount == 2:
        one = jax.random.randint(stream_key, (), max(1, total - bound), min(bound, total - 1) + 1)
        return jnp.stack([one, total - one])
    lengths = jnp.asarray(split_up(amount, total, bound, lean), jnp.int32)
    twos = (amount - 1) // 2
    donor, receiver = lengths[1:1 + 2 * twos:2], lengths[2:2 + 2 * twos:2]
    margin = jnp.minimum(donor - 1, bound - receiver)
    shifted = jax.random.randint(jax.random.fold_in(stream_key, 1), (twos,), 0, 1 << 20) % (margin + 1)
    lengths = lengths.at[1:1 + 2 * twos:2].set(donor - shifted).at[2:2 + 2 * twos:2].set(receiver + shifted)
    return lengths[jax.random.permutation(jax.random.fold_in(stream_key, 2), amount)]


def gaussian(key, dims, width, most, pieces=(), kind=jnp.bfloat16):
    factor_of = block_levels(key, dims, pieces, -0.22, 0.18) if pieces else 1.0
    drawn = jax.random.normal(key, dims, jnp.float32) * width * factor_of
    return jnp.minimum(jnp.maximum(drawn, -most), most).astype(kind)


def setup_inputs(seed: int = 0) -> dict:
    arg_keys = jax.random.split(jax.random.key(seed), 13)
    tokens = gaussian(arg_keys[0], (SEQS_ALL, LEN, D), 1.0, 6.0, ((0, 4), (1, 8)))
    seg_ids = jax.vmap(lambda own: jnp.searchsorted(jnp.cumsum(ragged_sizes(own, max(4, LEN // 512), LEN, LEN // 2, 0)), jnp.arange(LEN), side="right"))(jax.random.split(arg_keys[1], SEQS_ALL)).reshape((SEQS_ALL, LEN)).astype(jnp.int32)
    cotangent = gaussian(arg_keys[2], (SEQS_ALL, LEN, D), 1.0, 6.0, ((0, 4), (1, 8)))
    first_gain = jnp.clip(1.0 + 0.18 * jax.random.normal(arg_keys[3], (D,), jnp.float32), 0.099609375, 1.8984375).astype(jnp.bfloat16)
    in_proj = gaussian(arg_keys[4], (D, 2 * LRU), D ** -0.5, 0.15625, ((0, 8),))
    conv_taps = gaussian(arg_keys[5], (CONV, LRU), CONV ** -0.5, 3.0, ((1, 8),))
    decay_param = jnp.clip(4.0 + 6.0 * jax.random.uniform(arg_keys[6], (LRU,), jnp.float32) ** block_levels(arg_keys[6], (LRU,), ((0, 8),), -0.2, 0.2), 4.0, 10.0).astype(jnp.bfloat16)
    gate_heads = gaussian(arg_keys[7], (HEADS, HS, 2 * HS), HS ** -0.5, 0.5, ((0, 8),))
    out_proj = gaussian(arg_keys[8], (LRU, D), (LRU // 16) ** -0.5, 0.5, ((0, 8),))
    second_gain = jnp.clip(1.0 + 0.18 * jax.random.normal(arg_keys[9], (D,), jnp.float32), 0.099609375, 1.8984375).astype(jnp.bfloat16)
    up_proj = gaussian(arg_keys[10], (D, 2 * FF), D ** -0.5, 0.15625, ((0, 8),))
    down_proj = gaussian(arg_keys[11], (FF, D), (FF // 4) ** -0.5, 0.1875, ((0, 8),))
    return {"tokens": tokens, "seg_ids": seg_ids, "cotangent": cotangent, "first_gain": first_gain, "in_proj": in_proj, "conv_taps": conv_taps, "decay_param": decay_param, "gate_heads": gate_heads, "out_proj": out_proj, "second_gain": second_gain, "up_proj": up_proj, "down_proj": down_proj}


@jax.custom_vjp
def low(v):
    return lax.optimization_barrier(v.astype(jnp.bfloat16)).astype(jnp.float32)

@jax.custom_vjp
def low_back(v):
    return v

def low_keep(v):
    return (low(v), None)

def low_pass(kept, grad):
    return (grad,)

def back_keep(v):
    return (v, None)

def back_low(kept, grad):
    return (low(grad),)
low.defvjp(low_keep, low_pass)
low_back.defvjp(back_keep, back_low)

def matmul_high(left, right):
    return jnp.dot(left, right, precision=lax.Precision.HIGHEST, preferred_element_type=jnp.float32)

def rms_norm(values, gain):
    return values * lax.rsqrt(lax.optimization_barrier(jnp.mean(values * values, axis=-1, keepdims=True)) + 1e-06) * gain

def gelu_tanh(values):
    return jax.nn.gelu(values, approximate=True)

def combine_pairs(earlier, later_pair):
    return (earlier[0] * later_pair[0], later_pair[0] * earlier[1] + later_pair[1])

def sequence_forward(weights, inputs, segments):
    first_gain, in_proj, conv_taps, decay_param, gate_heads, out_proj, second_gain, up_proj, down_proj = weights
    normed = low(rms_norm(inputs, first_gain))
    projected = low_back(matmul_high(normed, in_proj))
    inner_low = low(projected[:, :LRU])
    gate_pre = projected[:, LRU:]
    padded = jnp.concatenate([jnp.zeros((CONV - 1, LRU), jnp.float32), inner_low], axis=0)
    padded_ids = jnp.concatenate([jnp.full((CONV - 1,), -1, jnp.int32), segments.astype(jnp.int32)], axis=0)
    conv_sum = jnp.zeros((LEN, LRU), jnp.float32)
    for tap_index in range(CONV):
        offset = CONV - 1 - tap_index
        same_doc = (padded_ids[offset:offset + LEN] == segments.astype(jnp.int32)).astype(jnp.float32)[:, None]
        conv_sum = conv_sum + conv_taps[tap_index] * padded[offset:offset + LEN] * same_doc
    conv_low = low(conv_sum)
    gate_raw = low_back(jnp.einsum('rhi,hij->rhj', conv_low.reshape(LEN, HEADS, HS), gate_heads, precision=lax.Precision.HIGHEST))
    rate_gate = jax.nn.sigmoid(gate_raw[:, :, :HS]).reshape(LEN, LRU)
    input_gate = jax.nn.sigmoid(gate_raw[:, :, HS:]).reshape(LEN, LRU)
    decay_step = jnp.exp(-8.0 * rate_gate * jax.nn.softplus(-decay_param))
    root_term = jnp.sqrt(1.0 - decay_step * decay_step + 0.001)
    drive_term = root_term * input_gate * conv_low
    starts = jnp.concatenate([jnp.ones((1,), jnp.float32), (segments[1:] != segments[:-1]).astype(jnp.float32)], axis=0)
    keep_rate = decay_step * (1.0 - starts)[:, None]
    lru_state = lax.associative_scan(combine_pairs, (keep_rate, drive_term))[1]
    branch = low(lru_state * gelu_tanh(gate_pre))
    mixed = inputs + low_back(matmul_high(branch, out_proj))
    second = low(rms_norm(mixed, second_gain))
    expanded = low_back(matmul_high(second, up_proj))
    hidden = low(gelu_tanh(expanded[:, :FF]) * expanded[:, FF:])
    return mixed + low_back(matmul_high(hidden, down_proj))

def reference(tokens, seg_ids, cotangent, first_gain, in_proj, conv_taps, decay_param, gate_heads, out_proj, second_gain, up_proj, down_proj):
    params = (first_gain.astype(jnp.float32), in_proj.astype(jnp.float32), conv_taps.astype(jnp.float32), decay_param.astype(jnp.float32), gate_heads.astype(jnp.float32), out_proj.astype(jnp.float32), second_gain.astype(jnp.float32), up_proj.astype(jnp.float32), down_proj.astype(jnp.float32))

    def one_sequence(totals, items):
        seq_tokens, seq_segments, seq_cotangent = items

        def forward(weights, inputs):
            return sequence_forward(weights, inputs, seq_segments)
        result, pullback = jax.vjp(forward, params, seq_tokens.astype(jnp.float32))
        grad_params, grad_inputs = pullback(seq_cotangent.astype(jnp.float32))
        totals = jax.tree.map(jnp.add, totals, grad_params)
        return (totals, (result.astype(jnp.bfloat16), grad_inputs.astype(jnp.bfloat16)))
    start_totals = jax.tree.map(jnp.zeros_like, params)
    totals, outputs = lax.scan(one_sequence, start_totals, (tokens, seg_ids, cotangent))
    return (outputs[0], outputs[1], totals[0], totals[1], totals[2], totals[3], totals[4], totals[5], totals[6], totals[7], totals[8])
```

```python
import functools

import jax
import jax.numpy as jnp
from jax import lax
from jax.experimental import pallas as pl
from jax.experimental.pallas import tpu as pltpu
from jax.sharding import PartitionSpec as P

D = 1536
HEADS = 16
HS = 128
LRU = 2048
FF = 4608
CONV = 4
CHUNKS = 8
HALO = 8
F32 = jnp.float32
BF16 = jnp.bfloat16


def from_behind(value, axis, steps):
    count = lax.axis_size(axis)
    first, last = (max(0, -steps), min(count, count - steps))
    return lax.ppermute(value, axis, [(source, source + steps) for source in range(first, last)])


def gelu_parts(v):
    k = 0.7978845608028654
    square = v * v
    t = jnp.tanh(k * v * (1.0 + 0.044715 * square))
    half = 0.5 * (1.0 + t)
    slope = half + 0.5 * v * (1.0 - t * t) * (k * (1.0 + 3.0 * 0.044715 * square))
    return v * half, slope


def gelu_tanh(v):
    k = 0.7978845608028654
    return 0.5 * v * (1.0 + jnp.tanh(k * v * (1.0 + 0.044715 * v * v)))


def sigmoid(v):
    return 0.5 * jnp.tanh(0.5 * v) + 0.5


def drive_values(q_rate, q_input, soft):
    rate = sigmoid(q_rate)
    inp = sigmoid(q_input)
    decay = jnp.exp(-8.0 * rate * soft)
    root = jnp.sqrt(1.0 - decay * decay + 0.001)
    return rate, inp, decay, root


def mixer_forward_kernel(
    u_ref, halo_ref, dist_ref, gates_ref, taps_ref, soft_ref,
    c_ref, keep_ref, state_ref, prod_ref, chunk_ref,
    ext_s, c_s, rate_s, inp_s,
):
    seqs, rows, _ = u_ref.shape
    step = rows // CHUNKS
    soft = soft_ref[...]
    for b in range(seqs):
        ext_s[b, pl.ds(0, HALO), :] = halo_ref[b].astype(F32)
        ext_s[b, pl.ds(HALO, rows), :] = u_ref[b].astype(F32)

        def conv_chunk(n, _):
            at = pl.multiple_of(n * 64, 64)
            total = taps_ref[0:1, :] * ext_s[b, pl.ds(at + HALO, 64), :]
            for k in range(1, CONV):
                same = (dist_ref[b, pl.ds(at, 64), :] >= float(k)).astype(F32)
                total = total + taps_ref[k : k + 1, :] * ext_s[b, pl.ds(at + HALO - k, 64), :] * same
            low = total.astype(BF16)
            c_ref[b, pl.ds(at, 64), :] = low
            c_s[b, pl.ds(at, 64), :] = low.astype(F32)
            return 0

        lax.fori_loop(0, rows // 64, conv_chunk, 0)
        both = jnp.dot(c_ref[b], gates_ref[0], preferred_element_type=F32)
        rate_s[b] = both[:, :HS]
        inp_s[b] = both[:, HS:]

    def scan_step(j, carry):
        new = []
        for b in range(seqs):
            at = pl.ds(j, CHUNKS, stride=step)
            state, prod = carry[b]
            _, inp, decay, root = drive_values(rate_s[b, at, :], inp_s[b, at, :], soft)
            keep = decay * (dist_ref[b, at, :] >= 1.0).astype(F32)
            state = keep * state + root * inp * c_s[b, at, :]
            prod = keep * prod
            keep_ref[b, at, :] = keep
            state_ref[b, at, :] = state
            prod_ref[b, at, :] = prod
            new.append((state, prod))
        return tuple(new)

    zero, one = jnp.zeros((CHUNKS, HS), F32), jnp.ones((CHUNKS, HS), F32)
    ends = lax.fori_loop(0, step, scan_step, ((zero, one),) * seqs, unroll=4)
    for b in range(seqs):
        chunk_ref[b, 0] = ends[b][0]
        chunk_ref[b, 1] = ends[b][1]


def reverse_kernel(
    grad_ref, gate_ref, keep_ref, state_ref,
    dg_ref, local_ref, prod_ref, chunk_ref,
    dh_s,
):
    seqs, rows, _ = grad_ref.shape
    step = rows // CHUNKS
    for b in range(seqs):

        def point(n, _):
            at = pl.ds(pl.multiple_of(n * 64, 64), 64)
            act, slope = gelu_parts(gate_ref[b, at, :])
            grad = grad_ref[b, at, :]
            dh_s[b, at, :] = grad * act
            dg_ref[b, at, :] = (grad * state_ref[b, at, :] * slope).astype(BF16)
            return 0

        lax.fori_loop(0, rows // 64, point, 0)

    def scan_step(n, carry):
        j = step - 1 - n
        new = []
        for b in range(seqs):
            at = pl.ds(j, CHUNKS, stride=step)
            pull, prod = carry[b]
            keep = keep_ref[b, at, :]
            local = dh_s[b, at, :] + pull
            local_ref[b, at, :] = local
            prod_ref[b, at, :] = prod
            new.append((keep * local, keep * prod))
        return tuple(new)

    zero, one = jnp.zeros((CHUNKS, HS), F32), jnp.ones((CHUNKS, HS), F32)
    ends = lax.fori_loop(0, step, scan_step, ((zero, one),) * seqs, unroll=4)
    for b in range(seqs):
        chunk_ref[b, 0] = ends[b][0]
        chunk_ref[b, 1] = ends[b][1]


def mixer_backward_kernel(
    local_ref, prod_ref, carry_ref, state_ref, before_ref, c_ref, u_ref, halo_ref, dist_ref,
    gates_ref, taps_ref, soft_ref,
    du_ref, tail_ref, edge_ref, ggate_ref, gtaps_ref, gdecay_ref,
    q_s, dq_s, dc_s, h_s, ext_s, dist_s,
):
    seqs, rows, _ = local_ref.shape
    step = rows // CHUNKS
    soft = soft_ref[...]
    ggate = jnp.zeros((HS, 2 * HS), F32)
    decay_sum = jnp.zeros((8, HS), F32)
    taps_sum = [jnp.zeros((8, HS), F32) for _ in range(CONV)]

    def fold(value):
        return jnp.sum(value.reshape(value.shape[0] // 8, 8, HS), axis=0)

    for b in range(seqs):
        q_s[...] = jnp.dot(c_ref[b], gates_ref[0], preferred_element_type=F32)
        h_s[pl.ds(0, HALO), :] = before_ref[b]
        h_s[pl.ds(HALO, rows), :] = state_ref[b]

        def point(n, total):
            at = pl.ds(pl.multiple_of(n * step, step), step)
            lam = local_ref[b, at, :] + prod_ref[b, at, :] * carry_ref[b, pl.ds(n, 1), :]
            rate, inp, decay, root = drive_values(q_s[at, :HS], q_s[at, HS:], soft)
            conv = c_ref[b, at, :].astype(F32)
            is_open = (dist_ref[b, at, :] >= 1.0).astype(F32)
            prev = h_s[pl.ds(pl.multiple_of(n * step, step) + HALO - 1, step), :]
            lam_root = lam * root
            lam_inp = lam * inp
            grad_decay = lam * prev * is_open - lam_inp * conv * decay / root
            grad_log = grad_decay * decay
            rated = grad_log * rate
            dq_s[at, :HS] = (-8.0 * soft * rated * (1.0 - rate)).astype(BF16)
            dq_s[at, HS:] = (lam_root * conv * inp * (1.0 - inp)).astype(BF16)
            dc_s[at, :] = lam_root * inp
            return total + fold(rated)

        decay_sum = lax.fori_loop(0, CHUNKS, point, decay_sum)
        dc_s[pl.ds(0, rows), :] += lax.dot_general(
            dq_s[...], gates_ref[0], (((1,), (1,)), ((), ())), preferred_element_type=F32
        )
        dc_s[pl.ds(rows, HALO), :] = jnp.zeros((HALO, HS), F32)
        ggate = ggate + lax.dot_general(
            c_ref[b], dq_s[...], (((0,), (0,)), ((), ())), preferred_element_type=F32
        )
        ext_s[pl.ds(0, HALO), :] = halo_ref[b].astype(F32)
        ext_s[pl.ds(HALO, rows), :] = u_ref[b].astype(F32)
        dist_s[pl.ds(0, rows), :] = dist_ref[b]
        dist_s[pl.ds(rows, HALO), :] = jnp.zeros((HALO, HS), F32)

        def conv_chunk(n, totals):
            at = pl.multiple_of(n * 64, 64)
            grad = dc_s[pl.ds(at, 64), :]
            far = dist_s[pl.ds(at, 64), :]
            out = taps_ref[0:1, :] * grad
            totals = list(totals)
            totals[0] = totals[0] + fold(grad * ext_s[pl.ds(at + HALO, 64), :])
            for k in range(1, CONV):
                masked = jnp.where(far >= float(k), grad, 0.0)
                totals[k] = totals[k] + fold(masked * ext_s[pl.ds(at + HALO - k, 64), :])
                ahead = jnp.where(
                    dist_s[pl.ds(at + k, 64), :] >= float(k), dc_s[pl.ds(at + k, 64), :], 0.0
                )
                out = out + taps_ref[k : k + 1, :] * ahead
            du_ref[b, pl.ds(at, 64), :] = out.astype(BF16)

            @pl.when(n == rows // 64 - 1)
            def _():
                tail_ref[b] = out[64 - HALO :, :]

            return tuple(totals)

        taps_sum = list(lax.fori_loop(0, rows // 64, conv_chunk, tuple(taps_sum)))
        head = dc_s[pl.ds(0, HALO), :]
        far = dist_s[pl.ds(0, HALO), :]
        zeros = jnp.zeros((HALO, HS), F32)
        edge = zeros
        for k in range(1, CONV):
            masked = jnp.where(far >= float(k), head, 0.0)
            both = jnp.concatenate([zeros, masked], axis=0)
            edge = edge + taps_ref[k : k + 1, :] * both[k : k + HALO, :]
        edge_ref[b] = edge
    ggate_ref[0] = ggate
    gdecay_ref[...] = jnp.broadcast_to(
        8.0 * jnp.sum(decay_sum, axis=0, keepdims=True), (8, HS)
    )
    gtaps_ref[...] = jnp.concatenate(
        [jnp.sum(t, axis=0, keepdims=True) for t in taps_sum] + [jnp.zeros((8 - CONV, HS), F32)],
        axis=0,
    )


def head_block(lead, rows):
    return pl.BlockSpec((lead, rows, HS), lambda h: (0, 0, h))


def shared_block(shape):
    return pl.BlockSpec(shape, lambda h: (0,) * len(shape))


def pair_block(seqs):
    return pl.BlockSpec((seqs, 2, CHUNKS, HS), lambda h: (0, 0, 0, h))


PARAMS = pltpu.CompilerParams(vmem_limit_bytes=40 * 1024 * 1024)


def mixer_forward(u, halo, dist, gates, taps, soft):
    seqs, rows, _ = u.shape
    full = head_block(seqs, rows)
    wide = jax.ShapeDtypeStruct((seqs, rows, LRU), F32)
    return pl.pallas_call(
        mixer_forward_kernel,
        grid=(HEADS,),
        in_specs=[
            full,
            head_block(seqs, HALO),
            shared_block((seqs, rows, HS)),
            pl.BlockSpec((1, HS, 2 * HS), lambda h: (h, 0, 0)),
            pl.BlockSpec((CONV, HS), lambda h: (0, h)),
            pl.BlockSpec((1, HS), lambda h: (0, h)),
        ],
        out_specs=[full, full, full, full, pair_block(seqs)],
        out_shape=[
            jax.ShapeDtypeStruct((seqs, rows, LRU), BF16),
            wide,
            wide,
            wide,
            jax.ShapeDtypeStruct((seqs, 2, CHUNKS, LRU), F32),
        ],
        scratch_shapes=[
            pltpu.VMEM((seqs, rows + HALO, HS), F32),
            pltpu.VMEM((seqs, rows, HS), F32),
            pltpu.VMEM((seqs, rows, HS), F32),
            pltpu.VMEM((seqs, rows, HS), F32),
        ],
        compiler_params=PARAMS,
        name="mixer_forward",
    )(u, halo, dist, gates, taps, soft)


def mixer_reverse(grad, gate, keep, state):
    seqs, rows, _ = grad.shape
    full = head_block(seqs, rows)
    wide = jax.ShapeDtypeStruct((seqs, rows, LRU), F32)
    return pl.pallas_call(
        reverse_kernel,
        grid=(HEADS,),
        in_specs=[full, full, full, full],
        out_specs=[full, full, full, pair_block(seqs)],
        out_shape=[
            jax.ShapeDtypeStruct((seqs, rows, LRU), BF16),
            wide,
            wide,
            jax.ShapeDtypeStruct((seqs, 2, CHUNKS, LRU), F32),
        ],
        scratch_shapes=[pltpu.VMEM((seqs, rows, HS), F32)],
        compiler_params=PARAMS,
        name="mixer_reverse",
    )(grad, gate, keep, state)


def mixer_backward(local, prod, carry, state, before, c, u, halo, dist, gates, taps, soft):
    seqs, rows, _ = local.shape
    full = head_block(seqs, rows)
    small = head_block(seqs, HALO)
    gate_block = pl.BlockSpec((1, HS, 2 * HS), lambda h: (h, 0, 0))
    row_block = pl.BlockSpec((8, HS), lambda h: (0, h))
    return pl.pallas_call(
        mixer_backward_kernel,
        grid=(HEADS,),
        in_specs=[
            full,
            full,
            head_block(seqs, CHUNKS),
            full,
            small,
            full,
            full,
            small,
            shared_block((seqs, rows, HS)),
            gate_block,
            pl.BlockSpec((CONV, HS), lambda h: (0, h)),
            pl.BlockSpec((1, HS), lambda h: (0, h)),
        ],
        out_specs=[full, small, small, gate_block, row_block, row_block],
        out_shape=[
            jax.ShapeDtypeStruct((seqs, rows, LRU), BF16),
            jax.ShapeDtypeStruct((seqs, HALO, LRU), F32),
            jax.ShapeDtypeStruct((seqs, HALO, LRU), F32),
            jax.ShapeDtypeStruct((HEADS, HS, 2 * HS), F32),
            jax.ShapeDtypeStruct((8, LRU), F32),
            jax.ShapeDtypeStruct((8, LRU), F32),
        ],
        scratch_shapes=[
            pltpu.VMEM((rows, 2 * HS), F32),
            pltpu.VMEM((rows, 2 * HS), BF16),
            pltpu.VMEM((rows + HALO, HS), F32),
            pltpu.VMEM((rows + HALO, HS), F32),
            pltpu.VMEM((rows + HALO, HS), F32),
            pltpu.VMEM((rows + HALO, HS), F32),
        ],
        compiler_params=PARAMS,
        name="mixer_backward",
    )(local, prod, carry, state, before, c, u, halo, dist, gates, taps, soft)


def gather_rows(shard):
    parts = lax.axis_size("grp")
    rows = shard.shape[0] // parts
    own = lax.dynamic_slice_in_dim(shard, lax.axis_index("grp") * rows, rows, 0)
    return lax.all_gather(own, ("seq", "grp"), axis=0, tiled=True)


def reduce_rows(partial):
    part = lax.psum_scatter(partial, ("seq", "grp"), scatter_dimension=0, tiled=True)
    return lax.all_gather(part, "grp", axis=0, tiled=True).astype(F32)


def shard_carry(ends, prods, reverse):
    count = lax.axis_size("seq")
    place = lax.axis_index("seq")
    both = lax.all_gather(jnp.stack([ends, prods]), "seq")
    carry = jnp.zeros_like(ends)
    for step in range(count - 1):
        source = count - 1 - step if reverse else step
        ahead = source > place if reverse else source < place
        carry = jnp.where(ahead, both[source, 0] + both[source, 1] * carry, carry)
    return carry


def chunk_ends(chunks, reverse):
    state = jnp.zeros_like(chunks[:, 0, 0])
    prod = jnp.ones_like(state)
    order = range(CHUNKS - 1, -1, -1) if reverse else range(CHUNKS)
    for n in order:
        state = chunks[:, 0, n] + chunks[:, 1, n] * state
        prod = chunks[:, 1, n] * prod
    return state, prod


def chunk_carries(chunks, carry, reverse):
    order = range(CHUNKS - 1, -1, -1) if reverse else range(CHUNKS)
    found = [None] * CHUNKS
    for n in order:
        found[n] = carry
        carry = chunks[:, 0, n] + chunks[:, 1, n] * carry
    return jnp.stack(found, axis=1)


def norm_back(values, scale, gain, grad_normed):
    weighted = grad_normed * gain
    grad_gain = jnp.sum(grad_normed * values * scale, axis=0)
    cubed = scale * scale * scale
    grad_values = scale * weighted - values * cubed * jnp.mean(
        weighted * values, axis=-1, keepdims=True
    )
    return (grad_gain, grad_values)


def body(
    tokens, seg_ids, cotangent, first_gain, in_proj, conv_taps, decay_param, gate_heads,
    out_proj, second_gain, up_proj, down_proj,
):
    seq_count, shard_len, _ = tokens.shape
    row_count = seq_count * shard_len
    edge_len = CONV - 1
    place = lax.axis_index("seq")
    last = lax.axis_size("seq") - 1

    small = jnp.concatenate(
        [first_gain, second_gain, decay_param, conv_taps.reshape(-1)]
    )
    small_all = lax.all_gather(small, "seq")
    n_gain, n_lru = first_gain.shape[0], decay_param.shape[0]
    gain_one = small_all[:, :n_gain].reshape(D).astype(F32)
    gain_two = small_all[:, n_gain : 2 * n_gain].reshape(D).astype(F32)
    decay_float = small_all[:, 2 * n_gain : 2 * n_gain + n_lru].reshape(LRU).astype(F32)
    taps_all = (
        small_all[:, 2 * n_gain + n_lru :].reshape(-1, CONV, n_lru).transpose(1, 0, 2)
    ).reshape(CONV, LRU).astype(F32)
    proj_in = gather_rows(in_proj)
    gates_all = lax.all_gather(gate_heads, "seq", axis=0, tiled=True)
    proj_out = gather_rows(out_proj)
    proj_up = gather_rows(up_proj)
    proj_down = gather_rows(down_proj)

    inputs = tokens.reshape(row_count, D).astype(F32)
    first_scale = lax.rsqrt(jnp.mean(inputs * inputs, axis=-1, keepdims=True) + 1e-06)
    first_normed = (inputs * first_scale * gain_one).astype(BF16)
    inner_low = jnp.dot(first_normed, proj_in[:, :LRU], preferred_element_type=F32).astype(BF16)
    inner_low = inner_low.reshape(seq_count, shard_len, LRU)
    gate_pre = jnp.dot(first_normed, proj_in[:, LRU:], preferred_element_type=F32)

    prev_inner = from_behind(inner_low[:, shard_len - HALO :], "seq", 1)
    prev_ids = from_behind(seg_ids[:, shard_len - edge_len :], "seq", 1)
    prev_ids = jnp.where(place == 0, -1, prev_ids)
    ext_ids = jnp.concatenate([prev_ids, seg_ids], axis=1)
    dist = jnp.zeros((seq_count, shard_len), F32)
    for k in range(1, CONV):
        dist = dist + (ext_ids[:, edge_len - k : edge_len - k + shard_len] == seg_ids).astype(F32)
    dist = jnp.broadcast_to(dist[:, :, None], (seq_count, shard_len, HS))
    soft = jax.nn.softplus(-decay_float).reshape(1, LRU)

    conv_low, keep, state_part, prod_part, chunks = mixer_forward(
        inner_low, prev_inner, dist, gates_all, taps_all, soft
    )
    end_state, end_prod = chunk_ends(chunks, False)
    carry_in = shard_carry(end_state, end_prod, False)
    carries = chunk_carries(chunks, carry_in, False)
    chunked = (seq_count, CHUNKS, shard_len // CHUNKS, LRU)
    state = (
        state_part.reshape(chunked) + prod_part.reshape(chunked) * carries[:, :, None, :]
    ).reshape(row_count, LRU)
    branch = (state * gelu_tanh(gate_pre)).astype(BF16)
    resid = inputs + jnp.dot(branch, proj_out, preferred_element_type=F32)
    second_scale = lax.rsqrt(jnp.mean(resid * resid, axis=-1, keepdims=True) + 1e-06)
    second_normed = (resid * second_scale * gain_two).astype(BF16)
    expanded_gate = jnp.dot(second_normed, proj_up[:, :FF], preferred_element_type=F32)
    expanded_up = jnp.dot(second_normed, proj_up[:, FF:], preferred_element_type=F32)
    hidden = (gelu_tanh(expanded_gate) * expanded_up).astype(BF16)
    ffn_out = jnp.dot(hidden, proj_down, preferred_element_type=F32)
    block_out = (resid + ffn_out).astype(BF16).reshape(seq_count, shard_len, D)

    grad_out = cotangent.reshape(row_count, D)
    grad_down = jnp.einsum("rf,rd->fd", hidden, grad_out, preferred_element_type=F32).astype(BF16)
    down_total = reduce_rows(grad_down)
    grad_hidden = jnp.einsum("rd,fd->rf", grad_out, proj_down, preferred_element_type=F32)
    act, slope = gelu_parts(expanded_gate)
    grad_expanded = jnp.concatenate(
        [(grad_hidden * expanded_up * slope).astype(BF16), (grad_hidden * act).astype(BF16)], axis=1
    )
    grad_up = jnp.einsum(
        "rd,rf->df", second_normed, grad_expanded, preferred_element_type=F32
    ).astype(BF16)
    up_total = reduce_rows(grad_up)
    grad_second_normed = jnp.einsum(
        "rf,df->rd", grad_expanded, proj_up, preferred_element_type=F32
    )
    grad_gain_two, grad_from_second = norm_back(resid, second_scale, gain_two, grad_second_normed)
    grad_resid = grad_out.astype(F32) + grad_from_second
    grad_mixer = grad_resid.astype(BF16)
    grad_out_proj = jnp.einsum(
        "rl,rd->ld", branch, grad_mixer, preferred_element_type=F32
    ).astype(BF16)
    out_total = reduce_rows(grad_out_proj)
    grad_branch = jnp.einsum("rd,ld->rl", grad_mixer, proj_out, preferred_element_type=F32)

    wide = (seq_count, shard_len, LRU)
    grad_gate, local, rev_prod, rev_chunks = mixer_reverse(
        grad_branch.reshape(wide), gate_pre.reshape(wide), keep, state.reshape(wide)
    )
    head_pull, head_prod = chunk_ends(rev_chunks, True)
    rev_carry = shard_carry(head_pull, head_prod, True)
    rev_carries = chunk_carries(rev_chunks, rev_carry, True)
    before = jnp.broadcast_to(carry_in[:, None], (seq_count, HALO, LRU))
    du, tail, edge, grad_gates, grad_taps, grad_decay = mixer_backward(
        local, rev_prod, rev_carries, state.reshape(wide), before, conv_low, inner_low,
        prev_inner, dist, gates_all, taps_all, soft,
    )
    gates_total = lax.psum_scatter(
        grad_gates.astype(BF16), "seq", scatter_dimension=0, tiled=True
    )
    gates_total = lax.psum(gates_total, "grp").astype(F32)
    returned = from_behind(edge[:, HALO - edge_len :].astype(BF16), "seq", -1).astype(F32)
    returned = jnp.pad(returned, ((0, 0), (HALO - edge_len, 0), (0, 0)))
    grad_inner = lax.dynamic_update_slice(
        du, (tail + returned).astype(BF16), (0, shard_len - HALO, 0)
    )
    grad_projected = jnp.concatenate(
        [grad_inner.reshape(row_count, LRU), grad_gate.reshape(row_count, LRU)], axis=1
    )
    grad_in = jnp.einsum(
        "rd,rp->dp", first_normed, grad_projected, preferred_element_type=F32
    ).astype(BF16)
    in_total = reduce_rows(grad_in)
    grad_first_normed = jnp.einsum(
        "rp,dp->rd", grad_projected, proj_in, preferred_element_type=F32
    )
    grad_gain_one, grad_from_first = norm_back(inputs, first_scale, gain_one, grad_first_normed)
    grad_tokens = (grad_resid + grad_from_first).astype(BF16).reshape(seq_count, shard_len, D)
    grad_decay_row = grad_decay[0] * jax.nn.sigmoid(-decay_float)
    flat = jnp.concatenate(
        [grad_gain_one, grad_gain_two, grad_decay_row, grad_taps[:CONV].reshape(-1)]
    )
    flat = lax.psum(flat, ("grp", "seq"))
    first_total = lax.dynamic_slice_in_dim(flat, place * n_gain, n_gain)
    second_total = lax.dynamic_slice_in_dim(flat, D + place * n_gain, n_gain)
    decay_total = lax.dynamic_slice_in_dim(flat, 2 * D + place * n_lru, n_lru)
    taps_total = lax.dynamic_slice_in_dim(
        flat[2 * D + LRU :].reshape(CONV, LRU), place * n_lru, n_lru, 1
    )
    return (
        block_out, grad_tokens, first_total, in_total, taps_total, decay_total, gates_total,
        out_total, second_total, up_total, down_total,
    )


def solution(mesh):
    in_specs = (
        P("grp", "seq", None),
        P("grp", "seq"),
        P("grp", "seq", None),
        P("seq"),
        P("seq", None),
        P(None, "seq"),
        P("seq"),
        P("seq", None, None),
        P("seq", None),
        P("seq"),
        P("seq", None),
        P("seq", None),
    )
    out_specs = (
        P("grp", "seq", None),
        P("grp", "seq", None),
        P("seq"),
        P("seq", None),
        P(None, "seq"),
        P("seq"),
        P("seq", None, None),
        P("seq", None),
        P("seq"),
        P("seq", None),
        P("seq", None),
    )
    return jax.shard_map(body, mesh=mesh, in_specs=in_specs, out_specs=out_specs, check_vma=False)
```

```python
import functools

import jax
import jax.numpy as jnp
from jax import lax
from jax.experimental import pallas as pl
from jax.experimental.pallas import tpu as pltpu
from jax.sharding import PartitionSpec as P

D = 1536
HEADS = 16
HS = 128
LRU = 2048
FF = 4608
CONV = 4
CHUNKS = 8
HALO = 8
F32 = jnp.float32
BF16 = jnp.bfloat16


def from_behind(value, axis, steps):
    count = lax.axis_size(axis)
    first, last = (max(0, -steps), min(count, count - steps))
    return lax.ppermute(value, axis, [(source, source + steps) for source in range(first, last)])


def gelu_parts(v):
    k = 0.7978845608028654
    square = v * v
    t = jnp.tanh(k * v * (1.0 + 0.044715 * square))
    half = 0.5 * (1.0 + t)
    slope = half + 0.5 * v * (1.0 - t * t) * (k * (1.0 + 3.0 * 0.044715 * square))
    return v * half, slope


def gelu_tanh(v):
    k = 0.7978845608028654
    return 0.5 * v * (1.0 + jnp.tanh(k * v * (1.0 + 0.044715 * v * v)))


def sigmoid(v):
    return 0.5 * jnp.tanh(0.5 * v) + 0.5


def drive_values(q_rate, q_input, soft):
    rate = sigmoid(q_rate)
    inp = sigmoid(q_input)
    decay = jnp.exp(-8.0 * rate * soft)
    root = jnp.sqrt(1.0 - decay * decay + 0.001)
    return rate, inp, decay, root


def mixer_forward_kernel(
    u_ref, halo_ref, dist_ref, gates_ref, taps_ref, soft_ref,
    c_ref, keep_ref, state_ref, prod_ref, chunk_ref,
    ext_s, c_s, rate_s, inp_s,
):
    seqs, rows, _ = u_ref.shape
    step = rows // CHUNKS
    soft = soft_ref[...]
    for b in range(seqs):
        ext_s[b, pl.ds(0, HALO), :] = halo_ref[b].astype(F32)
        ext_s[b, pl.ds(HALO, rows), :] = u_ref[b].astype(F32)

        def conv_chunk(n, _):
            at = pl.multiple_of(n * 64, 64)
            total = taps_ref[0:1, :] * ext_s[b, pl.ds(at + HALO, 64), :]
            for k in range(1, CONV):
                same = (dist_ref[b, pl.ds(at, 64), :] >= float(k)).astype(F32)
                total = total + taps_ref[k : k + 1, :] * ext_s[b, pl.ds(at + HALO - k, 64), :] * same
            low = total.astype(BF16)
            c_ref[b, pl.ds(at, 64), :] = low
            c_s[b, pl.ds(at, 64), :] = low.astype(F32)
            return 0

        lax.fori_loop(0, rows // 64, conv_chunk, 0)
        both = jnp.dot(c_ref[b], gates_ref[0], preferred_element_type=F32)
        rate_s[b] = both[:, :HS]
        inp_s[b] = both[:, HS:]

    def scan_step(j, carry):
        new = []
        for b in range(seqs):
            at = pl.ds(j, CHUNKS, stride=step)
            state, prod = carry[b]
            _, inp, decay, root = drive_values(rate_s[b, at, :], inp_s[b, at, :], soft)
            keep = decay * (dist_ref[b, at, :] >= 1.0).astype(F32)
            state = keep * state + root * inp * c_s[b, at, :]
            prod = keep * prod
            keep_ref[b, at, :] = keep
            state_ref[b, at, :] = state
            prod_ref[b, at, :] = prod
            new.append((state, prod))
        return tuple(new)

    zero, one = jnp.zeros((CHUNKS, HS), F32), jnp.ones((CHUNKS, HS), F32)
    ends = lax.fori_loop(0, step, scan_step, ((zero, one),) * seqs, unroll=4)
    for b in range(seqs):
        chunk_ref[b, 0] = ends[b][0]
        chunk_ref[b, 1] = ends[b][1]


def reverse_kernel(
    grad_ref, gate_ref, keep_ref, state_ref,
    dg_ref, local_ref, prod_ref, chunk_ref,
    dh_s,
):
    seqs, rows, _ = grad_ref.shape
    step = rows // CHUNKS
    for b in range(seqs):

        def point(n, _):
            at = pl.ds(pl.multiple_of(n * 64, 64), 64)
            act, slope = gelu_parts(gate_ref[b, at, :])
            grad = grad_ref[b, at, :]
            dh_s[b, at, :] = grad * act
            dg_ref[b, at, :] = (grad * state_ref[b, at, :] * slope).astype(BF16)
            return 0

        lax.fori_loop(0, rows // 64, point, 0)

    def scan_step(n, carry):
        j = step - 1 - n
        new = []
        for b in range(seqs):
            at = pl.ds(j, CHUNKS, stride=step)
            pull, prod = carry[b]
            keep = keep_ref[b, at, :]
            local = dh_s[b, at, :] + pull
            local_ref[b, at, :] = local
            prod_ref[b, at, :] = prod
            new.append((keep * local, keep * prod))
        return tuple(new)

    zero, one = jnp.zeros((CHUNKS, HS), F32), jnp.ones((CHUNKS, HS), F32)
    ends = lax.fori_loop(0, step, scan_step, ((zero, one),) * seqs, unroll=4)
    for b in range(seqs):
        chunk_ref[b, 0] = ends[b][0]
        chunk_ref[b, 1] = ends[b][1]


def mixer_backward_kernel(
    local_ref, prod_ref, carry_ref, state_ref, before_ref, c_ref, u_ref, halo_ref, dist_ref,
    gates_ref, taps_ref, soft_ref,
    du_ref, tail_ref, edge_ref, ggate_ref, gtaps_ref, gdecay_ref,
    q_s, dq_s, dc_s, h_s, ext_s, dist_s,
):
    seqs, rows, _ = local_ref.shape
    step = rows // CHUNKS
    soft = soft_ref[...]
    ggate = jnp.zeros((HS, 2 * HS), F32)
    decay_sum = jnp.zeros((8, HS), F32)
    taps_sum = [jnp.zeros((8, HS), F32) for _ in range(CONV)]

    def fold(value):
        return jnp.sum(value.reshape(value.shape[0] // 8, 8, HS), axis=0)

    for b in range(seqs):
        q_s[...] = jnp.dot(c_ref[b], gates_ref[0], preferred_element_type=F32)
        h_s[pl.ds(0, HALO), :] = before_ref[b]
        h_s[pl.ds(HALO, rows), :] = state_ref[b]

        def point(n, total):
            at = pl.ds(pl.multiple_of(n * step, step), step)
            lam = local_ref[b, at, :] + prod_ref[b, at, :] * carry_ref[b, pl.ds(n, 1), :]
            rate, inp, decay, root = drive_values(q_s[at, :HS], q_s[at, HS:], soft)
            conv = c_ref[b, at, :].astype(F32)
            is_open = (dist_ref[b, at, :] >= 1.0).astype(F32)
            prev = h_s[pl.ds(pl.multiple_of(n * step, step) + HALO - 1, step), :]
            lam_root = lam * root
            lam_inp = lam * inp
            grad_decay = lam * prev * is_open - lam_inp * conv * decay / root
            grad_log = grad_decay * decay
            rated = grad_log * rate
            dq_s[at, :HS] = (-8.0 * soft * rated * (1.0 - rate)).astype(BF16)
            dq_s[at, HS:] = (lam_root * conv * inp * (1.0 - inp)).astype(BF16)
            dc_s[at, :] = lam_root * inp
            return total + fold(rated)

        decay_sum = lax.fori_loop(0, CHUNKS, point, decay_sum)
        dc_s[pl.ds(0, rows), :] += lax.dot_general(
            dq_s[...], gates_ref[0], (((1,), (1,)), ((), ())), preferred_element_type=F32
        )
        dc_s[pl.ds(rows, HALO), :] = jnp.zeros((HALO, HS), F32)
        ggate = ggate + lax.dot_general(
            c_ref[b], dq_s[...], (((0,), (0,)), ((), ())), preferred_element_type=F32
        )
        ext_s[pl.ds(0, HALO), :] = halo_ref[b].astype(F32)
        ext_s[pl.ds(HALO, rows), :] = u_ref[b].astype(F32)
        dist_s[pl.ds(0, rows), :] = dist_ref[b]
        dist_s[pl.ds(rows, HALO), :] = jnp.zeros((HALO, HS), F32)

        def conv_chunk(n, totals):
            at = pl.multiple_of(n * 64, 64)
            grad = dc_s[pl.ds(at, 64), :]
            far = dist_s[pl.ds(at, 64), :]
            out = taps_ref[0:1, :] * grad
            totals = list(totals)
            totals[0] = totals[0] + fold(grad * ext_s[pl.ds(at + HALO, 64), :])
            for k in range(1, CONV):
                masked = jnp.where(far >= float(k), grad, 0.0)
                totals[k] = totals[k] + fold(masked * ext_s[pl.ds(at + HALO - k, 64), :])
                ahead = jnp.where(
                    dist_s[pl.ds(at + k, 64), :] >= float(k), dc_s[pl.ds(at + k, 64), :], 0.0
                )
                out = out + taps_ref[k : k + 1, :] * ahead
            du_ref[b, pl.ds(at, 64), :] = out.astype(BF16)

            @pl.when(n == rows // 64 - 1)
            def _():
                tail_ref[b] = out[64 - HALO :, :]

            return tuple(totals)

        taps_sum = list(lax.fori_loop(0, rows // 64, conv_chunk, tuple(taps_sum)))
        head = dc_s[pl.ds(0, HALO), :]
        far = dist_s[pl.ds(0, HALO), :]
        zeros = jnp.zeros((HALO, HS), F32)
        edge = zeros
        for k in range(1, CONV):
            masked = jnp.where(far >= float(k), head, 0.0)
            both = jnp.concatenate([zeros, masked], axis=0)
            edge = edge + taps_ref[k : k + 1, :] * both[k : k + HALO, :]
        edge_ref[b] = edge
    ggate_ref[0] = ggate
    gdecay_ref[...] = jnp.broadcast_to(
        8.0 * jnp.sum(decay_sum, axis=0, keepdims=True), (8, HS)
    )
    gtaps_ref[...] = jnp.concatenate(
        [jnp.sum(t, axis=0, keepdims=True) for t in taps_sum] + [jnp.zeros((8 - CONV, HS), F32)],
        axis=0,
    )


def head_block(lead, rows):
    return pl.BlockSpec((lead, rows, HS), lambda h: (0, 0, h))


def shared_block(shape):
    return pl.BlockSpec(shape, lambda h: (0,) * len(shape))


def pair_block(seqs):
    return pl.BlockSpec((seqs, 2, CHUNKS, HS), lambda h: (0, 0, 0, h))


PARAMS = pltpu.CompilerParams(vmem_limit_bytes=40 * 1024 * 1024)


def mixer_forward(u, halo, dist, gates, taps, soft):
    seqs, rows, _ = u.shape
    full = head_block(seqs, rows)
    wide = jax.ShapeDtypeStruct((seqs, rows, LRU), F32)
    return pl.pallas_call(
        mixer_forward_kernel,
        grid=(HEADS,),
        in_specs=[
            full,
            head_block(seqs, HALO),
            shared_block((seqs, rows, HS)),
            pl.BlockSpec((1, HS, 2 * HS), lambda h: (h, 0, 0)),
            pl.BlockSpec((CONV, HS), lambda h: (0, h)),
            pl.BlockSpec((1, HS), lambda h: (0, h)),
        ],
        out_specs=[full, full, full, full, pair_block(seqs)],
        out_shape=[
            jax.ShapeDtypeStruct((seqs, rows, LRU), BF16),
            wide,
            wide,
            wide,
            jax.ShapeDtypeStruct((seqs, 2, CHUNKS, LRU), F32),
        ],
        scratch_shapes=[
            pltpu.VMEM((seqs, rows + HALO, HS), F32),
            pltpu.VMEM((seqs, rows, HS), F32),
            pltpu.VMEM((seqs, rows, HS), F32),
            pltpu.VMEM((seqs, rows, HS), F32),
        ],
        compiler_params=PARAMS,
        name="mixer_forward",
    )(u, halo, dist, gates, taps, soft)


def mixer_reverse(grad, gate, keep, state):
    seqs, rows, _ = grad.shape
    full = head_block(seqs, rows)
    wide = jax.ShapeDtypeStruct((seqs, rows, LRU), F32)
    return pl.pallas_call(
        reverse_kernel,
        grid=(HEADS,),
        in_specs=[full, full, full, full],
        out_specs=[full, full, full, pair_block(seqs)],
        out_shape=[
            jax.ShapeDtypeStruct((seqs, rows, LRU), BF16),
            wide,
            wide,
            jax.ShapeDtypeStruct((seqs, 2, CHUNKS, LRU), F32),
        ],
        scratch_shapes=[pltpu.VMEM((seqs, rows, HS), F32)],
        compiler_params=PARAMS,
        name="mixer_reverse",
    )(grad, gate, keep, state)


def mixer_backward(local, prod, carry, state, before, c, u, halo, dist, gates, taps, soft):
    seqs, rows, _ = local.shape
    full = head_block(seqs, rows)
    small = head_block(seqs, HALO)
    gate_block = pl.BlockSpec((1, HS, 2 * HS), lambda h: (h, 0, 0))
    row_block = pl.BlockSpec((8, HS), lambda h: (0, h))
    return pl.pallas_call(
        mixer_backward_kernel,
        grid=(HEADS,),
        in_specs=[
            full,
            full,
            head_block(seqs, CHUNKS),
            full,
            small,
            full,
            full,
            small,
            shared_block((seqs, rows, HS)),
            gate_block,
            pl.BlockSpec((CONV, HS), lambda h: (0, h)),
            pl.BlockSpec((1, HS), lambda h: (0, h)),
        ],
        out_specs=[full, small, small, gate_block, row_block, row_block],
        out_shape=[
            jax.ShapeDtypeStruct((seqs, rows, LRU), BF16),
            jax.ShapeDtypeStruct((seqs, HALO, LRU), F32),
            jax.ShapeDtypeStruct((seqs, HALO, LRU), F32),
            jax.ShapeDtypeStruct((HEADS, HS, 2 * HS), F32),
            jax.ShapeDtypeStruct((8, LRU), F32),
            jax.ShapeDtypeStruct((8, LRU), F32),
        ],
        scratch_shapes=[
            pltpu.VMEM((rows, 2 * HS), F32),
            pltpu.VMEM((rows, 2 * HS), BF16),
            pltpu.VMEM((rows + HALO, HS), F32),
            pltpu.VMEM((rows + HALO, HS), F32),
            pltpu.VMEM((rows + HALO, HS), F32),
            pltpu.VMEM((rows + HALO, HS), F32),
        ],
        compiler_params=PARAMS,
        name="mixer_backward",
    )(local, prod, carry, state, before, c, u, halo, dist, gates, taps, soft)


def gather_rows(shard):
    parts = lax.axis_size("grp")
    rows = shard.shape[0] // parts
    own = lax.dynamic_slice_in_dim(shard, lax.axis_index("grp") * rows, rows, 0)
    return lax.all_gather(own, ("seq", "grp"), axis=0, tiled=True)


def tie(value, *after):
    return lax.optimization_barrier((value, *after))[0]


def xor_pairs(axis, bit):
    return [(i, i ^ bit) for i in range(lax.axis_size(axis))]


def ring_pairs(steps):
    count = lax.axis_size("seq")
    return [(i, (i + steps) % count) for i in range(count)]


def dot_rows(a, b):
    return lax.dot_general(a, b, (((0,), (0,)), ((), ())), preferred_element_type=F32)


def reduce_rows(partial):
    part = lax.psum_scatter(partial, "seq", scatter_dimension=0, tiled=True)
    part = lax.psum_scatter(part, "grp", scatter_dimension=0, tiled=True)
    return lax.all_gather(part, "grp", axis=0, tiled=True).astype(F32)


def reduce_product(a, b):
    count = lax.axis_size("seq")
    if lax.axis_size("grp") != 4:
        product = dot_rows(a, b).astype(BF16)
        return reduce_rows(product), (product,)
    place = lax.axis_index("seq")
    group = lax.axis_index("grp")
    chips = count // 2
    chip, core = place // 2, place % 2
    tokens, depth = a.shape
    rows = depth // count
    width = b.shape[1] // 4
    full = chips * rows
    half = full // 2
    split = a.reshape(tokens, chips, 2, rows)
    a_own = lax.dynamic_index_in_dim(split, core, 2, False).reshape(tokens, full)
    a_far = lax.dynamic_index_in_dim(split, 1 - core, 2, False).reshape(tokens, full)
    b_part = [lax.dynamic_slice_in_dim(b, (group ^ k) * width, width, 1) for k in range(4)]
    other = xor_pairs("seq", 1)
    x, y = xor_pairs("grp", 1), xor_pairs("grp", 2)
    far = {}
    for k in (3, 1, 2, 0):
        far[k] = lax.ppermute(dot_rows(a_far, b_part[k]).astype(BF16), "seq", other)

    def own(k, first, last):
        return dot_rows(a_own[:, first:last], b_part[k]) + far[k][first:last].astype(F32)

    early = [
        own(3, 0, half).astype(BF16),
        own(3, half, full).astype(BF16),
        own(1, 0, half).astype(BF16),
        own(2, half, full).astype(BF16),
    ]
    diag_a = lax.ppermute(early[0], "grp", x)
    diag_b = lax.ppermute(early[1], "grp", y)
    x_a = lax.ppermute(early[2], "grp", x)
    y_b = lax.ppermute(early[3], "grp", y)
    x_b = lax.ppermute((own(1, half, full) + diag_b.astype(F32)).astype(BF16), "grp", x)
    y_a = lax.ppermute((own(2, 0, half) + diag_a.astype(F32)).astype(BF16), "grp", y)
    mine_a = (own(0, 0, half) + x_a.astype(F32) + y_a.astype(F32)).astype(BF16)
    mine_b = (own(0, half, full) + x_b.astype(F32) + y_b.astype(F32)).astype(BF16)
    mine = jnp.concatenate([mine_a, mine_b], axis=0).reshape(chips, rows, width)
    total = lax.dynamic_index_in_dim(mine, chip, 0, False).astype(F32)
    for j in range(1, chips):
        sent = lax.dynamic_index_in_dim(mine, (chip + j) % chips, 0, False)
        total = total + lax.ppermute(sent, "seq", ring_pairs(2 * j)).astype(F32)
    parts = lax.all_gather(total.astype(BF16), "grp")
    return parts.transpose(1, 0, 2).reshape(rows, 4 * width).astype(F32), tuple(early)


def shard_carry(ends, prods, reverse):
    count = lax.axis_size("seq")
    place = lax.axis_index("seq")
    both = lax.all_gather(jnp.stack([ends, prods]), "seq")
    carry = jnp.zeros_like(ends)
    for step in range(count - 1):
        source = count - 1 - step if reverse else step
        ahead = source > place if reverse else source < place
        carry = jnp.where(ahead, both[source, 0] + both[source, 1] * carry, carry)
    return carry


def chunk_ends(chunks, reverse):
    state = jnp.zeros_like(chunks[:, 0, 0])
    prod = jnp.ones_like(state)
    order = range(CHUNKS - 1, -1, -1) if reverse else range(CHUNKS)
    for n in order:
        state = chunks[:, 0, n] + chunks[:, 1, n] * state
        prod = chunks[:, 1, n] * prod
    return state, prod


def chunk_carries(chunks, carry, reverse):
    order = range(CHUNKS - 1, -1, -1) if reverse else range(CHUNKS)
    found = [None] * CHUNKS
    for n in order:
        found[n] = carry
        carry = chunks[:, 0, n] + chunks[:, 1, n] * carry
    return jnp.stack(found, axis=1)


def norm_back(values, scale, gain, grad_normed):
    weighted = grad_normed * gain
    cubed = scale * scale * scale
    return scale * weighted - values * cubed * jnp.mean(weighted * values, axis=-1, keepdims=True)


def gain_grad(weight, grad_weight, gain):
    return jnp.sum(weight.astype(F32) * grad_weight, axis=1) / gain.astype(F32)


def body(
    tokens, seg_ids, cotangent, first_gain, in_proj, conv_taps, decay_param, gate_heads,
    out_proj, second_gain, up_proj, down_proj,
):
    seq_count, shard_len, _ = tokens.shape
    row_count = seq_count * shard_len
    edge_len = CONV - 1
    place = lax.axis_index("seq")
    last = lax.axis_size("seq") - 1

    small = jnp.concatenate(
        [first_gain, second_gain, decay_param, conv_taps.reshape(-1)]
    )
    small_all = lax.all_gather(small, "seq")
    n_gain, n_lru = first_gain.shape[0], decay_param.shape[0]
    gain_one = small_all[:, :n_gain].reshape(D).astype(F32)
    gain_two = small_all[:, n_gain : 2 * n_gain].reshape(D).astype(F32)
    decay_float = small_all[:, 2 * n_gain : 2 * n_gain + n_lru].reshape(LRU).astype(F32)
    taps_all = (
        small_all[:, 2 * n_gain + n_lru :].reshape(-1, CONV, n_lru).transpose(1, 0, 2)
    ).reshape(CONV, LRU).astype(F32)
    proj_in = gather_rows(in_proj)
    gates_all = lax.all_gather(gate_heads, "seq", axis=0, tiled=True)
    proj_out = gather_rows(out_proj)
    proj_up = gather_rows(up_proj)
    proj_down = gather_rows(down_proj)

    inputs = tokens.reshape(row_count, D).astype(F32)
    first_scale = lax.rsqrt(jnp.mean(inputs * inputs, axis=-1, keepdims=True) + 1e-06)
    first_normed = (inputs * first_scale * gain_one).astype(BF16)
    inner_low = jnp.dot(first_normed, proj_in[:, :LRU], preferred_element_type=F32).astype(BF16)
    inner_low = inner_low.reshape(seq_count, shard_len, LRU)
    gate_pre = jnp.dot(first_normed, proj_in[:, LRU:], preferred_element_type=F32)

    prev_inner = from_behind(inner_low[:, shard_len - HALO :], "seq", 1)
    prev_ids = from_behind(seg_ids[:, shard_len - edge_len :], "seq", 1)
    prev_ids = jnp.where(place == 0, -1, prev_ids)
    ext_ids = jnp.concatenate([prev_ids, seg_ids], axis=1)
    dist = jnp.zeros((seq_count, shard_len), F32)
    for k in range(1, CONV):
        dist = dist + (ext_ids[:, edge_len - k : edge_len - k + shard_len] == seg_ids).astype(F32)
    dist = jnp.broadcast_to(dist[:, :, None], (seq_count, shard_len, HS))
    soft = jax.nn.softplus(-decay_float).reshape(1, LRU)

    conv_low, keep, state_part, prod_part, chunks = mixer_forward(
        inner_low, prev_inner, dist, gates_all, taps_all, soft
    )
    end_state, end_prod = chunk_ends(chunks, False)
    carry_in = shard_carry(end_state, end_prod, False)
    carries = chunk_carries(chunks, carry_in, False)
    chunked = (seq_count, CHUNKS, shard_len // CHUNKS, LRU)
    state = (
        state_part.reshape(chunked) + prod_part.reshape(chunked) * carries[:, :, None, :]
    ).reshape(row_count, LRU)
    branch = (state * gelu_tanh(gate_pre)).astype(BF16)
    resid = inputs + jnp.dot(branch, proj_out, preferred_element_type=F32)
    second_scale = lax.rsqrt(jnp.mean(resid * resid, axis=-1, keepdims=True) + 1e-06)
    second_normed = (resid * second_scale * gain_two).astype(BF16)
    expanded_gate = jnp.dot(second_normed, proj_up[:, :FF], preferred_element_type=F32)
    expanded_up = jnp.dot(second_normed, proj_up[:, FF:], preferred_element_type=F32)
    hidden = (gelu_tanh(expanded_gate) * expanded_up).astype(BF16)
    ffn_out = jnp.dot(hidden, proj_down, preferred_element_type=F32)
    block_out = (resid + ffn_out).astype(BF16).reshape(seq_count, shard_len, D)

    grad_out = cotangent.reshape(row_count, D)
    grad_down = dot_rows(hidden, grad_out).astype(BF16)
    down_total = reduce_rows(grad_down)
    grad_hidden = jnp.einsum(
        "rd,fd->rf", tie(grad_out, grad_down), proj_down, preferred_element_type=F32
    )
    act, slope = gelu_parts(expanded_gate)
    grad_expanded = jnp.concatenate(
        [(grad_hidden * expanded_up * slope).astype(BF16), (grad_hidden * act).astype(BF16)], axis=1
    )
    up_total, sent = reduce_product(second_normed, grad_expanded)
    grad_second_normed = jnp.einsum(
        "rf,df->rd", tie(grad_expanded, *sent), proj_up, preferred_element_type=F32
    )
    grad_resid = grad_out.astype(F32) + norm_back(
        resid, second_scale, gain_two, grad_second_normed
    )
    grad_mixer = grad_resid.astype(BF16)
    out_total, sent = reduce_product(branch, grad_mixer)
    grad_branch = jnp.einsum(
        "rd,ld->rl", tie(grad_mixer, *sent), proj_out, preferred_element_type=F32
    )

    wide = (seq_count, shard_len, LRU)
    grad_gate, local, rev_prod, rev_chunks = mixer_reverse(
        grad_branch.reshape(wide), gate_pre.reshape(wide), keep, state.reshape(wide)
    )
    head_pull, head_prod = chunk_ends(rev_chunks, True)
    rev_carry = shard_carry(head_pull, head_prod, True)
    rev_carries = chunk_carries(rev_chunks, rev_carry, True)
    before = jnp.broadcast_to(carry_in[:, None], (seq_count, HALO, LRU))
    du, tail, edge, grad_gates, grad_taps, grad_decay = mixer_backward(
        local, rev_prod, rev_carries, state.reshape(wide), before, conv_low, inner_low,
        prev_inner, dist, gates_all, taps_all, soft,
    )
    grad_decay_row = grad_decay[0] * jax.nn.sigmoid(-decay_float)
    flat = jnp.concatenate(
        [
            grad_gates.reshape(last + 1, -1),
            grad_taps[:CONV].reshape(CONV, last + 1, n_lru).transpose(1, 0, 2).reshape(last + 1, -1),
            grad_decay_row.reshape(last + 1, n_lru),
        ],
        axis=1,
    ).astype(BF16)
    flat = lax.psum_scatter(flat.reshape(-1, HS), "seq", scatter_dimension=0, tiled=True)
    flat = lax.psum(flat, "grp").astype(F32).reshape(-1)
    n_gates = flat.shape[0] - (CONV + 1) * n_lru
    gates_total = flat[:n_gates].reshape(gate_heads.shape)
    taps_total = flat[n_gates : n_gates + CONV * n_lru].reshape(CONV, n_lru)
    decay_total = flat[n_gates + CONV * n_lru :]
    returned = from_behind(edge[:, HALO - edge_len :].astype(BF16), "seq", -1).astype(F32)
    returned = jnp.pad(returned, ((0, 0), (HALO - edge_len, 0), (0, 0)))
    grad_inner = lax.dynamic_update_slice(
        du, (tail + returned).astype(BF16), (0, shard_len - HALO, 0)
    )
    grad_projected = jnp.concatenate(
        [grad_inner.reshape(row_count, LRU), grad_gate.reshape(row_count, LRU)], axis=1
    )
    in_total, sent = reduce_product(first_normed, grad_projected)
    grad_first_normed = jnp.einsum(
        "rp,dp->rd", tie(grad_projected, *sent), proj_in, preferred_element_type=F32
    )
    grad_tokens = grad_resid + norm_back(inputs, first_scale, gain_one, grad_first_normed)
    grad_tokens = grad_tokens.astype(BF16).reshape(seq_count, shard_len, D)
    first_total = gain_grad(in_proj, in_total, first_gain)
    second_total = gain_grad(up_proj, up_total, second_gain)
    return (
        block_out, grad_tokens, first_total, in_total, taps_total, decay_total, gates_total,
        out_total, second_total, up_total, down_total,
    )


def solution(mesh):
    in_specs = (
        P("grp", "seq", None),
        P("grp", "seq"),
        P("grp", "seq", None),
        P("seq"),
        P("seq", None),
        P(None, "seq"),
        P("seq"),
        P("seq", None, None),
        P("seq", None),
        P("seq"),
        P("seq", None),
        P("seq", None),
    )
    out_specs = (
        P("grp", "seq", None),
        P("grp", "seq", None),
        P("seq"),
        P("seq", None),
        P(None, "seq"),
        P("seq"),
        P("seq", None, None),
        P("seq", None),
        P("seq"),
        P("seq", None),
        P("seq", None),
    )
    return jax.shard_map(body, mesh=mesh, in_specs=in_specs, out_specs=out_specs, check_vma=False)
```

```python
import functools

import jax
import jax.numpy as jnp
from jax import lax
from jax.experimental import pallas as pl
from jax.experimental.pallas import tpu as pltpu
from jax.sharding import PartitionSpec as P

D = 1536
HEADS = 16
HS = 128
LRU = 2048
FF = 4608
CONV = 4
CHUNKS = 8
HALO = 8
F32 = jnp.float32
BF16 = jnp.bfloat16


def from_behind(value, axis, steps):
    count = lax.axis_size(axis)
    first, last = (max(0, -steps), min(count, count - steps))
    return lax.ppermute(value, axis, [(source, source + steps) for source in range(first, last)])


def gelu_parts(v):
    k = 0.7978845608028654
    square = v * v
    t = jnp.tanh(k * v * (1.0 + 0.044715 * square))
    half = 0.5 * (1.0 + t)
    slope = half + 0.5 * v * (1.0 - t * t) * (k * (1.0 + 3.0 * 0.044715 * square))
    return v * half, slope


def gelu_tanh(v):
    k = 0.7978845608028654
    return 0.5 * v * (1.0 + jnp.tanh(k * v * (1.0 + 0.044715 * v * v)))


def sigmoid(v):
    return 0.5 * jnp.tanh(0.5 * v) + 0.5


def drive_values(q_rate, q_input, soft):
    rate = sigmoid(q_rate)
    inp = sigmoid(q_input)
    decay = jnp.exp(-8.0 * rate * soft)
    root = jnp.sqrt(1.0 - decay * decay + 0.001)
    return rate, inp, decay, root


def mixer_forward_kernel(
    u_ref, halo_ref, dist_ref, gates_ref, taps_ref, soft_ref,
    c_ref, keep_ref, state_ref, prod_ref, chunk_ref,
    ext_s, c_s, rate_s, inp_s,
):
    seqs, rows, _ = u_ref.shape
    step = rows // CHUNKS
    soft = soft_ref[...]
    for b in range(seqs):
        ext_s[b, pl.ds(0, HALO), :] = halo_ref[b].astype(F32)
        ext_s[b, pl.ds(HALO, rows), :] = u_ref[b].astype(F32)

        def conv_chunk(n, _):
            at = pl.multiple_of(n * 64, 64)
            total = taps_ref[0:1, :] * ext_s[b, pl.ds(at + HALO, 64), :]
            for k in range(1, CONV):
                same = (dist_ref[b, pl.ds(at, 64), :] >= float(k)).astype(F32)
                total = total + taps_ref[k : k + 1, :] * ext_s[b, pl.ds(at + HALO - k, 64), :] * same
            low = total.astype(BF16)
            c_ref[b, pl.ds(at, 64), :] = low
            c_s[b, pl.ds(at, 64), :] = low.astype(F32)
            return 0

        lax.fori_loop(0, rows // 64, conv_chunk, 0)
        both = jnp.dot(c_ref[b], gates_ref[0], preferred_element_type=F32)
        rate_s[b] = both[:, :HS]
        inp_s[b] = both[:, HS:]

    def scan_step(j, carry):
        new = []
        for b in range(seqs):
            at = pl.ds(j, CHUNKS, stride=step)
            state, prod = carry[b]
            _, inp, decay, root = drive_values(rate_s[b, at, :], inp_s[b, at, :], soft)
            keep = decay * (dist_ref[b, at, :] >= 1.0).astype(F32)
            state = keep * state + root * inp * c_s[b, at, :]
            prod = keep * prod
            keep_ref[b, at, :] = keep
            state_ref[b, at, :] = state
            prod_ref[b, at, :] = prod
            new.append((state, prod))
        return tuple(new)

    zero, one = jnp.zeros((CHUNKS, HS), F32), jnp.ones((CHUNKS, HS), F32)
    ends = lax.fori_loop(0, step, scan_step, ((zero, one),) * seqs, unroll=4)
    for b in range(seqs):
        chunk_ref[b, 0] = ends[b][0]
        chunk_ref[b, 1] = ends[b][1]


def reverse_kernel(
    grad_ref, gate_ref, keep_ref, state_ref,
    dg_ref, local_ref, prod_ref, chunk_ref,
    dh_s,
):
    seqs, rows, _ = grad_ref.shape
    step = rows // CHUNKS
    for b in range(seqs):

        def point(n, _):
            at = pl.ds(pl.multiple_of(n * 64, 64), 64)
            act, slope = gelu_parts(gate_ref[b, at, :])
            grad = grad_ref[b, at, :]
            dh_s[b, at, :] = grad * act
            dg_ref[b, at, :] = (grad * state_ref[b, at, :] * slope).astype(BF16)
            return 0

        lax.fori_loop(0, rows // 64, point, 0)

    def scan_step(n, carry):
        j = step - 1 - n
        new = []
        for b in range(seqs):
            at = pl.ds(j, CHUNKS, stride=step)
            pull, prod = carry[b]
            keep = keep_ref[b, at, :]
            local = dh_s[b, at, :] + pull
            local_ref[b, at, :] = local
            prod_ref[b, at, :] = prod
            new.append((keep * local, keep * prod))
        return tuple(new)

    zero, one = jnp.zeros((CHUNKS, HS), F32), jnp.ones((CHUNKS, HS), F32)
    ends = lax.fori_loop(0, step, scan_step, ((zero, one),) * seqs, unroll=4)
    for b in range(seqs):
        chunk_ref[b, 0] = ends[b][0]
        chunk_ref[b, 1] = ends[b][1]


def mixer_backward_kernel(
    local_ref, prod_ref, carry_ref, state_ref, before_ref, c_ref, u_ref, halo_ref, dist_ref,
    gates_ref, taps_ref, soft_ref,
    du_ref, tail_ref, edge_ref, ggate_ref, gtaps_ref, gdecay_ref,
    q_s, dq_s, dc_s, h_s, ext_s, dist_s,
):
    seqs, rows, _ = local_ref.shape
    step = rows // CHUNKS
    soft = soft_ref[...]
    ggate = jnp.zeros((HS, 2 * HS), F32)
    decay_sum = jnp.zeros((8, HS), F32)
    taps_sum = [jnp.zeros((8, HS), F32) for _ in range(CONV)]

    def fold(value):
        return jnp.sum(value.reshape(value.shape[0] // 8, 8, HS), axis=0)

    for b in range(seqs):
        q_s[...] = jnp.dot(c_ref[b], gates_ref[0], preferred_element_type=F32)
        h_s[pl.ds(0, HALO), :] = before_ref[b]
        h_s[pl.ds(HALO, rows), :] = state_ref[b]

        def point(n, total):
            at = pl.ds(pl.multiple_of(n * step, step), step)
            lam = local_ref[b, at, :] + prod_ref[b, at, :] * carry_ref[b, pl.ds(n, 1), :]
            rate, inp, decay, root = drive_values(q_s[at, :HS], q_s[at, HS:], soft)
            conv = c_ref[b, at, :].astype(F32)
            is_open = (dist_ref[b, at, :] >= 1.0).astype(F32)
            prev = h_s[pl.ds(pl.multiple_of(n * step, step) + HALO - 1, step), :]
            lam_root = lam * root
            lam_inp = lam * inp
            grad_decay = lam * prev * is_open - lam_inp * conv * decay / root
            grad_log = grad_decay * decay
            rated = grad_log * rate
            dq_s[at, :HS] = (-8.0 * soft * rated * (1.0 - rate)).astype(BF16)
            dq_s[at, HS:] = (lam_root * conv * inp * (1.0 - inp)).astype(BF16)
            dc_s[at, :] = lam_root * inp
            return total + fold(rated)

        decay_sum = lax.fori_loop(0, CHUNKS, point, decay_sum)
        dc_s[pl.ds(0, rows), :] += lax.dot_general(
            dq_s[...], gates_ref[0], (((1,), (1,)), ((), ())), preferred_element_type=F32
        )
        dc_s[pl.ds(rows, HALO), :] = jnp.zeros((HALO, HS), F32)
        ggate = ggate + lax.dot_general(
            c_ref[b], dq_s[...], (((0,), (0,)), ((), ())), preferred_element_type=F32
        )
        ext_s[pl.ds(0, HALO), :] = halo_ref[b].astype(F32)
        ext_s[pl.ds(HALO, rows), :] = u_ref[b].astype(F32)
        dist_s[pl.ds(0, rows), :] = dist_ref[b]
        dist_s[pl.ds(rows, HALO), :] = jnp.zeros((HALO, HS), F32)

        def conv_chunk(n, totals):
            at = pl.multiple_of(n * 64, 64)
            grad = dc_s[pl.ds(at, 64), :]
            far = dist_s[pl.ds(at, 64), :]
            out = taps_ref[0:1, :] * grad
            totals = list(totals)
            totals[0] = totals[0] + fold(grad * ext_s[pl.ds(at + HALO, 64), :])
            for k in range(1, CONV):
                masked = jnp.where(far >= float(k), grad, 0.0)
                totals[k] = totals[k] + fold(masked * ext_s[pl.ds(at + HALO - k, 64), :])
                ahead = jnp.where(
                    dist_s[pl.ds(at + k, 64), :] >= float(k), dc_s[pl.ds(at + k, 64), :], 0.0
                )
                out = out + taps_ref[k : k + 1, :] * ahead
            du_ref[b, pl.ds(at, 64), :] = out.astype(BF16)

            @pl.when(n == rows // 64 - 1)
            def _():
                tail_ref[b] = out[64 - HALO :, :]

            return tuple(totals)

        taps_sum = list(lax.fori_loop(0, rows // 64, conv_chunk, tuple(taps_sum)))
        head = dc_s[pl.ds(0, HALO), :]
        far = dist_s[pl.ds(0, HALO), :]
        zeros = jnp.zeros((HALO, HS), F32)
        edge = zeros
        for k in range(1, CONV):
            masked = jnp.where(far >= float(k), head, 0.0)
            both = jnp.concatenate([zeros, masked], axis=0)
            edge = edge + taps_ref[k : k + 1, :] * both[k : k + HALO, :]
        edge_ref[b] = edge
    ggate_ref[0] = ggate
    gdecay_ref[...] = jnp.broadcast_to(
        8.0 * jnp.sum(decay_sum, axis=0, keepdims=True), (8, HS)
    )
    gtaps_ref[...] = jnp.concatenate(
        [jnp.sum(t, axis=0, keepdims=True) for t in taps_sum] + [jnp.zeros((8 - CONV, HS), F32)],
        axis=0,
    )


def norm_kernel(shards, core_ref, x_ref, gain_ref, normed_ref, own_ref, far_ref, scale_ref):
    x = x_ref[...].astype(F32)
    scale = lax.rsqrt(jnp.mean(x * x, axis=-1, keepdims=True) + 1e-06)
    low = (x * scale * gain_ref[...]).astype(BF16)
    normed_ref[...] = low
    scale_ref[...] = jnp.broadcast_to(scale, scale_ref.shape)
    wide = low.astype(F32)
    size = D // shards
    even, odd = (
        jnp.concatenate([wide[:, n * size : (n + 1) * size] for n in range(c, shards, 2)], axis=1)
        for c in range(2)
    )
    first = core_ref[0] == 0
    own_ref[...] = jnp.where(first, even, odd).astype(BF16)
    far_ref[...] = jnp.where(first, odd, even).astype(BF16)


def ffn_forward_kernel(n_ref, gate_ref, up_ref, hidden_ref, pull_ref):
    for m in range(0, n_ref.shape[0], 256):
        at = pl.ds(m, 256)
        e1 = jnp.dot(n_ref[at, :], gate_ref[...], preferred_element_type=F32)
        e2 = jnp.dot(n_ref[at, :], up_ref[...], preferred_element_type=F32)
        act, slope = gelu_parts(e1)
        hidden_ref[at, :] = (act * e2).astype(BF16)
        pull_ref[0, at, :] = (slope * e2).astype(BF16)
        pull_ref[1, at, :] = act.astype(BF16)


def ffn_backward_kernel(grad_ref, down_ref, pull_ref, out_ref):
    for m in range(0, grad_ref.shape[0], 256):
        at = pl.ds(m, 256)
        dv = lax.dot_general(
            grad_ref[at, :], down_ref[...], (((1,), (1,)), ((), ())), preferred_element_type=F32
        )
        out_ref[0, at, :] = (dv * pull_ref[0, at, :].astype(F32)).astype(BF16)
        out_ref[1, at, :] = (dv * pull_ref[1, at, :].astype(F32)).astype(BF16)


def head_block(lead, rows):
    return pl.BlockSpec((lead, rows, HS), lambda h: (0, 0, h))


def shared_block(shape):
    return pl.BlockSpec(shape, lambda h: (0,) * len(shape))


def pair_block(seqs):
    return pl.BlockSpec((seqs, 2, CHUNKS, HS), lambda h: (0, 0, 0, h))


PARAMS = pltpu.CompilerParams(vmem_limit_bytes=40 * 1024 * 1024)


def mixer_forward(u, halo, dist, gates, taps, soft):
    seqs, rows, _ = u.shape
    full = head_block(seqs, rows)
    wide = jax.ShapeDtypeStruct((seqs, rows, LRU), F32)
    return pl.pallas_call(
        mixer_forward_kernel,
        grid=(HEADS,),
        in_specs=[
            full,
            head_block(seqs, HALO),
            shared_block((seqs, rows, HS)),
            pl.BlockSpec((1, HS, 2 * HS), lambda h: (h, 0, 0)),
            pl.BlockSpec((CONV, HS), lambda h: (0, h)),
            pl.BlockSpec((1, HS), lambda h: (0, h)),
        ],
        out_specs=[full, full, full, full, pair_block(seqs)],
        out_shape=[
            jax.ShapeDtypeStruct((seqs, rows, LRU), BF16),
            wide,
            wide,
            wide,
            jax.ShapeDtypeStruct((seqs, 2, CHUNKS, LRU), F32),
        ],
        scratch_shapes=[
            pltpu.VMEM((seqs, rows + HALO, HS), F32),
            pltpu.VMEM((seqs, rows, HS), F32),
            pltpu.VMEM((seqs, rows, HS), F32),
            pltpu.VMEM((seqs, rows, HS), F32),
        ],
        compiler_params=PARAMS,
        name="mixer_forward",
    )(u, halo, dist, gates, taps, soft)


def mixer_reverse(grad, gate, keep, state):
    seqs, rows, _ = grad.shape
    full = head_block(seqs, rows)
    wide = jax.ShapeDtypeStruct((seqs, rows, LRU), F32)
    return pl.pallas_call(
        reverse_kernel,
        grid=(HEADS,),
        in_specs=[full, full, full, full],
        out_specs=[full, full, full, pair_block(seqs)],
        out_shape=[
            jax.ShapeDtypeStruct((seqs, rows, LRU), BF16),
            wide,
            wide,
            jax.ShapeDtypeStruct((seqs, 2, CHUNKS, LRU), F32),
        ],
        scratch_shapes=[pltpu.VMEM((seqs, rows, HS), F32)],
        compiler_params=PARAMS,
        name="mixer_reverse",
    )(grad, gate, keep, state)


def mixer_backward(local, prod, carry, state, before, c, u, halo, dist, gates, taps, soft):
    seqs, rows, _ = local.shape
    full = head_block(seqs, rows)
    small = head_block(seqs, HALO)
    gate_block = pl.BlockSpec((1, HS, 2 * HS), lambda h: (h, 0, 0))
    row_block = pl.BlockSpec((8, HS), lambda h: (0, h))
    return pl.pallas_call(
        mixer_backward_kernel,
        grid=(HEADS,),
        in_specs=[
            full,
            full,
            head_block(seqs, CHUNKS),
            full,
            small,
            full,
            full,
            small,
            shared_block((seqs, rows, HS)),
            gate_block,
            pl.BlockSpec((CONV, HS), lambda h: (0, h)),
            pl.BlockSpec((1, HS), lambda h: (0, h)),
        ],
        out_specs=[full, small, small, gate_block, row_block, row_block],
        out_shape=[
            jax.ShapeDtypeStruct((seqs, rows, LRU), BF16),
            jax.ShapeDtypeStruct((seqs, HALO, LRU), F32),
            jax.ShapeDtypeStruct((seqs, HALO, LRU), F32),
            jax.ShapeDtypeStruct((HEADS, HS, 2 * HS), F32),
            jax.ShapeDtypeStruct((8, LRU), F32),
            jax.ShapeDtypeStruct((8, LRU), F32),
        ],
        scratch_shapes=[
            pltpu.VMEM((rows, 2 * HS), F32),
            pltpu.VMEM((rows, 2 * HS), BF16),
            pltpu.VMEM((rows + HALO, HS), F32),
            pltpu.VMEM((rows + HALO, HS), F32),
            pltpu.VMEM((rows + HALO, HS), F32),
            pltpu.VMEM((rows + HALO, HS), F32),
        ],
        compiler_params=PARAMS,
        name="mixer_backward",
    )(local, prod, carry, state, before, c, u, halo, dist, gates, taps, soft)


def rms_norm(x, gain, shards, core):
    rows = x.shape[0]
    block = min(rows, 256)
    return pl.pallas_call(
        functools.partial(norm_kernel, shards),
        grid=(rows // block,),
        in_specs=[
            pl.BlockSpec(memory_space=pltpu.SMEM),
            pl.BlockSpec((block, D), lambda n: (n, 0)),
            pl.BlockSpec((1, D), lambda n: (0, 0)),
        ],
        out_specs=[
            pl.BlockSpec((block, D), lambda n: (n, 0)),
            pl.BlockSpec((block, D // 2), lambda n: (n, 0)),
            pl.BlockSpec((block, D // 2), lambda n: (n, 0)),
            pl.BlockSpec((block, 128), lambda n: (n, 0)),
        ],
        out_shape=[
            jax.ShapeDtypeStruct((rows, D), BF16),
            jax.ShapeDtypeStruct((rows, D // 2), BF16),
            jax.ShapeDtypeStruct((rows, D // 2), BF16),
            jax.ShapeDtypeStruct((rows, 128), F32),
        ],
        compiler_params=PARAMS,
        name="rms_norm",
    )(core.reshape(1), x, gain.reshape(1, D))


FF_TILE = 512


def ffn_forward(normed, proj_up):
    rows = normed.shape[0]
    steps = FF // FF_TILE
    return pl.pallas_call(
        ffn_forward_kernel,
        grid=(steps,),
        in_specs=[
            pl.BlockSpec((rows, D), lambda n: (0, 0)),
            pl.BlockSpec((D, FF_TILE), lambda n: (0, n)),
            pl.BlockSpec((D, FF_TILE), lambda n: (0, n + steps)),
        ],
        out_specs=[
            pl.BlockSpec((rows, FF_TILE), lambda n: (0, n)),
            pl.BlockSpec((2, rows, FF_TILE), lambda n: (0, 0, n)),
        ],
        out_shape=[
            jax.ShapeDtypeStruct((rows, FF), BF16),
            jax.ShapeDtypeStruct((2, rows, FF), BF16),
        ],
        compiler_params=PARAMS,
        name="ffn_forward",
    )(normed, proj_up, proj_up)


def ffn_backward(grad, proj_down, pull):
    rows = grad.shape[0]
    return pl.pallas_call(
        ffn_backward_kernel,
        grid=(FF // FF_TILE,),
        in_specs=[
            pl.BlockSpec((rows, D), lambda n: (0, 0)),
            pl.BlockSpec((FF_TILE, D), lambda n: (n, 0)),
            pl.BlockSpec((2, rows, FF_TILE), lambda n: (0, 0, n)),
        ],
        out_specs=pl.BlockSpec((2, rows, FF_TILE), lambda n: (0, 0, n)),
        out_shape=jax.ShapeDtypeStruct((2, rows, FF), BF16),
        compiler_params=PARAMS,
        name="ffn_backward",
    )(grad, proj_down, pull)


def gather_rows(shard):
    parts = lax.axis_size("grp")
    rows = shard.shape[0] // parts
    own = lax.dynamic_slice_in_dim(shard, lax.axis_index("grp") * rows, rows, 0)
    return lax.all_gather(own, ("seq", "grp"), axis=0, tiled=True)


def tie(value, *after):
    return lax.optimization_barrier((value, *after))[0]


def xor_pairs(axis, bit):
    return [(i, i ^ bit) for i in range(lax.axis_size(axis))]


def ring_pairs(steps):
    count = lax.axis_size("seq")
    return [(i, (i + steps) % count) for i in range(count)]


def dot_rows(a, b):
    return lax.dot_general(a, b, (((0,), (0,)), ((), ())), preferred_element_type=F32)


def reduce_rows(partial):
    part = lax.psum_scatter(partial, "seq", scatter_dimension=0, tiled=True)
    part = lax.psum_scatter(part, "grp", scatter_dimension=0, tiled=True)
    return lax.all_gather(part, "grp", axis=0, tiled=True).astype(F32)


def dot_far(a, b):
    return lax.dot_general(a, b, (((1,), (1,)), ((), ())), preferred_element_type=F32)


def split_cores(a, shards, core):
    tokens, depth = a.shape
    split = a.reshape(tokens, shards // 2, 2, depth // shards)
    return tuple(
        lax.dynamic_index_in_dim(split, c, 2, False).reshape(tokens, depth // 2)
        for c in (core, 1 - core)
    )


class Reduction:
    def __init__(self, a_own, a_far, columns, width):
        self.simple = lax.axis_size("grp") != 4
        count = lax.axis_size("seq")
        place = lax.axis_index("seq")
        self.chips = count // 2
        self.chip, core = place // 2, place % 2
        self.width = width
        full = a_own.shape[1]
        self.rows = full // self.chips
        self.half = full // 2
        self.a_own = a_own
        if self.simple:
            parts = [columns(k) for k in range(4)]
            own, far = (
                jnp.concatenate([dot_rows(a, part) for part in parts], axis=1)
                for a in (a_own, a_far)
            )
            cores = jnp.stack(
                [jnp.where(core == c, own, far).reshape(self.chips, self.rows, -1) for c in (0, 1)],
                axis=1,
            )
            self.product = cores.reshape(2 * full, 4 * width).astype(BF16)
            self.sent = (self.product,)
            return
        group = lax.axis_index("grp")
        self.x, self.y = xor_pairs("grp", 1), xor_pairs("grp", 2)
        self.b = [columns(group ^ k) for k in range(4)]
        self.far = [None] * 4
        for k in (3, 1, 2, 0):
            product = dot_rows(a_far, self.b[k]).astype(BF16)
            self.far[k] = lax.ppermute(product, "seq", xor_pairs("seq", 1))
        half = self.half
        self.sent = (
            self.own(3, 0).astype(BF16),
            self.own(3, half).astype(BF16),
            self.own(1, 0).astype(BF16),
            self.own(2, half).astype(BF16),
        )
        self.diag_a = lax.ppermute(self.sent[0], "grp", self.x)
        self.diag_b = lax.ppermute(self.sent[1], "grp", self.y)
        self.x_a = lax.ppermute(self.sent[2], "grp", self.x)
        self.y_b = lax.ppermute(self.sent[3], "grp", self.y)

    def own(self, k, first):
        last = first + self.half
        product = dot_rows(self.a_own[:, first:last], self.b[k])
        return product + self.far[k][first:last].astype(F32)

    def second(self):
        if self.simple:
            return ()
        sent = (
            (self.own(1, self.half) + self.diag_b.astype(F32)).astype(BF16),
            (self.own(2, 0) + self.diag_a.astype(F32)).astype(BF16),
        )
        self.x_b = lax.ppermute(sent[0], "grp", self.x)
        self.y_a = lax.ppermute(sent[1], "grp", self.y)
        return sent

    def third(self):
        if self.simple:
            return ()
        first = self.own(0, 0) + self.x_a.astype(F32) + self.y_a.astype(F32)
        second = self.own(0, self.half) + self.x_b.astype(F32) + self.y_b.astype(F32)
        mine = jnp.concatenate([first.astype(BF16), second.astype(BF16)], axis=0)
        mine = mine.reshape(self.chips, self.rows, self.width)
        self.kept = lax.dynamic_index_in_dim(mine, self.chip, 0, False)
        sent = tuple(
            lax.dynamic_index_in_dim(mine, (self.chip + j) % self.chips, 0, False)
            for j in range(1, self.chips)
        )
        self.arrived = [
            lax.ppermute(part, "seq", ring_pairs(2 * j + 2)) for j, part in enumerate(sent)
        ]
        return sent

    def finish(self):
        if self.simple:
            return reduce_rows(self.product)
        total = self.kept.astype(F32)
        for part in self.arrived:
            total = total + part.astype(F32)
        parts = lax.all_gather(total.astype(BF16), "grp")
        return parts.transpose(1, 0, 2).reshape(self.rows, 4 * self.width).astype(F32)


def shard_carry(ends, prods, reverse):
    count = lax.axis_size("seq")
    place = lax.axis_index("seq")
    both = lax.all_gather(jnp.stack([ends, prods]), "seq")
    carry = jnp.zeros_like(ends)
    for step in range(count - 1):
        source = count - 1 - step if reverse else step
        ahead = source > place if reverse else source < place
        carry = jnp.where(ahead, both[source, 0] + both[source, 1] * carry, carry)
    return carry


def chunk_ends(chunks, reverse):
    state = jnp.zeros_like(chunks[:, 0, 0])
    prod = jnp.ones_like(state)
    order = range(CHUNKS - 1, -1, -1) if reverse else range(CHUNKS)
    for n in order:
        state = chunks[:, 0, n] + chunks[:, 1, n] * state
        prod = chunks[:, 1, n] * prod
    return state, prod


def chunk_carries(chunks, carry, reverse):
    order = range(CHUNKS - 1, -1, -1) if reverse else range(CHUNKS)
    found = [None] * CHUNKS
    for n in order:
        found[n] = carry
        carry = chunks[:, 0, n] + chunks[:, 1, n] * carry
    return jnp.stack(found, axis=1)


def norm_back(values, scale, gain, grad_normed):
    weighted = grad_normed * gain
    cubed = scale * scale * scale
    return scale * weighted - values * cubed * jnp.mean(weighted * values, axis=-1, keepdims=True)


def gain_grad(weight, grad_weight, gain):
    return jnp.sum(weight.astype(F32) * grad_weight, axis=1) / gain.astype(F32)


def body(
    tokens, seg_ids, cotangent, first_gain, in_proj, conv_taps, decay_param, gate_heads,
    out_proj, second_gain, up_proj, down_proj,
):
    seq_count, shard_len, _ = tokens.shape
    row_count = seq_count * shard_len
    edge_len = CONV - 1
    place = lax.axis_index("seq")
    last = lax.axis_size("seq") - 1

    small = jnp.concatenate(
        [first_gain, second_gain, decay_param, conv_taps.reshape(-1)]
    )
    small_all = lax.all_gather(small, "seq")
    n_gain, n_lru = first_gain.shape[0], decay_param.shape[0]
    gain_one = small_all[:, :n_gain].reshape(D).astype(F32)
    gain_two = small_all[:, n_gain : 2 * n_gain].reshape(D).astype(F32)
    decay_float = small_all[:, 2 * n_gain : 2 * n_gain + n_lru].reshape(LRU).astype(F32)
    taps_all = (
        small_all[:, 2 * n_gain + n_lru :].reshape(-1, CONV, n_lru).transpose(1, 0, 2)
    ).reshape(CONV, LRU).astype(F32)
    proj_in = gather_rows(in_proj)
    gates_all = lax.all_gather(gate_heads, "seq", axis=0, tiled=True)
    proj_out = gather_rows(out_proj)
    proj_up = gather_rows(up_proj)
    proj_down = gather_rows(down_proj)

    inputs = tokens.reshape(row_count, D).astype(F32)
    first_normed, first_own, first_far, first_scale = rms_norm(
        tokens.reshape(row_count, D), gain_one, last + 1, place % 2
    )
    first_scale = first_scale[:, :1]
    inner_low = jnp.dot(first_normed, proj_in[:, :LRU], preferred_element_type=F32).astype(BF16)
    inner_low = inner_low.reshape(seq_count, shard_len, LRU)
    gate_pre = jnp.dot(first_normed, proj_in[:, LRU:], preferred_element_type=F32)

    prev_inner = from_behind(inner_low[:, shard_len - HALO :], "seq", 1)
    prev_ids = from_behind(seg_ids[:, shard_len - edge_len :], "seq", 1)
    prev_ids = jnp.where(place == 0, -1, prev_ids)
    ext_ids = jnp.concatenate([prev_ids, seg_ids], axis=1)
    dist = jnp.zeros((seq_count, shard_len), F32)
    for k in range(1, CONV):
        dist = dist + (ext_ids[:, edge_len - k : edge_len - k + shard_len] == seg_ids).astype(F32)
    dist = jnp.broadcast_to(dist[:, :, None], (seq_count, shard_len, HS))
    soft = jax.nn.softplus(-decay_float).reshape(1, LRU)

    conv_low, keep, state_part, prod_part, chunks = mixer_forward(
        inner_low, prev_inner, dist, gates_all, taps_all, soft
    )
    end_state, end_prod = chunk_ends(chunks, False)
    carry_in = shard_carry(end_state, end_prod, False)
    carries = chunk_carries(chunks, carry_in, False)
    chunked = (seq_count, CHUNKS, shard_len // CHUNKS, LRU)
    state = (
        state_part.reshape(chunked) + prod_part.reshape(chunked) * carries[:, :, None, :]
    ).reshape(row_count, LRU)
    branch = (state * gelu_tanh(gate_pre)).astype(BF16)
    resid = inputs + jnp.dot(branch, proj_out, preferred_element_type=F32)
    second_normed, second_own, second_far, second_scale = rms_norm(
        resid, gain_two, last + 1, place % 2
    )
    second_scale = second_scale[:, :1]
    hidden, pull = ffn_forward(second_normed, proj_up)
    ffn_out = jnp.dot(hidden, proj_down, preferred_element_type=F32)
    block_out = (resid + ffn_out).astype(BF16).reshape(seq_count, shard_len, D)

    grad_out = cotangent.reshape(row_count, D)
    grad_down = dot_rows(hidden, grad_out).astype(BF16)
    down_total = reduce_rows(grad_down)
    grad_expanded = ffn_backward(tie(grad_out, grad_down), proj_down, pull)
    quarter = FF // 2

    def up_columns(n):
        part = lax.dynamic_slice(
            grad_expanded, (n // 2, 0, (n % 2) * quarter), (1, row_count, quarter)
        )
        return part[0]

    up_sum = Reduction(second_own, second_far, up_columns, quarter)
    grad_expanded = tie(grad_expanded, *up_sum.sent)
    grad_second_normed = dot_far(grad_expanded[0], proj_up[:, :FF]) + dot_far(
        grad_expanded[1], proj_up[:, FF:]
    )
    sent = up_sum.second()
    grad_second_normed = tie(grad_second_normed, *sent)
    grad_resid = grad_out.astype(F32) + norm_back(
        resid, second_scale, gain_two, grad_second_normed
    )
    grad_mixer = grad_resid.astype(BF16)
    out_sum = Reduction(
        *split_cores(branch, last + 1, place % 2),
        lambda n: lax.dynamic_slice_in_dim(grad_mixer, n * (D // 4), D // 4, 1),
        D // 4,
    )
    grad_branch = dot_far(tie(grad_mixer, *out_sum.sent), proj_out)

    wide = (seq_count, shard_len, LRU)
    grad_gate, local, rev_prod, rev_chunks = mixer_reverse(
        grad_branch.reshape(wide), gate_pre.reshape(wide), keep, state.reshape(wide)
    )
    grad_gate = grad_gate.reshape(row_count, LRU)
    width = LRU // 4
    in_gate_sum = Reduction(
        first_own,
        first_far,
        lambda n: lax.dynamic_slice_in_dim(grad_gate, n * width, width, 1),
        width,
    )
    sent = (*up_sum.third(), *out_sum.second(), *in_gate_sum.sent)
    local = tie(local, *sent)
    head_pull, head_prod = chunk_ends(rev_chunks, True)
    rev_carry = shard_carry(head_pull, head_prod, True)
    rev_carries = chunk_carries(rev_chunks, rev_carry, True)
    before = jnp.broadcast_to(carry_in[:, None], (seq_count, HALO, LRU))
    du, tail, edge, grad_gates, grad_taps, grad_decay = mixer_backward(
        local, rev_prod, rev_carries, state.reshape(wide), before, conv_low, inner_low,
        prev_inner, dist, gates_all, taps_all, soft,
    )
    grad_decay_row = grad_decay[0] * jax.nn.sigmoid(-decay_float)
    flat = jnp.concatenate(
        [
            grad_gates.reshape(last + 1, -1),
            grad_taps[:CONV].reshape(CONV, last + 1, n_lru).transpose(1, 0, 2).reshape(last + 1, -1),
            grad_decay_row.reshape(last + 1, n_lru),
        ],
        axis=1,
    ).astype(BF16)
    flat = lax.psum_scatter(flat.reshape(-1, HS), "seq", scatter_dimension=0, tiled=True)
    flat = lax.psum(flat, "grp").astype(F32).reshape(-1)
    n_gates = flat.shape[0] - (CONV + 1) * n_lru
    gates_total = flat[:n_gates].reshape(gate_heads.shape)
    taps_total = flat[n_gates : n_gates + CONV * n_lru].reshape(CONV, n_lru)
    decay_total = flat[n_gates + CONV * n_lru :]
    sent = (*in_gate_sum.second(), *out_sum.third())
    du = tie(du, *sent)
    up_total = up_sum.finish()
    returned = from_behind(edge[:, HALO - edge_len :].astype(BF16), "seq", -1).astype(F32)
    returned = jnp.pad(returned, ((0, 0), (HALO - edge_len, 0), (0, 0)))
    grad_inner = lax.dynamic_update_slice(
        du, (tail + returned).astype(BF16), (0, shard_len - HALO, 0)
    )
    grad_inner = grad_inner.reshape(row_count, LRU)
    in_value_sum = Reduction(
        first_own,
        first_far,
        lambda n: lax.dynamic_slice_in_dim(grad_inner, n * width, width, 1),
        width,
    )
    grad_inner = tie(grad_inner, *in_value_sum.sent)
    grad_first_normed = dot_far(grad_inner, proj_in[:, :LRU]) + dot_far(
        grad_gate, proj_in[:, LRU:]
    )
    sent = (*in_gate_sum.third(), *in_value_sum.second())
    grad_first_normed = tie(grad_first_normed, *sent)
    out_total = out_sum.finish()
    grad_tokens = grad_resid + norm_back(inputs, first_scale, gain_one, grad_first_normed)
    grad_tokens = grad_tokens.astype(BF16).reshape(seq_count, shard_len, D)
    in_value_sum.third()
    in_total = jnp.concatenate([in_value_sum.finish(), in_gate_sum.finish()], axis=1)
    first_total = gain_grad(in_proj, in_total, first_gain)
    second_total = gain_grad(up_proj, up_total, second_gain)
    return (
        block_out, grad_tokens, first_total, in_total, taps_total, decay_total, gates_total,
        out_total, second_total, up_total, down_total,
    )


def solution(mesh):
    in_specs = (
        P("grp", "seq", None),
        P("grp", "seq"),
        P("grp", "seq", None),
        P("seq"),
        P("seq", None),
        P(None, "seq"),
        P("seq"),
        P("seq", None, None),
        P("seq", None),
        P("seq"),
        P("seq", None),
        P("seq", None),
    )
    out_specs = (
        P("grp", "seq", None),
        P("grp", "seq", None),
        P("seq"),
        P("seq", None),
        P(None, "seq"),
        P("seq"),
        P("seq", None, None),
        P("seq", None),
        P("seq"),
        P("seq", None),
        P("seq", None),
    )
    return jax.shard_map(body, mesh=mesh, in_specs=in_specs, out_specs=out_specs, check_vma=False)
```

```python
import functools

import jax
import jax.numpy as jnp
from jax import lax
from jax.experimental import pallas as pl
from jax.experimental.pallas import tpu as pltpu
from jax.sharding import PartitionSpec as P

D = 1536
HEADS = 16
HS = 128
LRU = 2048
FF = 4608
CONV = 4
CHUNKS = 8
HALO = 8
BACK = 8 * (CONV - 1)
TAIL = 32
F32 = jnp.float32
BF16 = jnp.bfloat16


def from_behind(value, axis, steps):
    count = lax.axis_size(axis)
    first, last = (max(0, -steps), min(count, count - steps))
    return lax.ppermute(value, axis, [(source, source + steps) for source in range(first, last)])


def gelu_parts(v):
    k = 0.7978845608028654
    square = v * v
    t = jnp.tanh(k * v * (1.0 + 0.044715 * square))
    half = 0.5 * (1.0 + t)
    slope = half + 0.5 * v * (1.0 - t * t) * (k * (1.0 + 3.0 * 0.044715 * square))
    return v * half, slope


def gelu_tanh(v):
    k = 0.7978845608028654
    return 0.5 * v * (1.0 + jnp.tanh(k * v * (1.0 + 0.044715 * v * v)))


def sigmoid(v):
    return 0.5 * jnp.tanh(0.5 * v) + 0.5


def drive_values(q_rate, q_input, soft):
    rate = sigmoid(q_rate)
    inp = sigmoid(q_input)
    decay = jnp.exp(-8.0 * rate * soft)
    root = jnp.sqrt(1.0 - decay * decay + 0.001)
    return rate, inp, decay, root


def shifted_group(group, step, fill):
    row = lax.broadcasted_iota(jnp.int32, group.shape, 0)
    edge = 0 if step == 1 else CHUNKS - 1
    moved = pltpu.roll(group, step % CHUNKS, 0)
    return jnp.where(row == edge, fill, moved)


def extend_back(ext_s, u_ref, halo_ref, b):
    rows = u_ref.shape[1]
    ext_s[pl.ds(BACK, rows), :] = u_ref[b].astype(F32)
    halo = halo_ref[b].astype(F32)
    for m in range(CONV - 1):
        group = ext_s[pl.ds(BACK + rows - BACK + 8 * m, 8), :]
        fill = halo[HALO - CONV + 1 + m : HALO - CONV + 2 + m, :]
        ext_s[pl.ds(8 * m, 8), :] = shifted_group(group, 1, fill)


def mixer_forward_kernel(
    u_ref, halo_ref, dist_ref, gates_ref, taps_ref, soft_ref,
    c_ref, keep_ref, state_ref, prod_ref, chunk_ref,
    ext_s, c_s, rate_s, inp_s,
):
    seqs, rows, _ = u_ref.shape
    soft = soft_ref[...]
    for b in range(seqs):
        extend_back(ext_s, u_ref, halo_ref, b)

        def conv_chunk(n, _):
            at = pl.multiple_of(n * 64, 64)
            far = dist_ref[b, pl.ds(at, 64), :]
            total = taps_ref[0:1, :] * ext_s[pl.ds(at + BACK, 64), :]
            for k in range(1, CONV):
                window = taps_ref[k : k + 1, :] * ext_s[pl.ds(at + BACK - 8 * k, 64), :]
                total = total + jnp.where(far >= float(k), window, 0.0)
            low = total.astype(BF16)
            c_ref[b, pl.ds(at, 64), :] = low
            c_s[b, pl.ds(at, 64), :] = low.astype(F32)
            return 0

        lax.fori_loop(0, rows // 64, conv_chunk, 0)
        both = jnp.dot(c_ref[b], gates_ref[0], preferred_element_type=F32)
        rate_s[b] = both[:, :HS]
        inp_s[b] = both[:, HS:]

    def scan_step(j, carry):
        new = []
        for b in range(seqs):
            at = pl.ds(pl.multiple_of(j * 8, 8), 8)
            state, prod = carry[b]
            _, inp, decay, root = drive_values(rate_s[b, at, :], inp_s[b, at, :], soft)
            keep = jnp.where(dist_ref[b, at, :] >= 1.0, decay, 0.0)
            state = keep * state + root * inp * c_s[b, at, :]
            prod = keep * prod
            keep_ref[b, at, :] = keep
            state_ref[b, at, :] = state
            prod_ref[b, at, :] = prod
            new.append((state, prod))
        return tuple(new)

    zero, one = jnp.zeros((CHUNKS, HS), F32), jnp.ones((CHUNKS, HS), F32)
    ends = lax.fori_loop(0, rows // CHUNKS, scan_step, ((zero, one),) * seqs, unroll=8)
    for b in range(seqs):
        chunk_ref[b, 0] = ends[b][0]
        chunk_ref[b, 1] = ends[b][1]


def branch_kernel(core_ref, state_ref, prod_ref, carry_ref, gate_ref, out_ref, branch_ref, split_ref):
    del core_ref
    seqs, rows, _ = state_ref.shape
    for b in range(seqs):
        carry = jnp.concatenate([carry_ref[b]] * 4, axis=0)

        def point(n, _):
            at = pl.ds(pl.multiple_of(n * 32, 32), 32)
            state = state_ref[b, at, :] + prod_ref[b, at, :] * carry
            out_ref[b, at, :] = state
            low = (state * gelu_tanh(gate_ref[b, at, :])).astype(BF16)
            branch_ref[b, at, :] = low
            split_ref[0, b, at, :] = low
            return 0

        lax.fori_loop(0, rows // 32, point, 0, unroll=4)


def reverse_kernel(
    grad_ref, gate_ref, keep_ref, state_ref,
    dg_ref, local_ref, prod_ref, chunk_ref,
):
    seqs, rows, _ = grad_ref.shape
    pairs = rows // 16

    def scan_step(n, carry):
        first = pl.multiple_of((pairs - 1 - n) * 16, 16)
        at = pl.ds(first, 16)
        new = []
        for b in range(seqs):
            pull, prod = carry[b]
            act, slope = gelu_parts(gate_ref[b, at, :])
            grad = grad_ref[b, at, :]
            dg_ref[b, at, :] = (grad * state_ref[b, at, :] * slope).astype(BF16)
            dh = grad * act
            keep = keep_ref[b, at, :]
            late = dh[8:] + pull
            late_prod = prod
            pull, prod = keep[8:] * late, keep[8:] * prod
            early = dh[:8] + pull
            local_ref[b, at, :] = jnp.concatenate([early, late], axis=0)
            prod_ref[b, at, :] = jnp.concatenate([prod, late_prod], axis=0)
            new.append((keep[:8] * early, keep[:8] * prod))
        return tuple(new)

    zero, one = jnp.zeros((CHUNKS, HS), F32), jnp.ones((CHUNKS, HS), F32)
    ends = lax.fori_loop(0, pairs, scan_step, ((zero, one),) * seqs, unroll=4)
    for b in range(seqs):
        chunk_ref[b, 0] = ends[b][0]
        chunk_ref[b, 1] = ends[b][1]


def mixer_backward_kernel(
    local_ref, prod_ref, carry_ref, state_ref, before_ref, c_ref, u_ref, halo_ref, dist_ref,
    gates_ref, taps_ref, soft_ref,
    du_ref, tail_ref, edge_ref, ggate_ref, gtaps_ref, gdecay_ref,
    q_s, dq_s, dc_s, h_s, ext_s, dist_s,
):
    seqs, rows, _ = local_ref.shape
    soft = soft_ref[...]
    ggate = jnp.zeros((HS, 2 * HS), F32)
    decay_sum = jnp.zeros((8, HS), F32)
    taps_sum = [jnp.zeros((8, HS), F32) for _ in range(CONV)]

    def fold(value):
        return jnp.sum(value.reshape(value.shape[0] // 8, 8, HS), axis=0)

    for b in range(seqs):
        q_s[...] = jnp.dot(c_ref[b], gates_ref[0], preferred_element_type=F32)
        h_s[pl.ds(0, 8), :] = before_ref[b]
        h_s[pl.ds(8, rows), :] = state_ref[b]
        carry = jnp.concatenate([carry_ref[b]] * 4, axis=0)

        def point(n, total):
            first = pl.multiple_of(n * 32, 32)
            at = pl.ds(first, 32)
            lam = local_ref[b, at, :] + prod_ref[b, at, :] * carry
            rate, inp, decay, root = drive_values(q_s[at, :HS], q_s[at, HS:], soft)
            conv = c_ref[b, at, :].astype(F32)
            kept = jnp.where(dist_ref[b, at, :] >= 1.0, h_s[at, :], 0.0)
            lam_root = lam * root
            lam_inp = lam * inp
            grad_decay = lam * kept - lam_inp * conv * decay / root
            rated = grad_decay * decay * rate
            dq_s[at, :HS] = (-8.0 * soft * rated * (1.0 - rate)).astype(BF16)
            dq_s[at, HS:] = (lam_root * conv * inp * (1.0 - inp)).astype(BF16)
            dc_s[at, :] = lam_root * inp
            return total + fold(rated)

        decay_sum = lax.fori_loop(0, rows // 32, point, decay_sum, unroll=2)
        dc_s[pl.ds(0, rows), :] += lax.dot_general(
            dq_s[...], gates_ref[0], (((1,), (1,)), ((), ())), preferred_element_type=F32
        )
        ggate = ggate + lax.dot_general(
            c_ref[b], dq_s[...], (((0,), (0,)), ((), ())), preferred_element_type=F32
        )
        extend_back(ext_s, u_ref, halo_ref, b)
        dist_s[pl.ds(0, rows), :] = dist_ref[b]
        for m in range(CONV - 1):
            for held in (dc_s, dist_s):
                held[pl.ds(rows + 8 * m, 8), :] = shifted_group(held[pl.ds(8 * m, 8), :], -1, 0.0)

        def conv_chunk(n, totals):
            at = pl.multiple_of(n * 64, 64)
            grad = dc_s[pl.ds(at, 64), :]
            far = dist_s[pl.ds(at, 64), :]
            out = taps_ref[0:1, :] * grad
            totals = list(totals)
            totals[0] = totals[0] + fold(grad * ext_s[pl.ds(at + BACK, 64), :])
            for k in range(1, CONV):
                masked = jnp.where(far >= float(k), grad, 0.0)
                totals[k] = totals[k] + fold(masked * ext_s[pl.ds(at + BACK - 8 * k, 64), :])
                ahead = pl.ds(at + 8 * k, 64)
                value = taps_ref[k : k + 1, :] * dc_s[ahead, :]
                out = out + jnp.where(dist_s[ahead, :] >= float(k), value, 0.0)
            du_ref[b, pl.ds(at, 64), :] = out.astype(BF16)

            @pl.when(n == rows // 64 - 1)
            def _():
                tail_ref[b] = out[64 - TAIL :, :]

            return tuple(totals)

        taps_sum = list(lax.fori_loop(0, rows // 64, conv_chunk, tuple(taps_sum)))
        edges = [jnp.zeros((HALO - CONV + 1, HS), F32)]
        for m in range(CONV - 1, 0, -1):
            edge = jnp.zeros((1, HS), F32)
            for k in range(m, CONV):
                at = pl.ds(8 * (k - m), 1)
                masked = jnp.where(dist_s[at, :] >= float(k), dc_s[at, :], 0.0)
                edge = edge + taps_ref[k : k + 1, :] * masked
            edges.append(edge)
        edge_ref[b] = jnp.concatenate(edges, axis=0)
    ggate_ref[0] = ggate
    gdecay_ref[...] = jnp.broadcast_to(
        8.0 * jnp.sum(decay_sum, axis=0, keepdims=True), (8, HS)
    )
    gtaps_ref[...] = jnp.concatenate(
        [jnp.sum(t, axis=0, keepdims=True) for t in taps_sum] + [jnp.zeros((8 - CONV, HS), F32)],
        axis=0,
    )


def norm_kernel(shards, core_ref, x_ref, gain_ref, normed_ref, own_ref, far_ref, scale_ref):
    x = x_ref[...].astype(F32)
    scale = lax.rsqrt(jnp.mean(x * x, axis=-1, keepdims=True) + 1e-06)
    low = (x * scale * gain_ref[...]).astype(BF16)
    normed_ref[...] = low
    scale_ref[...] = jnp.broadcast_to(scale, scale_ref.shape)
    wide = low.astype(F32)
    size = D // shards
    even, odd = (
        jnp.concatenate([wide[:, n * size : (n + 1) * size] for n in range(c, shards, 2)], axis=1)
        for c in range(2)
    )
    first = core_ref[0] == 0
    own_ref[...] = jnp.where(first, even, odd).astype(BF16)
    far_ref[...] = jnp.where(first, odd, even).astype(BF16)


def ffn_forward_kernel(n_ref, gate_ref, up_ref, hidden_ref, pull_ref):
    for m in range(0, n_ref.shape[0], 256):
        at = pl.ds(m, 256)
        e1 = jnp.dot(n_ref[at, :], gate_ref[...], preferred_element_type=F32)
        e2 = jnp.dot(n_ref[at, :], up_ref[...], preferred_element_type=F32)
        act, slope = gelu_parts(e1)
        hidden_ref[at, :] = (act * e2).astype(BF16)
        pull_ref[0, at, :] = (slope * e2).astype(BF16)
        pull_ref[1, at, :] = act.astype(BF16)


def ffn_backward_kernel(grad_ref, down_ref, pull_ref, out_ref):
    for m in range(0, grad_ref.shape[0], 256):
        at = pl.ds(m, 256)
        dv = lax.dot_general(
            grad_ref[at, :], down_ref[...], (((1,), (1,)), ((), ())), preferred_element_type=F32
        )
        out_ref[0, at, :] = (dv * pull_ref[0, at, :].astype(F32)).astype(BF16)
        out_ref[1, at, :] = (dv * pull_ref[1, at, :].astype(F32)).astype(BF16)


def head_block(lead, rows):
    return pl.BlockSpec((lead, rows, HS), lambda h: (0, 0, h))


def shared_block(shape):
    return pl.BlockSpec(shape, lambda h: (0,) * len(shape))


def pair_block(seqs):
    return pl.BlockSpec((seqs, 2, CHUNKS, HS), lambda h: (0, 0, 0, h))


PARAMS = pltpu.CompilerParams(vmem_limit_bytes=40 * 1024 * 1024)


def mixer_forward(u, halo, dist, gates, taps, soft):
    seqs, rows, _ = u.shape
    full = head_block(seqs, rows)
    wide = jax.ShapeDtypeStruct((seqs, rows, LRU), F32)
    return pl.pallas_call(
        mixer_forward_kernel,
        grid=(HEADS,),
        in_specs=[
            full,
            head_block(seqs, HALO),
            shared_block((seqs, rows, HS)),
            pl.BlockSpec((1, HS, 2 * HS), lambda h: (h, 0, 0)),
            pl.BlockSpec((CONV, HS), lambda h: (0, h)),
            pl.BlockSpec((1, HS), lambda h: (0, h)),
        ],
        out_specs=[full, full, full, full, pair_block(seqs)],
        out_shape=[
            jax.ShapeDtypeStruct((seqs, rows, LRU), BF16),
            wide,
            wide,
            wide,
            jax.ShapeDtypeStruct((seqs, 2, CHUNKS, LRU), F32),
        ],
        scratch_shapes=[
            pltpu.VMEM((rows + BACK, HS), F32),
            pltpu.VMEM((seqs, rows, HS), F32),
            pltpu.VMEM((seqs, rows, HS), F32),
            pltpu.VMEM((seqs, rows, HS), F32),
        ],
        compiler_params=PARAMS,
        name="mixer_forward",
    )(u, halo, dist, gates, taps, soft)


def mixer_branch(state, prod, carry, gate, shards, core):
    seqs, rows, _ = state.shape
    per = HEADS // shards

    def at(h, core_ref):
        return (0, 0, h)

    def split_at(h, core_ref):
        shard = h // per
        return ((shard % 2 + core_ref[0]) % 2, 0, 0, (shard // 2) * per + h % per)

    full = pl.BlockSpec((seqs, rows, HS), at)
    return pl.pallas_call(
        branch_kernel,
        grid_spec=pltpu.PrefetchScalarGridSpec(
            num_scalar_prefetch=1,
            grid=(HEADS,),
            in_specs=[full, full, pl.BlockSpec((seqs, CHUNKS, HS), at), full],
            out_specs=[full, full, pl.BlockSpec((1, seqs, rows, HS), split_at)],
        ),
        out_shape=[
            jax.ShapeDtypeStruct((seqs, rows, LRU), F32),
            jax.ShapeDtypeStruct((seqs, rows, LRU), BF16),
            jax.ShapeDtypeStruct((2, seqs, rows, LRU // 2), BF16),
        ],
        compiler_params=PARAMS,
        name="mixer_branch",
    )(core.reshape(1), state, prod, carry, gate)


def mixer_reverse(grad, gate, keep, state):
    seqs, rows, _ = grad.shape
    full = head_block(seqs, rows)
    wide = jax.ShapeDtypeStruct((seqs, rows, LRU), F32)
    return pl.pallas_call(
        reverse_kernel,
        grid=(HEADS,),
        in_specs=[full, full, full, full],
        out_specs=[full, full, full, pair_block(seqs)],
        out_shape=[
            jax.ShapeDtypeStruct((seqs, rows, LRU), BF16),
            wide,
            wide,
            jax.ShapeDtypeStruct((seqs, 2, CHUNKS, LRU), F32),
        ],
        compiler_params=PARAMS,
        name="mixer_reverse",
    )(grad, gate, keep, state)


def mixer_backward(local, prod, carry, state, before, c, u, halo, dist, gates, taps, soft):
    seqs, rows, _ = local.shape
    full = head_block(seqs, rows)
    small = head_block(seqs, HALO)
    gate_block = pl.BlockSpec((1, HS, 2 * HS), lambda h: (h, 0, 0))
    row_block = pl.BlockSpec((8, HS), lambda h: (0, h))
    return pl.pallas_call(
        mixer_backward_kernel,
        grid=(HEADS,),
        in_specs=[
            full,
            full,
            head_block(seqs, CHUNKS),
            full,
            small,
            full,
            full,
            small,
            shared_block((seqs, rows, HS)),
            gate_block,
            pl.BlockSpec((CONV, HS), lambda h: (0, h)),
            pl.BlockSpec((1, HS), lambda h: (0, h)),
        ],
        out_specs=[full, head_block(seqs, TAIL), small, gate_block, row_block, row_block],
        out_shape=[
            jax.ShapeDtypeStruct((seqs, rows, LRU), BF16),
            jax.ShapeDtypeStruct((seqs, TAIL, LRU), F32),
            jax.ShapeDtypeStruct((seqs, HALO, LRU), F32),
            jax.ShapeDtypeStruct((HEADS, HS, 2 * HS), F32),
            jax.ShapeDtypeStruct((8, LRU), F32),
            jax.ShapeDtypeStruct((8, LRU), F32),
        ],
        scratch_shapes=[
            pltpu.VMEM((rows, 2 * HS), F32),
            pltpu.VMEM((rows, 2 * HS), BF16),
            pltpu.VMEM((rows + BACK, HS), F32),
            pltpu.VMEM((rows + 8, HS), F32),
            pltpu.VMEM((rows + BACK, HS), F32),
            pltpu.VMEM((rows + BACK, HS), F32),
        ],
        compiler_params=PARAMS,
        name="mixer_backward",
    )(local, prod, carry, state, before, c, u, halo, dist, gates, taps, soft)


def rms_norm(x, gain, shards, core):
    rows = x.shape[0]
    block = min(rows, 256)
    return pl.pallas_call(
        functools.partial(norm_kernel, shards),
        grid=(rows // block,),
        in_specs=[
            pl.BlockSpec(memory_space=pltpu.SMEM),
            pl.BlockSpec((block, D), lambda n: (n, 0)),
            pl.BlockSpec((1, D), lambda n: (0, 0)),
        ],
        out_specs=[
            pl.BlockSpec((block, D), lambda n: (n, 0)),
            pl.BlockSpec((block, D // 2), lambda n: (n, 0)),
            pl.BlockSpec((block, D // 2), lambda n: (n, 0)),
            pl.BlockSpec((block, 128), lambda n: (n, 0)),
        ],
        out_shape=[
            jax.ShapeDtypeStruct((rows, D), BF16),
            jax.ShapeDtypeStruct((rows, D // 2), BF16),
            jax.ShapeDtypeStruct((rows, D // 2), BF16),
            jax.ShapeDtypeStruct((rows, 128), F32),
        ],
        compiler_params=PARAMS,
        name="rms_norm",
    )(core.reshape(1), x, gain.reshape(1, D))


FF_TILE = 512


def ffn_forward(normed, proj_up):
    rows = normed.shape[0]
    steps = FF // FF_TILE
    return pl.pallas_call(
        ffn_forward_kernel,
        grid=(steps,),
        in_specs=[
            pl.BlockSpec((rows, D), lambda n: (0, 0)),
            pl.BlockSpec((D, FF_TILE), lambda n: (0, n)),
            pl.BlockSpec((D, FF_TILE), lambda n: (0, n + steps)),
        ],
        out_specs=[
            pl.BlockSpec((rows, FF_TILE), lambda n: (0, n)),
            pl.BlockSpec((2, rows, FF_TILE), lambda n: (0, 0, n)),
        ],
        out_shape=[
            jax.ShapeDtypeStruct((rows, FF), BF16),
            jax.ShapeDtypeStruct((2, rows, FF), BF16),
        ],
        compiler_params=PARAMS,
        name="ffn_forward",
    )(normed, proj_up, proj_up)


def ffn_backward(grad, proj_down, pull):
    rows = grad.shape[0]
    return pl.pallas_call(
        ffn_backward_kernel,
        grid=(FF // FF_TILE,),
        in_specs=[
            pl.BlockSpec((rows, D), lambda n: (0, 0)),
            pl.BlockSpec((FF_TILE, D), lambda n: (n, 0)),
            pl.BlockSpec((2, rows, FF_TILE), lambda n: (0, 0, n)),
        ],
        out_specs=pl.BlockSpec((2, rows, FF_TILE), lambda n: (0, 0, n)),
        out_shape=jax.ShapeDtypeStruct((2, rows, FF), BF16),
        compiler_params=PARAMS,
        name="ffn_backward",
    )(grad, proj_down, pull)


def gather_rows(shard):
    parts = lax.axis_size("grp")
    rows = shard.shape[0] // parts
    own = lax.dynamic_slice_in_dim(shard, lax.axis_index("grp") * rows, rows, 0)
    return lax.all_gather(own, ("seq", "grp"), axis=0, tiled=True)


def tie(value, *after):
    return lax.optimization_barrier((value, *after))[0]


def xor_pairs(axis, bit):
    return [(i, i ^ bit) for i in range(lax.axis_size(axis))]


def ring_pairs(steps):
    count = lax.axis_size("seq")
    return [(i, (i + steps) % count) for i in range(count)]


def dot_rows(a, b):
    return lax.dot_general(a, b, (((0,), (0,)), ((), ())), preferred_element_type=F32)


def reduce_rows(partial):
    part = lax.psum_scatter(partial, "seq", scatter_dimension=0, tiled=True)
    part = lax.psum_scatter(part, "grp", scatter_dimension=0, tiled=True)
    return lax.all_gather(part, "grp", axis=0, tiled=True).astype(F32)


def dot_far(a, b):
    return lax.dot_general(a, b, (((1,), (1,)), ((), ())), preferred_element_type=F32)


def by_position(a):
    seqs, rows = a.shape[:2]
    return a.reshape(seqs, CHUNKS, rows // CHUNKS, *a.shape[2:]).swapaxes(1, 2).reshape(a.shape)


def by_token(a):
    seqs, rows = a.shape[:2]
    return a.reshape(seqs, rows // CHUNKS, CHUNKS, *a.shape[2:]).swapaxes(1, 2).reshape(a.shape)


class Reduction:
    def __init__(self, a_own, a_far, columns, width):
        self.simple = lax.axis_size("grp") != 4
        count = lax.axis_size("seq")
        place = lax.axis_index("seq")
        self.chips = count // 2
        self.chip, core = place // 2, place % 2
        self.width = width
        full = a_own.shape[1]
        self.rows = full // self.chips
        self.half = full // 2
        self.a_own = a_own
        if self.simple:
            parts = [columns(k) for k in range(4)]
            own, far = (
                jnp.concatenate([dot_rows(a, part) for part in parts], axis=1)
                for a in (a_own, a_far)
            )
            cores = jnp.stack(
                [jnp.where(core == c, own, far).reshape(self.chips, self.rows, -1) for c in (0, 1)],
                axis=1,
            )
            self.product = cores.reshape(2 * full, 4 * width).astype(BF16)
            self.sent = (self.product,)
            return
        group = lax.axis_index("grp")
        self.x, self.y = xor_pairs("grp", 1), xor_pairs("grp", 2)
        self.b = [columns(group ^ k) for k in range(4)]
        self.far = [None] * 4
        for k in (3, 1, 2, 0):
            product = dot_rows(a_far, self.b[k]).astype(BF16)
            self.far[k] = lax.ppermute(product, "seq", xor_pairs("seq", 1))
        half = self.half
        self.sent = (
            self.own(3, 0, half).astype(BF16),
            self.own(3, half, full).astype(BF16),
        )
        self.diag_a = lax.ppermute(self.sent[0], "grp", self.x)
        self.diag_b = lax.ppermute(self.sent[1], "grp", self.y)

    def own(self, k, first, last):
        product = dot_rows(self.a_own[:, first:last], self.b[k])
        return product + self.far[k][first:last].astype(F32)

    def second(self, *after):
        if self.simple:
            return ()
        full, none = 2 * self.half, ((0, self.half), (0, 0))
        diag_a, diag_b = self.diag_a, self.diag_b
        if after:
            diag_a, diag_b = tie((diag_a, diag_b), *after)
        sent = (
            (self.own(1, 0, full) + jnp.pad(diag_b.astype(F32), (none[0][::-1], (0, 0)))).astype(BF16),
            (self.own(2, 0, full) + jnp.pad(diag_a.astype(F32), none)).astype(BF16),
        )
        self.from_x = lax.ppermute(sent[0], "grp", self.x)
        self.from_y = lax.ppermute(sent[1], "grp", self.y)
        return sent

    def third(self, *after, offload=False):
        if self.simple:
            return ()
        from_x, from_y = self.from_x, self.from_y
        if after:
            from_x, from_y = tie((from_x, from_y), *after)
        mine = self.own(0, 0, 2 * self.half) + from_x.astype(F32) + from_y.astype(F32)
        mine = mine.astype(BF16)
        self.kept = None
        if offload:
            count = 2 * self.chips
            cores = [list(range(c, count, 2)) for c in range(2)]
            self.arrived = lax.psum_scatter(
                mine, "seq", scatter_dimension=0, axis_index_groups=cores, tiled=True
            )
            return (mine,)
        mine = mine.reshape(self.chips, self.rows, self.width)
        self.kept = lax.dynamic_index_in_dim(mine, self.chip, 0, False)
        sent = tuple(
            lax.dynamic_index_in_dim(mine, (self.chip + j) % self.chips, 0, False)
            for j in range(1, self.chips)
        )
        self.arrived = [
            lax.ppermute(part, "seq", ring_pairs(2 * j + 2)) for j, part in enumerate(sent)
        ]
        return sent

    def finish(self):
        if self.simple:
            return reduce_rows(self.product)
        total = self.arrived
        if self.kept is not None:
            total = self.kept.astype(F32)
            for part in self.arrived:
                total = total + part.astype(F32)
        parts = lax.all_gather(total.astype(BF16), "grp")
        return parts.transpose(1, 0, 2).reshape(self.rows, 4 * self.width).astype(F32)


def shard_carry(ends, prods, reverse):
    count = lax.axis_size("seq")
    place = lax.axis_index("seq")
    both = lax.all_gather(jnp.stack([ends, prods]), "seq")
    carry = jnp.zeros_like(ends)
    for step in range(count - 1):
        source = count - 1 - step if reverse else step
        ahead = source > place if reverse else source < place
        carry = jnp.where(ahead, both[source, 0] + both[source, 1] * carry, carry)
    return carry


def chunk_ends(chunks, reverse):
    state = jnp.zeros_like(chunks[:, 0, 0])
    prod = jnp.ones_like(state)
    order = range(CHUNKS - 1, -1, -1) if reverse else range(CHUNKS)
    for n in order:
        state = chunks[:, 0, n] + chunks[:, 1, n] * state
        prod = chunks[:, 1, n] * prod
    return state, prod


def chunk_carries(chunks, carry, reverse):
    order = range(CHUNKS - 1, -1, -1) if reverse else range(CHUNKS)
    found = [None] * CHUNKS
    for n in order:
        found[n] = carry
        carry = chunks[:, 0, n] + chunks[:, 1, n] * carry
    return jnp.stack(found, axis=1)


def norm_back(values, scale, gain, grad_normed):
    weighted = grad_normed * gain
    cubed = scale * scale * scale
    return scale * weighted - values * cubed * jnp.mean(weighted * values, axis=-1, keepdims=True)


def gain_grad(weight, grad_weight, gain):
    return jnp.sum(weight.astype(F32) * grad_weight, axis=1) / gain.astype(F32)


def body(
    tokens, seg_ids, cotangent, first_gain, in_proj, conv_taps, decay_param, gate_heads,
    out_proj, second_gain, up_proj, down_proj,
):
    seq_count, shard_len, _ = tokens.shape
    row_count = seq_count * shard_len
    edge_len = CONV - 1
    place = lax.axis_index("seq")
    last = lax.axis_size("seq") - 1

    small = jnp.concatenate(
        [first_gain, second_gain, decay_param, conv_taps.reshape(-1)]
    )
    small_all = lax.all_gather(small, "seq")
    n_gain, n_lru = first_gain.shape[0], decay_param.shape[0]
    gain_one = small_all[:, :n_gain].reshape(D).astype(F32)
    gain_two = small_all[:, n_gain : 2 * n_gain].reshape(D).astype(F32)
    decay_float = small_all[:, 2 * n_gain : 2 * n_gain + n_lru].reshape(LRU).astype(F32)
    taps_all = (
        small_all[:, 2 * n_gain + n_lru :].reshape(-1, CONV, n_lru).transpose(1, 0, 2)
    ).reshape(CONV, LRU).astype(F32)
    proj_in = gather_rows(in_proj)
    gates_all = lax.all_gather(gate_heads, "seq", axis=0, tiled=True)
    proj_out = gather_rows(out_proj)
    proj_up = gather_rows(up_proj)
    proj_down = gather_rows(down_proj)

    tokens = by_position(tokens)
    cotangent = by_position(cotangent)
    inputs = tokens.reshape(row_count, D).astype(F32)
    first_normed, first_own, first_far, first_scale = rms_norm(
        tokens.reshape(row_count, D), gain_one, last + 1, place % 2
    )
    first_scale = first_scale[:, :1]
    wide = (seq_count, shard_len, LRU)
    inner_low = jnp.dot(first_normed, proj_in[:, :LRU], preferred_element_type=F32).astype(BF16)
    inner_low = inner_low.reshape(wide)

    step = shard_len // CHUNKS
    final = inner_low.reshape(seq_count, step, CHUNKS, LRU)[:, step - HALO :, CHUNKS - 1]
    prev_inner = from_behind(final, "seq", 1)
    prev_ids = from_behind(seg_ids[:, shard_len - edge_len :], "seq", 1)
    prev_ids = jnp.where(place == 0, -1, prev_ids)
    ext_ids = jnp.concatenate([prev_ids, seg_ids], axis=1)
    dist = jnp.zeros((seq_count, shard_len), F32)
    for k in range(1, CONV):
        dist = dist + (ext_ids[:, edge_len - k : edge_len - k + shard_len] == seg_ids).astype(F32)
    dist = jnp.broadcast_to(by_position(dist)[:, :, None], (seq_count, shard_len, HS))
    soft = jax.nn.softplus(-decay_float).reshape(1, LRU)

    conv_low, keep, state_part, prod_part, chunks = mixer_forward(
        inner_low, prev_inner, dist, gates_all, taps_all, soft
    )
    end_state, end_prod = chunk_ends(chunks, False)
    gate_pre = jnp.dot(first_normed, proj_in[:, LRU:], preferred_element_type=F32).reshape(wide)
    carry_in = shard_carry(end_state, end_prod, False)
    carries = chunk_carries(chunks, carry_in, False)
    state, branch, branch_split = mixer_branch(
        state_part, prod_part, carries, gate_pre, last + 1, place % 2
    )
    branch_split = branch_split.reshape(2, row_count, LRU // 2)
    resid = inputs + jnp.dot(
        branch.reshape(row_count, LRU), proj_out, preferred_element_type=F32
    )
    second_normed, second_own, second_far, second_scale = rms_norm(
        resid, gain_two, last + 1, place % 2
    )
    second_scale = second_scale[:, :1]
    hidden, pull = ffn_forward(second_normed, proj_up)

    grad_out = cotangent.reshape(row_count, D)
    grad_down = dot_rows(hidden, grad_out).astype(BF16)
    down_part = lax.psum_scatter(grad_down, "seq", scatter_dimension=0, tiled=True)
    grad_expanded = ffn_backward(tie(grad_out, grad_down), proj_down, pull)
    quarter = FF // 2

    def up_columns(n):
        part = lax.dynamic_slice(
            grad_expanded, (n // 2, 0, (n % 2) * quarter), (1, row_count, quarter)
        )
        return part[0]

    up_sum = Reduction(second_own, second_far, up_columns, quarter)
    grad_expanded = tie(grad_expanded, *up_sum.sent)
    grad_second_normed = dot_far(grad_expanded[0], proj_up[:, :FF]) + dot_far(
        grad_expanded[1], proj_up[:, FF:]
    )
    sent = up_sum.second(grad_second_normed)
    grad_second_normed = tie(grad_second_normed, *sent)
    grad_resid = grad_out.astype(F32) + norm_back(
        resid, second_scale, gain_two, grad_second_normed
    )
    grad_mixer = grad_resid.astype(BF16)
    out_sum = Reduction(
        branch_split[0],
        branch_split[1],
        lambda n: lax.dynamic_slice_in_dim(grad_mixer, n * (D // 4), D // 4, 1),
        D // 4,
    )
    grad_branch = dot_far(tie(grad_mixer, *out_sum.sent), proj_out)

    grad_gate, local, rev_prod, rev_chunks = mixer_reverse(
        grad_branch.reshape(wide), gate_pre, keep, state
    )
    head_pull, head_prod = chunk_ends(rev_chunks, True)
    grad_gate = grad_gate.reshape(row_count, LRU)
    width = LRU // 4
    sent = (*out_sum.second(head_pull), *up_sum.third(head_pull, down_part, offload=True))
    grad_gate = tie(grad_gate, *sent)
    in_gate_sum = Reduction(
        first_own,
        first_far,
        lambda n: lax.dynamic_slice_in_dim(grad_gate, n * width, width, 1),
        width,
    )
    rev_carry = shard_carry(head_pull, head_prod, True)
    rev_carries = chunk_carries(rev_chunks, rev_carry, True)
    local = tie(local, *in_gate_sum.sent)
    du, tail, edge, grad_gates, grad_taps, grad_decay = mixer_backward(
        local, rev_prod, rev_carries, state, carries, conv_low, inner_low,
        prev_inner, dist, gates_all, taps_all, soft,
    )
    returned = from_behind(edge[:, HALO - edge_len :].astype(BF16), "seq", -1).astype(F32)
    sent = (*out_sum.third(edge), *in_gate_sum.second(edge))
    gate_gate = tie(grad_gate, *sent)
    first_grad = dot_far(gate_gate, proj_in[:, LRU:])
    groups = TAIL // CHUNKS
    padded = jnp.pad(
        returned[:, :, None, :], ((0, 0), (groups - edge_len, 0), (CHUNKS - 1, 0), (0, 0))
    ).reshape(seq_count, TAIL, LRU)
    grad_inner = lax.dynamic_update_slice(
        du, (tail + padded).astype(BF16), (0, shard_len - TAIL, 0)
    )
    grad_inner = tie(grad_inner, first_grad).reshape(row_count, LRU)
    in_value_sum = Reduction(
        first_own,
        first_far,
        lambda n: lax.dynamic_slice_in_dim(grad_inner, n * width, width, 1),
        width,
    )
    grad_inner = tie(grad_inner, *in_value_sum.sent, *in_gate_sum.third())
    first_grad = first_grad + dot_far(grad_inner, proj_in[:, :LRU])

    shards = last + 1
    grad_decay_row = grad_decay[0] * jax.nn.sigmoid(-decay_float)
    flat = jnp.concatenate(
        [
            grad_gates.reshape(shards, -1, HS),
            grad_taps[:CONV].reshape(CONV, shards, -1, HS).swapaxes(0, 1).reshape(shards, -1, HS),
            grad_decay_row.reshape(shards, -1, HS),
        ],
        axis=1,
    )
    lines = flat.shape[1]
    whole = 16 * lax.axis_size("grp")
    flat = jnp.pad(flat, ((0, 0), (0, -lines % whole), (0, 0))).astype(BF16).reshape(-1, HS)
    flat = lax.psum_scatter(flat, ("seq", "grp"), scatter_dimension=0, tiled=True)
    flat = lax.all_gather(flat, "grp", axis=0, tiled=True)
    flat = flat[:lines].astype(F32).reshape(-1)
    n_gates = flat.shape[0] - (CONV + 1) * n_lru
    gates_total = flat[:n_gates].reshape(gate_heads.shape)
    taps_total = flat[n_gates : n_gates + CONV * n_lru].reshape(CONV, n_lru)
    decay_total = flat[n_gates + CONV * n_lru :]

    in_value_sum.second(first_grad)
    out_total = out_sum.finish()
    up_total = up_sum.finish()
    down_part = lax.psum_scatter(tie(down_part, up_total), "grp", scatter_dimension=0, tiled=True)
    down_total = lax.all_gather(down_part, "grp", axis=0, tiled=True).astype(F32)
    in_value_sum.third()
    in_total = jnp.concatenate([in_value_sum.finish(), in_gate_sum.finish()], axis=1)
    ffn_out = jnp.dot(hidden, proj_down, preferred_element_type=F32)
    block_out = by_token((resid + ffn_out).astype(BF16).reshape(tokens.shape))
    grad_tokens = grad_resid + norm_back(inputs, first_scale, gain_one, first_grad)
    grad_tokens = by_token(grad_tokens.astype(BF16).reshape(tokens.shape))
    first_total = gain_grad(in_proj, in_total, first_gain)
    second_total = gain_grad(up_proj, up_total, second_gain)
    return (
        block_out, grad_tokens, first_total, in_total, taps_total, decay_total, gates_total,
        out_total, second_total, up_total, down_total,
    )


def solution(mesh):
    in_specs = (
        P("grp", "seq", None),
        P("grp", "seq"),
        P("grp", "seq", None),
        P("seq"),
        P("seq", None),
        P(None, "seq"),
        P("seq"),
        P("seq", None, None),
        P("seq", None),
        P("seq"),
        P("seq", None),
        P("seq", None),
    )
    out_specs = (
        P("grp", "seq", None),
        P("grp", "seq", None),
        P("seq"),
        P("seq", None),
        P(None, "seq"),
        P("seq"),
        P("seq", None, None),
        P("seq", None),
        P("seq"),
        P("seq", None),
        P("seq", None),
    )
    return jax.shard_map(body, mesh=mesh, in_specs=in_specs, out_specs=out_specs, check_vma=False)
```

```python
import functools

import jax
import jax.numpy as jnp
from jax import lax
from jax.experimental import pallas as pl
from jax.experimental.pallas import tpu as pltpu
from jax.sharding import PartitionSpec as P

D = 1536
HEADS = 16
HS = 128
LRU = 2048
FF = 4608
CONV = 4
CHUNKS = 8
HALO = 8
BACK = 8 * (CONV - 1)
TAIL = 32
F32 = jnp.float32
BF16 = jnp.bfloat16


def from_behind(value, axis, steps):
    count = lax.axis_size(axis)
    first, last = (max(0, -steps), min(count, count - steps))
    return lax.ppermute(value, axis, [(source, source + steps) for source in range(first, last)])


def gelu_parts(v):
    k = 0.7978845608028654
    square = v * v
    t = jnp.tanh(k * v * (1.0 + 0.044715 * square))
    half = 0.5 * (1.0 + t)
    slope = half + 0.5 * v * (1.0 - t * t) * (k * (1.0 + 3.0 * 0.044715 * square))
    return v * half, slope


def gelu_tanh(v):
    k = 0.7978845608028654
    return 0.5 * v * (1.0 + jnp.tanh(k * v * (1.0 + 0.044715 * v * v)))


def sigmoid(v):
    return 0.5 * jnp.tanh(0.5 * v) + 0.5


def drive_values(q_rate, q_input, soft):
    rate = sigmoid(q_rate)
    inp = sigmoid(q_input)
    decay = jnp.exp(-8.0 * rate * soft)
    root = jnp.sqrt(1.0 - decay * decay + 0.001)
    return rate, inp, decay, root


def shifted_group(group, step, fill):
    row = lax.broadcasted_iota(jnp.int32, group.shape, 0)
    edge = 0 if step == 1 else CHUNKS - 1
    moved = pltpu.roll(group, step % CHUNKS, 0)
    return jnp.where(row == edge, fill, moved)


def extend_back(ext_s, u_ref, halo_ref, b):
    rows = u_ref.shape[1]
    ext_s[pl.ds(BACK, rows), :] = u_ref[b].astype(F32)
    halo = halo_ref[b].astype(F32)
    for m in range(CONV - 1):
        group = ext_s[pl.ds(BACK + rows - BACK + 8 * m, 8), :]
        fill = halo[HALO - CONV + 1 + m : HALO - CONV + 2 + m, :]
        ext_s[pl.ds(8 * m, 8), :] = shifted_group(group, 1, fill)


def mixer_forward_kernel(
    u_ref, halo_ref, dist_ref, gates_ref, taps_ref, soft_ref,
    c_ref, keep_ref, state_ref, prod_ref, chunk_ref,
    ext_s, c_s, rate_s, inp_s,
):
    seqs, rows, _ = u_ref.shape
    soft = soft_ref[...]
    for b in range(seqs):
        extend_back(ext_s, u_ref, halo_ref, b)

        def conv_chunk(n, _):
            at = pl.multiple_of(n * 64, 64)
            far = dist_ref[b, pl.ds(at, 64), :]
            total = taps_ref[0:1, :] * ext_s[pl.ds(at + BACK, 64), :]
            for k in range(1, CONV):
                window = taps_ref[k : k + 1, :] * ext_s[pl.ds(at + BACK - 8 * k, 64), :]
                total = total + jnp.where(far >= float(k), window, 0.0)
            low = total.astype(BF16)
            c_ref[b, pl.ds(at, 64), :] = low
            c_s[b, pl.ds(at, 64), :] = low.astype(F32)
            return 0

        lax.fori_loop(0, rows // 64, conv_chunk, 0)
        both = jnp.dot(c_ref[b], gates_ref[0], preferred_element_type=F32)
        rate_s[b] = both[:, :HS]
        inp_s[b] = both[:, HS:]

    def scan_step(j, carry):
        new = []
        for b in range(seqs):
            at = pl.ds(pl.multiple_of(j * 8, 8), 8)
            state, prod = carry[b]
            _, inp, decay, root = drive_values(rate_s[b, at, :], inp_s[b, at, :], soft)
            keep = jnp.where(dist_ref[b, at, :] >= 1.0, decay, 0.0)
            state = keep * state + root * inp * c_s[b, at, :]
            prod = keep * prod
            keep_ref[b, at, :] = keep
            state_ref[b, at, :] = state
            prod_ref[b, at, :] = prod
            new.append((state, prod))
        return tuple(new)

    zero, one = jnp.zeros((CHUNKS, HS), F32), jnp.ones((CHUNKS, HS), F32)
    ends = lax.fori_loop(0, rows // CHUNKS, scan_step, ((zero, one),) * seqs, unroll=8)
    for b in range(seqs):
        chunk_ref[b, 0] = ends[b][0]
        chunk_ref[b, 1] = ends[b][1]


def branch_kernel(core_ref, state_ref, prod_ref, carry_ref, gate_ref, out_ref, branch_ref, split_ref):
    del core_ref
    seqs, rows, _ = state_ref.shape
    for b in range(seqs):
        carry = jnp.concatenate([carry_ref[b]] * 4, axis=0)

        def point(n, _):
            at = pl.ds(pl.multiple_of(n * 32, 32), 32)
            state = state_ref[b, at, :] + prod_ref[b, at, :] * carry
            out_ref[b, at, :] = state
            low = (state * gelu_tanh(gate_ref[b, at, :])).astype(BF16)
            branch_ref[b, at, :] = low
            split_ref[0, b, at, :] = low
            return 0

        lax.fori_loop(0, rows // 32, point, 0, unroll=4)


def reverse_kernel(
    grad_ref, gate_ref, keep_ref, state_ref,
    dg_ref, local_ref, prod_ref, chunk_ref,
):
    seqs, rows, _ = grad_ref.shape
    pairs = rows // 16

    def scan_step(n, carry):
        first = pl.multiple_of((pairs - 1 - n) * 16, 16)
        at = pl.ds(first, 16)
        new = []
        for b in range(seqs):
            pull, prod = carry[b]
            act, slope = gelu_parts(gate_ref[b, at, :])
            grad = grad_ref[b, at, :]
            dg_ref[b, at, :] = (grad * state_ref[b, at, :] * slope).astype(BF16)
            dh = grad * act
            keep = keep_ref[b, at, :]
            late = dh[8:] + pull
            late_prod = prod
            pull, prod = keep[8:] * late, keep[8:] * prod
            early = dh[:8] + pull
            local_ref[b, at, :] = jnp.concatenate([early, late], axis=0)
            prod_ref[b, at, :] = jnp.concatenate([prod, late_prod], axis=0)
            new.append((keep[:8] * early, keep[:8] * prod))
        return tuple(new)

    zero, one = jnp.zeros((CHUNKS, HS), F32), jnp.ones((CHUNKS, HS), F32)
    ends = lax.fori_loop(0, pairs, scan_step, ((zero, one),) * seqs, unroll=4)
    for b in range(seqs):
        chunk_ref[b, 0] = ends[b][0]
        chunk_ref[b, 1] = ends[b][1]


def mixer_backward_kernel(
    local_ref, prod_ref, carry_ref, state_ref, before_ref, c_ref, u_ref, halo_ref, dist_ref,
    gates_ref, taps_ref, soft_ref,
    du_ref, tail_ref, edge_ref, ggate_ref, gtaps_ref, gdecay_ref,
    q_s, dq_s, dc_s, h_s, ext_s, dist_s,
):
    seqs, rows, _ = local_ref.shape
    soft = soft_ref[...]
    ggate = jnp.zeros((HS, 2 * HS), F32)
    decay_sum = jnp.zeros((8, HS), F32)
    taps_sum = [jnp.zeros((8, HS), F32) for _ in range(CONV)]

    def fold(value):
        return jnp.sum(value.reshape(value.shape[0] // 8, 8, HS), axis=0)

    for b in range(seqs):
        q_s[...] = jnp.dot(c_ref[b], gates_ref[0], preferred_element_type=F32)
        h_s[pl.ds(0, 8), :] = before_ref[b]
        h_s[pl.ds(8, rows), :] = state_ref[b]
        carry = jnp.concatenate([carry_ref[b]] * 4, axis=0)

        def point(n, total):
            first = pl.multiple_of(n * 32, 32)
            at = pl.ds(first, 32)
            lam = local_ref[b, at, :] + prod_ref[b, at, :] * carry
            rate, inp, decay, root = drive_values(q_s[at, :HS], q_s[at, HS:], soft)
            conv = c_ref[b, at, :].astype(F32)
            kept = jnp.where(dist_ref[b, at, :] >= 1.0, h_s[at, :], 0.0)
            lam_root = lam * root
            lam_inp = lam * inp
            grad_decay = lam * kept - lam_inp * conv * decay / root
            rated = grad_decay * decay * rate
            dq_s[at, :HS] = (-8.0 * soft * rated * (1.0 - rate)).astype(BF16)
            dq_s[at, HS:] = (lam_root * conv * inp * (1.0 - inp)).astype(BF16)
            dc_s[at, :] = lam_root * inp
            return total + fold(rated)

        decay_sum = lax.fori_loop(0, rows // 32, point, decay_sum, unroll=2)
        dc_s[pl.ds(0, rows), :] += lax.dot_general(
            dq_s[...], gates_ref[0], (((1,), (1,)), ((), ())), preferred_element_type=F32
        )
        ggate = ggate + lax.dot_general(
            c_ref[b], dq_s[...], (((0,), (0,)), ((), ())), preferred_element_type=F32
        )
        extend_back(ext_s, u_ref, halo_ref, b)
        dist_s[pl.ds(0, rows), :] = dist_ref[b]
        for m in range(CONV - 1):
            for held in (dc_s, dist_s):
                held[pl.ds(rows + 8 * m, 8), :] = shifted_group(held[pl.ds(8 * m, 8), :], -1, 0.0)

        def conv_chunk(n, totals):
            at = pl.multiple_of(n * 64, 64)
            grad = dc_s[pl.ds(at, 64), :]
            far = dist_s[pl.ds(at, 64), :]
            out = taps_ref[0:1, :] * grad
            totals = list(totals)
            totals[0] = totals[0] + fold(grad * ext_s[pl.ds(at + BACK, 64), :])
            for k in range(1, CONV):
                masked = jnp.where(far >= float(k), grad, 0.0)
                totals[k] = totals[k] + fold(masked * ext_s[pl.ds(at + BACK - 8 * k, 64), :])
                ahead = pl.ds(at + 8 * k, 64)
                value = taps_ref[k : k + 1, :] * dc_s[ahead, :]
                out = out + jnp.where(dist_s[ahead, :] >= float(k), value, 0.0)
            du_ref[b, pl.ds(at, 64), :] = out.astype(BF16)

            @pl.when(n == rows // 64 - 1)
            def _():
                tail_ref[b] = out[64 - TAIL :, :]

            return tuple(totals)

        taps_sum = list(lax.fori_loop(0, rows // 64, conv_chunk, tuple(taps_sum)))
        edges = [jnp.zeros((HALO - CONV + 1, HS), F32)]
        for m in range(CONV - 1, 0, -1):
            edge = jnp.zeros((1, HS), F32)
            for k in range(m, CONV):
                at = pl.ds(8 * (k - m), 1)
                masked = jnp.where(dist_s[at, :] >= float(k), dc_s[at, :], 0.0)
                edge = edge + taps_ref[k : k + 1, :] * masked
            edges.append(edge)
        edge_ref[b] = jnp.concatenate(edges, axis=0)
    ggate_ref[0] = ggate
    gdecay_ref[...] = jnp.broadcast_to(
        8.0 * jnp.sum(decay_sum, axis=0, keepdims=True), (8, HS)
    )
    gtaps_ref[...] = jnp.concatenate(
        [jnp.sum(t, axis=0, keepdims=True) for t in taps_sum] + [jnp.zeros((8 - CONV, HS), F32)],
        axis=0,
    )


def norm_kernel(shards, core_ref, x_ref, gain_ref, normed_ref, own_ref, far_ref, scale_ref):
    x = x_ref[...].astype(F32)
    scale = lax.rsqrt(jnp.mean(x * x, axis=-1, keepdims=True) + 1e-06)
    low = (x * scale * gain_ref[...]).astype(BF16)
    normed_ref[...] = low
    scale_ref[...] = jnp.broadcast_to(scale, scale_ref.shape)
    wide = low.astype(F32)
    size = D // shards
    even, odd = (
        jnp.concatenate([wide[:, n * size : (n + 1) * size] for n in range(c, shards, 2)], axis=1)
        for c in range(2)
    )
    first = core_ref[0] == 0
    own_ref[...] = jnp.where(first, even, odd).astype(BF16)
    far_ref[...] = jnp.where(first, odd, even).astype(BF16)


def ffn_forward_kernel(n_ref, gate_ref, up_ref, hidden_ref, pull_ref):
    for m in range(0, n_ref.shape[0], 256):
        at = pl.ds(m, 256)
        e1 = jnp.dot(n_ref[at, :], gate_ref[...], preferred_element_type=F32)
        e2 = jnp.dot(n_ref[at, :], up_ref[...], preferred_element_type=F32)
        act, slope = gelu_parts(e1)
        hidden_ref[at, :] = (act * e2).astype(BF16)
        pull_ref[0, at, :] = (slope * e2).astype(BF16)
        pull_ref[1, at, :] = act.astype(BF16)


def ffn_backward_kernel(grad_ref, down_ref, pull_ref, out_ref):
    for m in range(0, grad_ref.shape[0], 256):
        at = pl.ds(m, 256)
        dv = lax.dot_general(
            grad_ref[at, :], down_ref[...], (((1,), (1,)), ((), ())), preferred_element_type=F32
        )
        out_ref[0, at, :] = (dv * pull_ref[0, at, :].astype(F32)).astype(BF16)
        out_ref[1, at, :] = (dv * pull_ref[1, at, :].astype(F32)).astype(BF16)


def head_block(lead, rows):
    return pl.BlockSpec((lead, rows, HS), lambda h: (0, 0, h))


def shared_block(shape):
    return pl.BlockSpec(shape, lambda h: (0,) * len(shape))


def pair_block(seqs):
    return pl.BlockSpec((seqs, 2, CHUNKS, HS), lambda h: (0, 0, 0, h))


PARAMS = pltpu.CompilerParams(vmem_limit_bytes=40 * 1024 * 1024)


def mixer_forward(u, halo, dist, gates, taps, soft):
    seqs, rows, _ = u.shape
    full = head_block(seqs, rows)
    wide = jax.ShapeDtypeStruct((seqs, rows, LRU), F32)
    return pl.pallas_call(
        mixer_forward_kernel,
        grid=(HEADS,),
        in_specs=[
            full,
            head_block(seqs, HALO),
            shared_block((seqs, rows, HS)),
            pl.BlockSpec((1, HS, 2 * HS), lambda h: (h, 0, 0)),
            pl.BlockSpec((CONV, HS), lambda h: (0, h)),
            pl.BlockSpec((1, HS), lambda h: (0, h)),
        ],
        out_specs=[full, full, full, full, pair_block(seqs)],
        out_shape=[
            jax.ShapeDtypeStruct((seqs, rows, LRU), BF16),
            wide,
            wide,
            wide,
            jax.ShapeDtypeStruct((seqs, 2, CHUNKS, LRU), F32),
        ],
        scratch_shapes=[
            pltpu.VMEM((rows + BACK, HS), F32),
            pltpu.VMEM((seqs, rows, HS), F32),
            pltpu.VMEM((seqs, rows, HS), F32),
            pltpu.VMEM((seqs, rows, HS), F32),
        ],
        compiler_params=PARAMS,
        name="mixer_forward",
    )(u, halo, dist, gates, taps, soft)


def mixer_branch(state, prod, carry, gate, shards, core):
    seqs, rows, _ = state.shape
    per = HEADS // shards

    def at(h, core_ref):
        return (0, 0, h)

    def split_at(h, core_ref):
        shard = h // per
        return ((shard % 2 + core_ref[0]) % 2, 0, 0, (shard // 2) * per + h % per)

    full = pl.BlockSpec((seqs, rows, HS), at)
    return pl.pallas_call(
        branch_kernel,
        grid_spec=pltpu.PrefetchScalarGridSpec(
            num_scalar_prefetch=1,
            grid=(HEADS,),
            in_specs=[full, full, pl.BlockSpec((seqs, CHUNKS, HS), at), full],
            out_specs=[full, full, pl.BlockSpec((1, seqs, rows, HS), split_at)],
        ),
        out_shape=[
            jax.ShapeDtypeStruct((seqs, rows, LRU), F32),
            jax.ShapeDtypeStruct((seqs, rows, LRU), BF16),
            jax.ShapeDtypeStruct((2, seqs, rows, LRU // 2), BF16),
        ],
        compiler_params=PARAMS,
        name="mixer_branch",
    )(core.reshape(1), state, prod, carry, gate)


def mixer_reverse(grad, gate, keep, state):
    seqs, rows, _ = grad.shape
    full = head_block(seqs, rows)
    wide = jax.ShapeDtypeStruct((seqs, rows, LRU), F32)
    return pl.pallas_call(
        reverse_kernel,
        grid=(HEADS,),
        in_specs=[full, full, full, full],
        out_specs=[full, full, full, pair_block(seqs)],
        out_shape=[
            jax.ShapeDtypeStruct((seqs, rows, LRU), BF16),
            wide,
            wide,
            jax.ShapeDtypeStruct((seqs, 2, CHUNKS, LRU), F32),
        ],
        compiler_params=PARAMS,
        name="mixer_reverse",
    )(grad, gate, keep, state)


def mixer_backward(local, prod, carry, state, before, c, u, halo, dist, gates, taps, soft):
    seqs, rows, _ = local.shape
    full = head_block(seqs, rows)
    small = head_block(seqs, HALO)
    gate_block = pl.BlockSpec((1, HS, 2 * HS), lambda h: (h, 0, 0))
    row_block = pl.BlockSpec((8, HS), lambda h: (0, h))
    return pl.pallas_call(
        mixer_backward_kernel,
        grid=(HEADS,),
        in_specs=[
            full,
            full,
            head_block(seqs, CHUNKS),
            full,
            small,
            full,
            full,
            small,
            shared_block((seqs, rows, HS)),
            gate_block,
            pl.BlockSpec((CONV, HS), lambda h: (0, h)),
            pl.BlockSpec((1, HS), lambda h: (0, h)),
        ],
        out_specs=[full, head_block(seqs, TAIL), small, gate_block, row_block, row_block],
        out_shape=[
            jax.ShapeDtypeStruct((seqs, rows, LRU), BF16),
            jax.ShapeDtypeStruct((seqs, TAIL, LRU), F32),
            jax.ShapeDtypeStruct((seqs, HALO, LRU), F32),
            jax.ShapeDtypeStruct((HEADS, HS, 2 * HS), F32),
            jax.ShapeDtypeStruct((8, LRU), F32),
            jax.ShapeDtypeStruct((8, LRU), F32),
        ],
        scratch_shapes=[
            pltpu.VMEM((rows, 2 * HS), F32),
            pltpu.VMEM((rows, 2 * HS), BF16),
            pltpu.VMEM((rows + BACK, HS), F32),
            pltpu.VMEM((rows + 8, HS), F32),
            pltpu.VMEM((rows + BACK, HS), F32),
            pltpu.VMEM((rows + BACK, HS), F32),
        ],
        compiler_params=PARAMS,
        name="mixer_backward",
    )(local, prod, carry, state, before, c, u, halo, dist, gates, taps, soft)


def rms_norm(x, gain, shards, core):
    rows = x.shape[0]
    block = min(rows, 256)
    return pl.pallas_call(
        functools.partial(norm_kernel, shards),
        grid=(rows // block,),
        in_specs=[
            pl.BlockSpec(memory_space=pltpu.SMEM),
            pl.BlockSpec((block, D), lambda n: (n, 0)),
            pl.BlockSpec((1, D), lambda n: (0, 0)),
        ],
        out_specs=[
            pl.BlockSpec((block, D), lambda n: (n, 0)),
            pl.BlockSpec((block, D // 2), lambda n: (n, 0)),
            pl.BlockSpec((block, D // 2), lambda n: (n, 0)),
            pl.BlockSpec((block, 128), lambda n: (n, 0)),
        ],
        out_shape=[
            jax.ShapeDtypeStruct((rows, D), BF16),
            jax.ShapeDtypeStruct((rows, D // 2), BF16),
            jax.ShapeDtypeStruct((rows, D // 2), BF16),
            jax.ShapeDtypeStruct((rows, 128), F32),
        ],
        compiler_params=PARAMS,
        name="rms_norm",
    )(core.reshape(1), x, gain.reshape(1, D))


FF_TILE = 512


def ffn_forward(normed, proj_up):
    rows = normed.shape[0]
    steps = FF // FF_TILE
    return pl.pallas_call(
        ffn_forward_kernel,
        grid=(steps,),
        in_specs=[
            pl.BlockSpec((rows, D), lambda n: (0, 0)),
            pl.BlockSpec((D, FF_TILE), lambda n: (0, n)),
            pl.BlockSpec((D, FF_TILE), lambda n: (0, n + steps)),
        ],
        out_specs=[
            pl.BlockSpec((rows, FF_TILE), lambda n: (0, n)),
            pl.BlockSpec((2, rows, FF_TILE), lambda n: (0, 0, n)),
        ],
        out_shape=[
            jax.ShapeDtypeStruct((rows, FF), BF16),
            jax.ShapeDtypeStruct((2, rows, FF), BF16),
        ],
        compiler_params=PARAMS,
        name="ffn_forward",
    )(normed, proj_up, proj_up)


def ffn_backward(grad, proj_down, pull):
    rows = grad.shape[0]
    return pl.pallas_call(
        ffn_backward_kernel,
        grid=(FF // FF_TILE,),
        in_specs=[
            pl.BlockSpec((rows, D), lambda n: (0, 0)),
            pl.BlockSpec((FF_TILE, D), lambda n: (n, 0)),
            pl.BlockSpec((2, rows, FF_TILE), lambda n: (0, 0, n)),
        ],
        out_specs=pl.BlockSpec((2, rows, FF_TILE), lambda n: (0, 0, n)),
        out_shape=jax.ShapeDtypeStruct((2, rows, FF), BF16),
        compiler_params=PARAMS,
        name="ffn_backward",
    )(grad, proj_down, pull)


def gather_rows(shard):
    parts = lax.axis_size("grp")
    rows = shard.shape[0] // parts
    own = lax.dynamic_slice_in_dim(shard, lax.axis_index("grp") * rows, rows, 0)
    return lax.all_gather(own, ("seq", "grp"), axis=0, tiled=True)


def tie(value, *after):
    return lax.optimization_barrier((value, *after))[0]


def xor_pairs(axis, bit):
    return [(i, i ^ bit) for i in range(lax.axis_size(axis))]


def ring_pairs(steps):
    count = lax.axis_size("seq")
    return [(i, (i + steps) % count) for i in range(count)]


def dot_rows(a, b):
    return lax.dot_general(a, b, (((0,), (0,)), ((), ())), preferred_element_type=F32)


def reduce_rows(partial):
    part = lax.psum_scatter(partial, "seq", scatter_dimension=0, tiled=True)
    part = lax.psum_scatter(part, "grp", scatter_dimension=0, tiled=True)
    return lax.all_gather(part, "grp", axis=0, tiled=True).astype(F32)


def dot_far(a, b):
    return lax.dot_general(a, b, (((1,), (1,)), ((), ())), preferred_element_type=F32)


def by_position(a):
    seqs, rows = a.shape[:2]
    return a.reshape(seqs, CHUNKS, rows // CHUNKS, *a.shape[2:]).swapaxes(1, 2).reshape(a.shape)


def by_token(a):
    seqs, rows = a.shape[:2]
    return a.reshape(seqs, rows // CHUNKS, CHUNKS, *a.shape[2:]).swapaxes(1, 2).reshape(a.shape)


def place_kernel(where_ref, *refs):
    *pieces, out_ref, sems = refs
    own, far = pieces[:6], pieces[6:]
    rows, columns = own[0].shape
    width = columns // 4
    depth = own[1].shape[0]
    half = own[4].shape[0]
    chips = depth // rows + 1
    chip, core, group = where_ref[0], where_ref[1], where_ref[2]
    copies = []

    def copy(source, row, column, count, wide):
        row, column = pl.multiple_of(row, 16), pl.multiple_of(column, 128)
        target = out_ref.at[pl.ds(row, count), pl.ds(column, wide)]
        copies.append(pltpu.make_async_copy(source, target, sems.at[len(copies)]))

    for c, (shard, *parts) in enumerate((own, far)):
        side = lax.rem(core + c, 2)
        copy(shard, (chip * 2 + side) * rows, 0, rows, columns)
        for j in range(1, chips):
            start = (lax.rem(chip + chips - j, chips) * 2 + side) * rows
            first = (j - 1) * rows
            for k in range(3):
                column = lax.bitwise_xor(group, k) * width
                copy(parts[k].at[pl.ds(first, rows)], start, column, rows, width)
            column = lax.bitwise_xor(group, 3) * width
            for n in range(2):
                low, high = max(first, n * half), min(first + rows, (n + 1) * half)
                if low < high:
                    source = parts[3 + n].at[pl.ds(low - n * half, high - low)]
                    copy(source, start + low - first, column, high - low, width)
    for one in copies:
        one.start()
    for one in copies:
        one.wait()


class Gather:
    def __init__(self, shard):
        self.shard = shard
        self.chips = lax.axis_size("seq") // 2
        half = (self.chips - 1) * shard.shape[0] // 2
        self.simple = lax.axis_size("grp") != 4 or half % 16 != 0
        if self.simple:
            self.whole = gather_rows(shard)
            return
        group = lax.axis_index("grp")
        width = shard.shape[1] // 4
        own = lax.dynamic_slice_in_dim(shard, group * width, width, 1)
        self.near = jnp.concatenate(
            [lax.ppermute(own, "seq", ring_pairs(2 * j)) for j in range(1, self.chips)], axis=0
        )
        self.half = half

    def first(self):
        if self.simple:
            return ()
        self.from_x = lax.ppermute(self.near, "grp", xor_pairs("grp", 1))
        self.from_y = lax.ppermute(self.near, "grp", xor_pairs("grp", 2))
        return (self.near,)

    def second(self, *after):
        if self.simple:
            return ()
        self.from_x, self.from_y = tie((self.from_x, self.from_y), *after)
        self.halves = (self.from_y[: self.half], self.from_x[self.half :])
        return self.halves

    def whole_weight(self):
        if self.simple:
            return self.whole
        diag_a = lax.ppermute(self.halves[0], "grp", xor_pairs("grp", 1))
        diag_b = lax.ppermute(self.halves[1], "grp", xor_pairs("grp", 2))
        own = (self.shard, self.near, self.from_x, self.from_y, diag_a, diag_b)
        far = tuple(lax.ppermute(piece, "seq", xor_pairs("seq", 1)) for piece in own)
        place = lax.axis_index("seq")
        where = jnp.stack([place // 2, place % 2, lax.axis_index("grp")]).astype(jnp.int32)
        rows, columns = self.shard.shape
        count = 2 * (1 + (self.chips - 1) * 5)
        anywhere = pl.BlockSpec(memory_space=pl.ANY)
        return pl.pallas_call(
            place_kernel,
            in_specs=[pl.BlockSpec(memory_space=pltpu.SMEM)] + [anywhere] * 12,
            out_specs=anywhere,
            out_shape=jax.ShapeDtypeStruct((2 * self.chips * rows, columns), BF16),
            scratch_shapes=[pltpu.SemaphoreType.DMA((count,))],
            compiler_params=PARAMS,
            name="place_pieces",
        )(where, *own, *far)


class Reduction:
    def __init__(self, a_own, a_far, columns, width):
        self.simple = lax.axis_size("grp") != 4
        count = lax.axis_size("seq")
        place = lax.axis_index("seq")
        self.chips = count // 2
        self.chip, core = place // 2, place % 2
        self.width = width
        full = a_own.shape[1]
        self.rows = full // self.chips
        self.half = full // 2
        self.a_own = a_own
        if self.simple:
            parts = [columns(k) for k in range(4)]
            own, far = (
                jnp.concatenate([dot_rows(a, part) for part in parts], axis=1)
                for a in (a_own, a_far)
            )
            cores = jnp.stack(
                [jnp.where(core == c, own, far).reshape(self.chips, self.rows, -1) for c in (0, 1)],
                axis=1,
            )
            self.product = cores.reshape(2 * full, 4 * width).astype(BF16)
            self.sent = (self.product,)
            return
        group = lax.axis_index("grp")
        self.x, self.y = xor_pairs("grp", 1), xor_pairs("grp", 2)
        self.b = [columns(group ^ k) for k in range(4)]
        self.far = [None] * 4
        for k in (3, 1, 2, 0):
            product = dot_rows(a_far, self.b[k]).astype(BF16)
            self.far[k] = lax.ppermute(product, "seq", xor_pairs("seq", 1))
        half = self.half
        self.sent = (
            self.own(3, 0, half).astype(BF16),
            self.own(3, half, full).astype(BF16),
        )
        self.diag_a = lax.ppermute(self.sent[0], "grp", self.x)
        self.diag_b = lax.ppermute(self.sent[1], "grp", self.y)

    def own(self, k, first, last):
        product = dot_rows(self.a_own[:, first:last], self.b[k])
        return product + self.far[k][first:last].astype(F32)

    def second(self, *after):
        if self.simple:
            return ()
        full, none = 2 * self.half, ((0, self.half), (0, 0))
        diag_a, diag_b = self.diag_a, self.diag_b
        if after:
            diag_a, diag_b = tie((diag_a, diag_b), *after)
        sent = (
            (self.own(1, 0, full) + jnp.pad(diag_b.astype(F32), (none[0][::-1], (0, 0)))).astype(BF16),
            (self.own(2, 0, full) + jnp.pad(diag_a.astype(F32), none)).astype(BF16),
        )
        self.from_x = lax.ppermute(sent[0], "grp", self.x)
        self.from_y = lax.ppermute(sent[1], "grp", self.y)
        return sent

    def third(self, *after, offload=False):
        if self.simple:
            return ()
        from_x, from_y = self.from_x, self.from_y
        if after:
            from_x, from_y = tie((from_x, from_y), *after)
        mine = self.own(0, 0, 2 * self.half) + from_x.astype(F32) + from_y.astype(F32)
        mine = mine.astype(BF16)
        self.kept = None
        if offload:
            count = 2 * self.chips
            cores = [list(range(c, count, 2)) for c in range(2)]
            self.arrived = lax.psum_scatter(
                mine, "seq", scatter_dimension=0, axis_index_groups=cores, tiled=True
            )
            return (mine,)
        mine = mine.reshape(self.chips, self.rows, self.width)
        self.kept = lax.dynamic_index_in_dim(mine, self.chip, 0, False)
        sent = tuple(
            lax.dynamic_index_in_dim(mine, (self.chip + j) % self.chips, 0, False)
            for j in range(1, self.chips)
        )
        self.arrived = [
            lax.ppermute(part, "seq", ring_pairs(2 * j + 2)) for j, part in enumerate(sent)
        ]
        return sent

    def finish(self, *after):
        if self.simple:
            return reduce_rows(self.product)
        total = self.arrived
        if after:
            total = tie(total, *after)
        if self.kept is not None:
            total = self.kept.astype(F32)
            for part in self.arrived:
                total = total + part.astype(F32)
        parts = lax.all_gather(total.astype(BF16), "grp")
        return parts.transpose(1, 0, 2).reshape(self.rows, 4 * self.width).astype(F32)


def shard_carry(ends, prods, reverse):
    count = lax.axis_size("seq")
    place = lax.axis_index("seq")
    both = lax.all_gather(jnp.stack([ends, prods]), "seq")
    carry = jnp.zeros_like(ends)
    for step in range(count - 1):
        source = count - 1 - step if reverse else step
        ahead = source > place if reverse else source < place
        carry = jnp.where(ahead, both[source, 0] + both[source, 1] * carry, carry)
    return carry


def chunk_ends(chunks, reverse):
    state = jnp.zeros_like(chunks[:, 0, 0])
    prod = jnp.ones_like(state)
    order = range(CHUNKS - 1, -1, -1) if reverse else range(CHUNKS)
    for n in order:
        state = chunks[:, 0, n] + chunks[:, 1, n] * state
        prod = chunks[:, 1, n] * prod
    return state, prod


def chunk_carries(chunks, carry, reverse):
    order = range(CHUNKS - 1, -1, -1) if reverse else range(CHUNKS)
    found = [None] * CHUNKS
    for n in order:
        found[n] = carry
        carry = chunks[:, 0, n] + chunks[:, 1, n] * carry
    return jnp.stack(found, axis=1)


def norm_back(values, scale, gain, grad_normed):
    weighted = grad_normed * gain
    cubed = scale * scale * scale
    return scale * weighted - values * cubed * jnp.mean(weighted * values, axis=-1, keepdims=True)


def gain_grad(weight, grad_weight, gain):
    return jnp.sum(weight.astype(F32) * grad_weight, axis=1) / gain.astype(F32)


def body(
    tokens, seg_ids, cotangent, first_gain, in_proj, conv_taps, decay_param, gate_heads,
    out_proj, second_gain, up_proj, down_proj,
):
    seq_count, shard_len, _ = tokens.shape
    row_count = seq_count * shard_len
    edge_len = CONV - 1
    place = lax.axis_index("seq")
    last = lax.axis_size("seq") - 1

    small = jnp.concatenate(
        [first_gain, second_gain, decay_param, conv_taps.reshape(-1)]
    )
    small_all = lax.all_gather(small, "seq")
    n_gain, n_lru = first_gain.shape[0], decay_param.shape[0]
    gain_one = small_all[:, :n_gain].reshape(D).astype(F32)
    gain_two = small_all[:, n_gain : 2 * n_gain].reshape(D).astype(F32)
    decay_float = small_all[:, 2 * n_gain : 2 * n_gain + n_lru].reshape(LRU).astype(F32)
    taps_all = (
        small_all[:, 2 * n_gain + n_lru :].reshape(-1, CONV, n_lru).transpose(1, 0, 2)
    ).reshape(CONV, LRU).astype(F32)
    proj_in = gather_rows(in_proj)
    gates_all = lax.all_gather(gate_heads, "seq", axis=0, tiled=True)
    proj_out = gather_rows(out_proj)
    up_gather = Gather(up_proj)
    proj_down = gather_rows(down_proj)

    tokens = by_position(tokens)
    cotangent = by_position(cotangent)
    inputs = tokens.reshape(row_count, D).astype(F32)
    first_normed, first_own, first_far, first_scale = rms_norm(
        tokens.reshape(row_count, D), gain_one, last + 1, place % 2
    )
    first_scale = first_scale[:, :1]
    wide = (seq_count, shard_len, LRU)
    first_normed = tie(first_normed, *up_gather.first())
    inner_low = jnp.dot(first_normed, proj_in[:, :LRU], preferred_element_type=F32).astype(BF16)
    inner_low = inner_low.reshape(wide)

    step = shard_len // CHUNKS
    final = inner_low.reshape(seq_count, step, CHUNKS, LRU)[:, step - HALO :, CHUNKS - 1]
    prev_inner = from_behind(final, "seq", 1)
    prev_ids = from_behind(seg_ids[:, shard_len - edge_len :], "seq", 1)
    prev_ids = jnp.where(place == 0, -1, prev_ids)
    ext_ids = jnp.concatenate([prev_ids, seg_ids], axis=1)
    dist = jnp.zeros((seq_count, shard_len), F32)
    for k in range(1, CONV):
        dist = dist + (ext_ids[:, edge_len - k : edge_len - k + shard_len] == seg_ids).astype(F32)
    dist = jnp.broadcast_to(by_position(dist)[:, :, None], (seq_count, shard_len, HS))
    soft = jax.nn.softplus(-decay_float).reshape(1, LRU)

    conv_low, keep, state_part, prod_part, chunks = mixer_forward(
        inner_low, prev_inner, dist, gates_all, taps_all, soft
    )
    end_state, end_prod = chunk_ends(chunks, False)
    gate_pre = jnp.dot(first_normed, proj_in[:, LRU:], preferred_element_type=F32).reshape(wide)
    carry_in = shard_carry(end_state, end_prod, False)
    carries = chunk_carries(chunks, carry_in, False)
    state, branch, branch_split = mixer_branch(
        tie(state_part, *up_gather.second(chunks)), prod_part, carries, gate_pre, last + 1, place % 2
    )
    branch_split = branch_split.reshape(2, row_count, LRU // 2)
    resid = inputs + jnp.dot(
        branch.reshape(row_count, LRU), proj_out, preferred_element_type=F32
    )
    second_normed, second_own, second_far, second_scale = rms_norm(
        resid, gain_two, last + 1, place % 2
    )
    second_scale = second_scale[:, :1]
    proj_up = up_gather.whole_weight()
    hidden, pull = ffn_forward(second_normed, proj_up)

    grad_out = cotangent.reshape(row_count, D)
    grad_down = dot_rows(hidden, grad_out).astype(BF16)
    down_part = lax.psum_scatter(grad_down, "seq", scatter_dimension=0, tiled=True)
    grad_expanded = ffn_backward(tie(grad_out, grad_down), proj_down, pull)
    quarter = FF // 2

    def up_columns(n):
        part = lax.dynamic_slice(
            grad_expanded, (n // 2, 0, (n % 2) * quarter), (1, row_count, quarter)
        )
        return part[0]

    up_sum = Reduction(second_own, second_far, up_columns, quarter)
    grad_expanded = tie(grad_expanded, *up_sum.sent)
    grad_second_normed = dot_far(grad_expanded[0], proj_up[:, :FF]) + dot_far(
        grad_expanded[1], proj_up[:, FF:]
    )
    sent = up_sum.second(grad_second_normed)
    grad_second_normed = tie(grad_second_normed, *sent)
    grad_resid = grad_out.astype(F32) + norm_back(
        resid, second_scale, gain_two, grad_second_normed
    )
    grad_mixer = grad_resid.astype(BF16)
    out_sum = Reduction(
        branch_split[0],
        branch_split[1],
        lambda n: lax.dynamic_slice_in_dim(grad_mixer, n * (D // 4), D // 4, 1),
        D // 4,
    )
    grad_branch = dot_far(tie(grad_mixer, *out_sum.sent), proj_out)

    grad_gate, local, rev_prod, rev_chunks = mixer_reverse(
        grad_branch.reshape(wide), gate_pre, keep, state
    )
    head_pull, head_prod = chunk_ends(rev_chunks, True)
    grad_gate = grad_gate.reshape(row_count, LRU)
    width = LRU // 4
    sent = (*out_sum.second(head_pull), *up_sum.third(head_pull, down_part, offload=True))
    grad_gate = tie(grad_gate, *sent)
    in_gate_sum = Reduction(
        first_own,
        first_far,
        lambda n: lax.dynamic_slice_in_dim(grad_gate, n * width, width, 1),
        width,
    )
    rev_carry = shard_carry(head_pull, head_prod, True)
    rev_carries = chunk_carries(rev_chunks, rev_carry, True)
    local = tie(local, *in_gate_sum.sent)
    du, tail, edge, grad_gates, grad_taps, grad_decay = mixer_backward(
        local, rev_prod, rev_carries, state, carries, conv_low, inner_low,
        prev_inner, dist, gates_all, taps_all, soft,
    )
    returned = from_behind(edge[:, HALO - edge_len :].astype(BF16), "seq", -1).astype(F32)
    sent = (*out_sum.third(edge), *in_gate_sum.second(edge))
    gate_gate = tie(grad_gate, *sent)
    first_grad = dot_far(gate_gate, proj_in[:, LRU:])
    groups = TAIL // CHUNKS
    padded = jnp.pad(
        returned[:, :, None, :], ((0, 0), (groups - edge_len, 0), (CHUNKS - 1, 0), (0, 0))
    ).reshape(seq_count, TAIL, LRU)
    grad_inner = lax.dynamic_update_slice(
        du, (tail + padded).astype(BF16), (0, shard_len - TAIL, 0)
    )
    grad_inner = tie(grad_inner, first_grad).reshape(row_count, LRU)
    in_value_sum = Reduction(
        first_own,
        first_far,
        lambda n: lax.dynamic_slice_in_dim(grad_inner, n * width, width, 1),
        width,
    )
    grad_inner = tie(grad_inner, *in_value_sum.sent, *in_gate_sum.third())
    first_grad = first_grad + dot_far(grad_inner, proj_in[:, :LRU])

    shards = last + 1
    grad_decay_row = grad_decay[0] * jax.nn.sigmoid(-decay_float)
    flat = jnp.concatenate(
        [
            grad_gates.reshape(shards, -1, HS),
            grad_taps[:CONV].reshape(CONV, shards, -1, HS).swapaxes(0, 1).reshape(shards, -1, HS),
            grad_decay_row.reshape(shards, -1, HS),
        ],
        axis=1,
    )
    lines = flat.shape[1]
    whole = 16 * lax.axis_size("grp")
    flat = jnp.pad(flat, ((0, 0), (0, -lines % whole), (0, 0))).astype(BF16).reshape(-1, HS)
    flat = lax.psum_scatter(flat, ("seq", "grp"), scatter_dimension=0, tiled=True)
    flat = lax.all_gather(flat, "grp", axis=0, tiled=True)
    flat = flat[:lines].astype(F32).reshape(-1)
    n_gates = flat.shape[0] - (CONV + 1) * n_lru
    gates_total = flat[:n_gates].reshape(gate_heads.shape)
    taps_total = flat[n_gates : n_gates + CONV * n_lru].reshape(CONV, n_lru)
    decay_total = flat[n_gates + CONV * n_lru :]

    sent = in_value_sum.second(first_grad)
    out_total = out_sum.finish()
    up_total = up_sum.finish(edge)
    down_part = lax.psum_scatter(tie(down_part, up_total), "grp", scatter_dimension=0, tiled=True)
    down_total = lax.all_gather(down_part, "grp", axis=0, tiled=True).astype(F32)
    in_value_sum.third()
    in_total = jnp.concatenate([in_value_sum.finish(), in_gate_sum.finish()], axis=1)
    ffn_out = jnp.dot(tie(hidden, *sent), proj_down, preferred_element_type=F32)
    block_out = by_token((resid + ffn_out).astype(BF16).reshape(tokens.shape))
    grad_tokens = grad_resid + norm_back(inputs, first_scale, gain_one, first_grad)
    grad_tokens = by_token(grad_tokens.astype(BF16).reshape(tokens.shape))
    first_total = gain_grad(in_proj, in_total, first_gain)
    second_total = gain_grad(up_proj, up_total, second_gain)
    return (
        block_out, grad_tokens, first_total, in_total, taps_total, decay_total, gates_total,
        out_total, second_total, up_total, down_total,
    )


def solution(mesh):
    in_specs = (
        P("grp", "seq", None),
        P("grp", "seq"),
        P("grp", "seq", None),
        P("seq"),
        P("seq", None),
        P(None, "seq"),
        P("seq"),
        P("seq", None, None),
        P("seq", None),
        P("seq"),
        P("seq", None),
        P("seq", None),
    )
    out_specs = (
        P("grp", "seq", None),
        P("grp", "seq", None),
        P("seq"),
        P("seq", None),
        P(None, "seq"),
        P("seq"),
        P("seq", None, None),
        P("seq", None),
        P("seq"),
        P("seq", None),
        P("seq", None),
    )
    return jax.shard_map(body, mesh=mesh, in_specs=in_specs, out_specs=out_specs, check_vma=False)
```

```python
import functools

import jax
import jax.numpy as jnp
from jax import lax
from jax.experimental import pallas as pl
from jax.experimental.pallas import tpu as pltpu
from jax.sharding import PartitionSpec as P

D = 1536
HEADS = 16
HS = 128
LRU = 2048
FF = 4608
CONV = 4
CHUNKS = 8
HALO = 8
BACK = 8 * (CONV - 1)
TAIL = 32
F32 = jnp.float32
BF16 = jnp.bfloat16


def from_behind(value, axis, steps):
    count = lax.axis_size(axis)
    first, last = (max(0, -steps), min(count, count - steps))
    return lax.ppermute(value, axis, [(source, source + steps) for source in range(first, last)])


def gelu_parts(v):
    k = 0.7978845608028654
    square = v * v
    t = jnp.tanh(k * v * (1.0 + 0.044715 * square))
    half = 0.5 * (1.0 + t)
    slope = half + 0.5 * v * (1.0 - t * t) * (k * (1.0 + 3.0 * 0.044715 * square))
    return v * half, slope


def gelu_tanh(v):
    k = 0.7978845608028654
    return 0.5 * v * (1.0 + jnp.tanh(k * v * (1.0 + 0.044715 * v * v)))


def sigmoid(v):
    return 0.5 * jnp.tanh(0.5 * v) + 0.5


def drive_values(q_rate, q_input, soft):
    rate = sigmoid(q_rate)
    inp = sigmoid(q_input)
    decay = jnp.exp(-8.0 * rate * soft)
    root = jnp.sqrt(1.0 - decay * decay + 0.001)
    return rate, inp, decay, root


def shifted_group(group, step, fill):
    row = lax.broadcasted_iota(jnp.int32, group.shape, 0)
    edge = 0 if step == 1 else CHUNKS - 1
    moved = pltpu.roll(group, step % CHUNKS, 0)
    return jnp.where(row == edge, fill, moved)


def extend_back(ext_s, u_ref, halo_ref, b):
    rows = u_ref.shape[1]
    ext_s[pl.ds(BACK, rows), :] = u_ref[b].astype(F32)
    halo = halo_ref[b].astype(F32)
    for m in range(CONV - 1):
        group = ext_s[pl.ds(BACK + rows - BACK + 8 * m, 8), :]
        fill = halo[HALO - CONV + 1 + m : HALO - CONV + 2 + m, :]
        ext_s[pl.ds(8 * m, 8), :] = shifted_group(group, 1, fill)


def mixer_forward_kernel(
    u_ref, halo_ref, dist_ref, gates_ref, taps_ref, soft_ref,
    c_ref, keep_ref, state_ref, prod_ref, chunk_ref,
    ext_s, c_s, rate_s, inp_s,
):
    seqs, rows, _ = u_ref.shape
    soft = soft_ref[...]
    for b in range(seqs):
        extend_back(ext_s, u_ref, halo_ref, b)

        def conv_chunk(n, _):
            at = pl.multiple_of(n * 64, 64)
            far = dist_ref[b, pl.ds(at, 64), :]
            total = taps_ref[0:1, :] * ext_s[pl.ds(at + BACK, 64), :]
            for k in range(1, CONV):
                window = taps_ref[k : k + 1, :] * ext_s[pl.ds(at + BACK - 8 * k, 64), :]
                total = total + jnp.where(far >= float(k), window, 0.0)
            low = total.astype(BF16)
            c_ref[b, pl.ds(at, 64), :] = low
            c_s[b, pl.ds(at, 64), :] = low.astype(F32)
            return 0

        lax.fori_loop(0, rows // 64, conv_chunk, 0)
        both = jnp.dot(c_ref[b], gates_ref[0], preferred_element_type=F32)
        rate_s[b] = both[:, :HS]
        inp_s[b] = both[:, HS:]

    def scan_step(j, carry):
        new = []
        for b in range(seqs):
            at = pl.ds(pl.multiple_of(j * 8, 8), 8)
            state, prod = carry[b]
            _, inp, decay, root = drive_values(rate_s[b, at, :], inp_s[b, at, :], soft)
            keep = jnp.where(dist_ref[b, at, :] >= 1.0, decay, 0.0)
            state = keep * state + root * inp * c_s[b, at, :]
            prod = keep * prod
            keep_ref[b, at, :] = keep
            state_ref[b, at, :] = state
            prod_ref[b, at, :] = prod
            new.append((state, prod))
        return tuple(new)

    zero, one = jnp.zeros((CHUNKS, HS), F32), jnp.ones((CHUNKS, HS), F32)
    ends = lax.fori_loop(0, rows // CHUNKS, scan_step, ((zero, one),) * seqs, unroll=8)
    for b in range(seqs):
        chunk_ref[b, 0] = ends[b][0]
        chunk_ref[b, 1] = ends[b][1]


def branch_kernel(core_ref, state_ref, prod_ref, carry_ref, gate_ref, out_ref, branch_ref, split_ref):
    del core_ref
    seqs, rows, _ = state_ref.shape
    for b in range(seqs):
        carry = jnp.concatenate([carry_ref[b]] * 4, axis=0)

        def point(n, _):
            at = pl.ds(pl.multiple_of(n * 32, 32), 32)
            state = state_ref[b, at, :] + prod_ref[b, at, :] * carry
            out_ref[b, at, :] = state
            low = (state * gelu_tanh(gate_ref[b, at, :])).astype(BF16)
            branch_ref[b, at, :] = low
            split_ref[0, b, at, :] = low
            return 0

        lax.fori_loop(0, rows // 32, point, 0, unroll=4)


def reverse_kernel(
    grad_ref, gate_ref, keep_ref, state_ref,
    dg_ref, local_ref, prod_ref, chunk_ref,
):
    seqs, rows, _ = grad_ref.shape
    pairs = rows // 16

    def scan_step(n, carry):
        first = pl.multiple_of((pairs - 1 - n) * 16, 16)
        at = pl.ds(first, 16)
        new = []
        for b in range(seqs):
            pull, prod = carry[b]
            act, slope = gelu_parts(gate_ref[b, at, :])
            grad = grad_ref[b, at, :]
            dg_ref[b, at, :] = (grad * state_ref[b, at, :] * slope).astype(BF16)
            dh = grad * act
            keep = keep_ref[b, at, :]
            late = dh[8:] + pull
            late_prod = prod
            pull, prod = keep[8:] * late, keep[8:] * prod
            early = dh[:8] + pull
            local_ref[b, at, :] = jnp.concatenate([early, late], axis=0)
            prod_ref[b, at, :] = jnp.concatenate([prod, late_prod], axis=0)
            new.append((keep[:8] * early, keep[:8] * prod))
        return tuple(new)

    zero, one = jnp.zeros((CHUNKS, HS), F32), jnp.ones((CHUNKS, HS), F32)
    ends = lax.fori_loop(0, pairs, scan_step, ((zero, one),) * seqs, unroll=4)
    for b in range(seqs):
        chunk_ref[b, 0] = ends[b][0]
        chunk_ref[b, 1] = ends[b][1]


def mixer_backward_kernel(
    local_ref, prod_ref, carry_ref, state_ref, before_ref, c_ref, u_ref, halo_ref, dist_ref,
    gates_ref, taps_ref, soft_ref,
    du_ref, tail_ref, edge_ref, ggate_ref, gtaps_ref, gdecay_ref,
    q_s, dq_s, dc_s, h_s, ext_s, dist_s,
):
    seqs, rows, _ = local_ref.shape
    soft = soft_ref[...]
    ggate = jnp.zeros((HS, 2 * HS), F32)
    decay_sum = jnp.zeros((8, HS), F32)
    taps_sum = [jnp.zeros((8, HS), F32) for _ in range(CONV)]

    def fold(value):
        return jnp.sum(value.reshape(value.shape[0] // 8, 8, HS), axis=0)

    for b in range(seqs):
        q_s[...] = jnp.dot(c_ref[b], gates_ref[0], preferred_element_type=F32)
        h_s[pl.ds(0, 8), :] = before_ref[b]
        h_s[pl.ds(8, rows), :] = state_ref[b]
        carry = jnp.concatenate([carry_ref[b]] * 4, axis=0)

        def point(n, total):
            first = pl.multiple_of(n * 32, 32)
            at = pl.ds(first, 32)
            lam = local_ref[b, at, :] + prod_ref[b, at, :] * carry
            rate, inp, decay, root = drive_values(q_s[at, :HS], q_s[at, HS:], soft)
            conv = c_ref[b, at, :].astype(F32)
            kept = jnp.where(dist_ref[b, at, :] >= 1.0, h_s[at, :], 0.0)
            lam_root = lam * root
            lam_inp = lam * inp
            grad_decay = lam * kept - lam_inp * conv * decay / root
            rated = grad_decay * decay * rate
            dq_s[at, :HS] = (-8.0 * soft * rated * (1.0 - rate)).astype(BF16)
            dq_s[at, HS:] = (lam_root * conv * inp * (1.0 - inp)).astype(BF16)
            dc_s[at, :] = lam_root * inp
            return total + fold(rated)

        decay_sum = lax.fori_loop(0, rows // 32, point, decay_sum, unroll=2)
        dc_s[pl.ds(0, rows), :] += lax.dot_general(
            dq_s[...], gates_ref[0], (((1,), (1,)), ((), ())), preferred_element_type=F32
        )
        ggate = ggate + lax.dot_general(
            c_ref[b], dq_s[...], (((0,), (0,)), ((), ())), preferred_element_type=F32
        )
        extend_back(ext_s, u_ref, halo_ref, b)
        dist_s[pl.ds(0, rows), :] = dist_ref[b]
        for m in range(CONV - 1):
            for held in (dc_s, dist_s):
                held[pl.ds(rows + 8 * m, 8), :] = shifted_group(held[pl.ds(8 * m, 8), :], -1, 0.0)

        def conv_chunk(n, totals):
            at = pl.multiple_of(n * 64, 64)
            grad = dc_s[pl.ds(at, 64), :]
            far = dist_s[pl.ds(at, 64), :]
            out = taps_ref[0:1, :] * grad
            totals = list(totals)
            totals[0] = totals[0] + fold(grad * ext_s[pl.ds(at + BACK, 64), :])
            for k in range(1, CONV):
                masked = jnp.where(far >= float(k), grad, 0.0)
                totals[k] = totals[k] + fold(masked * ext_s[pl.ds(at + BACK - 8 * k, 64), :])
                ahead = pl.ds(at + 8 * k, 64)
                value = taps_ref[k : k + 1, :] * dc_s[ahead, :]
                out = out + jnp.where(dist_s[ahead, :] >= float(k), value, 0.0)
            du_ref[b, pl.ds(at, 64), :] = out.astype(BF16)

            @pl.when(n == rows // 64 - 1)
            def _():
                tail_ref[b] = out[64 - TAIL :, :]

            return tuple(totals)

        taps_sum = list(lax.fori_loop(0, rows // 64, conv_chunk, tuple(taps_sum)))
        edges = [jnp.zeros((HALO - CONV + 1, HS), F32)]
        for m in range(CONV - 1, 0, -1):
            edge = jnp.zeros((1, HS), F32)
            for k in range(m, CONV):
                at = pl.ds(8 * (k - m), 1)
                masked = jnp.where(dist_s[at, :] >= float(k), dc_s[at, :], 0.0)
                edge = edge + taps_ref[k : k + 1, :] * masked
            edges.append(edge)
        edge_ref[b] = jnp.concatenate(edges, axis=0)
    ggate_ref[0] = ggate
    gdecay_ref[...] = jnp.broadcast_to(
        8.0 * jnp.sum(decay_sum, axis=0, keepdims=True), (8, HS)
    )
    gtaps_ref[...] = jnp.concatenate(
        [jnp.sum(t, axis=0, keepdims=True) for t in taps_sum] + [jnp.zeros((8 - CONV, HS), F32)],
        axis=0,
    )


def norm_kernel(shards, core_ref, x_ref, gain_ref, normed_ref, own_ref, far_ref, scale_ref):
    x = x_ref[...].astype(F32)
    scale = lax.rsqrt(jnp.mean(x * x, axis=-1, keepdims=True) + 1e-06)
    low = (x * scale * gain_ref[...]).astype(BF16)
    normed_ref[...] = low
    scale_ref[...] = jnp.broadcast_to(scale, scale_ref.shape)
    wide = low.astype(F32)
    size = D // shards
    even, odd = (
        jnp.concatenate([wide[:, n * size : (n + 1) * size] for n in range(c, shards, 2)], axis=1)
        for c in range(2)
    )
    first = core_ref[0] == 0
    own_ref[...] = jnp.where(first, even, odd).astype(BF16)
    far_ref[...] = jnp.where(first, odd, even).astype(BF16)


def ffn_forward_kernel(n_ref, gate_ref, up_ref, hidden_ref, pull_ref):
    for m in range(0, n_ref.shape[0], 256):
        at = pl.ds(m, 256)
        e1 = jnp.dot(n_ref[at, :], gate_ref[...], preferred_element_type=F32)
        e2 = jnp.dot(n_ref[at, :], up_ref[...], preferred_element_type=F32)
        act, slope = gelu_parts(e1)
        hidden_ref[at, :] = (act * e2).astype(BF16)
        pull_ref[0, at, :] = (slope * e2).astype(BF16)
        pull_ref[1, at, :] = act.astype(BF16)


def ffn_backward_kernel(grad_ref, down_ref, pull_ref, out_ref):
    for m in range(0, grad_ref.shape[0], 256):
        at = pl.ds(m, 256)
        dv = lax.dot_general(
            grad_ref[at, :], down_ref[...], (((1,), (1,)), ((), ())), preferred_element_type=F32
        )
        out_ref[0, at, :] = (dv * pull_ref[0, at, :].astype(F32)).astype(BF16)
        out_ref[1, at, :] = (dv * pull_ref[1, at, :].astype(F32)).astype(BF16)


def head_block(lead, rows):
    return pl.BlockSpec((lead, rows, HS), lambda h: (0, 0, h))


def shared_block(shape):
    return pl.BlockSpec(shape, lambda h: (0,) * len(shape))


def pair_block(seqs):
    return pl.BlockSpec((seqs, 2, CHUNKS, HS), lambda h: (0, 0, 0, h))


PARAMS = pltpu.CompilerParams(vmem_limit_bytes=40 * 1024 * 1024)


def mixer_forward(u, halo, dist, gates, taps, soft):
    seqs, rows, _ = u.shape
    full = head_block(seqs, rows)
    wide = jax.ShapeDtypeStruct((seqs, rows, LRU), F32)
    return pl.pallas_call(
        mixer_forward_kernel,
        grid=(HEADS,),
        in_specs=[
            full,
            head_block(seqs, HALO),
            shared_block((seqs, rows, HS)),
            pl.BlockSpec((1, HS, 2 * HS), lambda h: (h, 0, 0)),
            pl.BlockSpec((CONV, HS), lambda h: (0, h)),
            pl.BlockSpec((1, HS), lambda h: (0, h)),
        ],
        out_specs=[full, full, full, full, pair_block(seqs)],
        out_shape=[
            jax.ShapeDtypeStruct((seqs, rows, LRU), BF16),
            wide,
            wide,
            wide,
            jax.ShapeDtypeStruct((seqs, 2, CHUNKS, LRU), F32),
        ],
        scratch_shapes=[
            pltpu.VMEM((rows + BACK, HS), F32),
            pltpu.VMEM((seqs, rows, HS), F32),
            pltpu.VMEM((seqs, rows, HS), F32),
            pltpu.VMEM((seqs, rows, HS), F32),
        ],
        compiler_params=PARAMS,
        name="mixer_forward",
    )(u, halo, dist, gates, taps, soft)


def mixer_branch(state, prod, carry, gate, shards, core):
    seqs, rows, _ = state.shape
    per = HEADS // shards

    def at(h, core_ref):
        return (0, 0, h)

    def split_at(h, core_ref):
        shard = h // per
        return ((shard % 2 + core_ref[0]) % 2, 0, 0, (shard // 2) * per + h % per)

    full = pl.BlockSpec((seqs, rows, HS), at)
    return pl.pallas_call(
        branch_kernel,
        grid_spec=pltpu.PrefetchScalarGridSpec(
            num_scalar_prefetch=1,
            grid=(HEADS,),
            in_specs=[full, full, pl.BlockSpec((seqs, CHUNKS, HS), at), full],
            out_specs=[full, full, pl.BlockSpec((1, seqs, rows, HS), split_at)],
        ),
        out_shape=[
            jax.ShapeDtypeStruct((seqs, rows, LRU), F32),
            jax.ShapeDtypeStruct((seqs, rows, LRU), BF16),
            jax.ShapeDtypeStruct((2, seqs, rows, LRU // 2), BF16),
        ],
        compiler_params=PARAMS,
        name="mixer_branch",
    )(core.reshape(1), state, prod, carry, gate)


def mixer_reverse(grad, gate, keep, state):
    seqs, rows, _ = grad.shape
    full = head_block(seqs, rows)
    wide = jax.ShapeDtypeStruct((seqs, rows, LRU), F32)
    return pl.pallas_call(
        reverse_kernel,
        grid=(HEADS,),
        in_specs=[full, full, full, full],
        out_specs=[full, full, full, pair_block(seqs)],
        out_shape=[
            jax.ShapeDtypeStruct((seqs, rows, LRU), BF16),
            wide,
            wide,
            jax.ShapeDtypeStruct((seqs, 2, CHUNKS, LRU), F32),
        ],
        compiler_params=PARAMS,
        name="mixer_reverse",
    )(grad, gate, keep, state)


def mixer_backward(local, prod, carry, state, before, c, u, halo, dist, gates, taps, soft):
    seqs, rows, _ = local.shape
    full = head_block(seqs, rows)
    small = head_block(seqs, HALO)
    gate_block = pl.BlockSpec((1, HS, 2 * HS), lambda h: (h, 0, 0))
    row_block = pl.BlockSpec((8, HS), lambda h: (0, h))
    return pl.pallas_call(
        mixer_backward_kernel,
        grid=(HEADS,),
        in_specs=[
            full,
            full,
            head_block(seqs, CHUNKS),
            full,
            small,
            full,
            full,
            small,
            shared_block((seqs, rows, HS)),
            gate_block,
            pl.BlockSpec((CONV, HS), lambda h: (0, h)),
            pl.BlockSpec((1, HS), lambda h: (0, h)),
        ],
        out_specs=[full, head_block(seqs, TAIL), small, gate_block, row_block, row_block],
        out_shape=[
            jax.ShapeDtypeStruct((seqs, rows, LRU), BF16),
            jax.ShapeDtypeStruct((seqs, TAIL, LRU), F32),
            jax.ShapeDtypeStruct((seqs, HALO, LRU), F32),
            jax.ShapeDtypeStruct((HEADS, HS, 2 * HS), F32),
            jax.ShapeDtypeStruct((8, LRU), F32),
            jax.ShapeDtypeStruct((8, LRU), F32),
        ],
        scratch_shapes=[
            pltpu.VMEM((rows, 2 * HS), F32),
            pltpu.VMEM((rows, 2 * HS), BF16),
            pltpu.VMEM((rows + BACK, HS), F32),
            pltpu.VMEM((rows + 8, HS), F32),
            pltpu.VMEM((rows + BACK, HS), F32),
            pltpu.VMEM((rows + BACK, HS), F32),
        ],
        compiler_params=PARAMS,
        name="mixer_backward",
    )(local, prod, carry, state, before, c, u, halo, dist, gates, taps, soft)


def rms_norm(x, gain, shards, core):
    rows = x.shape[0]
    block = min(rows, 256)
    return pl.pallas_call(
        functools.partial(norm_kernel, shards),
        grid=(rows // block,),
        in_specs=[
            pl.BlockSpec(memory_space=pltpu.SMEM),
            pl.BlockSpec((block, D), lambda n: (n, 0)),
            pl.BlockSpec((1, D), lambda n: (0, 0)),
        ],
        out_specs=[
            pl.BlockSpec((block, D), lambda n: (n, 0)),
            pl.BlockSpec((block, D // 2), lambda n: (n, 0)),
            pl.BlockSpec((block, D // 2), lambda n: (n, 0)),
            pl.BlockSpec((block, 128), lambda n: (n, 0)),
        ],
        out_shape=[
            jax.ShapeDtypeStruct((rows, D), BF16),
            jax.ShapeDtypeStruct((rows, D // 2), BF16),
            jax.ShapeDtypeStruct((rows, D // 2), BF16),
            jax.ShapeDtypeStruct((rows, 128), F32),
        ],
        compiler_params=PARAMS,
        name="rms_norm",
    )(core.reshape(1), x, gain.reshape(1, D))


FF_TILE = 512
GATHER_TILE = 768


def ffn_forward(normed, proj_up):
    rows = normed.shape[0]
    steps = FF // FF_TILE
    return pl.pallas_call(
        ffn_forward_kernel,
        grid=(steps,),
        in_specs=[
            pl.BlockSpec((rows, D), lambda n: (0, 0)),
            pl.BlockSpec((D, FF_TILE), lambda n: (0, n)),
            pl.BlockSpec((D, FF_TILE), lambda n: (0, n + steps)),
        ],
        out_specs=[
            pl.BlockSpec((rows, FF_TILE), lambda n: (0, n)),
            pl.BlockSpec((2, rows, FF_TILE), lambda n: (0, 0, n)),
        ],
        out_shape=[
            jax.ShapeDtypeStruct((rows, FF), BF16),
            jax.ShapeDtypeStruct((2, rows, FF), BF16),
        ],
        compiler_params=PARAMS,
        name="ffn_forward",
    )(normed, proj_up, proj_up)


def ffn_backward(grad, proj_down, pull):
    rows = grad.shape[0]
    return pl.pallas_call(
        ffn_backward_kernel,
        grid=(FF // FF_TILE,),
        in_specs=[
            pl.BlockSpec((rows, D), lambda n: (0, 0)),
            pl.BlockSpec((FF_TILE, D), lambda n: (n, 0)),
            pl.BlockSpec((2, rows, FF_TILE), lambda n: (0, 0, n)),
        ],
        out_specs=pl.BlockSpec((2, rows, FF_TILE), lambda n: (0, 0, n)),
        out_shape=jax.ShapeDtypeStruct((2, rows, FF), BF16),
        compiler_params=PARAMS,
        name="ffn_backward",
    )(grad, proj_down, pull)


def gather_rows(shard):
    parts = lax.axis_size("grp")
    rows = shard.shape[0] // parts
    own = lax.dynamic_slice_in_dim(shard, lax.axis_index("grp") * rows, rows, 0)
    return lax.all_gather(own, ("seq", "grp"), axis=0, tiled=True)


def tie(value, *after):
    return lax.optimization_barrier((value, *after))[0]


def xor_pairs(axis, bit):
    return [(i, i ^ bit) for i in range(lax.axis_size(axis))]


def ring_pairs(steps):
    count = lax.axis_size("seq")
    return [(i, (i + steps) % count) for i in range(count)]


def dot_rows(a, b):
    return lax.dot_general(a, b, (((0,), (0,)), ((), ())), preferred_element_type=F32)


def reduce_rows(partial):
    part = lax.psum_scatter(partial, "seq", scatter_dimension=0, tiled=True)
    part = lax.psum_scatter(part, "grp", scatter_dimension=0, tiled=True)
    return lax.all_gather(part, "grp", axis=0, tiled=True).astype(F32)


def dot_far(a, b):
    return lax.dot_general(a, b, (((1,), (1,)), ((), ())), preferred_element_type=F32)


def by_position(a):
    seqs, rows = a.shape[:2]
    return a.reshape(seqs, CHUNKS, rows // CHUNKS, *a.shape[2:]).swapaxes(1, 2).reshape(a.shape)


def by_token(a):
    seqs, rows = a.shape[:2]
    return a.reshape(seqs, rows // CHUNKS, CHUNKS, *a.shape[2:]).swapaxes(1, 2).reshape(a.shape)


def gathered_ffn_kernel(where_ref, n_ref, *refs):
    pieces, (hidden_ref, pull_ref, gate_ref, up_ref, held, sems) = refs[:12], refs[12:]
    own, far = pieces[:6], pieces[6:]
    step, steps = pl.program_id(0), pl.num_programs(0)
    rows, columns = own[0].shape
    width = columns // 4
    tile = hidden_ref.shape[1]
    depth, half = own[1].shape[0], own[4].shape[0]
    chips = depth // rows + 1
    chip, core, group = where_ref[0], where_ref[1], where_ref[2]

    def fetch(n, slot):
        for side in range(2):
            start = n * tile + side * (columns // 2)
            quarter = start // width
            offset = pl.multiple_of(start - quarter * width, 128)
            start = pl.multiple_of(start, 128)
            relation = lax.bitwise_xor(group, quarter)
            target, sem = held.at[slot, side], sems.at[slot, side]

            def copy(source, row, count):
                place = target.at[pl.ds(pl.multiple_of(row, 16), count), :]
                pltpu.make_async_copy(source, place, sem).start()

            for c, (shard, *parts) in enumerate((own, far)):
                other = lax.rem(core + c, 2)
                copy(shard.at[:, pl.ds(start, tile)], (chip * 2 + other) * rows, rows)
                for j in range(1, chips):
                    row = (lax.rem(chip + chips - j, chips) * 2 + other) * rows
                    first = (j - 1) * rows
                    for k in range(3):

                        @pl.when(relation == k)
                        def _():
                            source = parts[k].at[pl.ds(first, rows), pl.ds(offset, tile)]
                            copy(source, row, rows)

                    @pl.when(relation == 3)
                    def _():
                        for m in range(2):
                            low, high = max(first, m * half), min(first + rows, (m + 1) * half)
                            if low < high:
                                at = pl.ds(low - m * half, high - low)
                                source = parts[3 + m].at[at, pl.ds(offset, tile)]
                                copy(source, row + (low - first), high - low)

    slot = lax.rem(step, 2)

    @pl.when(step == 0)
    def _():
        fetch(step, slot)

    @pl.when(step + 1 < steps)
    def _():
        fetch(step + 1, 1 - slot)

    for side in range(2):
        whole = held.at[slot, side]
        pltpu.make_async_copy(whole, whole, sems.at[slot, side]).wait()
    gate_ref[...] = held[slot, 0]
    up_ref[...] = held[slot, 1]
    ffn_forward_kernel(n_ref, gate_ref, up_ref, hidden_ref, pull_ref)


class Gather:
    def __init__(self, shard, *after):
        self.shard = shard
        self.chips = lax.axis_size("seq") // 2
        half = (self.chips - 1) * shard.shape[0] // 2
        self.simple = lax.axis_size("grp") != 4 or half % 16 != 0
        if self.simple:
            self.whole = gather_rows(shard)
            return
        group = lax.axis_index("grp")
        width = shard.shape[1] // 4
        own = tie(lax.dynamic_slice_in_dim(shard, group * width, width, 1), *after)
        self.near = jnp.concatenate(
            [lax.ppermute(own, "seq", ring_pairs(2 * j)) for j in range(1, self.chips)], axis=0
        )
        self.half = half

    def first(self):
        if self.simple:
            return ()
        self.from_x = lax.ppermute(self.near, "grp", xor_pairs("grp", 1))
        self.from_y = lax.ppermute(self.near, "grp", xor_pairs("grp", 2))
        return (self.near,)

    def second(self, *after):
        if self.simple:
            return ()
        self.from_x, self.from_y = tie((self.from_x, self.from_y), *after)
        self.halves = (self.from_y[: self.half], self.from_x[self.half :])
        return self.halves

    def ffn_forward(self, normed):
        if self.simple:
            hidden, pull = ffn_forward(normed, self.whole)
            return hidden, pull, self.whole[:, :FF], self.whole[:, FF:]
        diag_a = lax.ppermute(self.halves[0], "grp", xor_pairs("grp", 1))
        diag_b = lax.ppermute(self.halves[1], "grp", xor_pairs("grp", 2))
        own = (self.shard, self.near, self.from_x, self.from_y, diag_a, diag_b)
        far = tuple(lax.ppermute(piece, "seq", xor_pairs("seq", 1)) for piece in own)
        place = lax.axis_index("seq")
        where = jnp.stack([place // 2, place % 2, lax.axis_index("grp")]).astype(jnp.int32)
        rows = normed.shape[0]
        tile = GATHER_TILE
        weight = pl.BlockSpec((D, tile), lambda n: (0, n))
        return pl.pallas_call(
            gathered_ffn_kernel,
            grid=(FF // tile,),
            in_specs=[
                pl.BlockSpec(memory_space=pltpu.SMEM),
                pl.BlockSpec((rows, D), lambda n: (0, 0)),
            ]
            + [pl.BlockSpec(memory_space=pl.ANY)] * 12,
            out_specs=[
                pl.BlockSpec((rows, tile), lambda n: (0, n)),
                pl.BlockSpec((2, rows, tile), lambda n: (0, 0, n)),
                weight,
                weight,
            ],
            out_shape=[
                jax.ShapeDtypeStruct((rows, FF), BF16),
                jax.ShapeDtypeStruct((2, rows, FF), BF16),
                jax.ShapeDtypeStruct((D, FF), BF16),
                jax.ShapeDtypeStruct((D, FF), BF16),
            ],
            scratch_shapes=[
                pltpu.VMEM((2, 2, D, tile), BF16),
                pltpu.SemaphoreType.DMA((2, 2)),
            ],
            compiler_params=pltpu.CompilerParams(vmem_limit_bytes=56 * 1024 * 1024),
            name="gathered_ffn",
        )(where, normed, *own, *far)


class Reduction:
    def __init__(self, a_own, a_far, columns, width):
        self.simple = lax.axis_size("grp") != 4
        count = lax.axis_size("seq")
        place = lax.axis_index("seq")
        self.chips = count // 2
        self.chip, core = place // 2, place % 2
        self.width = width
        full = a_own.shape[1]
        self.rows = full // self.chips
        self.half = full // 2
        self.a_own = a_own
        if self.simple:
            parts = [columns(k) for k in range(4)]
            own, far = (
                jnp.concatenate([dot_rows(a, part) for part in parts], axis=1)
                for a in (a_own, a_far)
            )
            cores = jnp.stack(
                [jnp.where(core == c, own, far).reshape(self.chips, self.rows, -1) for c in (0, 1)],
                axis=1,
            )
            self.product = cores.reshape(2 * full, 4 * width).astype(BF16)
            self.arrived = self.product
            self.sent = (self.product,)
            return
        group = lax.axis_index("grp")
        self.x, self.y = xor_pairs("grp", 1), xor_pairs("grp", 2)
        self.b = [columns(group ^ k) for k in range(4)]
        self.far = [None] * 4
        for k in (3, 1, 2, 0):
            product = dot_rows(a_far, self.b[k]).astype(BF16)
            self.far[k] = lax.ppermute(product, "seq", xor_pairs("seq", 1))
        half = self.half
        self.sent = (
            self.own(3, 0, half).astype(BF16),
            self.own(3, half, full).astype(BF16),
        )
        self.diag_a = lax.ppermute(self.sent[0], "grp", self.x)
        self.diag_b = lax.ppermute(self.sent[1], "grp", self.y)

    def own(self, k, first, last):
        product = dot_rows(self.a_own[:, first:last], self.b[k])
        return product + self.far[k][first:last].astype(F32)

    def second(self, *after):
        if self.simple:
            return ()
        full, none = 2 * self.half, ((0, self.half), (0, 0))
        diag_a, diag_b = self.diag_a, self.diag_b
        if after:
            diag_a, diag_b = tie((diag_a, diag_b), *after)
        sent = (
            (self.own(1, 0, full) + jnp.pad(diag_b.astype(F32), (none[0][::-1], (0, 0)))).astype(BF16),
            (self.own(2, 0, full) + jnp.pad(diag_a.astype(F32), none)).astype(BF16),
        )
        self.from_x = lax.ppermute(sent[0], "grp", self.x)
        self.from_y = lax.ppermute(sent[1], "grp", self.y)
        return sent

    def mine(self, *after):
        from_x, from_y = self.from_x, self.from_y
        if after:
            from_x, from_y = tie((from_x, from_y), *after)
        mine = self.own(0, 0, 2 * self.half) + from_x.astype(F32) + from_y.astype(F32)
        return mine.astype(BF16)

    def along_z(self, mine):
        mine = mine.reshape(self.chips, self.rows, -1)
        self.kept = lax.dynamic_index_in_dim(mine, self.chip, 0, False)
        sent = tuple(
            lax.dynamic_index_in_dim(mine, (self.chip + j) % self.chips, 0, False)
            for j in range(1, self.chips)
        )
        self.arrived = [
            lax.ppermute(part, "seq", ring_pairs(2 * j + 2)) for j, part in enumerate(sent)
        ]
        return sent

    def third(self, *after, offload=False):
        if self.simple:
            return ()
        mine = self.mine(*after)
        if not offload:
            return self.along_z(mine)
        count = 2 * self.chips
        cores = [list(range(c, count, 2)) for c in range(2)]
        self.kept = None
        self.arrived = lax.psum_scatter(
            mine, "seq", scatter_dimension=0, axis_index_groups=cores, tiled=True
        )
        return (mine,)

    def total(self):
        if self.kept is None:
            return self.arrived
        total = self.kept.astype(F32)
        for part in self.arrived:
            total = total + part.astype(F32)
        return total

    def finish(self, *after):
        if self.simple:
            return reduce_rows(self.product)
        total = self.total()
        if after:
            total = tie(total, *after)
        parts = lax.all_gather(total.astype(BF16), "grp")
        return parts.transpose(1, 0, 2).reshape(self.rows, 4 * self.width).astype(F32)


def gather_parts(lines, sums):
    if sums[0].simple:
        return lax.all_gather(lines, "grp", axis=0, tiled=True), [one.finish() for one in sums]
    pieces = [lines]
    for one in sums:
        total = one.total().astype(BF16)
        pieces += [total[:, n : n + HS] for n in range(0, one.width, HS)]
    parts = lax.all_gather(jnp.concatenate(pieces, axis=0), "grp")
    at = lines.shape[0]
    found = []
    for one in sums:
        blocks = one.width // HS
        part = parts[:, at : at + blocks * one.rows].reshape(4, blocks, one.rows, HS)
        found.append(part.transpose(2, 0, 1, 3).reshape(one.rows, 4 * one.width).astype(F32))
        at += blocks * one.rows
    return parts[:, : lines.shape[0]].reshape(-1, HS), found


def shard_carry(ends, prods, reverse):
    count = lax.axis_size("seq")
    place = lax.axis_index("seq")
    both = lax.all_gather(jnp.stack([ends, prods]), "seq")
    carry = jnp.zeros_like(ends)
    for step in range(count - 1):
        source = count - 1 - step if reverse else step
        ahead = source > place if reverse else source < place
        carry = jnp.where(ahead, both[source, 0] + both[source, 1] * carry, carry)
    return carry


def chunk_ends(chunks, reverse):
    state = jnp.zeros_like(chunks[:, 0, 0])
    prod = jnp.ones_like(state)
    order = range(CHUNKS - 1, -1, -1) if reverse else range(CHUNKS)
    for n in order:
        state = chunks[:, 0, n] + chunks[:, 1, n] * state
        prod = chunks[:, 1, n] * prod
    return state, prod


def chunk_carries(chunks, carry, reverse):
    order = range(CHUNKS - 1, -1, -1) if reverse else range(CHUNKS)
    found = [None] * CHUNKS
    for n in order:
        found[n] = carry
        carry = chunks[:, 0, n] + chunks[:, 1, n] * carry
    return jnp.stack(found, axis=1)


def norm_back(values, scale, gain, grad_normed):
    weighted = grad_normed * gain
    cubed = scale * scale * scale
    return scale * weighted - values * cubed * jnp.mean(weighted * values, axis=-1, keepdims=True)


def gain_grad(weight, grad_weight, gain):
    return jnp.sum(weight.astype(F32) * grad_weight, axis=1) / gain.astype(F32)


def body(
    tokens, seg_ids, cotangent, first_gain, in_proj, conv_taps, decay_param, gate_heads,
    out_proj, second_gain, up_proj, down_proj,
):
    seq_count, shard_len, _ = tokens.shape
    row_count = seq_count * shard_len
    edge_len = CONV - 1
    place = lax.axis_index("seq")
    last = lax.axis_size("seq") - 1

    small = jnp.concatenate(
        [first_gain, second_gain, decay_param, conv_taps.reshape(-1)]
    )
    small_all = lax.all_gather(small, "seq")
    n_gain, n_lru = first_gain.shape[0], decay_param.shape[0]
    gain_one = small_all[:, :n_gain].reshape(D).astype(F32)
    gain_two = small_all[:, n_gain : 2 * n_gain].reshape(D).astype(F32)
    decay_float = small_all[:, 2 * n_gain : 2 * n_gain + n_lru].reshape(LRU).astype(F32)
    taps_all = (
        small_all[:, 2 * n_gain + n_lru :].reshape(-1, CONV, n_lru).transpose(1, 0, 2)
    ).reshape(CONV, LRU).astype(F32)
    proj_in = gather_rows(in_proj)
    gates_all = lax.all_gather(gate_heads, "seq", axis=0, tiled=True)
    proj_out = gather_rows(out_proj)
    proj_down = gather_rows(down_proj)

    tokens = by_position(tokens)
    cotangent = by_position(cotangent)
    inputs = tokens.reshape(row_count, D).astype(F32)
    first_normed, first_own, first_far, first_scale = rms_norm(
        tokens.reshape(row_count, D), gain_one, last + 1, place % 2
    )
    first_scale = first_scale[:, :1]
    wide = (seq_count, shard_len, LRU)
    up_gather = Gather(up_proj, first_normed)
    inner_low = jnp.dot(first_normed, proj_in[:, :LRU], preferred_element_type=F32).astype(BF16)
    inner_low = inner_low.reshape(wide)

    step = shard_len // CHUNKS
    final = inner_low.reshape(seq_count, step, CHUNKS, LRU)[:, step - HALO :, CHUNKS - 1]
    prev_inner = from_behind(final, "seq", 1)
    prev_ids = from_behind(seg_ids[:, shard_len - edge_len :], "seq", 1)
    prev_ids = jnp.where(place == 0, -1, prev_ids)
    ext_ids = jnp.concatenate([prev_ids, seg_ids], axis=1)
    dist = jnp.zeros((seq_count, shard_len), F32)
    for k in range(1, CONV):
        dist = dist + (ext_ids[:, edge_len - k : edge_len - k + shard_len] == seg_ids).astype(F32)
    dist = jnp.broadcast_to(by_position(dist)[:, :, None], (seq_count, shard_len, HS))
    soft = jax.nn.softplus(-decay_float).reshape(1, LRU)

    conv_low, keep, state_part, prod_part, chunks = mixer_forward(
        tie(inner_low, *up_gather.first()), prev_inner, dist, gates_all, taps_all, soft
    )
    end_state, end_prod = chunk_ends(chunks, False)
    gate_pre = jnp.dot(first_normed, proj_in[:, LRU:], preferred_element_type=F32).reshape(wide)
    carry_in = shard_carry(end_state, end_prod, False)
    carries = chunk_carries(chunks, carry_in, False)
    state, branch, branch_split = mixer_branch(
        tie(state_part, *up_gather.second(carries)), prod_part, carries, gate_pre, last + 1, place % 2
    )
    branch_split = branch_split.reshape(2, row_count, LRU // 2)
    resid = inputs + jnp.dot(
        branch.reshape(row_count, LRU), proj_out, preferred_element_type=F32
    )
    second_normed, second_own, second_far, second_scale = rms_norm(
        resid, gain_two, last + 1, place % 2
    )
    second_scale = second_scale[:, :1]
    hidden, pull, proj_gate, proj_up = up_gather.ffn_forward(second_normed)

    grad_out = cotangent.reshape(row_count, D)
    grad_down = dot_rows(hidden, grad_out).astype(BF16)
    down_sum = lax.psum_scatter(grad_down, "seq", scatter_dimension=0, tiled=True)
    down_sum = lax.psum(down_sum, "grp")
    grad_expanded = ffn_backward(tie(grad_out, grad_down), proj_down, pull)
    quarter = FF // 2

    def up_columns(n):
        part = lax.dynamic_slice(
            grad_expanded, (n // 2, 0, (n % 2) * quarter), (1, row_count, quarter)
        )
        return part[0]

    up_sum = Reduction(second_own, second_far, up_columns, quarter)
    grad_expanded = tie(grad_expanded, *up_sum.sent)
    grad_second_normed = dot_far(grad_expanded[0], proj_gate) + dot_far(
        grad_expanded[1], proj_up
    )
    sent = up_sum.second(grad_second_normed)
    grad_second_normed = tie(grad_second_normed, *sent)
    grad_resid = grad_out.astype(F32) + norm_back(
        resid, second_scale, gain_two, grad_second_normed
    )
    grad_mixer = grad_resid.astype(BF16)
    out_sum = Reduction(
        branch_split[0],
        branch_split[1],
        lambda n: lax.dynamic_slice_in_dim(grad_mixer, n * (D // 4), D // 4, 1),
        D // 4,
    )
    grad_branch = dot_far(tie(grad_mixer, *out_sum.sent), proj_out)

    grad_gate, local, rev_prod, rev_chunks = mixer_reverse(
        grad_branch.reshape(wide), gate_pre, keep, state
    )
    head_pull, head_prod = chunk_ends(rev_chunks, True)
    grad_gate = grad_gate.reshape(row_count, LRU)
    width = LRU // 4
    grad_gate = tie(grad_gate, *out_sum.second(head_pull))
    in_gate_sum = Reduction(
        first_own,
        first_far,
        lambda n: lax.dynamic_slice_in_dim(grad_gate, n * width, width, 1),
        width,
    )
    rev_carry = shard_carry(head_pull, head_prod, True)
    rev_carries = chunk_carries(rev_chunks, rev_carry, True)
    sent = up_sum.third(rev_carry, down_sum, *in_gate_sum.sent, offload=True)
    local = tie(local, *in_gate_sum.sent, *sent)
    du, tail, edge, grad_gates, grad_taps, grad_decay = mixer_backward(
        local, rev_prod, rev_carries, state, carries, conv_low, inner_low,
        prev_inner, dist, gates_all, taps_all, soft,
    )
    returned = from_behind(edge[:, HALO - edge_len :].astype(BF16), "seq", -1).astype(F32)
    grad_gate = tie(grad_gate, *out_sum.third(edge), *in_gate_sum.second(edge))
    first_grad = dot_far(grad_gate, proj_in[:, LRU:])
    groups = TAIL // CHUNKS
    padded = jnp.pad(
        returned[:, :, None, :], ((0, 0), (groups - edge_len, 0), (CHUNKS - 1, 0), (0, 0))
    ).reshape(seq_count, TAIL, LRU)
    grad_inner = lax.dynamic_update_slice(
        du, (tail + padded).astype(BF16), (0, shard_len - TAIL, 0)
    )
    grad_inner = tie(grad_inner, first_grad).reshape(row_count, LRU)
    in_value_sum = Reduction(
        first_own,
        first_far,
        lambda n: lax.dynamic_slice_in_dim(grad_inner, n * width, width, 1),
        width,
    )
    grad_inner = tie(grad_inner, *in_value_sum.sent)

    shards = last + 1
    grad_decay_row = grad_decay[0] * jax.nn.sigmoid(-decay_float)
    flat = jnp.concatenate(
        [
            grad_gates.reshape(shards, -1, HS),
            grad_taps[:CONV].reshape(CONV, shards, -1, HS).swapaxes(0, 1).reshape(shards, -1, HS),
            grad_decay_row.reshape(shards, -1, HS),
        ],
        axis=1,
    )
    lines = flat.shape[1]
    whole = 16 * lax.axis_size("grp")
    flat = jnp.pad(flat, ((0, 0), (0, -lines % whole), (0, 0))).astype(BF16).reshape(-1, HS)
    flat = lax.psum_scatter(flat, ("seq", "grp"), scatter_dimension=0, tiled=True)
    flat, (out_total,) = gather_parts(flat, [out_sum])
    flat = flat[:lines].astype(F32).reshape(-1)
    n_gates = flat.shape[0] - (CONV + 1) * n_lru
    gates_total = flat[:n_gates].reshape(gate_heads.shape)
    taps_total = flat[n_gates : n_gates + CONV * n_lru].reshape(CONV, n_lru)
    decay_total = flat[n_gates + CONV * n_lru :]

    first_grad = first_grad + dot_far(grad_inner, proj_in[:, :LRU])
    sent = in_value_sum.second(first_grad, up_sum.arrived)
    up_total = up_sum.finish(edge)
    down_total = down_sum.astype(F32)
    if in_value_sum.simple:
        in_total = jnp.concatenate([in_value_sum.finish(), in_gate_sum.finish()], axis=1)
    else:
        both = jnp.concatenate([in_value_sum.mine(), in_gate_sum.mine()], axis=1)
        in_value_sum.along_z(both)
        both = in_value_sum.total().astype(BF16)
        in_total = jnp.concatenate(
            [
                lax.all_gather(both[:, n * width : (n + 1) * width], "grp")
                .transpose(1, 0, 2)
                .reshape(-1, LRU)
                for n in range(2)
            ],
            axis=1,
        ).astype(F32)
    ffn_out = jnp.dot(tie(hidden, *sent), proj_down, preferred_element_type=F32)
    block_out = by_token((resid + ffn_out).astype(BF16).reshape(tokens.shape))
    grad_tokens = grad_resid + norm_back(inputs, first_scale, gain_one, first_grad)
    grad_tokens = by_token(grad_tokens.astype(BF16).reshape(tokens.shape))
    first_total = gain_grad(in_proj, in_total, first_gain)
    second_total = gain_grad(up_proj, up_total, second_gain)
    return (
        block_out, grad_tokens, first_total, in_total, taps_total, decay_total, gates_total,
        out_total, second_total, up_total, down_total,
    )


def solution(mesh):
    in_specs = (
        P("grp", "seq", None),
        P("grp", "seq"),
        P("grp", "seq", None),
        P("seq"),
        P("seq", None),
        P(None, "seq"),
        P("seq"),
        P("seq", None, None),
        P("seq", None),
        P("seq"),
        P("seq", None),
        P("seq", None),
    )
    out_specs = (
        P("grp", "seq", None),
        P("grp", "seq", None),
        P("seq"),
        P("seq", None),
        P(None, "seq"),
        P("seq"),
        P("seq", None, None),
        P("seq", None),
        P("seq"),
        P("seq", None),
        P("seq", None),
    )
    return jax.shard_map(body, mesh=mesh, in_specs=in_specs, out_specs=out_specs, check_vma=False)
```

```python
import functools

import jax
import jax.numpy as jnp
from jax import lax
from jax.experimental import pallas as pl
from jax.experimental.pallas import tpu as pltpu
from jax.sharding import PartitionSpec as P

D = 1536
HEADS = 16
HS = 128
LRU = 2048
FF = 4608
CONV = 4
CHUNKS = 8
HALO = 8
BACK = 8 * (CONV - 1)
TAIL = 32
F32 = jnp.float32
BF16 = jnp.bfloat16


def from_behind(value, axis, steps):
    count = lax.axis_size(axis)
    first, last = (max(0, -steps), min(count, count - steps))
    return lax.ppermute(value, axis, [(source, source + steps) for source in range(first, last)])


def gelu_parts(v):
    k = 0.7978845608028654
    square = v * v
    t = jnp.tanh(k * v * (1.0 + 0.044715 * square))
    half = 0.5 * (1.0 + t)
    slope = half + 0.5 * v * (1.0 - t * t) * (k * (1.0 + 3.0 * 0.044715 * square))
    return v * half, slope


def gelu_tanh(v):
    k = 0.7978845608028654
    return 0.5 * v * (1.0 + jnp.tanh(k * v * (1.0 + 0.044715 * v * v)))


def sigmoid(v):
    return 0.5 * jnp.tanh(0.5 * v) + 0.5


def drive_values(q_rate, q_input, soft):
    rate = sigmoid(q_rate)
    inp = sigmoid(q_input)
    decay = jnp.exp(-8.0 * rate * soft)
    root = jnp.sqrt(1.0 - decay * decay + 0.001)
    return rate, inp, decay, root


def shifted_group(group, step, fill):
    row = lax.broadcasted_iota(jnp.int32, group.shape, 0)
    edge = 0 if step == 1 else CHUNKS - 1
    moved = pltpu.roll(group, step % CHUNKS, 0)
    return jnp.where(row == edge, fill, moved)


def extend_back(ext_s, u_ref, halo_ref, b):
    rows = u_ref.shape[1]
    ext_s[pl.ds(BACK, rows), :] = u_ref[b].astype(F32)
    halo = halo_ref[b].astype(F32)
    for m in range(CONV - 1):
        group = ext_s[pl.ds(BACK + rows - BACK + 8 * m, 8), :]
        fill = halo[HALO - CONV + 1 + m : HALO - CONV + 2 + m, :]
        ext_s[pl.ds(8 * m, 8), :] = shifted_group(group, 1, fill)


def mixer_forward_kernel(
    u_ref, halo_ref, dist_ref, gates_ref, taps_ref, soft_ref,
    c_ref, keep_ref, state_ref, prod_ref, chunk_ref,
    ext_s, c_s, rate_s, inp_s,
):
    seqs, rows, _ = u_ref.shape
    soft = soft_ref[...]
    for b in range(seqs):
        extend_back(ext_s, u_ref, halo_ref, b)

        def conv_chunk(n, _):
            at = pl.multiple_of(n * 64, 64)
            far = dist_ref[b, pl.ds(at, 64), :]
            total = taps_ref[0:1, :] * ext_s[pl.ds(at + BACK, 64), :]
            for k in range(1, CONV):
                window = taps_ref[k : k + 1, :] * ext_s[pl.ds(at + BACK - 8 * k, 64), :]
                total = total + jnp.where(far >= float(k), window, 0.0)
            low = total.astype(BF16)
            c_ref[b, pl.ds(at, 64), :] = low
            c_s[b, pl.ds(at, 64), :] = low.astype(F32)
            return 0

        lax.fori_loop(0, rows // 64, conv_chunk, 0)
        both = jnp.dot(c_ref[b], gates_ref[0], preferred_element_type=F32)
        rate_s[b] = both[:, :HS]
        inp_s[b] = both[:, HS:]

    def scan_step(j, carry):
        new = []
        for b in range(seqs):
            at = pl.ds(pl.multiple_of(j * 8, 8), 8)
            state, prod = carry[b]
            _, inp, decay, root = drive_values(rate_s[b, at, :], inp_s[b, at, :], soft)
            keep = jnp.where(dist_ref[b, at, :] >= 1.0, decay, 0.0)
            state = keep * state + root * inp * c_s[b, at, :]
            prod = keep * prod
            keep_ref[b, at, :] = keep
            state_ref[b, at, :] = state
            prod_ref[b, at, :] = prod
            new.append((state, prod))
        return tuple(new)

    zero, one = jnp.zeros((CHUNKS, HS), F32), jnp.ones((CHUNKS, HS), F32)
    ends = lax.fori_loop(0, rows // CHUNKS, scan_step, ((zero, one),) * seqs, unroll=8)
    for b in range(seqs):
        chunk_ref[b, 0] = ends[b][0]
        chunk_ref[b, 1] = ends[b][1]


def branch_kernel(core_ref, state_ref, prod_ref, carry_ref, gate_ref, out_ref, branch_ref, split_ref):
    del core_ref
    seqs, rows, _ = state_ref.shape
    for b in range(seqs):
        carry = jnp.concatenate([carry_ref[b]] * 4, axis=0)

        def point(n, _):
            at = pl.ds(pl.multiple_of(n * 32, 32), 32)
            state = state_ref[b, at, :] + prod_ref[b, at, :] * carry
            out_ref[b, at, :] = state
            low = (state * gelu_tanh(gate_ref[b, at, :])).astype(BF16)
            branch_ref[b, at, :] = low
            split_ref[0, b, at, :] = low
            return 0

        lax.fori_loop(0, rows // 32, point, 0, unroll=4)


def reverse_kernel(
    grad_ref, gate_ref, keep_ref, state_ref,
    dg_ref, local_ref, prod_ref, chunk_ref,
):
    seqs, rows, _ = grad_ref.shape
    pairs = rows // 16

    def scan_step(n, carry):
        first = pl.multiple_of((pairs - 1 - n) * 16, 16)
        at = pl.ds(first, 16)
        new = []
        for b in range(seqs):
            pull, prod = carry[b]
            act, slope = gelu_parts(gate_ref[b, at, :])
            grad = grad_ref[b, at, :]
            dg_ref[b, at, :] = (grad * state_ref[b, at, :] * slope).astype(BF16)
            dh = grad * act
            keep = keep_ref[b, at, :]
            late = dh[8:] + pull
            late_prod = prod
            pull, prod = keep[8:] * late, keep[8:] * prod
            early = dh[:8] + pull
            local_ref[b, at, :] = jnp.concatenate([early, late], axis=0)
            prod_ref[b, at, :] = jnp.concatenate([prod, late_prod], axis=0)
            new.append((keep[:8] * early, keep[:8] * prod))
        return tuple(new)

    zero, one = jnp.zeros((CHUNKS, HS), F32), jnp.ones((CHUNKS, HS), F32)
    ends = lax.fori_loop(0, pairs, scan_step, ((zero, one),) * seqs, unroll=4)
    for b in range(seqs):
        chunk_ref[b, 0] = ends[b][0]
        chunk_ref[b, 1] = ends[b][1]


def mixer_backward_kernel(
    local_ref, prod_ref, carry_ref, state_ref, before_ref, c_ref, u_ref, halo_ref, dist_ref,
    gates_ref, taps_ref, soft_ref,
    du_ref, tail_ref, edge_ref, ggate_ref, gtaps_ref, gdecay_ref,
    q_s, dq_s, dc_s, h_s, ext_s, dist_s,
):
    seqs, rows, _ = local_ref.shape
    soft = soft_ref[...]
    ggate = jnp.zeros((HS, 2 * HS), F32)
    decay_sum = jnp.zeros((8, HS), F32)
    taps_sum = [jnp.zeros((8, HS), F32) for _ in range(CONV)]

    def fold(value):
        return jnp.sum(value.reshape(value.shape[0] // 8, 8, HS), axis=0)

    for b in range(seqs):
        q_s[...] = jnp.dot(c_ref[b], gates_ref[0], preferred_element_type=F32)
        h_s[pl.ds(0, 8), :] = before_ref[b]
        h_s[pl.ds(8, rows), :] = state_ref[b]
        carry = jnp.concatenate([carry_ref[b]] * 4, axis=0)

        def point(n, total):
            first = pl.multiple_of(n * 32, 32)
            at = pl.ds(first, 32)
            lam = local_ref[b, at, :] + prod_ref[b, at, :] * carry
            rate, inp, decay, root = drive_values(q_s[at, :HS], q_s[at, HS:], soft)
            conv = c_ref[b, at, :].astype(F32)
            kept = jnp.where(dist_ref[b, at, :] >= 1.0, h_s[at, :], 0.0)
            lam_root = lam * root
            lam_inp = lam * inp
            grad_decay = lam * kept - lam_inp * conv * decay / root
            rated = grad_decay * decay * rate
            dq_s[at, :HS] = (-8.0 * soft * rated * (1.0 - rate)).astype(BF16)
            dq_s[at, HS:] = (lam_root * conv * inp * (1.0 - inp)).astype(BF16)
            dc_s[at, :] = lam_root * inp
            return total + fold(rated)

        decay_sum = lax.fori_loop(0, rows // 32, point, decay_sum, unroll=2)
        dc_s[pl.ds(0, rows), :] += lax.dot_general(
            dq_s[...], gates_ref[0], (((1,), (1,)), ((), ())), preferred_element_type=F32
        )
        ggate = ggate + lax.dot_general(
            c_ref[b], dq_s[...], (((0,), (0,)), ((), ())), preferred_element_type=F32
        )
        extend_back(ext_s, u_ref, halo_ref, b)
        dist_s[pl.ds(0, rows), :] = dist_ref[b]
        for m in range(CONV - 1):
            for held in (dc_s, dist_s):
                held[pl.ds(rows + 8 * m, 8), :] = shifted_group(held[pl.ds(8 * m, 8), :], -1, 0.0)

        def conv_chunk(n, totals):
            at = pl.multiple_of(n * 64, 64)
            grad = dc_s[pl.ds(at, 64), :]
            far = dist_s[pl.ds(at, 64), :]
            out = taps_ref[0:1, :] * grad
            totals = list(totals)
            totals[0] = totals[0] + fold(grad * ext_s[pl.ds(at + BACK, 64), :])
            for k in range(1, CONV):
                masked = jnp.where(far >= float(k), grad, 0.0)
                totals[k] = totals[k] + fold(masked * ext_s[pl.ds(at + BACK - 8 * k, 64), :])
                ahead = pl.ds(at + 8 * k, 64)
                value = taps_ref[k : k + 1, :] * dc_s[ahead, :]
                out = out + jnp.where(dist_s[ahead, :] >= float(k), value, 0.0)
            du_ref[b, pl.ds(at, 64), :] = out.astype(BF16)

            @pl.when(n == rows // 64 - 1)
            def _():
                tail_ref[b] = out[64 - TAIL :, :]

            return tuple(totals)

        taps_sum = list(lax.fori_loop(0, rows // 64, conv_chunk, tuple(taps_sum)))
        edges = [jnp.zeros((HALO - CONV + 1, HS), F32)]
        for m in range(CONV - 1, 0, -1):
            edge = jnp.zeros((1, HS), F32)
            for k in range(m, CONV):
                at = pl.ds(8 * (k - m), 1)
                masked = jnp.where(dist_s[at, :] >= float(k), dc_s[at, :], 0.0)
                edge = edge + taps_ref[k : k + 1, :] * masked
            edges.append(edge)
        edge_ref[b] = jnp.concatenate(edges, axis=0)
    ggate_ref[0] = ggate
    gdecay_ref[...] = jnp.broadcast_to(
        8.0 * jnp.sum(decay_sum, axis=0, keepdims=True), (8, HS)
    )
    gtaps_ref[...] = jnp.concatenate(
        [jnp.sum(t, axis=0, keepdims=True) for t in taps_sum] + [jnp.zeros((8 - CONV, HS), F32)],
        axis=0,
    )


def norm_kernel(shards, core_ref, x_ref, gain_ref, normed_ref, own_ref, far_ref, scale_ref):
    x = x_ref[...].astype(F32)
    scale = lax.rsqrt(jnp.mean(x * x, axis=-1, keepdims=True) + 1e-06)
    low = (x * scale * gain_ref[...]).astype(BF16)
    normed_ref[...] = low
    scale_ref[...] = jnp.broadcast_to(scale, scale_ref.shape)
    wide = low.astype(F32)
    size = D // shards
    even, odd = (
        jnp.concatenate([wide[:, n * size : (n + 1) * size] for n in range(c, shards, 2)], axis=1)
        for c in range(2)
    )
    first = core_ref[0] == 0
    own_ref[...] = jnp.where(first, even, odd).astype(BF16)
    far_ref[...] = jnp.where(first, odd, even).astype(BF16)


def ffn_forward_kernel(n_ref, gate_ref, up_ref, hidden_ref, pull_ref):
    for m in range(0, n_ref.shape[0], 256):
        at = pl.ds(m, 256)
        e1 = jnp.dot(n_ref[at, :], gate_ref[...], preferred_element_type=F32)
        e2 = jnp.dot(n_ref[at, :], up_ref[...], preferred_element_type=F32)
        act, slope = gelu_parts(e1)
        hidden_ref[at, :] = (act * e2).astype(BF16)
        pull_ref[0, at, :] = (slope * e2).astype(BF16)
        pull_ref[1, at, :] = act.astype(BF16)


def ffn_backward_kernel(grad_ref, down_ref, pull_ref, out_ref):
    for m in range(0, grad_ref.shape[0], 256):
        at = pl.ds(m, 256)
        dv = lax.dot_general(
            grad_ref[at, :], down_ref[...], (((1,), (1,)), ((), ())), preferred_element_type=F32
        )
        out_ref[0, at, :] = (dv * pull_ref[0, at, :].astype(F32)).astype(BF16)
        out_ref[1, at, :] = (dv * pull_ref[1, at, :].astype(F32)).astype(BF16)


def head_block(lead, rows):
    return pl.BlockSpec((lead, rows, HS), lambda h: (0, 0, h))


def shared_block(shape):
    return pl.BlockSpec(shape, lambda h: (0,) * len(shape))


def pair_block(seqs):
    return pl.BlockSpec((seqs, 2, CHUNKS, HS), lambda h: (0, 0, 0, h))


PARAMS = pltpu.CompilerParams(vmem_limit_bytes=40 * 1024 * 1024)


def mixer_forward(u, halo, dist, gates, taps, soft):
    seqs, rows, _ = u.shape
    full = head_block(seqs, rows)
    wide = jax.ShapeDtypeStruct((seqs, rows, LRU), F32)
    return pl.pallas_call(
        mixer_forward_kernel,
        grid=(HEADS,),
        in_specs=[
            full,
            head_block(seqs, HALO),
            shared_block((seqs, rows, HS)),
            pl.BlockSpec((1, HS, 2 * HS), lambda h: (h, 0, 0)),
            pl.BlockSpec((CONV, HS), lambda h: (0, h)),
            pl.BlockSpec((1, HS), lambda h: (0, h)),
        ],
        out_specs=[full, full, full, full, pair_block(seqs)],
        out_shape=[
            jax.ShapeDtypeStruct((seqs, rows, LRU), BF16),
            wide,
            wide,
            wide,
            jax.ShapeDtypeStruct((seqs, 2, CHUNKS, LRU), F32),
        ],
        scratch_shapes=[
            pltpu.VMEM((rows + BACK, HS), F32),
            pltpu.VMEM((seqs, rows, HS), F32),
            pltpu.VMEM((seqs, rows, HS), F32),
            pltpu.VMEM((seqs, rows, HS), F32),
        ],
        compiler_params=PARAMS,
        name="mixer_forward",
    )(u, halo, dist, gates, taps, soft)


def mixer_branch(state, prod, carry, gate, shards, core):
    seqs, rows, _ = state.shape
    per = HEADS // shards

    def at(h, core_ref):
        return (0, 0, h)

    def split_at(h, core_ref):
        shard = h // per
        return ((shard % 2 + core_ref[0]) % 2, 0, 0, (shard // 2) * per + h % per)

    full = pl.BlockSpec((seqs, rows, HS), at)
    return pl.pallas_call(
        branch_kernel,
        grid_spec=pltpu.PrefetchScalarGridSpec(
            num_scalar_prefetch=1,
            grid=(HEADS,),
            in_specs=[full, full, pl.BlockSpec((seqs, CHUNKS, HS), at), full],
            out_specs=[full, full, pl.BlockSpec((1, seqs, rows, HS), split_at)],
        ),
        out_shape=[
            jax.ShapeDtypeStruct((seqs, rows, LRU), F32),
            jax.ShapeDtypeStruct((seqs, rows, LRU), BF16),
            jax.ShapeDtypeStruct((2, seqs, rows, LRU // 2), BF16),
        ],
        compiler_params=PARAMS,
        name="mixer_branch",
    )(core.reshape(1), state, prod, carry, gate)


def mixer_reverse(grad, gate, keep, state):
    seqs, rows, _ = grad.shape
    full = head_block(seqs, rows)
    wide = jax.ShapeDtypeStruct((seqs, rows, LRU), F32)
    return pl.pallas_call(
        reverse_kernel,
        grid=(HEADS,),
        in_specs=[full, full, full, full],
        out_specs=[full, full, full, pair_block(seqs)],
        out_shape=[
            jax.ShapeDtypeStruct((seqs, rows, LRU), BF16),
            wide,
            wide,
            jax.ShapeDtypeStruct((seqs, 2, CHUNKS, LRU), F32),
        ],
        compiler_params=PARAMS,
        name="mixer_reverse",
    )(grad, gate, keep, state)


def mixer_backward(local, prod, carry, state, before, c, u, halo, dist, gates, taps, soft):
    seqs, rows, _ = local.shape
    full = head_block(seqs, rows)
    small = head_block(seqs, HALO)
    gate_block = pl.BlockSpec((1, HS, 2 * HS), lambda h: (h, 0, 0))
    row_block = pl.BlockSpec((8, HS), lambda h: (0, h))
    return pl.pallas_call(
        mixer_backward_kernel,
        grid=(HEADS,),
        in_specs=[
            full,
            full,
            head_block(seqs, CHUNKS),
            full,
            small,
            full,
            full,
            small,
            shared_block((seqs, rows, HS)),
            gate_block,
            pl.BlockSpec((CONV, HS), lambda h: (0, h)),
            pl.BlockSpec((1, HS), lambda h: (0, h)),
        ],
        out_specs=[full, head_block(seqs, TAIL), small, gate_block, row_block, row_block],
        out_shape=[
            jax.ShapeDtypeStruct((seqs, rows, LRU), BF16),
            jax.ShapeDtypeStruct((seqs, TAIL, LRU), F32),
            jax.ShapeDtypeStruct((seqs, HALO, LRU), F32),
            jax.ShapeDtypeStruct((HEADS, HS, 2 * HS), F32),
            jax.ShapeDtypeStruct((8, LRU), F32),
            jax.ShapeDtypeStruct((8, LRU), F32),
        ],
        scratch_shapes=[
            pltpu.VMEM((rows, 2 * HS), F32),
            pltpu.VMEM((rows, 2 * HS), BF16),
            pltpu.VMEM((rows + BACK, HS), F32),
            pltpu.VMEM((rows + 8, HS), F32),
            pltpu.VMEM((rows + BACK, HS), F32),
            pltpu.VMEM((rows + BACK, HS), F32),
        ],
        compiler_params=PARAMS,
        name="mixer_backward",
    )(local, prod, carry, state, before, c, u, halo, dist, gates, taps, soft)


def rms_norm(x, gain, shards, core):
    rows = x.shape[0]
    block = min(rows, 256)
    return pl.pallas_call(
        functools.partial(norm_kernel, shards),
        grid=(rows // block,),
        in_specs=[
            pl.BlockSpec(memory_space=pltpu.SMEM),
            pl.BlockSpec((block, D), lambda n: (n, 0)),
            pl.BlockSpec((1, D), lambda n: (0, 0)),
        ],
        out_specs=[
            pl.BlockSpec((block, D), lambda n: (n, 0)),
            pl.BlockSpec((block, D // 2), lambda n: (n, 0)),
            pl.BlockSpec((block, D // 2), lambda n: (n, 0)),
            pl.BlockSpec((block, 128), lambda n: (n, 0)),
        ],
        out_shape=[
            jax.ShapeDtypeStruct((rows, D), BF16),
            jax.ShapeDtypeStruct((rows, D // 2), BF16),
            jax.ShapeDtypeStruct((rows, D // 2), BF16),
            jax.ShapeDtypeStruct((rows, 128), F32),
        ],
        compiler_params=PARAMS,
        name="rms_norm",
    )(core.reshape(1), x, gain.reshape(1, D))


FF_TILE = 512
GATHER_TILE = 768
DOT_TILE = 512


def ffn_forward(normed, proj_up):
    rows = normed.shape[0]
    steps = FF // FF_TILE
    return pl.pallas_call(
        ffn_forward_kernel,
        grid=(steps,),
        in_specs=[
            pl.BlockSpec((rows, D), lambda n: (0, 0)),
            pl.BlockSpec((D, FF_TILE), lambda n: (0, n)),
            pl.BlockSpec((D, FF_TILE), lambda n: (0, n + steps)),
        ],
        out_specs=[
            pl.BlockSpec((rows, FF_TILE), lambda n: (0, n)),
            pl.BlockSpec((2, rows, FF_TILE), lambda n: (0, 0, n)),
        ],
        out_shape=[
            jax.ShapeDtypeStruct((rows, FF), BF16),
            jax.ShapeDtypeStruct((2, rows, FF), BF16),
        ],
        compiler_params=PARAMS,
        name="ffn_forward",
    )(normed, proj_up, proj_up)


def ffn_backward(grad, proj_down, pull):
    rows = grad.shape[0]
    return pl.pallas_call(
        ffn_backward_kernel,
        grid=(FF // FF_TILE,),
        in_specs=[
            pl.BlockSpec((rows, D), lambda n: (0, 0)),
            pl.BlockSpec((FF_TILE, D), lambda n: (n, 0)),
            pl.BlockSpec((2, rows, FF_TILE), lambda n: (0, 0, n)),
        ],
        out_specs=pl.BlockSpec((2, rows, FF_TILE), lambda n: (0, 0, n)),
        out_shape=jax.ShapeDtypeStruct((2, rows, FF), BF16),
        compiler_params=PARAMS,
        name="ffn_backward",
    )(grad, proj_down, pull)


def gather_rows(shard):
    parts = lax.axis_size("grp")
    rows = shard.shape[0] // parts
    own = lax.dynamic_slice_in_dim(shard, lax.axis_index("grp") * rows, rows, 0)
    return lax.all_gather(own, ("seq", "grp"), axis=0, tiled=True)


def tie(value, *after):
    return lax.optimization_barrier((value, *after))[0]


def xor_pairs(axis, bit):
    return [(i, i ^ bit) for i in range(lax.axis_size(axis))]


def ring_pairs(steps):
    count = lax.axis_size("seq")
    return [(i, (i + steps) % count) for i in range(count)]


def same_cores():
    count = lax.axis_size("seq")
    return [list(range(core, count, 2)) for core in range(2)]


def dot_rows(a, b):
    return lax.dot_general(a, b, (((0,), (0,)), ((), ())), preferred_element_type=F32)


def reduce_rows(partial):
    part = lax.psum_scatter(partial, "seq", scatter_dimension=0, tiled=True)
    part = lax.psum_scatter(part, "grp", scatter_dimension=0, tiled=True)
    return lax.all_gather(part, "grp", axis=0, tiled=True).astype(F32)


def dot_far(a, b):
    return lax.dot_general(a, b, (((1,), (1,)), ((), ())), preferred_element_type=F32)


def by_position(a):
    seqs, rows = a.shape[:2]
    return a.reshape(seqs, CHUNKS, rows // CHUNKS, *a.shape[2:]).swapaxes(1, 2).reshape(a.shape)


def by_token(a):
    seqs, rows = a.shape[:2]
    return a.reshape(seqs, rows // CHUNKS, CHUNKS, *a.shape[2:]).swapaxes(1, 2).reshape(a.shape)


def fetch_columns(where_ref, pieces, start, target, sem):
    own, far = pieces[:6], pieces[6:]
    rows, columns = own[0].shape
    width, tile = columns // 4, target.shape[1]
    depth, half = own[1].shape[0], own[4].shape[0]
    chips = depth // rows + 1
    chip, core, group = where_ref[0], where_ref[1], where_ref[2]
    quarter = start // width
    offset = pl.multiple_of(start - quarter * width, 128)
    start = pl.multiple_of(start, 128)
    relation = lax.bitwise_xor(group, quarter)

    def copy(source, row, count):
        place = target.at[pl.ds(pl.multiple_of(row, 16), count), :]
        pltpu.make_async_copy(source, place, sem).start()

    for c, (shard, *parts) in enumerate((own, far)):
        other = lax.rem(core + c, 2)
        copy(shard.at[:, pl.ds(start, tile)], (chip * 2 + other) * rows, rows)
        for j in range(1, chips):
            row = (lax.rem(chip + j, chips) * 2 + other) * rows
            first = (j - 1) * rows
            for k in range(3):

                @pl.when(relation == k)
                def _():
                    copy(parts[k].at[pl.ds(first, rows), pl.ds(offset, tile)], row, rows)

            @pl.when(relation == 3)
            def _():
                for m in range(2):
                    low, high = max(first, m * half), min(first + rows, (m + 1) * half)
                    if low < high:
                        at = pl.ds(low - m * half, high - low)
                        source = parts[3 + m].at[at, pl.ds(offset, tile)]
                        copy(source, row + (low - first), high - low)


def gathered_tiles(fetch, held, sems):
    step, steps = pl.program_id(0), pl.num_programs(0)
    slot = lax.rem(step, 2)

    @pl.when(step == 0)
    def _():
        fetch(step, slot)

    @pl.when(step + 1 < steps)
    def _():
        fetch(step + 1, 1 - slot)

    for side in range(held.shape[1]):
        whole = held.at[slot, side]
        pltpu.make_async_copy(whole, whole, sems.at[slot, side]).wait()
    return slot


def gathered_ffn_kernel(where_ref, n_ref, *refs):
    pieces, (hidden_ref, pull_ref, gate_ref, up_ref, held, sems) = refs[:12], refs[12:]
    tile = hidden_ref.shape[1]

    def fetch(n, slot):
        for side in range(2):
            start = n * tile + side * (pieces[0].shape[1] // 2)
            fetch_columns(where_ref, pieces, start, held.at[slot, side], sems.at[slot, side])

    slot = gathered_tiles(fetch, held, sems)
    gate_ref[...] = held[slot, 0]
    up_ref[...] = held[slot, 1]
    ffn_forward_kernel(n_ref, gate_ref, up_ref, hidden_ref, pull_ref)


def gathered_dot_kernel(base, where_ref, n_ref, *refs):
    pieces, (out_ref, weight_ref, held, sems) = refs[:12], refs[12:]
    tile = out_ref.shape[1]

    def fetch(n, slot):
        start = base + n * tile
        fetch_columns(where_ref, pieces, start, held.at[slot, 0], sems.at[slot, 0])

    slot = gathered_tiles(fetch, held, sems)
    weight_ref[...] = held[slot, 0]
    out_ref[...] = jnp.dot(n_ref[...], weight_ref[...], preferred_element_type=F32).astype(
        out_ref.dtype
    )


class Gather:
    def __init__(self, shard, offload=False):
        self.shard = shard
        self.chips = lax.axis_size("seq") // 2
        half = (self.chips - 1) * shard.shape[0] // 2
        self.simple = lax.axis_size("grp") != 4 or half % 16 != 0
        if self.simple:
            self.whole = gather_rows(shard)
            return
        group = lax.axis_index("grp")
        width = shard.shape[1] // 4
        own = lax.dynamic_slice_in_dim(shard, group * width, width, 1)
        others = range(1, self.chips)
        if offload:
            slabs = lax.all_gather(own, "seq", axis_index_groups=same_cores())
            chip = lax.axis_index("seq") // 2
            slabs = [
                lax.dynamic_index_in_dim(slabs, (chip + j) % self.chips, 0, False) for j in others
            ]
        else:
            slabs = [lax.ppermute(own, "seq", ring_pairs(-2 * j)) for j in others]
        self.near = jnp.concatenate(slabs, axis=0)
        self.half = half

    def first(self):
        if self.simple:
            return ()
        self.from_x = lax.ppermute(self.near, "grp", xor_pairs("grp", 1))
        self.from_y = lax.ppermute(self.near, "grp", xor_pairs("grp", 2))
        return (self.near,)

    def second(self, *after):
        if self.simple:
            return ()
        if after:
            self.from_x, self.from_y = tie((self.from_x, self.from_y), *after)
        self.halves = (self.from_y[: self.half], self.from_x[self.half :])
        return self.halves

    def third(self):
        if self.simple:
            return
        diag_a = lax.ppermute(self.halves[0], "grp", xor_pairs("grp", 1))
        diag_b = lax.ppermute(self.halves[1], "grp", xor_pairs("grp", 2))
        own = (self.shard, self.near, self.from_x, self.from_y, diag_a, diag_b)
        far = tuple(lax.ppermute(piece, "seq", xor_pairs("seq", 1)) for piece in own)
        place = lax.axis_index("seq")
        where = jnp.stack([place // 2, place % 2, lax.axis_index("grp")]).astype(jnp.int32)
        self.pieces = (where, own, far)

    def call(self, kernel, normed, steps, tile, weights, out_specs, out_shape, name):
        where, own, far = self.pieces
        rows, depth = normed.shape
        return pl.pallas_call(
            kernel,
            grid=(steps,),
            in_specs=[
                pl.BlockSpec(memory_space=pltpu.SMEM),
                pl.BlockSpec((rows, depth), lambda n: (0, 0)),
            ]
            + [pl.BlockSpec(memory_space=pl.ANY)] * 12,
            out_specs=out_specs + [pl.BlockSpec((depth, tile), lambda n: (0, n))] * weights,
            out_shape=out_shape + [jax.ShapeDtypeStruct((depth, steps * tile), BF16)] * weights,
            scratch_shapes=[
                pltpu.VMEM((2, weights, depth, tile), BF16),
                pltpu.SemaphoreType.DMA((2, weights)),
            ],
            compiler_params=pltpu.CompilerParams(vmem_limit_bytes=56 * 1024 * 1024),
            name=name,
        )(where, normed, *own, *far)

    def dot(self, normed, half, dtype):
        columns = self.shard.shape[1] // 2
        base = half * columns
        if self.simple:
            weight = self.whole[:, base : base + columns]
            return jnp.dot(normed, weight, preferred_element_type=F32).astype(dtype), weight
        rows, tile = normed.shape[0], DOT_TILE
        return self.call(
            functools.partial(gathered_dot_kernel, base),
            normed,
            columns // tile,
            tile,
            1,
            [pl.BlockSpec((rows, tile), lambda n: (0, n))],
            [jax.ShapeDtypeStruct((rows, columns), dtype)],
            "gathered_dot",
        )

    def ffn_forward(self, normed):
        if self.simple:
            hidden, pull = ffn_forward(normed, self.whole)
            return hidden, pull, self.whole[:, :FF], self.whole[:, FF:]
        rows, tile = normed.shape[0], GATHER_TILE
        return self.call(
            gathered_ffn_kernel,
            normed,
            FF // tile,
            tile,
            2,
            [
                pl.BlockSpec((rows, tile), lambda n: (0, n)),
                pl.BlockSpec((2, rows, tile), lambda n: (0, 0, n)),
            ],
            [
                jax.ShapeDtypeStruct((rows, FF), BF16),
                jax.ShapeDtypeStruct((2, rows, FF), BF16),
            ],
            "gathered_ffn",
        )


class Reduction:
    def __init__(self, a_own, a_far, columns, width, fused=False):
        self.simple = lax.axis_size("grp") != 4
        count = lax.axis_size("seq")
        place = lax.axis_index("seq")
        self.chips = count // 2
        self.chip, core = place // 2, place % 2
        self.width = width
        full = a_own.shape[1]
        self.rows = full // self.chips
        self.half = full // 2
        self.a_own = a_own
        if self.simple:
            parts = [columns(k) for k in range(4)]
            own, far = (
                jnp.concatenate([dot_rows(a, part) for part in parts], axis=1)
                for a in (a_own, a_far)
            )
            cores = jnp.stack(
                [jnp.where(core == c, own, far).reshape(self.chips, self.rows, -1) for c in (0, 1)],
                axis=1,
            )
            self.product = cores.reshape(2 * full, 4 * width).astype(BF16)
            self.arrived = self.product
            self.sent = (self.product,)
            return
        group = lax.axis_index("grp")
        self.x, self.y = xor_pairs("grp", 1), xor_pairs("grp", 2)
        self.b = [columns(group ^ k) for k in range(4)]
        self.far = [None] * 4
        self.product = None
        other = xor_pairs("seq", 1)
        if fused:
            b_all = jnp.concatenate(self.b, axis=1)
            far = lax.ppermute(dot_rows(a_far, b_all).astype(BF16), "seq", other)
            self.product = (dot_rows(a_own, b_all) + far.astype(F32)).astype(BF16)
        for k in () if fused else (3, 1, 2, 0):
            product = dot_rows(a_far, self.b[k]).astype(BF16)
            self.far[k] = lax.ppermute(product, "seq", other)
        half = self.half
        self.sent = (
            self.own(3, 0, half).astype(BF16),
            self.own(3, half, full).astype(BF16),
        )
        self.diag_a = lax.ppermute(self.sent[0], "grp", self.x)
        self.diag_b = lax.ppermute(self.sent[1], "grp", self.y)

    def own(self, k, first, last):
        if self.product is not None:
            left = k * self.width
            return self.product[first:last, left : left + self.width].astype(F32)
        product = dot_rows(self.a_own[:, first:last], self.b[k])
        return product + self.far[k][first:last].astype(F32)

    def second(self, *after):
        if self.simple:
            return ()
        full, none = 2 * self.half, ((0, self.half), (0, 0))
        diag_a, diag_b = self.diag_a, self.diag_b
        if after:
            diag_a, diag_b = tie((diag_a, diag_b), *after)
        sent = (
            (self.own(1, 0, full) + jnp.pad(diag_b.astype(F32), (none[0][::-1], (0, 0)))).astype(BF16),
            (self.own(2, 0, full) + jnp.pad(diag_a.astype(F32), none)).astype(BF16),
        )
        self.from_x = lax.ppermute(sent[0], "grp", self.x)
        self.from_y = lax.ppermute(sent[1], "grp", self.y)
        return sent

    def mine(self, *after):
        from_x, from_y = self.from_x, self.from_y
        if after:
            from_x, from_y = tie((from_x, from_y), *after)
        mine = self.own(0, 0, 2 * self.half) + from_x.astype(F32) + from_y.astype(F32)
        return mine.astype(BF16)

    def along_z(self, mine):
        mine = mine.reshape(self.chips, self.rows, -1)
        self.kept = lax.dynamic_index_in_dim(mine, self.chip, 0, False)
        sent = tuple(
            lax.dynamic_index_in_dim(mine, (self.chip + j) % self.chips, 0, False)
            for j in range(1, self.chips)
        )
        self.arrived = [
            lax.ppermute(part, "seq", ring_pairs(2 * j + 2)) for j, part in enumerate(sent)
        ]
        return sent

    def third(self, *after, offload=False):
        if self.simple:
            return ()
        mine = self.mine(*after)
        if not offload:
            return self.along_z(mine)
        self.kept = None
        self.arrived = lax.psum_scatter(
            mine, "seq", scatter_dimension=0, axis_index_groups=same_cores(), tiled=True
        )
        return (mine,)

    def total(self):
        if self.kept is None:
            return self.arrived
        total = self.kept.astype(F32)
        for part in self.arrived:
            total = total + part.astype(F32)
        return total

    def finish(self, *after):
        if self.simple:
            return reduce_rows(self.product)
        total = self.total()
        if after:
            total = tie(total, *after)
        parts = lax.all_gather(total.astype(BF16), "grp")
        return parts.transpose(1, 0, 2).reshape(self.rows, 4 * self.width).astype(F32)


def gather_parts(lines, sums):
    if sums[0].simple:
        return lax.all_gather(lines, "grp", axis=0, tiled=True), [one.finish() for one in sums]
    pieces = [lines]
    for one in sums:
        total = one.total().astype(BF16)
        pieces += [total[:, n : n + HS] for n in range(0, one.width, HS)]
    parts = lax.all_gather(jnp.concatenate(pieces, axis=0), "grp")
    at = lines.shape[0]
    found = []
    for one in sums:
        blocks = one.width // HS
        part = parts[:, at : at + blocks * one.rows].reshape(4, blocks, one.rows, HS)
        found.append(part.transpose(2, 0, 1, 3).reshape(one.rows, 4 * one.width).astype(F32))
        at += blocks * one.rows
    return parts[:, : lines.shape[0]].reshape(-1, HS), found


def shard_carry(ends, prods, reverse):
    count = lax.axis_size("seq")
    place = lax.axis_index("seq")
    both = lax.all_gather(jnp.stack([ends, prods]), "seq")
    carry = jnp.zeros_like(ends)
    for step in range(count - 1):
        source = count - 1 - step if reverse else step
        ahead = source > place if reverse else source < place
        carry = jnp.where(ahead, both[source, 0] + both[source, 1] * carry, carry)
    return carry


def chunk_ends(chunks, reverse):
    state = jnp.zeros_like(chunks[:, 0, 0])
    prod = jnp.ones_like(state)
    order = range(CHUNKS - 1, -1, -1) if reverse else range(CHUNKS)
    for n in order:
        state = chunks[:, 0, n] + chunks[:, 1, n] * state
        prod = chunks[:, 1, n] * prod
    return state, prod


def chunk_carries(chunks, carry, reverse):
    order = range(CHUNKS - 1, -1, -1) if reverse else range(CHUNKS)
    found = [None] * CHUNKS
    for n in order:
        found[n] = carry
        carry = chunks[:, 0, n] + chunks[:, 1, n] * carry
    return jnp.stack(found, axis=1)


def norm_back(values, scale, gain, grad_normed):
    weighted = grad_normed * gain
    cubed = scale * scale * scale
    return scale * weighted - values * cubed * jnp.mean(weighted * values, axis=-1, keepdims=True)


def gain_grad(weight, grad_weight, gain):
    return jnp.sum(weight.astype(F32) * grad_weight, axis=1) / gain.astype(F32)


def body(
    tokens, seg_ids, cotangent, first_gain, in_proj, conv_taps, decay_param, gate_heads,
    out_proj, second_gain, up_proj, down_proj,
):
    seq_count, shard_len, _ = tokens.shape
    row_count = seq_count * shard_len
    edge_len = CONV - 1
    place = lax.axis_index("seq")
    last = lax.axis_size("seq") - 1

    small = jnp.concatenate(
        [first_gain, second_gain, decay_param, conv_taps.reshape(-1)]
    )
    small_all = lax.all_gather(small, "seq")
    n_gain, n_lru = first_gain.shape[0], decay_param.shape[0]
    gain_one = small_all[:, :n_gain].reshape(D).astype(F32)
    gain_two = small_all[:, n_gain : 2 * n_gain].reshape(D).astype(F32)
    decay_float = small_all[:, 2 * n_gain : 2 * n_gain + n_lru].reshape(LRU).astype(F32)
    taps_all = (
        small_all[:, 2 * n_gain + n_lru :].reshape(-1, CONV, n_lru).transpose(1, 0, 2)
    ).reshape(CONV, LRU).astype(F32)
    in_gather = Gather(in_proj)
    up_gather = Gather(up_proj, offload=True)
    in_gather.first()
    in_gather.second()
    in_gather.third()
    gates_all = lax.all_gather(gate_heads, "seq", axis=0, tiled=True)
    proj_out = gather_rows(out_proj)
    proj_down = gather_rows(down_proj)

    tokens = by_position(tokens)
    cotangent = by_position(cotangent)
    inputs = tokens.reshape(row_count, D).astype(F32)
    first_normed, first_own, first_far, first_scale = rms_norm(
        tokens.reshape(row_count, D), gain_one, last + 1, place % 2
    )
    first_scale = first_scale[:, :1]
    wide = (seq_count, shard_len, LRU)
    inner_low, in_value = in_gather.dot(first_normed, 0, BF16)
    inner_low = inner_low.reshape(wide)

    step = shard_len // CHUNKS
    final = inner_low.reshape(seq_count, step, CHUNKS, LRU)[:, step - HALO :, CHUNKS - 1]
    prev_inner = from_behind(final, "seq", 1)
    prev_ids = from_behind(seg_ids[:, shard_len - edge_len :], "seq", 1)
    prev_ids = jnp.where(place == 0, -1, prev_ids)
    ext_ids = jnp.concatenate([prev_ids, seg_ids], axis=1)
    dist = jnp.zeros((seq_count, shard_len), F32)
    for k in range(1, CONV):
        dist = dist + (ext_ids[:, edge_len - k : edge_len - k + shard_len] == seg_ids).astype(F32)
    dist = jnp.broadcast_to(by_position(dist)[:, :, None], (seq_count, shard_len, HS))
    soft = jax.nn.softplus(-decay_float).reshape(1, LRU)

    conv_low, keep, state_part, prod_part, chunks = mixer_forward(
        tie(inner_low, *up_gather.first()), prev_inner, dist, gates_all, taps_all, soft
    )
    end_state, end_prod = chunk_ends(chunks, False)
    gate_pre, in_gate = in_gather.dot(first_normed, 1, F32)
    gate_pre = gate_pre.reshape(wide)
    carry_in = shard_carry(end_state, end_prod, False)
    carries = chunk_carries(chunks, carry_in, False)
    state, branch, branch_split = mixer_branch(
        tie(state_part, *up_gather.second(carries)), prod_part, carries, gate_pre, last + 1, place % 2
    )
    branch_split = branch_split.reshape(2, row_count, LRU // 2)
    resid = inputs + jnp.dot(
        branch.reshape(row_count, LRU), proj_out, preferred_element_type=F32
    )
    second_normed, second_own, second_far, second_scale = rms_norm(
        resid, gain_two, last + 1, place % 2
    )
    second_scale = second_scale[:, :1]
    up_gather.third()
    hidden, pull, proj_gate, proj_up = up_gather.ffn_forward(second_normed)

    grad_out = cotangent.reshape(row_count, D)
    grad_down = dot_rows(hidden, grad_out).astype(BF16)
    down_part = lax.psum_scatter(grad_down, "seq", scatter_dimension=0, tiled=True)
    down_sum = lax.psum(down_part, "grp")
    grad_expanded = ffn_backward(tie(grad_out, grad_down), proj_down, pull)
    quarter = FF // 2

    def up_columns(n):
        part = lax.dynamic_slice(
            grad_expanded, (n // 2, 0, (n % 2) * quarter), (1, row_count, quarter)
        )
        return part[0]

    up_sum = Reduction(second_own, second_far, up_columns, quarter)
    grad_expanded = tie(grad_expanded, *up_sum.sent)
    grad_second_normed = dot_far(grad_expanded[0], proj_gate) + dot_far(
        grad_expanded[1], proj_up
    )
    sent = up_sum.second(grad_second_normed)
    grad_second_normed = tie(grad_second_normed, *sent)
    grad_resid = grad_out.astype(F32) + norm_back(
        resid, second_scale, gain_two, grad_second_normed
    )
    grad_mixer = grad_resid.astype(BF16)
    grad_branch = dot_far(grad_mixer, proj_out)

    grad_gate, local, rev_prod, rev_chunks = mixer_reverse(
        tie(grad_branch, down_part).reshape(wide), gate_pre, keep, state
    )
    head_pull, head_prod = chunk_ends(rev_chunks, True)
    grad_gate = grad_gate.reshape(row_count, LRU)
    width = LRU // 4
    rev_carry = shard_carry(head_pull, head_prod, True)
    rev_carries = chunk_carries(rev_chunks, rev_carry, True)
    grad_mixer, grad_gate = tie((grad_mixer, grad_gate), rev_carry)
    out_sum = Reduction(
        branch_split[0],
        branch_split[1],
        lambda n: lax.dynamic_slice_in_dim(grad_mixer, n * (D // 4), D // 4, 1),
        D // 4,
        True,
    )
    in_gate_sum = Reduction(
        first_own,
        first_far,
        lambda n: lax.dynamic_slice_in_dim(grad_gate, n * width, width, 1),
        width,
        True,
    )
    sent = (*out_sum.sent, *in_gate_sum.sent)
    sent = up_sum.third(*sent)
    local = tie(local, down_sum, *sent)
    du, tail, edge, grad_gates, grad_taps, grad_decay = mixer_backward(
        local, rev_prod, rev_carries, state, carries, conv_low, inner_low,
        prev_inner, dist, gates_all, taps_all, soft,
    )
    returned = from_behind(edge[:, HALO - edge_len :].astype(BF16), "seq", -1).astype(F32)
    grad_gate = tie(grad_gate, *out_sum.second(edge), *in_gate_sum.second(edge))
    first_grad = dot_far(grad_gate, in_gate)
    groups = TAIL // CHUNKS
    padded = jnp.pad(
        returned[:, :, None, :], ((0, 0), (groups - edge_len, 0), (CHUNKS - 1, 0), (0, 0))
    ).reshape(seq_count, TAIL, LRU)
    grad_inner = lax.dynamic_update_slice(
        du, (tail + padded).astype(BF16), (0, shard_len - TAIL, 0)
    )
    grad_inner = tie(grad_inner, first_grad).reshape(row_count, LRU)
    in_value_sum = Reduction(
        first_own,
        first_far,
        lambda n: lax.dynamic_slice_in_dim(grad_inner, n * width, width, 1),
        width,
        True,
    )
    grad_inner = tie(grad_inner, *in_value_sum.sent, *out_sum.third())

    shards = last + 1
    grad_decay_row = grad_decay[0] * jax.nn.sigmoid(-decay_float)
    flat = jnp.concatenate(
        [
            grad_gates.reshape(shards, -1, HS),
            grad_taps[:CONV].reshape(CONV, shards, -1, HS).swapaxes(0, 1).reshape(shards, -1, HS),
            grad_decay_row.reshape(shards, -1, HS),
        ],
        axis=1,
    )
    lines = flat.shape[1]
    whole = 16 * lax.axis_size("grp")
    flat = jnp.pad(flat, ((0, 0), (0, -lines % whole), (0, 0))).astype(BF16).reshape(-1, HS)
    flat = lax.psum_scatter(flat, ("seq", "grp"), scatter_dimension=0, tiled=True)
    flat, (out_total,) = gather_parts(flat, [out_sum])
    flat = flat[:lines].astype(F32).reshape(-1)
    n_gates = flat.shape[0] - (CONV + 1) * n_lru
    gates_total = flat[:n_gates].reshape(gate_heads.shape)
    taps_total = flat[n_gates : n_gates + CONV * n_lru].reshape(CONV, n_lru)
    decay_total = flat[n_gates + CONV * n_lru :]

    first_grad = first_grad + dot_far(grad_inner, in_value)
    sent = in_value_sum.second(first_grad)
    up_total = up_sum.finish(edge)
    down_total = down_sum.astype(F32)
    if in_value_sum.simple:
        in_total = jnp.concatenate([in_value_sum.finish(), in_gate_sum.finish()], axis=1)
    else:
        both = jnp.concatenate([in_value_sum.mine(), in_gate_sum.mine()], axis=1)
        in_value_sum.along_z(both)
        both = in_value_sum.total().astype(BF16)
        in_total = jnp.concatenate(
            [
                lax.all_gather(both[:, n * width : (n + 1) * width], "grp")
                .transpose(1, 0, 2)
                .reshape(-1, LRU)
                for n in range(2)
            ],
            axis=1,
        ).astype(F32)
    ffn_out = jnp.dot(tie(hidden, *sent), proj_down, preferred_element_type=F32)
    block_out = by_token((resid + ffn_out).astype(BF16).reshape(tokens.shape))
    grad_tokens = grad_resid + norm_back(inputs, first_scale, gain_one, first_grad)
    grad_tokens = by_token(grad_tokens.astype(BF16).reshape(tokens.shape))
    first_total = gain_grad(in_proj, in_total, first_gain)
    second_total = gain_grad(up_proj, up_total, second_gain)
    return (
        block_out, grad_tokens, first_total, in_total, taps_total, decay_total, gates_total,
        out_total, second_total, up_total, down_total,
    )


def solution(mesh):
    in_specs = (
        P("grp", "seq", None),
        P("grp", "seq"),
        P("grp", "seq", None),
        P("seq"),
        P("seq", None),
        P(None, "seq"),
        P("seq"),
        P("seq", None, None),
        P("seq", None),
        P("seq"),
        P("seq", None),
        P("seq", None),
    )
    out_specs = (
        P("grp", "seq", None),
        P("grp", "seq", None),
        P("seq"),
        P("seq", None),
        P(None, "seq"),
        P("seq"),
        P("seq", None, None),
        P("seq", None),
        P("seq"),
        P("seq", None),
        P("seq", None),
    )
    return jax.shard_map(body, mesh=mesh, in_specs=in_specs, out_specs=out_specs, check_vma=False)
```

```python
import functools

import jax
import jax.numpy as jnp
from jax import lax
from jax.experimental import pallas as pl
from jax.experimental.pallas import tpu as pltpu
from jax.sharding import PartitionSpec as P

D = 1536
HEADS = 16
HS = 128
LRU = 2048
FF = 4608
CONV = 4
CHUNKS = 8
HALO = 8
BACK = 8 * (CONV - 1)
TAIL = 32
F32 = jnp.float32
BF16 = jnp.bfloat16


def from_behind(value, axis, steps):
    count = lax.axis_size(axis)
    first, last = (max(0, -steps), min(count, count - steps))
    return lax.ppermute(value, axis, [(source, source + steps) for source in range(first, last)])


def gelu_parts(v):
    k = 0.7978845608028654
    square = v * v
    t = jnp.tanh(k * v * (1.0 + 0.044715 * square))
    half = 0.5 * (1.0 + t)
    slope = half + 0.5 * v * (1.0 - t * t) * (k * (1.0 + 3.0 * 0.044715 * square))
    return v * half, slope


def gelu_tanh(v):
    k = 0.7978845608028654
    return 0.5 * v * (1.0 + jnp.tanh(k * v * (1.0 + 0.044715 * v * v)))


def sigmoid(v):
    return 0.5 * jnp.tanh(0.5 * v) + 0.5


def drive_values(q_rate, q_input, soft):
    rate = sigmoid(q_rate)
    inp = sigmoid(q_input)
    decay = jnp.exp(-8.0 * rate * soft)
    root = jnp.sqrt(1.0 - decay * decay + 0.001)
    return rate, inp, decay, root


def shifted_group(group, step, fill):
    row = lax.broadcasted_iota(jnp.int32, group.shape, 0)
    edge = 0 if step == 1 else CHUNKS - 1
    moved = pltpu.roll(group, step % CHUNKS, 0)
    return jnp.where(row == edge, fill, moved)


def extend_back(ext_s, u_ref, halo_ref, b):
    rows = u_ref.shape[1]
    ext_s[pl.ds(BACK, rows), :] = u_ref[b].astype(F32)
    halo = halo_ref[b].astype(F32)
    for m in range(CONV - 1):
        group = ext_s[pl.ds(BACK + rows - BACK + 8 * m, 8), :]
        fill = halo[HALO - CONV + 1 + m : HALO - CONV + 2 + m, :]
        ext_s[pl.ds(8 * m, 8), :] = shifted_group(group, 1, fill)


def mixer_forward_kernel(
    u_ref, halo_ref, dist_ref, gates_ref, taps_ref, soft_ref,
    c_ref, keep_ref, state_ref, prod_ref, chunk_ref,
    ext_s, c_s, rate_s, inp_s,
):
    seqs, rows, _ = u_ref.shape
    soft = soft_ref[...]
    for b in range(seqs):
        extend_back(ext_s, u_ref, halo_ref, b)

        def conv_chunk(n, _):
            at = pl.multiple_of(n * 64, 64)
            far = dist_ref[b, pl.ds(at, 64), :]
            total = taps_ref[0:1, :] * ext_s[pl.ds(at + BACK, 64), :]
            for k in range(1, CONV):
                window = taps_ref[k : k + 1, :] * ext_s[pl.ds(at + BACK - 8 * k, 64), :]
                total = total + jnp.where(far >= float(k), window, 0.0)
            low = total.astype(BF16)
            c_ref[b, pl.ds(at, 64), :] = low
            c_s[b, pl.ds(at, 64), :] = low.astype(F32)
            return 0

        lax.fori_loop(0, rows // 64, conv_chunk, 0)
        both = jnp.dot(c_ref[b], gates_ref[0], preferred_element_type=F32)
        rate_s[b] = both[:, :HS]
        inp_s[b] = both[:, HS:]

    def scan_step(j, carry):
        new = []
        for b in range(seqs):
            at = pl.ds(pl.multiple_of(j * 8, 8), 8)
            state, prod = carry[b]
            _, inp, decay, root = drive_values(rate_s[b, at, :], inp_s[b, at, :], soft)
            keep = jnp.where(dist_ref[b, at, :] >= 1.0, decay, 0.0)
            state = keep * state + root * inp * c_s[b, at, :]
            prod = keep * prod
            keep_ref[b, at, :] = keep
            state_ref[b, at, :] = state
            prod_ref[b, at, :] = prod
            new.append((state, prod))
        return tuple(new)

    zero, one = jnp.zeros((CHUNKS, HS), F32), jnp.ones((CHUNKS, HS), F32)
    ends = lax.fori_loop(0, rows // CHUNKS, scan_step, ((zero, one),) * seqs, unroll=8)
    for b in range(seqs):
        chunk_ref[b, 0] = ends[b][0]
        chunk_ref[b, 1] = ends[b][1]


def branch_kernel(core_ref, state_ref, prod_ref, carry_ref, gate_ref, out_ref, branch_ref, split_ref):
    del core_ref
    seqs, rows, _ = state_ref.shape
    for b in range(seqs):
        carry = jnp.concatenate([carry_ref[b]] * 4, axis=0)

        def point(n, _):
            at = pl.ds(pl.multiple_of(n * 32, 32), 32)
            state = state_ref[b, at, :] + prod_ref[b, at, :] * carry
            out_ref[b, at, :] = state
            low = (state * gelu_tanh(gate_ref[b, at, :])).astype(BF16)
            branch_ref[b, at, :] = low
            split_ref[0, b, at, :] = low
            return 0

        lax.fori_loop(0, rows // 32, point, 0, unroll=4)


def reverse_kernel(
    grad_ref, gate_ref, keep_ref, state_ref,
    dg_ref, local_ref, prod_ref, chunk_ref,
):
    seqs, rows, _ = grad_ref.shape
    pairs = rows // 16

    def scan_step(n, carry):
        first = pl.multiple_of((pairs - 1 - n) * 16, 16)
        at = pl.ds(first, 16)
        new = []
        for b in range(seqs):
            pull, prod = carry[b]
            act, slope = gelu_parts(gate_ref[b, at, :])
            grad = grad_ref[b, at, :]
            dg_ref[b, at, :] = (grad * state_ref[b, at, :] * slope).astype(BF16)
            dh = grad * act
            keep = keep_ref[b, at, :]
            late = dh[8:] + pull
            late_prod = prod
            pull, prod = keep[8:] * late, keep[8:] * prod
            early = dh[:8] + pull
            local_ref[b, at, :] = jnp.concatenate([early, late], axis=0)
            prod_ref[b, at, :] = jnp.concatenate([prod, late_prod], axis=0)
            new.append((keep[:8] * early, keep[:8] * prod))
        return tuple(new)

    zero, one = jnp.zeros((CHUNKS, HS), F32), jnp.ones((CHUNKS, HS), F32)
    ends = lax.fori_loop(0, pairs, scan_step, ((zero, one),) * seqs, unroll=4)
    for b in range(seqs):
        chunk_ref[b, 0] = ends[b][0]
        chunk_ref[b, 1] = ends[b][1]


def mixer_backward_kernel(
    local_ref, prod_ref, carry_ref, state_ref, before_ref, c_ref, u_ref, halo_ref, dist_ref,
    gates_ref, taps_ref, soft_ref,
    du_ref, tail_ref, edge_ref, ggate_ref, gtaps_ref, gdecay_ref,
    q_s, dq_s, dc_s, h_s, ext_s, dist_s,
):
    seqs, rows, _ = local_ref.shape
    soft = soft_ref[...]
    ggate = jnp.zeros((HS, 2 * HS), F32)
    decay_sum = jnp.zeros((8, HS), F32)
    taps_sum = [jnp.zeros((8, HS), F32) for _ in range(CONV)]

    def fold(value):
        return jnp.sum(value.reshape(value.shape[0] // 8, 8, HS), axis=0)

    for b in range(seqs):
        q_s[...] = jnp.dot(c_ref[b], gates_ref[0], preferred_element_type=F32)
        h_s[pl.ds(0, 8), :] = before_ref[b]
        h_s[pl.ds(8, rows), :] = state_ref[b]
        carry = jnp.concatenate([carry_ref[b]] * 4, axis=0)

        def point(n, total):
            first = pl.multiple_of(n * 32, 32)
            at = pl.ds(first, 32)
            lam = local_ref[b, at, :] + prod_ref[b, at, :] * carry
            rate, inp, decay, root = drive_values(q_s[at, :HS], q_s[at, HS:], soft)
            conv = c_ref[b, at, :].astype(F32)
            kept = jnp.where(dist_ref[b, at, :] >= 1.0, h_s[at, :], 0.0)
            lam_root = lam * root
            lam_inp = lam * inp
            grad_decay = lam * kept - lam_inp * conv * decay / root
            rated = grad_decay * decay * rate
            dq_s[at, :HS] = (-8.0 * soft * rated * (1.0 - rate)).astype(BF16)
            dq_s[at, HS:] = (lam_root * conv * inp * (1.0 - inp)).astype(BF16)
            dc_s[at, :] = lam_root * inp
            return total + fold(rated)

        decay_sum = lax.fori_loop(0, rows // 32, point, decay_sum, unroll=2)
        dc_s[pl.ds(0, rows), :] += lax.dot_general(
            dq_s[...], gates_ref[0], (((1,), (1,)), ((), ())), preferred_element_type=F32
        )
        ggate = ggate + lax.dot_general(
            c_ref[b], dq_s[...], (((0,), (0,)), ((), ())), preferred_element_type=F32
        )
        extend_back(ext_s, u_ref, halo_ref, b)
        dist_s[pl.ds(0, rows), :] = dist_ref[b]
        for m in range(CONV - 1):
            for held in (dc_s, dist_s):
                held[pl.ds(rows + 8 * m, 8), :] = shifted_group(held[pl.ds(8 * m, 8), :], -1, 0.0)

        def conv_chunk(n, totals):
            at = pl.multiple_of(n * 64, 64)
            grad = dc_s[pl.ds(at, 64), :]
            far = dist_s[pl.ds(at, 64), :]
            out = taps_ref[0:1, :] * grad
            totals = list(totals)
            totals[0] = totals[0] + fold(grad * ext_s[pl.ds(at + BACK, 64), :])
            for k in range(1, CONV):
                masked = jnp.where(far >= float(k), grad, 0.0)
                totals[k] = totals[k] + fold(masked * ext_s[pl.ds(at + BACK - 8 * k, 64), :])
                ahead = pl.ds(at + 8 * k, 64)
                value = taps_ref[k : k + 1, :] * dc_s[ahead, :]
                out = out + jnp.where(dist_s[ahead, :] >= float(k), value, 0.0)
            du_ref[b, pl.ds(at, 64), :] = out.astype(BF16)

            @pl.when(n == rows // 64 - 1)
            def _():
                tail_ref[b] = out[64 - TAIL :, :]

            return tuple(totals)

        taps_sum = list(lax.fori_loop(0, rows // 64, conv_chunk, tuple(taps_sum)))
        edges = [jnp.zeros((HALO - CONV + 1, HS), F32)]
        for m in range(CONV - 1, 0, -1):
            edge = jnp.zeros((1, HS), F32)
            for k in range(m, CONV):
                at = pl.ds(8 * (k - m), 1)
                masked = jnp.where(dist_s[at, :] >= float(k), dc_s[at, :], 0.0)
                edge = edge + taps_ref[k : k + 1, :] * masked
            edges.append(edge)
        edge_ref[b] = jnp.concatenate(edges, axis=0)
    ggate_ref[0] = ggate
    gdecay_ref[...] = jnp.broadcast_to(
        8.0 * jnp.sum(decay_sum, axis=0, keepdims=True), (8, HS)
    )
    gtaps_ref[...] = jnp.concatenate(
        [jnp.sum(t, axis=0, keepdims=True) for t in taps_sum] + [jnp.zeros((8 - CONV, HS), F32)],
        axis=0,
    )


def norm_kernel(shards, core_ref, x_ref, gain_ref, normed_ref, own_ref, far_ref, scale_ref):
    x = x_ref[...].astype(F32)
    scale = lax.rsqrt(jnp.mean(x * x, axis=-1, keepdims=True) + 1e-06)
    low = (x * scale * gain_ref[...]).astype(BF16)
    normed_ref[...] = low
    scale_ref[...] = jnp.broadcast_to(scale, scale_ref.shape)
    wide = low.astype(F32)
    size = D // shards
    even, odd = (
        jnp.concatenate([wide[:, n * size : (n + 1) * size] for n in range(c, shards, 2)], axis=1)
        for c in range(2)
    )
    first = core_ref[0] == 0
    own_ref[...] = jnp.where(first, even, odd).astype(BF16)
    far_ref[...] = jnp.where(first, odd, even).astype(BF16)


def ffn_forward_kernel(n_ref, gate_ref, up_ref, hidden_ref, pull_ref):
    for m in range(0, n_ref.shape[0], 256):
        at = pl.ds(m, 256)
        e1 = jnp.dot(n_ref[at, :], gate_ref[...], preferred_element_type=F32)
        e2 = jnp.dot(n_ref[at, :], up_ref[...], preferred_element_type=F32)
        act, slope = gelu_parts(e1)
        hidden_ref[at, :] = (act * e2).astype(BF16)
        pull_ref[0, at, :] = (slope * e2).astype(BF16)
        pull_ref[1, at, :] = act.astype(BF16)


def ffn_backward_kernel(grad_ref, down_ref, pull_ref, out_ref):
    for m in range(0, grad_ref.shape[0], 256):
        at = pl.ds(m, 256)
        dv = lax.dot_general(
            grad_ref[at, :], down_ref[...], (((1,), (1,)), ((), ())), preferred_element_type=F32
        )
        out_ref[0, at, :] = (dv * pull_ref[0, at, :].astype(F32)).astype(BF16)
        out_ref[1, at, :] = (dv * pull_ref[1, at, :].astype(F32)).astype(BF16)


def head_block(lead, rows):
    return pl.BlockSpec((lead, rows, HS), lambda h: (0, 0, h))


def shared_block(shape):
    return pl.BlockSpec(shape, lambda h: (0,) * len(shape))


def pair_block(seqs):
    return pl.BlockSpec((seqs, 2, CHUNKS, HS), lambda h: (0, 0, 0, h))


PARAMS = pltpu.CompilerParams(vmem_limit_bytes=40 * 1024 * 1024)


def mixer_forward(u, halo, dist, gates, taps, soft):
    seqs, rows, _ = u.shape
    full = head_block(seqs, rows)
    wide = jax.ShapeDtypeStruct((seqs, rows, LRU), F32)
    return pl.pallas_call(
        mixer_forward_kernel,
        grid=(HEADS,),
        in_specs=[
            full,
            head_block(seqs, HALO),
            shared_block((seqs, rows, HS)),
            pl.BlockSpec((1, HS, 2 * HS), lambda h: (h, 0, 0)),
            pl.BlockSpec((CONV, HS), lambda h: (0, h)),
            pl.BlockSpec((1, HS), lambda h: (0, h)),
        ],
        out_specs=[full, full, full, full, pair_block(seqs)],
        out_shape=[
            jax.ShapeDtypeStruct((seqs, rows, LRU), BF16),
            wide,
            wide,
            wide,
            jax.ShapeDtypeStruct((seqs, 2, CHUNKS, LRU), F32),
        ],
        scratch_shapes=[
            pltpu.VMEM((rows + BACK, HS), F32),
            pltpu.VMEM((seqs, rows, HS), F32),
            pltpu.VMEM((seqs, rows, HS), F32),
            pltpu.VMEM((seqs, rows, HS), F32),
        ],
        compiler_params=PARAMS,
        name="mixer_forward",
    )(u, halo, dist, gates, taps, soft)


def mixer_branch(state, prod, carry, gate, shards, core):
    seqs, rows, _ = state.shape
    per = HEADS // shards

    def at(h, core_ref):
        return (0, 0, h)

    def split_at(h, core_ref):
        shard = h // per
        return ((shard % 2 + core_ref[0]) % 2, 0, 0, (shard // 2) * per + h % per)

    full = pl.BlockSpec((seqs, rows, HS), at)
    return pl.pallas_call(
        branch_kernel,
        grid_spec=pltpu.PrefetchScalarGridSpec(
            num_scalar_prefetch=1,
            grid=(HEADS,),
            in_specs=[full, full, pl.BlockSpec((seqs, CHUNKS, HS), at), full],
            out_specs=[full, full, pl.BlockSpec((1, seqs, rows, HS), split_at)],
        ),
        out_shape=[
            jax.ShapeDtypeStruct((seqs, rows, LRU), F32),
            jax.ShapeDtypeStruct((seqs, rows, LRU), BF16),
            jax.ShapeDtypeStruct((2, seqs, rows, LRU // 2), BF16),
        ],
        compiler_params=PARAMS,
        name="mixer_branch",
    )(core.reshape(1), state, prod, carry, gate)


def mixer_reverse(grad, gate, keep, state):
    seqs, rows, _ = grad.shape
    full = head_block(seqs, rows)
    wide = jax.ShapeDtypeStruct((seqs, rows, LRU), F32)
    return pl.pallas_call(
        reverse_kernel,
        grid=(HEADS,),
        in_specs=[full, full, full, full],
        out_specs=[full, full, full, pair_block(seqs)],
        out_shape=[
            jax.ShapeDtypeStruct((seqs, rows, LRU), BF16),
            wide,
            wide,
            jax.ShapeDtypeStruct((seqs, 2, CHUNKS, LRU), F32),
        ],
        compiler_params=PARAMS,
        name="mixer_reverse",
    )(grad, gate, keep, state)


def mixer_backward(local, prod, carry, state, before, c, u, halo, dist, gates, taps, soft):
    seqs, rows, _ = local.shape
    full = head_block(seqs, rows)
    small = head_block(seqs, HALO)
    gate_block = pl.BlockSpec((1, HS, 2 * HS), lambda h: (h, 0, 0))
    row_block = pl.BlockSpec((8, HS), lambda h: (0, h))
    return pl.pallas_call(
        mixer_backward_kernel,
        grid=(HEADS,),
        in_specs=[
            full,
            full,
            head_block(seqs, CHUNKS),
            full,
            small,
            full,
            full,
            small,
            shared_block((seqs, rows, HS)),
            gate_block,
            pl.BlockSpec((CONV, HS), lambda h: (0, h)),
            pl.BlockSpec((1, HS), lambda h: (0, h)),
        ],
        out_specs=[full, head_block(seqs, TAIL), small, gate_block, row_block, row_block],
        out_shape=[
            jax.ShapeDtypeStruct((seqs, rows, LRU), BF16),
            jax.ShapeDtypeStruct((seqs, TAIL, LRU), F32),
            jax.ShapeDtypeStruct((seqs, HALO, LRU), F32),
            jax.ShapeDtypeStruct((HEADS, HS, 2 * HS), F32),
            jax.ShapeDtypeStruct((8, LRU), F32),
            jax.ShapeDtypeStruct((8, LRU), F32),
        ],
        scratch_shapes=[
            pltpu.VMEM((rows, 2 * HS), F32),
            pltpu.VMEM((rows, 2 * HS), BF16),
            pltpu.VMEM((rows + BACK, HS), F32),
            pltpu.VMEM((rows + 8, HS), F32),
            pltpu.VMEM((rows + BACK, HS), F32),
            pltpu.VMEM((rows + BACK, HS), F32),
        ],
        compiler_params=PARAMS,
        name="mixer_backward",
    )(local, prod, carry, state, before, c, u, halo, dist, gates, taps, soft)


def rms_norm(x, gain, shards, core):
    rows = x.shape[0]
    block = min(rows, 256)
    return pl.pallas_call(
        functools.partial(norm_kernel, shards),
        grid=(rows // block,),
        in_specs=[
            pl.BlockSpec(memory_space=pltpu.SMEM),
            pl.BlockSpec((block, D), lambda n: (n, 0)),
            pl.BlockSpec((1, D), lambda n: (0, 0)),
        ],
        out_specs=[
            pl.BlockSpec((block, D), lambda n: (n, 0)),
            pl.BlockSpec((block, D // 2), lambda n: (n, 0)),
            pl.BlockSpec((block, D // 2), lambda n: (n, 0)),
            pl.BlockSpec((block, 128), lambda n: (n, 0)),
        ],
        out_shape=[
            jax.ShapeDtypeStruct((rows, D), BF16),
            jax.ShapeDtypeStruct((rows, D // 2), BF16),
            jax.ShapeDtypeStruct((rows, D // 2), BF16),
            jax.ShapeDtypeStruct((rows, 128), F32),
        ],
        compiler_params=PARAMS,
        name="rms_norm",
    )(core.reshape(1), x, gain.reshape(1, D))


FF_TILE = 512
GATHER_TILE = 768
DOT_TILE = 512


def ffn_forward(normed, proj_up):
    rows = normed.shape[0]
    steps = FF // FF_TILE
    return pl.pallas_call(
        ffn_forward_kernel,
        grid=(steps,),
        in_specs=[
            pl.BlockSpec((rows, D), lambda n: (0, 0)),
            pl.BlockSpec((D, FF_TILE), lambda n: (0, n)),
            pl.BlockSpec((D, FF_TILE), lambda n: (0, n + steps)),
        ],
        out_specs=[
            pl.BlockSpec((rows, FF_TILE), lambda n: (0, n)),
            pl.BlockSpec((2, rows, FF_TILE), lambda n: (0, 0, n)),
        ],
        out_shape=[
            jax.ShapeDtypeStruct((rows, FF), BF16),
            jax.ShapeDtypeStruct((2, rows, FF), BF16),
        ],
        compiler_params=PARAMS,
        name="ffn_forward",
    )(normed, proj_up, proj_up)


def ffn_backward(grad, proj_down, pull):
    rows = grad.shape[0]
    return pl.pallas_call(
        ffn_backward_kernel,
        grid=(FF // FF_TILE,),
        in_specs=[
            pl.BlockSpec((rows, D), lambda n: (0, 0)),
            pl.BlockSpec((FF_TILE, D), lambda n: (n, 0)),
            pl.BlockSpec((2, rows, FF_TILE), lambda n: (0, 0, n)),
        ],
        out_specs=pl.BlockSpec((2, rows, FF_TILE), lambda n: (0, 0, n)),
        out_shape=jax.ShapeDtypeStruct((2, rows, FF), BF16),
        compiler_params=PARAMS,
        name="ffn_backward",
    )(grad, proj_down, pull)


def gather_rows(shard):
    parts = lax.axis_size("grp")
    rows = shard.shape[0] // parts
    own = lax.dynamic_slice_in_dim(shard, lax.axis_index("grp") * rows, rows, 0)
    return lax.all_gather(own, ("seq", "grp"), axis=0, tiled=True)


def tie(value, *after):
    return lax.optimization_barrier((value, *after))[0]


def xor_pairs(axis, bit):
    return [(i, i ^ bit) for i in range(lax.axis_size(axis))]


def ring_pairs(steps):
    count = lax.axis_size("seq")
    return [(i, (i + steps) % count) for i in range(count)]


def same_cores():
    count = lax.axis_size("seq")
    return [list(range(core, count, 2)) for core in range(2)]


def dot_rows(a, b):
    return lax.dot_general(a, b, (((0,), (0,)), ((), ())), preferred_element_type=F32)


def reduce_rows(partial):
    part = lax.psum_scatter(partial, "seq", scatter_dimension=0, tiled=True)
    part = lax.psum_scatter(part, "grp", scatter_dimension=0, tiled=True)
    return lax.all_gather(part, "grp", axis=0, tiled=True).astype(F32)


def dot_far(a, b):
    return lax.dot_general(a, b, (((1,), (1,)), ((), ())), preferred_element_type=F32)


def by_position(a):
    seqs, rows = a.shape[:2]
    return a.reshape(seqs, CHUNKS, rows // CHUNKS, *a.shape[2:]).swapaxes(1, 2).reshape(a.shape)


def by_token(a):
    seqs, rows = a.shape[:2]
    return a.reshape(seqs, rows // CHUNKS, CHUNKS, *a.shape[2:]).swapaxes(1, 2).reshape(a.shape)


def fetch_columns(where_ref, pieces, start, target, sem):
    own, far = pieces[:6], pieces[6:]
    rows, columns = own[0].shape
    width, tile = columns // 4, target.shape[1]
    depth, half = own[1].shape[0], own[4].shape[0]
    chips = depth // rows + 1
    chip, core, group = where_ref[0], where_ref[1], where_ref[2]
    quarter = start // width
    offset = pl.multiple_of(start - quarter * width, 128)
    start = pl.multiple_of(start, 128)
    relation = lax.bitwise_xor(group, quarter)

    def copy(source, row, count):
        place = target.at[pl.ds(pl.multiple_of(row, 16), count), :]
        pltpu.make_async_copy(source, place, sem).start()

    for c, (shard, *parts) in enumerate((own, far)):
        other = lax.rem(core + c, 2)
        copy(shard.at[:, pl.ds(start, tile)], (chip * 2 + other) * rows, rows)
        for j in range(1, chips):
            row = (lax.rem(chip + j, chips) * 2 + other) * rows
            first = (j - 1) * rows
            for k in range(3):

                @pl.when(relation == k)
                def _():
                    copy(parts[k].at[pl.ds(first, rows), pl.ds(offset, tile)], row, rows)

            @pl.when(relation == 3)
            def _():
                for m in range(2):
                    low, high = max(first, m * half), min(first + rows, (m + 1) * half)
                    if low < high:
                        at = pl.ds(low - m * half, high - low)
                        source = parts[3 + m].at[at, pl.ds(offset, tile)]
                        copy(source, row + (low - first), high - low)


def gathered_tiles(fetch, held, sems):
    step, steps = pl.program_id(0), pl.num_programs(0)
    slot = lax.rem(step, 2)

    @pl.when(step == 0)
    def _():
        fetch(step, slot)

    @pl.when(step + 1 < steps)
    def _():
        fetch(step + 1, 1 - slot)

    for side in range(held.shape[1]):
        whole = held.at[slot, side]
        pltpu.make_async_copy(whole, whole, sems.at[slot, side]).wait()
    return slot


def gathered_ffn_kernel(where_ref, n_ref, *refs):
    pieces, (hidden_ref, pull_ref, gate_ref, up_ref, held, sems) = refs[:12], refs[12:]
    tile = hidden_ref.shape[1]

    def fetch(n, slot):
        for side in range(2):
            start = n * tile + side * (pieces[0].shape[1] // 2)
            fetch_columns(where_ref, pieces, start, held.at[slot, side], sems.at[slot, side])

    slot = gathered_tiles(fetch, held, sems)
    gate_ref[...] = held[slot, 0]
    up_ref[...] = held[slot, 1]
    ffn_forward_kernel(n_ref, gate_ref, up_ref, hidden_ref, pull_ref)


def gathered_dot_kernel(base, where_ref, n_ref, *refs):
    pieces, (out_ref, weight_ref, held, sems) = refs[:12], refs[12:]
    tile = out_ref.shape[1]

    def fetch(n, slot):
        start = base + n * tile
        fetch_columns(where_ref, pieces, start, held.at[slot, 0], sems.at[slot, 0])

    slot = gathered_tiles(fetch, held, sems)
    weight_ref[...] = held[slot, 0]
    out_ref[...] = jnp.dot(n_ref[...], weight_ref[...], preferred_element_type=F32).astype(
        out_ref.dtype
    )


class Gather:
    def __init__(self, shard, *after, offload=False):
        self.shard = shard
        self.chips = lax.axis_size("seq") // 2
        half = (self.chips - 1) * shard.shape[0] // 2
        self.simple = lax.axis_size("grp") != 4 or half % 16 != 0
        if self.simple:
            self.whole = gather_rows(shard)
            return
        group = lax.axis_index("grp")
        width = shard.shape[1] // 4
        own = lax.dynamic_slice_in_dim(shard, group * width, width, 1)
        if after:
            own = tie(own, *after)
        others = range(1, self.chips)
        if offload:
            slabs = lax.all_gather(own, "seq", axis_index_groups=same_cores())
            chip = lax.axis_index("seq") // 2
            slabs = [
                lax.dynamic_index_in_dim(slabs, (chip + j) % self.chips, 0, False) for j in others
            ]
        else:
            slabs = [lax.ppermute(own, "seq", ring_pairs(-2 * j)) for j in others]
        self.near = jnp.concatenate(slabs, axis=0)
        self.half = half

    def first(self):
        if self.simple:
            return ()
        self.from_x = lax.ppermute(self.near, "grp", xor_pairs("grp", 1))
        self.from_y = lax.ppermute(self.near, "grp", xor_pairs("grp", 2))
        return (self.near,)

    def second(self, *after):
        if self.simple:
            return ()
        if after:
            self.from_x, self.from_y = tie((self.from_x, self.from_y), *after)
        self.halves = (self.from_y[: self.half], self.from_x[self.half :])
        return self.halves

    def third(self):
        if self.simple:
            return
        diag_a = lax.ppermute(self.halves[0], "grp", xor_pairs("grp", 1))
        diag_b = lax.ppermute(self.halves[1], "grp", xor_pairs("grp", 2))
        own = (self.shard, self.near, self.from_x, self.from_y, diag_a, diag_b)
        far = tuple(lax.ppermute(piece, "seq", xor_pairs("seq", 1)) for piece in own)
        place = lax.axis_index("seq")
        where = jnp.stack([place // 2, place % 2, lax.axis_index("grp")]).astype(jnp.int32)
        self.pieces = (where, own, far)

    def call(self, kernel, normed, steps, tile, weights, out_specs, out_shape, name):
        where, own, far = self.pieces
        rows, depth = normed.shape
        return pl.pallas_call(
            kernel,
            grid=(steps,),
            in_specs=[
                pl.BlockSpec(memory_space=pltpu.SMEM),
                pl.BlockSpec((rows, depth), lambda n: (0, 0)),
            ]
            + [pl.BlockSpec(memory_space=pl.ANY)] * 12,
            out_specs=out_specs + [pl.BlockSpec((depth, tile), lambda n: (0, n))] * weights,
            out_shape=out_shape + [jax.ShapeDtypeStruct((depth, steps * tile), BF16)] * weights,
            scratch_shapes=[
                pltpu.VMEM((2, weights, depth, tile), BF16),
                pltpu.SemaphoreType.DMA((2, weights)),
            ],
            compiler_params=pltpu.CompilerParams(vmem_limit_bytes=56 * 1024 * 1024),
            name=name,
        )(where, normed, *own, *far)

    def dot(self, normed, half, dtype):
        columns = self.shard.shape[1] // 2
        base = half * columns
        if self.simple:
            weight = self.whole[:, base : base + columns]
            return jnp.dot(normed, weight, preferred_element_type=F32).astype(dtype), weight
        rows, tile = normed.shape[0], DOT_TILE
        return self.call(
            functools.partial(gathered_dot_kernel, base),
            normed,
            columns // tile,
            tile,
            1,
            [pl.BlockSpec((rows, tile), lambda n: (0, n))],
            [jax.ShapeDtypeStruct((rows, columns), dtype)],
            "gathered_dot",
        )

    def ffn_forward(self, normed):
        if self.simple:
            hidden, pull = ffn_forward(normed, self.whole)
            return hidden, pull, self.whole[:, :FF], self.whole[:, FF:]
        rows, tile = normed.shape[0], GATHER_TILE
        return self.call(
            gathered_ffn_kernel,
            normed,
            FF // tile,
            tile,
            2,
            [
                pl.BlockSpec((rows, tile), lambda n: (0, n)),
                pl.BlockSpec((2, rows, tile), lambda n: (0, 0, n)),
            ],
            [
                jax.ShapeDtypeStruct((rows, FF), BF16),
                jax.ShapeDtypeStruct((2, rows, FF), BF16),
            ],
            "gathered_ffn",
        )


class Reduction:
    def __init__(self, a_own, a_far, columns, width, fused=False):
        self.simple = lax.axis_size("grp") != 4
        count = lax.axis_size("seq")
        place = lax.axis_index("seq")
        self.chips = count // 2
        self.chip, core = place // 2, place % 2
        self.width = width
        full = a_own.shape[1]
        self.rows = full // self.chips
        self.half = full // 2
        self.a_own = a_own
        if self.simple:
            parts = [columns(k) for k in range(4)]
            own, far = (
                jnp.concatenate([dot_rows(a, part) for part in parts], axis=1)
                for a in (a_own, a_far)
            )
            cores = jnp.stack(
                [jnp.where(core == c, own, far).reshape(self.chips, self.rows, -1) for c in (0, 1)],
                axis=1,
            )
            self.product = cores.reshape(2 * full, 4 * width).astype(BF16)
            self.arrived = self.product
            self.sent = (self.product,)
            return
        group = lax.axis_index("grp")
        self.x, self.y = xor_pairs("grp", 1), xor_pairs("grp", 2)
        self.b = [columns(group ^ k) for k in range(4)]
        self.far = [None] * 4
        self.product = None
        other = xor_pairs("seq", 1)
        if fused:
            b_all = jnp.concatenate(self.b, axis=1)
            far = lax.ppermute(dot_rows(a_far, b_all).astype(BF16), "seq", other)
            self.product = (dot_rows(a_own, b_all) + far.astype(F32)).astype(BF16)
        for k in () if fused else (3, 1, 2, 0):
            product = dot_rows(a_far, self.b[k]).astype(BF16)
            self.far[k] = lax.ppermute(product, "seq", other)
        half = self.half
        self.sent = (
            self.own(3, 0, half).astype(BF16),
            self.own(3, half, full).astype(BF16),
        )
        self.diag_a = lax.ppermute(self.sent[0], "grp", self.x)
        self.diag_b = lax.ppermute(self.sent[1], "grp", self.y)

    def own(self, k, first, last):
        if self.product is not None:
            left = k * self.width
            return self.product[first:last, left : left + self.width].astype(F32)
        product = dot_rows(self.a_own[:, first:last], self.b[k])
        return product + self.far[k][first:last].astype(F32)

    def second(self, *after):
        if self.simple:
            return ()
        full, none = 2 * self.half, ((0, self.half), (0, 0))
        diag_a, diag_b = self.diag_a, self.diag_b
        if after:
            diag_a, diag_b = tie((diag_a, diag_b), *after)
        sent = (
            (self.own(1, 0, full) + jnp.pad(diag_b.astype(F32), (none[0][::-1], (0, 0)))).astype(BF16),
            (self.own(2, 0, full) + jnp.pad(diag_a.astype(F32), none)).astype(BF16),
        )
        self.from_x = lax.ppermute(sent[0], "grp", self.x)
        self.from_y = lax.ppermute(sent[1], "grp", self.y)
        return sent

    def mine(self, *after):
        from_x, from_y = self.from_x, self.from_y
        if after:
            from_x, from_y = tie((from_x, from_y), *after)
        mine = self.own(0, 0, 2 * self.half) + from_x.astype(F32) + from_y.astype(F32)
        return mine.astype(BF16)

    def along_z(self, mine):
        mine = mine.reshape(self.chips, self.rows, -1)
        self.kept = lax.dynamic_index_in_dim(mine, self.chip, 0, False)
        sent = tuple(
            lax.dynamic_index_in_dim(mine, (self.chip + j) % self.chips, 0, False)
            for j in range(1, self.chips)
        )
        self.arrived = [
            lax.ppermute(part, "seq", ring_pairs(2 * j + 2)) for j, part in enumerate(sent)
        ]
        return sent

    def third(self, *after, offload=False):
        if self.simple:
            return ()
        mine = self.mine(*after)
        if not offload:
            return self.along_z(mine)
        self.kept = None
        self.arrived = lax.psum_scatter(
            mine, "seq", scatter_dimension=0, axis_index_groups=same_cores(), tiled=True
        )
        return (mine,)

    def total(self):
        if self.kept is None:
            return self.arrived
        total = self.kept.astype(F32)
        for part in self.arrived:
            total = total + part.astype(F32)
        return total

    def finish(self, *after):
        if self.simple:
            return reduce_rows(self.product)
        total = self.total()
        if after:
            total = tie(total, *after)
        parts = lax.all_gather(total.astype(BF16), "grp")
        return parts.transpose(1, 0, 2).reshape(self.rows, 4 * self.width).astype(F32)


def gather_parts(lines, sums):
    if sums[0].simple:
        return lax.all_gather(lines, "grp", axis=0, tiled=True), [one.finish() for one in sums]
    pieces = [lines]
    for one in sums:
        total = one.total().astype(BF16)
        pieces += [total[:, n : n + HS] for n in range(0, one.width, HS)]
    parts = lax.all_gather(jnp.concatenate(pieces, axis=0), "grp")
    at = lines.shape[0]
    found = []
    for one in sums:
        blocks = one.width // HS
        part = parts[:, at : at + blocks * one.rows].reshape(4, blocks, one.rows, HS)
        found.append(part.transpose(2, 0, 1, 3).reshape(one.rows, 4 * one.width).astype(F32))
        at += blocks * one.rows
    return parts[:, : lines.shape[0]].reshape(-1, HS), found


def shard_carry(ends, prods, reverse):
    count = lax.axis_size("seq")
    place = lax.axis_index("seq")
    both = lax.all_gather(jnp.stack([ends, prods]), "seq")
    carry = jnp.zeros_like(ends)
    for step in range(count - 1):
        source = count - 1 - step if reverse else step
        ahead = source > place if reverse else source < place
        carry = jnp.where(ahead, both[source, 0] + both[source, 1] * carry, carry)
    return carry


def chunk_ends(chunks, reverse):
    state = jnp.zeros_like(chunks[:, 0, 0])
    prod = jnp.ones_like(state)
    order = range(CHUNKS - 1, -1, -1) if reverse else range(CHUNKS)
    for n in order:
        state = chunks[:, 0, n] + chunks[:, 1, n] * state
        prod = chunks[:, 1, n] * prod
    return state, prod


def chunk_carries(chunks, carry, reverse):
    order = range(CHUNKS - 1, -1, -1) if reverse else range(CHUNKS)
    found = [None] * CHUNKS
    for n in order:
        found[n] = carry
        carry = chunks[:, 0, n] + chunks[:, 1, n] * carry
    return jnp.stack(found, axis=1)


def norm_back(values, scale, gain, grad_normed):
    weighted = grad_normed * gain
    cubed = scale * scale * scale
    return scale * weighted - values * cubed * jnp.mean(weighted * values, axis=-1, keepdims=True)


def gain_grad(weight, grad_weight, gain):
    return jnp.sum(weight.astype(F32) * grad_weight, axis=1) / gain.astype(F32)


def body(
    tokens, seg_ids, cotangent, first_gain, in_proj, conv_taps, decay_param, gate_heads,
    out_proj, second_gain, up_proj, down_proj,
):
    seq_count, shard_len, _ = tokens.shape
    row_count = seq_count * shard_len
    edge_len = CONV - 1
    place = lax.axis_index("seq")
    last = lax.axis_size("seq") - 1

    small = jnp.concatenate(
        [first_gain, second_gain, decay_param, conv_taps.reshape(-1)]
    )
    small_all = lax.all_gather(small, "seq")
    n_gain, n_lru = first_gain.shape[0], decay_param.shape[0]
    gain_one = small_all[:, :n_gain].reshape(D).astype(F32)
    gain_two = small_all[:, n_gain : 2 * n_gain].reshape(D).astype(F32)
    decay_float = small_all[:, 2 * n_gain : 2 * n_gain + n_lru].reshape(LRU).astype(F32)
    taps_all = (
        small_all[:, 2 * n_gain + n_lru :].reshape(-1, CONV, n_lru).transpose(1, 0, 2)
    ).reshape(CONV, LRU).astype(F32)
    in_gather = Gather(in_proj)
    near = in_gather.first()
    in_gather.second()
    in_gather.third()
    gates_all = lax.all_gather(gate_heads, "seq", axis=0, tiled=True)
    up_gather = Gather(up_proj, gates_all, *near, offload=True)
    proj_out = gather_rows(out_proj)
    proj_down = gather_rows(down_proj)

    tokens = by_position(tokens)
    cotangent = by_position(cotangent)
    inputs = tokens.reshape(row_count, D).astype(F32)
    first_normed, first_own, first_far, first_scale = rms_norm(
        tokens.reshape(row_count, D), gain_one, last + 1, place % 2
    )
    first_scale = first_scale[:, :1]
    wide = (seq_count, shard_len, LRU)
    inner_low, in_value = in_gather.dot(first_normed, 0, BF16)
    inner_low = inner_low.reshape(wide)

    step = shard_len // CHUNKS
    final = inner_low.reshape(seq_count, step, CHUNKS, LRU)[:, step - HALO :, CHUNKS - 1]
    prev_inner = from_behind(final, "seq", 1)
    prev_ids = from_behind(seg_ids[:, shard_len - edge_len :], "seq", 1)
    prev_ids = jnp.where(place == 0, -1, prev_ids)
    ext_ids = jnp.concatenate([prev_ids, seg_ids], axis=1)
    dist = jnp.zeros((seq_count, shard_len), F32)
    for k in range(1, CONV):
        dist = dist + (ext_ids[:, edge_len - k : edge_len - k + shard_len] == seg_ids).astype(F32)
    dist = jnp.broadcast_to(by_position(dist)[:, :, None], (seq_count, shard_len, HS))
    soft = jax.nn.softplus(-decay_float).reshape(1, LRU)

    conv_low, keep, state_part, prod_part, chunks = mixer_forward(
        tie(inner_low, *up_gather.first()), prev_inner, dist, gates_all, taps_all, soft
    )
    end_state, end_prod = chunk_ends(chunks, False)
    gate_pre, in_gate = in_gather.dot(first_normed, 1, F32)
    gate_pre = gate_pre.reshape(wide)
    carry_in = shard_carry(end_state, end_prod, False)
    carries = chunk_carries(chunks, carry_in, False)
    state, branch, branch_split = mixer_branch(
        tie(state_part, *up_gather.second(carries)), prod_part, carries, gate_pre, last + 1, place % 2
    )
    branch_split = branch_split.reshape(2, row_count, LRU // 2)
    resid = inputs + jnp.dot(
        branch.reshape(row_count, LRU), proj_out, preferred_element_type=F32
    )
    second_normed, second_own, second_far, second_scale = rms_norm(
        resid, gain_two, last + 1, place % 2
    )
    second_scale = second_scale[:, :1]
    up_gather.third()
    hidden, pull, proj_gate, proj_up = up_gather.ffn_forward(second_normed)

    grad_out = cotangent.reshape(row_count, D)
    grad_down = dot_rows(hidden, grad_out).astype(BF16)
    down_part = lax.psum_scatter(grad_down, ("seq", "grp"), scatter_dimension=0, tiled=True)
    down_sum = lax.all_gather(down_part, "grp", axis=0, tiled=True)
    grad_expanded = ffn_backward(tie(grad_out, grad_down), proj_down, pull)
    quarter = FF // 2

    def up_columns(n):
        part = lax.dynamic_slice(
            grad_expanded, (n // 2, 0, (n % 2) * quarter), (1, row_count, quarter)
        )
        return part[0]

    up_sum = Reduction(second_own, second_far, up_columns, quarter)
    grad_expanded = tie(grad_expanded, *up_sum.sent)
    grad_second_normed = dot_far(grad_expanded[0], proj_gate) + dot_far(
        grad_expanded[1], proj_up
    )
    sent = up_sum.second(grad_second_normed)
    grad_second_normed = tie(grad_second_normed, *sent)
    grad_resid = grad_out.astype(F32) + norm_back(
        resid, second_scale, gain_two, grad_second_normed
    )
    grad_mixer = grad_resid.astype(BF16)
    grad_branch = dot_far(grad_mixer, proj_out)

    grad_gate, local, rev_prod, rev_chunks = mixer_reverse(
        tie(grad_branch, down_part).reshape(wide), gate_pre, keep, state
    )
    head_pull, head_prod = chunk_ends(rev_chunks, True)
    grad_gate = grad_gate.reshape(row_count, LRU)
    width = LRU // 4
    rev_carry = shard_carry(head_pull, head_prod, True)
    rev_carries = chunk_carries(rev_chunks, rev_carry, True)
    grad_mixer, grad_gate = tie((grad_mixer, grad_gate), rev_carry)
    out_sum = Reduction(
        branch_split[0],
        branch_split[1],
        lambda n: lax.dynamic_slice_in_dim(grad_mixer, n * (D // 4), D // 4, 1),
        D // 4,
        True,
    )
    in_gate_sum = Reduction(
        first_own,
        first_far,
        lambda n: lax.dynamic_slice_in_dim(grad_gate, n * width, width, 1),
        width,
        True,
    )
    sent = (*out_sum.sent, *in_gate_sum.sent)
    sent = up_sum.third(down_sum, *sent, offload=True)
    local = tie(local, *sent)
    du, tail, edge, grad_gates, grad_taps, grad_decay = mixer_backward(
        local, rev_prod, rev_carries, state, carries, conv_low, inner_low,
        prev_inner, dist, gates_all, taps_all, soft,
    )
    returned = from_behind(edge[:, HALO - edge_len :].astype(BF16), "seq", -1).astype(F32)
    grad_gate = tie(grad_gate, *out_sum.second(edge), *in_gate_sum.second(edge))
    first_grad = dot_far(grad_gate, in_gate)
    groups = TAIL // CHUNKS
    padded = jnp.pad(
        returned[:, :, None, :], ((0, 0), (groups - edge_len, 0), (CHUNKS - 1, 0), (0, 0))
    ).reshape(seq_count, TAIL, LRU)
    grad_inner = lax.dynamic_update_slice(
        du, (tail + padded).astype(BF16), (0, shard_len - TAIL, 0)
    )
    grad_inner = tie(grad_inner, first_grad).reshape(row_count, LRU)
    in_value_sum = Reduction(
        first_own,
        first_far,
        lambda n: lax.dynamic_slice_in_dim(grad_inner, n * width, width, 1),
        width,
        True,
    )
    grad_inner = tie(grad_inner, *in_value_sum.sent)

    shards = last + 1
    grad_decay_row = grad_decay[0] * jax.nn.sigmoid(-decay_float)
    flat = jnp.concatenate(
        [
            grad_gates.reshape(shards, -1, HS),
            grad_taps[:CONV].reshape(CONV, shards, -1, HS).swapaxes(0, 1).reshape(shards, -1, HS),
            grad_decay_row.reshape(shards, -1, HS),
        ],
        axis=1,
    )
    lines = flat.shape[1]
    whole = 16 * lax.axis_size("grp")
    flat = jnp.pad(flat, ((0, 0), (0, -lines % whole), (0, 0))).astype(BF16).reshape(-1, HS)
    flat = lax.psum_scatter(flat, ("seq", "grp"), scatter_dimension=0, tiled=True)
    first_grad = first_grad + dot_far(grad_inner, in_value)
    sent = in_value_sum.second(first_grad)
    out_sum.third(*sent)
    flat, (out_total,) = gather_parts(flat, [out_sum])
    flat = flat[:lines].astype(F32).reshape(-1)
    n_gates = flat.shape[0] - (CONV + 1) * n_lru
    gates_total = flat[:n_gates].reshape(gate_heads.shape)
    taps_total = flat[n_gates : n_gates + CONV * n_lru].reshape(CONV, n_lru)
    decay_total = flat[n_gates + CONV * n_lru :]

    up_total = up_sum.finish(edge)
    down_total = down_sum.astype(F32)
    if in_value_sum.simple:
        in_total = jnp.concatenate([in_value_sum.finish(), in_gate_sum.finish()], axis=1)
    else:
        both = jnp.concatenate([in_value_sum.mine(), in_gate_sum.mine()], axis=1)
        in_value_sum.along_z(both)
        both = in_value_sum.total().astype(BF16)
        in_total = jnp.concatenate(
            [
                lax.all_gather(both[:, n * width : (n + 1) * width], "grp")
                .transpose(1, 0, 2)
                .reshape(-1, LRU)
                for n in range(2)
            ],
            axis=1,
        ).astype(F32)
    ffn_out = jnp.dot(tie(hidden, *sent), proj_down, preferred_element_type=F32)
    block_out = by_token((resid + ffn_out).astype(BF16).reshape(tokens.shape))
    grad_tokens = grad_resid + norm_back(inputs, first_scale, gain_one, first_grad)
    grad_tokens = by_token(grad_tokens.astype(BF16).reshape(tokens.shape))
    first_total = gain_grad(in_proj, in_total, first_gain)
    second_total = gain_grad(up_proj, up_total, second_gain)
    return (
        block_out, grad_tokens, first_total, in_total, taps_total, decay_total, gates_total,
        out_total, second_total, up_total, down_total,
    )


def solution(mesh):
    in_specs = (
        P("grp", "seq", None),
        P("grp", "seq"),
        P("grp", "seq", None),
        P("seq"),
        P("seq", None),
        P(None, "seq"),
        P("seq"),
        P("seq", None, None),
        P("seq", None),
        P("seq"),
        P("seq", None),
        P("seq", None),
    )
    out_specs = (
        P("grp", "seq", None),
        P("grp", "seq", None),
        P("seq"),
        P("seq", None),
        P(None, "seq"),
        P("seq"),
        P("seq", None, None),
        P("seq", None),
        P("seq"),
        P("seq", None),
        P("seq", None),
    )
    return jax.shard_map(body, mesh=mesh, in_specs=in_specs, out_specs=out_specs, check_vma=False)
```

```python
import functools

import jax
import jax.numpy as jnp
from jax import lax
from jax.experimental import pallas as pl
from jax.experimental.pallas import tpu as pltpu
from jax.sharding import PartitionSpec as P

D = 1536
HEADS = 16
HS = 128
LRU = 2048
FF = 4608
CONV = 4
CHUNKS = 8
HALO = 8
BACK = 8 * (CONV - 1)
TAIL = 32
F32 = jnp.float32
BF16 = jnp.bfloat16


def from_behind(value, axis, steps):
    count = lax.axis_size(axis)
    first, last = (max(0, -steps), min(count, count - steps))
    return lax.ppermute(value, axis, [(source, source + steps) for source in range(first, last)])


def gelu_parts(v):
    k = 0.7978845608028654
    square = v * v
    t = jnp.tanh(k * v * (1.0 + 0.044715 * square))
    half = 0.5 * (1.0 + t)
    slope = half + 0.5 * v * (1.0 - t * t) * (k * (1.0 + 3.0 * 0.044715 * square))
    return v * half, slope


def gelu_tanh(v):
    k = 0.7978845608028654
    return 0.5 * v * (1.0 + jnp.tanh(k * v * (1.0 + 0.044715 * v * v)))


def sigmoid(v):
    return 0.5 * jnp.tanh(0.5 * v) + 0.5


def drive_values(q_rate, q_input, soft):
    rate = sigmoid(q_rate)
    inp = sigmoid(q_input)
    decay = jnp.exp(-8.0 * rate * soft)
    root = jnp.sqrt(1.0 - decay * decay + 0.001)
    return rate, inp, decay, root


def shifted_group(group, step, fill):
    row = lax.broadcasted_iota(jnp.int32, group.shape, 0)
    edge = 0 if step == 1 else CHUNKS - 1
    moved = pltpu.roll(group, step % CHUNKS, 0)
    return jnp.where(row == edge, fill, moved)


def extend_back(ext_s, u_ref, halo_ref, b):
    rows = u_ref.shape[1]
    ext_s[pl.ds(BACK, rows), :] = u_ref[b].astype(F32)
    halo = halo_ref[b].astype(F32)
    for m in range(CONV - 1):
        group = ext_s[pl.ds(BACK + rows - BACK + 8 * m, 8), :]
        fill = halo[HALO - CONV + 1 + m : HALO - CONV + 2 + m, :]
        ext_s[pl.ds(8 * m, 8), :] = shifted_group(group, 1, fill)


def mixer_forward_kernel(
    u_ref, halo_ref, dist_ref, gates_ref, taps_ref, soft_ref,
    c_ref, keep_ref, state_ref, prod_ref, chunk_ref,
    ext_s, c_s, rate_s, inp_s,
):
    seqs, rows, _ = u_ref.shape
    soft = soft_ref[...]
    for b in range(seqs):
        extend_back(ext_s, u_ref, halo_ref, b)

        def conv_chunk(n, _):
            at = pl.multiple_of(n * 64, 64)
            far = dist_ref[b, pl.ds(at, 64), :]
            total = taps_ref[0:1, :] * ext_s[pl.ds(at + BACK, 64), :]
            for k in range(1, CONV):
                window = taps_ref[k : k + 1, :] * ext_s[pl.ds(at + BACK - 8 * k, 64), :]
                total = total + jnp.where(far >= float(k), window, 0.0)
            low = total.astype(BF16)
            c_ref[b, pl.ds(at, 64), :] = low
            c_s[b, pl.ds(at, 64), :] = low.astype(F32)
            return 0

        lax.fori_loop(0, rows // 64, conv_chunk, 0)
        both = jnp.dot(c_ref[b], gates_ref[0], preferred_element_type=F32)
        rate_s[b] = both[:, :HS]
        inp_s[b] = both[:, HS:]

    def scan_step(j, carry):
        new = []
        for b in range(seqs):
            at = pl.ds(pl.multiple_of(j * 8, 8), 8)
            state, prod = carry[b]
            _, inp, decay, root = drive_values(rate_s[b, at, :], inp_s[b, at, :], soft)
            keep = jnp.where(dist_ref[b, at, :] >= 1.0, decay, 0.0)
            state = keep * state + root * inp * c_s[b, at, :]
            prod = keep * prod
            keep_ref[b, at, :] = keep
            state_ref[b, at, :] = state
            prod_ref[b, at, :] = prod
            new.append((state, prod))
        return tuple(new)

    zero, one = jnp.zeros((CHUNKS, HS), F32), jnp.ones((CHUNKS, HS), F32)
    ends = lax.fori_loop(0, rows // CHUNKS, scan_step, ((zero, one),) * seqs, unroll=8)
    for b in range(seqs):
        chunk_ref[b, 0] = ends[b][0]
        chunk_ref[b, 1] = ends[b][1]


def branch_kernel(core_ref, state_ref, prod_ref, carry_ref, gate_ref, out_ref, branch_ref, split_ref):
    del core_ref
    seqs, rows, _ = state_ref.shape
    for b in range(seqs):
        carry = jnp.concatenate([carry_ref[b]] * 4, axis=0)

        def point(n, _):
            at = pl.ds(pl.multiple_of(n * 32, 32), 32)
            state = state_ref[b, at, :] + prod_ref[b, at, :] * carry
            out_ref[b, at, :] = state
            low = (state * gelu_tanh(gate_ref[b, at, :])).astype(BF16)
            branch_ref[b, at, :] = low
            split_ref[0, b, at, :] = low
            return 0

        lax.fori_loop(0, rows // 32, point, 0, unroll=4)


def reverse_kernel(
    grad_ref, gate_ref, keep_ref, state_ref,
    dg_ref, local_ref, prod_ref, chunk_ref,
):
    seqs, rows, _ = grad_ref.shape
    pairs = rows // 16

    def scan_step(n, carry):
        first = pl.multiple_of((pairs - 1 - n) * 16, 16)
        at = pl.ds(first, 16)
        new = []
        for b in range(seqs):
            pull, prod = carry[b]
            act, slope = gelu_parts(gate_ref[b, at, :])
            grad = grad_ref[b, at, :]
            dg_ref[b, at, :] = (grad * state_ref[b, at, :] * slope).astype(BF16)
            dh = grad * act
            keep = keep_ref[b, at, :]
            late = dh[8:] + pull
            late_prod = prod
            pull, prod = keep[8:] * late, keep[8:] * prod
            early = dh[:8] + pull
            local_ref[b, at, :] = jnp.concatenate([early, late], axis=0)
            prod_ref[b, at, :] = jnp.concatenate([prod, late_prod], axis=0)
            new.append((keep[:8] * early, keep[:8] * prod))
        return tuple(new)

    zero, one = jnp.zeros((CHUNKS, HS), F32), jnp.ones((CHUNKS, HS), F32)
    ends = lax.fori_loop(0, pairs, scan_step, ((zero, one),) * seqs, unroll=4)
    for b in range(seqs):
        chunk_ref[b, 0] = ends[b][0]
        chunk_ref[b, 1] = ends[b][1]


def mixer_backward_kernel(
    local_ref, prod_ref, carry_ref, state_ref, before_ref, c_ref, u_ref, halo_ref, dist_ref,
    gates_ref, taps_ref, soft_ref,
    du_ref, tail_ref, edge_ref, ggate_ref, gtaps_ref, gdecay_ref,
    q_s, dq_s, dc_s, h_s, ext_s, dist_s,
):
    seqs, rows, _ = local_ref.shape
    soft = soft_ref[...]
    ggate = jnp.zeros((HS, 2 * HS), F32)
    decay_sum = jnp.zeros((8, HS), F32)
    taps_sum = [jnp.zeros((8, HS), F32) for _ in range(CONV)]

    def fold(value):
        return jnp.sum(value.reshape(value.shape[0] // 8, 8, HS), axis=0)

    for b in range(seqs):
        q_s[...] = jnp.dot(c_ref[b], gates_ref[0], preferred_element_type=F32)
        h_s[pl.ds(0, 8), :] = before_ref[b]
        h_s[pl.ds(8, rows), :] = state_ref[b]
        carry = jnp.concatenate([carry_ref[b]] * 4, axis=0)

        def point(n, total):
            first = pl.multiple_of(n * 32, 32)
            at = pl.ds(first, 32)
            lam = local_ref[b, at, :] + prod_ref[b, at, :] * carry
            rate, inp, decay, root = drive_values(q_s[at, :HS], q_s[at, HS:], soft)
            conv = c_ref[b, at, :].astype(F32)
            kept = jnp.where(dist_ref[b, at, :] >= 1.0, h_s[at, :], 0.0)
            lam_root = lam * root
            lam_inp = lam * inp
            grad_decay = lam * kept - lam_inp * conv * decay / root
            rated = grad_decay * decay * rate
            dq_s[at, :HS] = (-8.0 * soft * rated * (1.0 - rate)).astype(BF16)
            dq_s[at, HS:] = (lam_root * conv * inp * (1.0 - inp)).astype(BF16)
            dc_s[at, :] = lam_root * inp
            return total + fold(rated)

        decay_sum = lax.fori_loop(0, rows // 32, point, decay_sum, unroll=2)
        dc_s[pl.ds(0, rows), :] += lax.dot_general(
            dq_s[...], gates_ref[0], (((1,), (1,)), ((), ())), preferred_element_type=F32
        )
        ggate = ggate + lax.dot_general(
            c_ref[b], dq_s[...], (((0,), (0,)), ((), ())), preferred_element_type=F32
        )
        extend_back(ext_s, u_ref, halo_ref, b)
        dist_s[pl.ds(0, rows), :] = dist_ref[b]
        for m in range(CONV - 1):
            for held in (dc_s, dist_s):
                held[pl.ds(rows + 8 * m, 8), :] = shifted_group(held[pl.ds(8 * m, 8), :], -1, 0.0)

        def conv_chunk(n, totals):
            at = pl.multiple_of(n * 64, 64)
            grad = dc_s[pl.ds(at, 64), :]
            far = dist_s[pl.ds(at, 64), :]
            out = taps_ref[0:1, :] * grad
            totals = list(totals)
            totals[0] = totals[0] + fold(grad * ext_s[pl.ds(at + BACK, 64), :])
            for k in range(1, CONV):
                masked = jnp.where(far >= float(k), grad, 0.0)
                totals[k] = totals[k] + fold(masked * ext_s[pl.ds(at + BACK - 8 * k, 64), :])
                ahead = pl.ds(at + 8 * k, 64)
                value = taps_ref[k : k + 1, :] * dc_s[ahead, :]
                out = out + jnp.where(dist_s[ahead, :] >= float(k), value, 0.0)
            du_ref[b, pl.ds(at, 64), :] = out.astype(BF16)

            @pl.when(n == rows // 64 - 1)
            def _():
                tail_ref[b] = out[64 - TAIL :, :]

            return tuple(totals)

        taps_sum = list(lax.fori_loop(0, rows // 64, conv_chunk, tuple(taps_sum)))
        edges = [jnp.zeros((HALO - CONV + 1, HS), F32)]
        for m in range(CONV - 1, 0, -1):
            edge = jnp.zeros((1, HS), F32)
            for k in range(m, CONV):
                at = pl.ds(8 * (k - m), 1)
                masked = jnp.where(dist_s[at, :] >= float(k), dc_s[at, :], 0.0)
                edge = edge + taps_ref[k : k + 1, :] * masked
            edges.append(edge)
        edge_ref[b] = jnp.concatenate(edges, axis=0)
    ggate_ref[0] = ggate
    gdecay_ref[...] = jnp.broadcast_to(
        8.0 * jnp.sum(decay_sum, axis=0, keepdims=True), (8, HS)
    )
    gtaps_ref[...] = jnp.concatenate(
        [jnp.sum(t, axis=0, keepdims=True) for t in taps_sum] + [jnp.zeros((8 - CONV, HS), F32)],
        axis=0,
    )


def norm_kernel(shards, core_ref, x_ref, gain_ref, normed_ref, own_ref, far_ref, scale_ref):
    x = x_ref[...].astype(F32)
    scale = lax.rsqrt(jnp.mean(x * x, axis=-1, keepdims=True) + 1e-06)
    low = (x * scale * gain_ref[...]).astype(BF16)
    normed_ref[...] = low
    scale_ref[...] = jnp.broadcast_to(scale, scale_ref.shape)
    wide = low.astype(F32)
    size = D // shards
    even, odd = (
        jnp.concatenate([wide[:, n * size : (n + 1) * size] for n in range(c, shards, 2)], axis=1)
        for c in range(2)
    )
    first = core_ref[0] == 0
    own_ref[...] = jnp.where(first, even, odd).astype(BF16)
    far_ref[...] = jnp.where(first, odd, even).astype(BF16)


def ffn_forward_kernel(n_ref, gate_ref, up_ref, hidden_ref, pull_ref):
    for m in range(0, n_ref.shape[0], 256):
        at = pl.ds(m, 256)
        e1 = jnp.dot(n_ref[at, :], gate_ref[...], preferred_element_type=F32)
        e2 = jnp.dot(n_ref[at, :], up_ref[...], preferred_element_type=F32)
        act, slope = gelu_parts(e1)
        hidden_ref[at, :] = (act * e2).astype(BF16)
        pull_ref[0, at, :] = (slope * e2).astype(BF16)
        pull_ref[1, at, :] = act.astype(BF16)


def ffn_backward_kernel(grad_ref, down_ref, pull_ref, out_ref):
    for m in range(0, grad_ref.shape[0], 256):
        at = pl.ds(m, 256)
        dv = lax.dot_general(
            grad_ref[at, :], down_ref[...], (((1,), (1,)), ((), ())), preferred_element_type=F32
        )
        out_ref[0, at, :] = (dv * pull_ref[0, at, :].astype(F32)).astype(BF16)
        out_ref[1, at, :] = (dv * pull_ref[1, at, :].astype(F32)).astype(BF16)


def head_block(lead, rows):
    return pl.BlockSpec((lead, rows, HS), lambda h: (0, 0, h))


def shared_block(shape):
    return pl.BlockSpec(shape, lambda h: (0,) * len(shape))


def pair_block(seqs):
    return pl.BlockSpec((seqs, 2, CHUNKS, HS), lambda h: (0, 0, 0, h))


PARAMS = pltpu.CompilerParams(vmem_limit_bytes=40 * 1024 * 1024)


def mixer_forward(u, halo, dist, gates, taps, soft):
    seqs, rows, _ = u.shape
    full = head_block(seqs, rows)
    wide = jax.ShapeDtypeStruct((seqs, rows, LRU), F32)
    return pl.pallas_call(
        mixer_forward_kernel,
        grid=(HEADS,),
        in_specs=[
            full,
            head_block(seqs, HALO),
            shared_block((seqs, rows, HS)),
            pl.BlockSpec((1, HS, 2 * HS), lambda h: (h, 0, 0)),
            pl.BlockSpec((CONV, HS), lambda h: (0, h)),
            pl.BlockSpec((1, HS), lambda h: (0, h)),
        ],
        out_specs=[full, full, full, full, pair_block(seqs)],
        out_shape=[
            jax.ShapeDtypeStruct((seqs, rows, LRU), BF16),
            wide,
            wide,
            wide,
            jax.ShapeDtypeStruct((seqs, 2, CHUNKS, LRU), F32),
        ],
        scratch_shapes=[
            pltpu.VMEM((rows + BACK, HS), F32),
            pltpu.VMEM((seqs, rows, HS), F32),
            pltpu.VMEM((seqs, rows, HS), F32),
            pltpu.VMEM((seqs, rows, HS), F32),
        ],
        compiler_params=PARAMS,
        name="mixer_forward",
    )(u, halo, dist, gates, taps, soft)


def mixer_branch(state, prod, carry, gate, shards, core):
    seqs, rows, _ = state.shape
    per = HEADS // shards

    def at(h, core_ref):
        return (0, 0, h)

    def split_at(h, core_ref):
        shard = h // per
        return ((shard % 2 + core_ref[0]) % 2, 0, 0, (shard // 2) * per + h % per)

    full = pl.BlockSpec((seqs, rows, HS), at)
    return pl.pallas_call(
        branch_kernel,
        grid_spec=pltpu.PrefetchScalarGridSpec(
            num_scalar_prefetch=1,
            grid=(HEADS,),
            in_specs=[full, full, pl.BlockSpec((seqs, CHUNKS, HS), at), full],
            out_specs=[full, full, pl.BlockSpec((1, seqs, rows, HS), split_at)],
        ),
        out_shape=[
            jax.ShapeDtypeStruct((seqs, rows, LRU), F32),
            jax.ShapeDtypeStruct((seqs, rows, LRU), BF16),
            jax.ShapeDtypeStruct((2, seqs, rows, LRU // 2), BF16),
        ],
        compiler_params=PARAMS,
        name="mixer_branch",
    )(core.reshape(1), state, prod, carry, gate)


def mixer_reverse(grad, gate, keep, state):
    seqs, rows, _ = grad.shape
    full = head_block(seqs, rows)
    wide = jax.ShapeDtypeStruct((seqs, rows, LRU), F32)
    return pl.pallas_call(
        reverse_kernel,
        grid=(HEADS,),
        in_specs=[full, full, full, full],
        out_specs=[full, full, full, pair_block(seqs)],
        out_shape=[
            jax.ShapeDtypeStruct((seqs, rows, LRU), BF16),
            wide,
            wide,
            jax.ShapeDtypeStruct((seqs, 2, CHUNKS, LRU), F32),
        ],
        compiler_params=PARAMS,
        name="mixer_reverse",
    )(grad, gate, keep, state)


def mixer_backward(local, prod, carry, state, before, c, u, halo, dist, gates, taps, soft):
    seqs, rows, _ = local.shape
    full = head_block(seqs, rows)
    small = head_block(seqs, HALO)
    gate_block = pl.BlockSpec((1, HS, 2 * HS), lambda h: (h, 0, 0))
    row_block = pl.BlockSpec((8, HS), lambda h: (0, h))
    return pl.pallas_call(
        mixer_backward_kernel,
        grid=(HEADS,),
        in_specs=[
            full,
            full,
            head_block(seqs, CHUNKS),
            full,
            small,
            full,
            full,
            small,
            shared_block((seqs, rows, HS)),
            gate_block,
            pl.BlockSpec((CONV, HS), lambda h: (0, h)),
            pl.BlockSpec((1, HS), lambda h: (0, h)),
        ],
        out_specs=[full, head_block(seqs, TAIL), small, gate_block, row_block, row_block],
        out_shape=[
            jax.ShapeDtypeStruct((seqs, rows, LRU), BF16),
            jax.ShapeDtypeStruct((seqs, TAIL, LRU), F32),
            jax.ShapeDtypeStruct((seqs, HALO, LRU), F32),
            jax.ShapeDtypeStruct((HEADS, HS, 2 * HS), F32),
            jax.ShapeDtypeStruct((8, LRU), F32),
            jax.ShapeDtypeStruct((8, LRU), F32),
        ],
        scratch_shapes=[
            pltpu.VMEM((rows, 2 * HS), F32),
            pltpu.VMEM((rows, 2 * HS), BF16),
            pltpu.VMEM((rows + BACK, HS), F32),
            pltpu.VMEM((rows + 8, HS), F32),
            pltpu.VMEM((rows + BACK, HS), F32),
            pltpu.VMEM((rows + BACK, HS), F32),
        ],
        compiler_params=PARAMS,
        name="mixer_backward",
    )(local, prod, carry, state, before, c, u, halo, dist, gates, taps, soft)


def rms_norm(x, gain, shards, core):
    rows = x.shape[0]
    block = min(rows, 256)
    return pl.pallas_call(
        functools.partial(norm_kernel, shards),
        grid=(rows // block,),
        in_specs=[
            pl.BlockSpec(memory_space=pltpu.SMEM),
            pl.BlockSpec((block, D), lambda n: (n, 0)),
            pl.BlockSpec((1, D), lambda n: (0, 0)),
        ],
        out_specs=[
            pl.BlockSpec((block, D), lambda n: (n, 0)),
            pl.BlockSpec((block, D // 2), lambda n: (n, 0)),
            pl.BlockSpec((block, D // 2), lambda n: (n, 0)),
            pl.BlockSpec((block, 128), lambda n: (n, 0)),
        ],
        out_shape=[
            jax.ShapeDtypeStruct((rows, D), BF16),
            jax.ShapeDtypeStruct((rows, D // 2), BF16),
            jax.ShapeDtypeStruct((rows, D // 2), BF16),
            jax.ShapeDtypeStruct((rows, 128), F32),
        ],
        compiler_params=PARAMS,
        name="rms_norm",
    )(core.reshape(1), x, gain.reshape(1, D))


FF_TILE = 512
GATHER_TILE = 768
DOT_TILE = 512


def ffn_forward(normed, proj_up):
    rows = normed.shape[0]
    steps = FF // FF_TILE
    return pl.pallas_call(
        ffn_forward_kernel,
        grid=(steps,),
        in_specs=[
            pl.BlockSpec((rows, D), lambda n: (0, 0)),
            pl.BlockSpec((D, FF_TILE), lambda n: (0, n)),
            pl.BlockSpec((D, FF_TILE), lambda n: (0, n + steps)),
        ],
        out_specs=[
            pl.BlockSpec((rows, FF_TILE), lambda n: (0, n)),
            pl.BlockSpec((2, rows, FF_TILE), lambda n: (0, 0, n)),
        ],
        out_shape=[
            jax.ShapeDtypeStruct((rows, FF), BF16),
            jax.ShapeDtypeStruct((2, rows, FF), BF16),
        ],
        compiler_params=PARAMS,
        name="ffn_forward",
    )(normed, proj_up, proj_up)


def ffn_backward(grad, proj_down, pull):
    rows = grad.shape[0]
    return pl.pallas_call(
        ffn_backward_kernel,
        grid=(FF // FF_TILE,),
        in_specs=[
            pl.BlockSpec((rows, D), lambda n: (0, 0)),
            pl.BlockSpec((FF_TILE, D), lambda n: (n, 0)),
            pl.BlockSpec((2, rows, FF_TILE), lambda n: (0, 0, n)),
        ],
        out_specs=pl.BlockSpec((2, rows, FF_TILE), lambda n: (0, 0, n)),
        out_shape=jax.ShapeDtypeStruct((2, rows, FF), BF16),
        compiler_params=PARAMS,
        name="ffn_backward",
    )(grad, proj_down, pull)


def gather_rows(shard):
    parts = lax.axis_size("grp")
    rows = shard.shape[0] // parts
    own = lax.dynamic_slice_in_dim(shard, lax.axis_index("grp") * rows, rows, 0)
    return lax.all_gather(own, ("seq", "grp"), axis=0, tiled=True)


def tie(value, *after):
    return lax.optimization_barrier((value, *after))[0]


def xor_pairs(axis, bit):
    return [(i, i ^ bit) for i in range(lax.axis_size(axis))]


def ring_pairs(steps):
    count = lax.axis_size("seq")
    return [(i, (i + steps) % count) for i in range(count)]


def same_cores():
    count = lax.axis_size("seq")
    return [list(range(core, count, 2)) for core in range(2)]


def dot_rows(a, b):
    return lax.dot_general(a, b, (((0,), (0,)), ((), ())), preferred_element_type=F32)


def reduce_rows(partial):
    part = lax.psum_scatter(partial, "seq", scatter_dimension=0, tiled=True)
    part = lax.psum_scatter(part, "grp", scatter_dimension=0, tiled=True)
    return lax.all_gather(part, "grp", axis=0, tiled=True).astype(F32)


def dot_far(a, b):
    return lax.dot_general(a, b, (((1,), (1,)), ((), ())), preferred_element_type=F32)


def by_position(a):
    seqs, rows = a.shape[:2]
    return a.reshape(seqs, CHUNKS, rows // CHUNKS, *a.shape[2:]).swapaxes(1, 2).reshape(a.shape)


def by_token(a):
    seqs, rows = a.shape[:2]
    return a.reshape(seqs, rows // CHUNKS, CHUNKS, *a.shape[2:]).swapaxes(1, 2).reshape(a.shape)


def fetch_columns(where_ref, pieces, start, target, sem):
    own, far = pieces[:6], pieces[6:]
    rows, columns = own[0].shape
    width, tile = columns // 4, target.shape[1]
    depth, half = own[1].shape[0], own[4].shape[0]
    chips = depth // rows + 1
    chip, core, group = where_ref[0], where_ref[1], where_ref[2]
    quarter = start // width
    offset = pl.multiple_of(start - quarter * width, 128)
    start = pl.multiple_of(start, 128)
    relation = lax.bitwise_xor(group, quarter)

    def copy(source, row, count):
        place = target.at[pl.ds(pl.multiple_of(row, 16), count), :]
        pltpu.make_async_copy(source, place, sem).start()

    for c, (shard, *parts) in enumerate((own, far)):
        other = lax.rem(core + c, 2)
        copy(shard.at[:, pl.ds(start, tile)], (chip * 2 + other) * rows, rows)
        for j in range(1, chips):
            row = (lax.rem(chip + j, chips) * 2 + other) * rows
            first = (j - 1) * rows
            for k in range(3):

                @pl.when(relation == k)
                def _():
                    copy(parts[k].at[pl.ds(first, rows), pl.ds(offset, tile)], row, rows)

            @pl.when(relation == 3)
            def _():
                for m in range(2):
                    low, high = max(first, m * half), min(first + rows, (m + 1) * half)
                    if low < high:
                        at = pl.ds(low - m * half, high - low)
                        source = parts[3 + m].at[at, pl.ds(offset, tile)]
                        copy(source, row + (low - first), high - low)


def gathered_tiles(fetch, held, sems):
    step, steps = pl.program_id(0), pl.num_programs(0)
    slot = lax.rem(step, 2)

    @pl.when(step == 0)
    def _():
        fetch(step, slot)

    @pl.when(step + 1 < steps)
    def _():
        fetch(step + 1, 1 - slot)

    for side in range(held.shape[1]):
        whole = held.at[slot, side]
        pltpu.make_async_copy(whole, whole, sems.at[slot, side]).wait()
    return slot


def gathered_ffn_kernel(where_ref, n_ref, *refs):
    pieces, (hidden_ref, pull_ref, gate_ref, up_ref, held, sems) = refs[:12], refs[12:]
    tile = hidden_ref.shape[1]

    def fetch(n, slot):
        for side in range(2):
            start = n * tile + side * (pieces[0].shape[1] // 2)
            fetch_columns(where_ref, pieces, start, held.at[slot, side], sems.at[slot, side])

    slot = gathered_tiles(fetch, held, sems)
    gate_ref[...] = held[slot, 0]
    up_ref[...] = held[slot, 1]
    ffn_forward_kernel(n_ref, gate_ref, up_ref, hidden_ref, pull_ref)


def gathered_dot_kernel(base, where_ref, n_ref, *refs):
    pieces, (out_ref, weight_ref, held, sems) = refs[:12], refs[12:]
    tile = out_ref.shape[1]

    def fetch(n, slot):
        start = base + n * tile
        fetch_columns(where_ref, pieces, start, held.at[slot, 0], sems.at[slot, 0])

    slot = gathered_tiles(fetch, held, sems)
    weight_ref[...] = held[slot, 0]
    out_ref[...] = jnp.dot(n_ref[...], weight_ref[...], preferred_element_type=F32).astype(
        out_ref.dtype
    )


class Gather:
    def __init__(self, shard, *after, offload=False):
        self.shard = shard
        self.chips = lax.axis_size("seq") // 2
        half = (self.chips - 1) * shard.shape[0] // 2
        self.simple = lax.axis_size("grp") != 4 or half % 16 != 0
        if self.simple:
            self.whole = gather_rows(shard)
            return
        group = lax.axis_index("grp")
        width = shard.shape[1] // 4
        own = lax.dynamic_slice_in_dim(shard, group * width, width, 1)
        if after:
            own = tie(own, *after)
        if offload:
            self.slabs = lax.all_gather(own, "seq", axis_index_groups=same_cores())
        else:
            self.slabs = [
                lax.ppermute(own, "seq", ring_pairs(-2 * j)) for j in range(1, self.chips)
            ]
        self.half = half

    def first(self, *after):
        if self.simple:
            return ()
        slabs = tie(self.slabs, *after) if after else self.slabs
        if not isinstance(slabs, list):
            chip = lax.axis_index("seq") // 2
            slabs = [
                lax.dynamic_index_in_dim(slabs, (chip + j) % self.chips, 0, False)
                for j in range(1, self.chips)
            ]
        self.near = jnp.concatenate(slabs, axis=0)
        self.from_x = lax.ppermute(self.near, "grp", xor_pairs("grp", 1))
        self.from_y = lax.ppermute(self.near, "grp", xor_pairs("grp", 2))
        return (self.near,)

    def second(self, *after):
        if self.simple:
            return ()
        if after:
            self.from_x, self.from_y = tie((self.from_x, self.from_y), *after)
        self.halves = (self.from_y[: self.half], self.from_x[self.half :])
        return self.halves

    def third(self):
        if self.simple:
            return
        diag_a = lax.ppermute(self.halves[0], "grp", xor_pairs("grp", 1))
        diag_b = lax.ppermute(self.halves[1], "grp", xor_pairs("grp", 2))
        own = (self.shard, self.near, self.from_x, self.from_y, diag_a, diag_b)
        far = tuple(lax.ppermute(piece, "seq", xor_pairs("seq", 1)) for piece in own)
        place = lax.axis_index("seq")
        where = jnp.stack([place // 2, place % 2, lax.axis_index("grp")]).astype(jnp.int32)
        self.pieces = (where, own, far)

    def call(self, kernel, normed, steps, tile, weights, out_specs, out_shape, name):
        where, own, far = self.pieces
        rows, depth = normed.shape
        return pl.pallas_call(
            kernel,
            grid=(steps,),
            in_specs=[
                pl.BlockSpec(memory_space=pltpu.SMEM),
                pl.BlockSpec((rows, depth), lambda n: (0, 0)),
            ]
            + [pl.BlockSpec(memory_space=pl.ANY)] * 12,
            out_specs=out_specs + [pl.BlockSpec((depth, tile), lambda n: (0, n))] * weights,
            out_shape=out_shape + [jax.ShapeDtypeStruct((depth, steps * tile), BF16)] * weights,
            scratch_shapes=[
                pltpu.VMEM((2, weights, depth, tile), BF16),
                pltpu.SemaphoreType.DMA((2, weights)),
            ],
            compiler_params=pltpu.CompilerParams(vmem_limit_bytes=56 * 1024 * 1024),
            name=name,
        )(where, normed, *own, *far)

    def dot(self, normed, half, dtype):
        columns = self.shard.shape[1] // 2
        base = half * columns
        if self.simple:
            weight = self.whole[:, base : base + columns]
            return jnp.dot(normed, weight, preferred_element_type=F32).astype(dtype), weight
        rows, tile = normed.shape[0], DOT_TILE
        return self.call(
            functools.partial(gathered_dot_kernel, base),
            normed,
            columns // tile,
            tile,
            1,
            [pl.BlockSpec((rows, tile), lambda n: (0, n))],
            [jax.ShapeDtypeStruct((rows, columns), dtype)],
            "gathered_dot",
        )

    def ffn_forward(self, normed):
        if self.simple:
            hidden, pull = ffn_forward(normed, self.whole)
            return hidden, pull, self.whole[:, :FF], self.whole[:, FF:]
        rows, tile = normed.shape[0], GATHER_TILE
        return self.call(
            gathered_ffn_kernel,
            normed,
            FF // tile,
            tile,
            2,
            [
                pl.BlockSpec((rows, tile), lambda n: (0, n)),
                pl.BlockSpec((2, rows, tile), lambda n: (0, 0, n)),
            ],
            [
                jax.ShapeDtypeStruct((rows, FF), BF16),
                jax.ShapeDtypeStruct((2, rows, FF), BF16),
            ],
            "gathered_ffn",
        )


class Reduction:
    def __init__(self, a_own, a_far, columns, width, fused=False):
        self.simple = lax.axis_size("grp") != 4
        count = lax.axis_size("seq")
        place = lax.axis_index("seq")
        self.chips = count // 2
        self.chip, core = place // 2, place % 2
        self.width = width
        full = a_own.shape[1]
        self.rows = full // self.chips
        self.half = full // 2
        self.a_own = a_own
        if self.simple:
            parts = [columns(k) for k in range(4)]
            own, far = (
                jnp.concatenate([dot_rows(a, part) for part in parts], axis=1)
                for a in (a_own, a_far)
            )
            cores = jnp.stack(
                [jnp.where(core == c, own, far).reshape(self.chips, self.rows, -1) for c in (0, 1)],
                axis=1,
            )
            self.product = cores.reshape(2 * full, 4 * width).astype(BF16)
            self.arrived = self.product
            self.sent = (self.product,)
            return
        group = lax.axis_index("grp")
        self.x, self.y = xor_pairs("grp", 1), xor_pairs("grp", 2)
        self.b = [columns(group ^ k) for k in range(4)]
        self.far = [None] * 4
        self.product = None
        other = xor_pairs("seq", 1)
        if fused:
            b_all = jnp.concatenate(self.b, axis=1)
            far = lax.ppermute(dot_rows(a_far, b_all).astype(BF16), "seq", other)
            self.product = (dot_rows(a_own, b_all) + far.astype(F32)).astype(BF16)
        for k in () if fused else (3, 1, 2, 0):
            product = dot_rows(a_far, self.b[k]).astype(BF16)
            self.far[k] = lax.ppermute(product, "seq", other)
        half = self.half
        self.sent = (
            self.own(3, 0, half).astype(BF16),
            self.own(3, half, full).astype(BF16),
        )
        self.diag_a = lax.ppermute(self.sent[0], "grp", self.x)
        self.diag_b = lax.ppermute(self.sent[1], "grp", self.y)

    def own(self, k, first, last):
        if self.product is not None:
            left = k * self.width
            return self.product[first:last, left : left + self.width].astype(F32)
        product = dot_rows(self.a_own[:, first:last], self.b[k])
        return product + self.far[k][first:last].astype(F32)

    def second(self, *after):
        if self.simple:
            return ()
        full, none = 2 * self.half, ((0, self.half), (0, 0))
        diag_a, diag_b = self.diag_a, self.diag_b
        if after:
            diag_a, diag_b = tie((diag_a, diag_b), *after)
        sent = (
            (self.own(1, 0, full) + jnp.pad(diag_b.astype(F32), (none[0][::-1], (0, 0)))).astype(BF16),
            (self.own(2, 0, full) + jnp.pad(diag_a.astype(F32), none)).astype(BF16),
        )
        self.from_x = lax.ppermute(sent[0], "grp", self.x)
        self.from_y = lax.ppermute(sent[1], "grp", self.y)
        return sent

    def mine(self, *after):
        from_x, from_y = self.from_x, self.from_y
        if after:
            from_x, from_y = tie((from_x, from_y), *after)
        mine = self.own(0, 0, 2 * self.half) + from_x.astype(F32) + from_y.astype(F32)
        return mine.astype(BF16)

    def along_z(self, mine):
        mine = mine.reshape(self.chips, self.rows, -1)
        self.kept = lax.dynamic_index_in_dim(mine, self.chip, 0, False)
        sent = tuple(
            lax.dynamic_index_in_dim(mine, (self.chip + j) % self.chips, 0, False)
            for j in range(1, self.chips)
        )
        self.arrived = [
            lax.ppermute(part, "seq", ring_pairs(2 * j + 2)) for j, part in enumerate(sent)
        ]
        return sent

    def third(self, *after, offload=False):
        if self.simple:
            return ()
        mine = self.mine(*after)
        if not offload:
            return self.along_z(mine)
        self.kept = None
        self.arrived = lax.psum_scatter(
            mine, "seq", scatter_dimension=0, axis_index_groups=same_cores(), tiled=True
        )
        return (mine,)

    def total(self):
        if self.kept is None:
            return self.arrived
        total = self.kept.astype(F32)
        for part in self.arrived:
            total = total + part.astype(F32)
        return total

    def finish(self, *after):
        if self.simple:
            return reduce_rows(self.product)
        total = self.total()
        if after:
            total = tie(total, *after)
        parts = lax.all_gather(total.astype(BF16), "grp")
        return parts.transpose(1, 0, 2).reshape(self.rows, 4 * self.width).astype(F32)


def shard_carry(ends, prods, reverse):
    count = lax.axis_size("seq")
    place = lax.axis_index("seq")
    both = lax.all_gather(jnp.stack([ends, prods]), "seq")
    carry = jnp.zeros_like(ends)
    for step in range(count - 1):
        source = count - 1 - step if reverse else step
        ahead = source > place if reverse else source < place
        carry = jnp.where(ahead, both[source, 0] + both[source, 1] * carry, carry)
    return carry


def chunk_ends(chunks, reverse):
    state = jnp.zeros_like(chunks[:, 0, 0])
    prod = jnp.ones_like(state)
    order = range(CHUNKS - 1, -1, -1) if reverse else range(CHUNKS)
    for n in order:
        state = chunks[:, 0, n] + chunks[:, 1, n] * state
        prod = chunks[:, 1, n] * prod
    return state, prod


def chunk_carries(chunks, carry, reverse):
    order = range(CHUNKS - 1, -1, -1) if reverse else range(CHUNKS)
    found = [None] * CHUNKS
    for n in order:
        found[n] = carry
        carry = chunks[:, 0, n] + chunks[:, 1, n] * carry
    return jnp.stack(found, axis=1)


def norm_back(values, scale, gain, grad_normed):
    weighted = grad_normed * gain
    cubed = scale * scale * scale
    return scale * weighted - values * cubed * jnp.mean(weighted * values, axis=-1, keepdims=True)


def gain_grad(weight, grad_weight, gain):
    return jnp.sum(weight.astype(F32) * grad_weight, axis=1) / gain.astype(F32)


def body(
    tokens, seg_ids, cotangent, first_gain, in_proj, conv_taps, decay_param, gate_heads,
    out_proj, second_gain, up_proj, down_proj,
):
    seq_count, shard_len, _ = tokens.shape
    row_count = seq_count * shard_len
    edge_len = CONV - 1
    place = lax.axis_index("seq")
    last = lax.axis_size("seq") - 1

    small = jnp.concatenate(
        [first_gain, second_gain, decay_param, conv_taps.reshape(-1)]
    )
    small_all = lax.all_gather(small, "seq")
    n_gain, n_lru = first_gain.shape[0], decay_param.shape[0]
    gain_one = small_all[:, :n_gain].reshape(D).astype(F32)
    gain_two = small_all[:, n_gain : 2 * n_gain].reshape(D).astype(F32)
    decay_float = small_all[:, 2 * n_gain : 2 * n_gain + n_lru].reshape(LRU).astype(F32)
    taps_all = (
        small_all[:, 2 * n_gain + n_lru :].reshape(-1, CONV, n_lru).transpose(1, 0, 2)
    ).reshape(CONV, LRU).astype(F32)
    in_gather = Gather(in_proj)
    near = in_gather.first()
    in_gather.second()
    in_gather.third()
    gates_all = lax.all_gather(gate_heads, "seq", axis=0, tiled=True)
    up_gather = Gather(up_proj, gates_all, *near, offload=True)
    proj_out = gather_rows(out_proj)
    proj_down = gather_rows(down_proj)

    tokens = by_position(tokens)
    cotangent = by_position(cotangent)
    inputs = tokens.reshape(row_count, D).astype(F32)
    first_normed, first_own, first_far, first_scale = rms_norm(
        tokens.reshape(row_count, D), gain_one, last + 1, place % 2
    )
    first_scale = first_scale[:, :1]
    wide = (seq_count, shard_len, LRU)
    inner_low, in_value = in_gather.dot(first_normed, 0, BF16)
    inner_low = inner_low.reshape(wide)

    step = shard_len // CHUNKS
    final = inner_low.reshape(seq_count, step, CHUNKS, LRU)[:, step - HALO :, CHUNKS - 1]
    prev_inner = from_behind(final, "seq", 1)
    prev_ids = from_behind(seg_ids[:, shard_len - edge_len :], "seq", 1)
    prev_ids = jnp.where(place == 0, -1, prev_ids)
    ext_ids = jnp.concatenate([prev_ids, seg_ids], axis=1)
    dist = jnp.zeros((seq_count, shard_len), F32)
    for k in range(1, CONV):
        dist = dist + (ext_ids[:, edge_len - k : edge_len - k + shard_len] == seg_ids).astype(F32)
    dist = jnp.broadcast_to(by_position(dist)[:, :, None], (seq_count, shard_len, HS))
    soft = jax.nn.softplus(-decay_float).reshape(1, LRU)

    conv_low, keep, state_part, prod_part, chunks = mixer_forward(
        tie(inner_low, *up_gather.first(inner_low)), prev_inner, dist, gates_all, taps_all, soft
    )
    end_state, end_prod = chunk_ends(chunks, False)
    gate_pre, in_gate = in_gather.dot(first_normed, 1, F32)
    gate_pre = gate_pre.reshape(wide)
    carry_in = shard_carry(end_state, end_prod, False)
    carries = chunk_carries(chunks, carry_in, False)
    state, branch, branch_split = mixer_branch(
        tie(state_part, *up_gather.second(carries)), prod_part, carries, gate_pre, last + 1, place % 2
    )
    branch_split = branch_split.reshape(2, row_count, LRU // 2)
    resid = inputs + jnp.dot(
        branch.reshape(row_count, LRU), proj_out, preferred_element_type=F32
    )
    second_normed, second_own, second_far, second_scale = rms_norm(
        resid, gain_two, last + 1, place % 2
    )
    second_scale = second_scale[:, :1]
    up_gather.third()
    hidden, pull, proj_gate, proj_up = up_gather.ffn_forward(second_normed)

    grad_out = cotangent.reshape(row_count, D)
    grad_down = dot_rows(hidden, grad_out).astype(BF16)
    down_part = lax.psum_scatter(grad_down, ("seq", "grp"), scatter_dimension=0, tiled=True)
    grad_expanded = ffn_backward(tie(grad_out, grad_down), proj_down, pull)
    quarter = FF // 2

    def up_columns(n):
        part = lax.dynamic_slice(
            grad_expanded, (n // 2, 0, (n % 2) * quarter), (1, row_count, quarter)
        )
        return part[0]

    up_sum = Reduction(second_own, second_far, up_columns, quarter)
    grad_expanded = tie(grad_expanded, *up_sum.sent)
    grad_second_normed = dot_far(grad_expanded[0], proj_gate) + dot_far(
        grad_expanded[1], proj_up
    )
    sent = up_sum.second(grad_second_normed)
    grad_second_normed = tie(grad_second_normed, *sent)
    grad_resid = grad_out.astype(F32) + norm_back(
        resid, second_scale, gain_two, grad_second_normed
    )
    grad_mixer = grad_resid.astype(BF16)
    grad_branch = dot_far(grad_mixer, proj_out)

    grad_gate, local, rev_prod, rev_chunks = mixer_reverse(
        grad_branch.reshape(wide), gate_pre, keep, state
    )
    down_sum = lax.all_gather(tie(down_part, rev_chunks), "grp", axis=0, tiled=True)
    head_pull, head_prod = chunk_ends(rev_chunks, True)
    grad_gate = grad_gate.reshape(row_count, LRU)
    width = LRU // 4
    rev_carry = shard_carry(head_pull, head_prod, True)
    rev_carries = chunk_carries(rev_chunks, rev_carry, True)
    grad_mixer, grad_gate = tie((grad_mixer, grad_gate), rev_carry)
    out_sum = Reduction(
        branch_split[0],
        branch_split[1],
        lambda n: lax.dynamic_slice_in_dim(grad_mixer, n * (D // 4), D // 4, 1),
        D // 4,
        True,
    )
    in_gate_sum = Reduction(
        first_own,
        first_far,
        lambda n: lax.dynamic_slice_in_dim(grad_gate, n * width, width, 1),
        width,
        True,
    )
    sent = (*out_sum.sent, *in_gate_sum.sent)
    sent = up_sum.third(down_sum, *sent, offload=True)
    local = tie(local, *sent)
    du, tail, edge, grad_gates, grad_taps, grad_decay = mixer_backward(
        local, rev_prod, rev_carries, state, carries, conv_low, inner_low,
        prev_inner, dist, gates_all, taps_all, soft,
    )
    returned = from_behind(edge[:, HALO - edge_len :].astype(BF16), "seq", -1).astype(F32)
    grad_gate = tie(grad_gate, *out_sum.second(edge), *in_gate_sum.second(edge))
    first_grad = dot_far(grad_gate, in_gate)
    groups = TAIL // CHUNKS
    padded = jnp.pad(
        returned[:, :, None, :], ((0, 0), (groups - edge_len, 0), (CHUNKS - 1, 0), (0, 0))
    ).reshape(seq_count, TAIL, LRU)
    grad_inner = lax.dynamic_update_slice(
        du, (tail + padded).astype(BF16), (0, shard_len - TAIL, 0)
    )
    grad_inner = tie(grad_inner, first_grad).reshape(row_count, LRU)
    in_value_sum = Reduction(
        first_own,
        first_far,
        lambda n: lax.dynamic_slice_in_dim(grad_inner, n * width, width, 1),
        width,
        True,
    )
    grad_inner = tie(grad_inner, *in_value_sum.sent)

    shards = last + 1
    grad_decay_row = grad_decay[0] * jax.nn.sigmoid(-decay_float)
    flat = jnp.concatenate(
        [
            grad_gates.reshape(shards, -1, HS),
            grad_taps[:CONV].reshape(CONV, shards, -1, HS).swapaxes(0, 1).reshape(shards, -1, HS),
            grad_decay_row.reshape(shards, -1, HS),
        ],
        axis=1,
    )
    lines = flat.shape[1]
    flat = jnp.pad(flat, ((0, 0), (0, -lines % 16), (0, 0))).astype(BF16).reshape(-1, HS)
    flat = lax.psum_scatter(flat, "seq", scatter_dimension=0, tiled=True)
    first_grad = first_grad + dot_far(grad_inner, in_value)
    sent = in_value_sum.second(first_grad)
    out_sum.third(*sent)
    flat = lax.all_gather(tie(flat, *sent), "grp").astype(F32)
    flat = jnp.sum(flat, axis=0)[:lines].reshape(-1)
    n_gates = flat.shape[0] - (CONV + 1) * n_lru
    gates_total = flat[:n_gates].reshape(gate_heads.shape)
    taps_total = flat[n_gates : n_gates + CONV * n_lru].reshape(CONV, n_lru)
    decay_total = flat[n_gates + CONV * n_lru :]

    up_total = up_sum.finish(edge)
    down_total = down_sum.astype(F32)
    if in_value_sum.simple:
        in_total = jnp.concatenate([in_value_sum.finish(), in_gate_sum.finish()], axis=1)
        last_sent = ()
    else:
        both = jnp.concatenate([in_value_sum.mine(), in_gate_sum.mine()], axis=1)
        last_sent = in_value_sum.along_z(both)
        both = in_value_sum.total().astype(BF16)
        in_total = jnp.concatenate(
            [
                lax.all_gather(both[:, n * width : (n + 1) * width], "grp")
                .transpose(1, 0, 2)
                .reshape(-1, LRU)
                for n in range(2)
            ],
            axis=1,
        ).astype(F32)
    out_total = out_sum.finish(*last_sent)
    ffn_out = jnp.dot(tie(hidden, *sent), proj_down, preferred_element_type=F32)
    block_out = by_token((resid + ffn_out).astype(BF16).reshape(tokens.shape))
    grad_tokens = grad_resid + norm_back(inputs, first_scale, gain_one, first_grad)
    grad_tokens = by_token(grad_tokens.astype(BF16).reshape(tokens.shape))
    first_total = gain_grad(in_proj, in_total, first_gain)
    second_total = gain_grad(up_proj, up_total, second_gain)
    return (
        block_out, grad_tokens, first_total, in_total, taps_total, decay_total, gates_total,
        out_total, second_total, up_total, down_total,
    )


def solution(mesh):
    in_specs = (
        P("grp", "seq", None),
        P("grp", "seq"),
        P("grp", "seq", None),
        P("seq"),
        P("seq", None),
        P(None, "seq"),
        P("seq"),
        P("seq", None, None),
        P("seq", None),
        P("seq"),
        P("seq", None),
        P("seq", None),
    )
    out_specs = (
        P("grp", "seq", None),
        P("grp", "seq", None),
        P("seq"),
        P("seq", None),
        P(None, "seq"),
        P("seq"),
        P("seq", None, None),
        P("seq", None),
        P("seq"),
        P("seq", None),
        P("seq", None),
    )
    return jax.shard_map(body, mesh=mesh, in_specs=in_specs, out_specs=out_specs, check_vma=False)
```

```python
import functools

import jax
import jax.numpy as jnp
from jax import lax
from jax.experimental import pallas as pl
from jax.experimental.pallas import tpu as pltpu
from jax.sharding import PartitionSpec as P

D = 1536
HEADS = 16
HS = 128
LRU = 2048
FF = 4608
CONV = 4
CHUNKS = 8
HALO = 8
BACK = 8 * (CONV - 1)
TAIL = 32
F32 = jnp.float32
BF16 = jnp.bfloat16


def from_behind(value, axis, steps):
    count = lax.axis_size(axis)
    first, last = (max(0, -steps), min(count, count - steps))
    return lax.ppermute(value, axis, [(source, source + steps) for source in range(first, last)])


def gelu_parts(v):
    k = 0.7978845608028654
    square = v * v
    t = jnp.tanh(k * v * (1.0 + 0.044715 * square))
    half = 0.5 * (1.0 + t)
    slope = half + 0.5 * v * (1.0 - t * t) * (k * (1.0 + 3.0 * 0.044715 * square))
    return v * half, slope


def gelu_tanh(v):
    k = 0.7978845608028654
    return 0.5 * v * (1.0 + jnp.tanh(k * v * (1.0 + 0.044715 * v * v)))


def sigmoid(v):
    return 0.5 * jnp.tanh(0.5 * v) + 0.5


def drive_values(q_rate, q_input, soft):
    rate = sigmoid(q_rate)
    inp = sigmoid(q_input)
    decay = jnp.exp(-8.0 * rate * soft)
    root = jnp.sqrt(1.0 - decay * decay + 0.001)
    return rate, inp, decay, root


def shifted_group(group, step, fill):
    row = lax.broadcasted_iota(jnp.int32, group.shape, 0)
    edge = 0 if step == 1 else CHUNKS - 1
    moved = pltpu.roll(group, step % CHUNKS, 0)
    return jnp.where(row == edge, fill, moved)


def extend_back(ext_s, u_ref, halo_ref, b):
    rows = u_ref.shape[1]
    ext_s[pl.ds(BACK, rows), :] = u_ref[b].astype(F32)
    halo = halo_ref[b].astype(F32)
    for m in range(CONV - 1):
        group = ext_s[pl.ds(BACK + rows - BACK + 8 * m, 8), :]
        fill = halo[HALO - CONV + 1 + m : HALO - CONV + 2 + m, :]
        ext_s[pl.ds(8 * m, 8), :] = shifted_group(group, 1, fill)


def mixer_forward_kernel(
    u_ref, halo_ref, dist_ref, gates_ref, taps_ref, soft_ref,
    c_ref, keep_ref, state_ref, prod_ref, chunk_ref,
    ext_s, c_s, rate_s, inp_s,
):
    seqs, rows, _ = u_ref.shape
    soft = soft_ref[...]
    for b in range(seqs):
        extend_back(ext_s, u_ref, halo_ref, b)

        def conv_chunk(n, _):
            at = pl.multiple_of(n * 64, 64)
            far = dist_ref[b, pl.ds(at, 64), :]
            total = taps_ref[0:1, :] * ext_s[pl.ds(at + BACK, 64), :]
            for k in range(1, CONV):
                window = taps_ref[k : k + 1, :] * ext_s[pl.ds(at + BACK - 8 * k, 64), :]
                total = total + jnp.where(far >= float(k), window, 0.0)
            low = total.astype(BF16)
            c_ref[b, pl.ds(at, 64), :] = low
            c_s[b, pl.ds(at, 64), :] = low.astype(F32)
            return 0

        lax.fori_loop(0, rows // 64, conv_chunk, 0)
        both = jnp.dot(c_ref[b], gates_ref[0], preferred_element_type=F32)
        rate_s[b] = both[:, :HS]
        inp_s[b] = both[:, HS:]

    def scan_step(j, carry):
        new = []
        for b in range(seqs):
            at = pl.ds(pl.multiple_of(j * 8, 8), 8)
            state, prod = carry[b]
            _, inp, decay, root = drive_values(rate_s[b, at, :], inp_s[b, at, :], soft)
            keep = jnp.where(dist_ref[b, at, :] >= 1.0, decay, 0.0)
            state = keep * state + root * inp * c_s[b, at, :]
            prod = keep * prod
            keep_ref[b, at, :] = keep
            state_ref[b, at, :] = state
            prod_ref[b, at, :] = prod
            new.append((state, prod))
        return tuple(new)

    zero, one = jnp.zeros((CHUNKS, HS), F32), jnp.ones((CHUNKS, HS), F32)
    ends = lax.fori_loop(0, rows // CHUNKS, scan_step, ((zero, one),) * seqs, unroll=8)
    for b in range(seqs):
        chunk_ref[b, 0] = ends[b][0]
        chunk_ref[b, 1] = ends[b][1]


def branch_kernel(core_ref, state_ref, prod_ref, carry_ref, gate_ref, out_ref, branch_ref, split_ref):
    del core_ref
    seqs, rows, _ = state_ref.shape
    for b in range(seqs):
        carry = jnp.concatenate([carry_ref[b]] * 4, axis=0)

        def point(n, _):
            at = pl.ds(pl.multiple_of(n * 32, 32), 32)
            state = state_ref[b, at, :] + prod_ref[b, at, :] * carry
            out_ref[b, at, :] = state
            low = (state * gelu_tanh(gate_ref[b, at, :])).astype(BF16)
            branch_ref[b, at, :] = low
            split_ref[0, b, at, :] = low
            return 0

        lax.fori_loop(0, rows // 32, point, 0, unroll=4)


def reverse_kernel(
    grad_ref, gate_ref, keep_ref, state_ref,
    dg_ref, local_ref, prod_ref, chunk_ref,
):
    seqs, rows, _ = grad_ref.shape
    pairs = rows // 16

    def scan_step(n, carry):
        first = pl.multiple_of((pairs - 1 - n) * 16, 16)
        at = pl.ds(first, 16)
        new = []
        for b in range(seqs):
            pull, prod = carry[b]
            act, slope = gelu_parts(gate_ref[b, at, :])
            grad = grad_ref[b, at, :]
            dg_ref[b, at, :] = (grad * state_ref[b, at, :] * slope).astype(BF16)
            dh = grad * act
            keep = keep_ref[b, at, :]
            late = dh[8:] + pull
            late_prod = prod
            pull, prod = keep[8:] * late, keep[8:] * prod
            early = dh[:8] + pull
            local_ref[b, at, :] = jnp.concatenate([early, late], axis=0)
            prod_ref[b, at, :] = jnp.concatenate([prod, late_prod], axis=0)
            new.append((keep[:8] * early, keep[:8] * prod))
        return tuple(new)

    zero, one = jnp.zeros((CHUNKS, HS), F32), jnp.ones((CHUNKS, HS), F32)
    ends = lax.fori_loop(0, pairs, scan_step, ((zero, one),) * seqs, unroll=4)
    for b in range(seqs):
        chunk_ref[b, 0] = ends[b][0]
        chunk_ref[b, 1] = ends[b][1]


def mixer_backward_kernel(
    local_ref, prod_ref, carry_ref, state_ref, before_ref, c_ref, u_ref, halo_ref, dist_ref,
    gates_ref, taps_ref, soft_ref,
    du_ref, tail_ref, edge_ref, ggate_ref, gtaps_ref, gdecay_ref,
    q_s, dq_s, dc_s, h_s, ext_s, dist_s,
):
    seqs, rows, _ = local_ref.shape
    soft = soft_ref[...]
    ggate = jnp.zeros((HS, 2 * HS), F32)
    decay_sum = jnp.zeros((8, HS), F32)
    taps_sum = [jnp.zeros((8, HS), F32) for _ in range(CONV)]

    def fold(value):
        return jnp.sum(value.reshape(value.shape[0] // 8, 8, HS), axis=0)

    for b in range(seqs):
        q_s[...] = jnp.dot(c_ref[b], gates_ref[0], preferred_element_type=F32)
        h_s[pl.ds(0, 8), :] = before_ref[b]
        h_s[pl.ds(8, rows), :] = state_ref[b]
        carry = jnp.concatenate([carry_ref[b]] * 4, axis=0)

        def point(n, total):
            first = pl.multiple_of(n * 32, 32)
            at = pl.ds(first, 32)
            lam = local_ref[b, at, :] + prod_ref[b, at, :] * carry
            rate, inp, decay, root = drive_values(q_s[at, :HS], q_s[at, HS:], soft)
            conv = c_ref[b, at, :].astype(F32)
            kept = jnp.where(dist_ref[b, at, :] >= 1.0, h_s[at, :], 0.0)
            lam_root = lam * root
            lam_inp = lam * inp
            grad_decay = lam * kept - lam_inp * conv * decay / root
            rated = grad_decay * decay * rate
            dq_s[at, :HS] = (-8.0 * soft * rated * (1.0 - rate)).astype(BF16)
            dq_s[at, HS:] = (lam_root * conv * inp * (1.0 - inp)).astype(BF16)
            dc_s[at, :] = lam_root * inp
            return total + fold(rated)

        decay_sum = lax.fori_loop(0, rows // 32, point, decay_sum, unroll=2)
        dc_s[pl.ds(0, rows), :] += lax.dot_general(
            dq_s[...], gates_ref[0], (((1,), (1,)), ((), ())), preferred_element_type=F32
        )
        ggate = ggate + lax.dot_general(
            c_ref[b], dq_s[...], (((0,), (0,)), ((), ())), preferred_element_type=F32
        )
        extend_back(ext_s, u_ref, halo_ref, b)
        dist_s[pl.ds(0, rows), :] = dist_ref[b]
        for m in range(CONV - 1):
            for held in (dc_s, dist_s):
                held[pl.ds(rows + 8 * m, 8), :] = shifted_group(held[pl.ds(8 * m, 8), :], -1, 0.0)

        def conv_chunk(n, totals):
            at = pl.multiple_of(n * 64, 64)
            grad = dc_s[pl.ds(at, 64), :]
            far = dist_s[pl.ds(at, 64), :]
            out = taps_ref[0:1, :] * grad
            totals = list(totals)
            totals[0] = totals[0] + fold(grad * ext_s[pl.ds(at + BACK, 64), :])
            for k in range(1, CONV):
                masked = jnp.where(far >= float(k), grad, 0.0)
                totals[k] = totals[k] + fold(masked * ext_s[pl.ds(at + BACK - 8 * k, 64), :])
                ahead = pl.ds(at + 8 * k, 64)
                value = taps_ref[k : k + 1, :] * dc_s[ahead, :]
                out = out + jnp.where(dist_s[ahead, :] >= float(k), value, 0.0)
            du_ref[b, pl.ds(at, 64), :] = out.astype(BF16)

            @pl.when(n == rows // 64 - 1)
            def _():
                tail_ref[b] = out[64 - TAIL :, :]

            return tuple(totals)

        taps_sum = list(lax.fori_loop(0, rows // 64, conv_chunk, tuple(taps_sum)))
        edges = [jnp.zeros((HALO - CONV + 1, HS), F32)]
        for m in range(CONV - 1, 0, -1):
            edge = jnp.zeros((1, HS), F32)
            for k in range(m, CONV):
                at = pl.ds(8 * (k - m), 1)
                masked = jnp.where(dist_s[at, :] >= float(k), dc_s[at, :], 0.0)
                edge = edge + taps_ref[k : k + 1, :] * masked
            edges.append(edge)
        edge_ref[b] = jnp.concatenate(edges, axis=0)
    ggate_ref[0] = ggate
    gdecay_ref[...] = jnp.broadcast_to(
        8.0 * jnp.sum(decay_sum, axis=0, keepdims=True), (8, HS)
    )
    gtaps_ref[...] = jnp.concatenate(
        [jnp.sum(t, axis=0, keepdims=True) for t in taps_sum] + [jnp.zeros((8 - CONV, HS), F32)],
        axis=0,
    )


def norm_kernel(shards, core_ref, x_ref, gain_ref, normed_ref, own_ref, far_ref, scale_ref):
    x = x_ref[...].astype(F32)
    scale = lax.rsqrt(jnp.mean(x * x, axis=-1, keepdims=True) + 1e-06)
    low = (x * scale * gain_ref[...]).astype(BF16)
    normed_ref[...] = low
    scale_ref[...] = jnp.broadcast_to(scale, scale_ref.shape)
    wide = low.astype(F32)
    size = D // shards
    even, odd = (
        jnp.concatenate([wide[:, n * size : (n + 1) * size] for n in range(c, shards, 2)], axis=1)
        for c in range(2)
    )
    first = core_ref[0] == 0
    own_ref[...] = jnp.where(first, even, odd).astype(BF16)
    far_ref[...] = jnp.where(first, odd, even).astype(BF16)


def ffn_forward_kernel(n_ref, gate_ref, up_ref, hidden_ref, pull_ref):
    for m in range(0, n_ref.shape[0], 256):
        at = pl.ds(m, 256)
        e1 = jnp.dot(n_ref[at, :], gate_ref[...], preferred_element_type=F32)
        e2 = jnp.dot(n_ref[at, :], up_ref[...], preferred_element_type=F32)
        act, slope = gelu_parts(e1)
        hidden_ref[at, :] = (act * e2).astype(BF16)
        pull_ref[0, at, :] = (slope * e2).astype(BF16)
        pull_ref[1, at, :] = act.astype(BF16)


def ffn_backward_kernel(grad_ref, down_ref, pull_ref, out_ref):
    for m in range(0, grad_ref.shape[0], 256):
        at = pl.ds(m, 256)
        dv = lax.dot_general(
            grad_ref[at, :], down_ref[...], (((1,), (1,)), ((), ())), preferred_element_type=F32
        )
        out_ref[0, at, :] = (dv * pull_ref[0, at, :].astype(F32)).astype(BF16)
        out_ref[1, at, :] = (dv * pull_ref[1, at, :].astype(F32)).astype(BF16)


def quarter_kernel(places, quarter_ref, a_ref, b_ref, *refs):
    del quarter_ref
    *adds, out_ref = refs
    total = dot_rows(a_ref[...], b_ref[0])
    half = out_ref.shape[0] // 2
    for first in (0, half):
        part = total[first : first + half]
        for place, add in zip(places, adds):
            if place <= first < place + add.shape[0]:
                part = part + add[pl.ds(first - place, half), :].astype(F32)
        out_ref[pl.ds(first, half), :] = part.astype(BF16)


def quarter_dot(a, first, last, b, quarter, adds):
    tokens, size = a.shape[0], last - first
    width = b.shape[2] // 2
    tile = max(t for t in (128, 256, 384, 768) if width % t == 0)
    steps = width // tile
    specs = [
        pl.BlockSpec((tokens, size), lambda n, q: (0, first // size)),
        pl.BlockSpec((1, tokens, tile), lambda n, q: (q[0] // 2, 0, (q[0] % 2) * steps + n)),
    ]
    for _, add, start, count in adds:
        specs.append(pl.BlockSpec((count, tile), lambda n, q, block=start // count: (block, n)))
    return pl.pallas_call(
        functools.partial(quarter_kernel, tuple(add[0] for add in adds)),
        grid_spec=pltpu.PrefetchScalarGridSpec(
            num_scalar_prefetch=1,
            grid=(steps,),
            in_specs=specs,
            out_specs=pl.BlockSpec((size, tile), lambda n, q: (0, n)),
        ),
        out_shape=jax.ShapeDtypeStruct((size, width), BF16),
        compiler_params=PARAMS,
        name="quarter_dot",
    )(quarter.reshape(1), a, b, *(add[1] for add in adds))


def head_block(lead, rows):
    return pl.BlockSpec((lead, rows, HS), lambda h: (0, 0, h))


def shared_block(shape):
    return pl.BlockSpec(shape, lambda h: (0,) * len(shape))


def pair_block(seqs):
    return pl.BlockSpec((seqs, 2, CHUNKS, HS), lambda h: (0, 0, 0, h))


PARAMS = pltpu.CompilerParams(vmem_limit_bytes=40 * 1024 * 1024)


def mixer_forward(u, halo, dist, gates, taps, soft):
    seqs, rows, _ = u.shape
    full = head_block(seqs, rows)
    wide = jax.ShapeDtypeStruct((seqs, rows, LRU), F32)
    return pl.pallas_call(
        mixer_forward_kernel,
        grid=(HEADS,),
        in_specs=[
            full,
            head_block(seqs, HALO),
            shared_block((seqs, rows, HS)),
            pl.BlockSpec((1, HS, 2 * HS), lambda h: (h, 0, 0)),
            pl.BlockSpec((CONV, HS), lambda h: (0, h)),
            pl.BlockSpec((1, HS), lambda h: (0, h)),
        ],
        out_specs=[full, full, full, full, pair_block(seqs)],
        out_shape=[
            jax.ShapeDtypeStruct((seqs, rows, LRU), BF16),
            wide,
            wide,
            wide,
            jax.ShapeDtypeStruct((seqs, 2, CHUNKS, LRU), F32),
        ],
        scratch_shapes=[
            pltpu.VMEM((rows + BACK, HS), F32),
            pltpu.VMEM((seqs, rows, HS), F32),
            pltpu.VMEM((seqs, rows, HS), F32),
            pltpu.VMEM((seqs, rows, HS), F32),
        ],
        compiler_params=PARAMS,
        name="mixer_forward",
    )(u, halo, dist, gates, taps, soft)


def mixer_branch(state, prod, carry, gate, shards, core):
    seqs, rows, _ = state.shape
    per = HEADS // shards

    def at(h, core_ref):
        return (0, 0, h)

    def split_at(h, core_ref):
        shard = h // per
        return ((shard % 2 + core_ref[0]) % 2, 0, 0, (shard // 2) * per + h % per)

    full = pl.BlockSpec((seqs, rows, HS), at)
    return pl.pallas_call(
        branch_kernel,
        grid_spec=pltpu.PrefetchScalarGridSpec(
            num_scalar_prefetch=1,
            grid=(HEADS,),
            in_specs=[full, full, pl.BlockSpec((seqs, CHUNKS, HS), at), full],
            out_specs=[full, full, pl.BlockSpec((1, seqs, rows, HS), split_at)],
        ),
        out_shape=[
            jax.ShapeDtypeStruct((seqs, rows, LRU), F32),
            jax.ShapeDtypeStruct((seqs, rows, LRU), BF16),
            jax.ShapeDtypeStruct((2, seqs, rows, LRU // 2), BF16),
        ],
        compiler_params=PARAMS,
        name="mixer_branch",
    )(core.reshape(1), state, prod, carry, gate)


def mixer_reverse(grad, gate, keep, state):
    seqs, rows, _ = grad.shape
    full = head_block(seqs, rows)
    wide = jax.ShapeDtypeStruct((seqs, rows, LRU), F32)
    return pl.pallas_call(
        reverse_kernel,
        grid=(HEADS,),
        in_specs=[full, full, full, full],
        out_specs=[full, full, full, pair_block(seqs)],
        out_shape=[
            jax.ShapeDtypeStruct((seqs, rows, LRU), BF16),
            wide,
            wide,
            jax.ShapeDtypeStruct((seqs, 2, CHUNKS, LRU), F32),
        ],
        compiler_params=PARAMS,
        name="mixer_reverse",
    )(grad, gate, keep, state)


def mixer_backward(local, prod, carry, state, before, c, u, halo, dist, gates, taps, soft):
    seqs, rows, _ = local.shape
    full = head_block(seqs, rows)
    small = head_block(seqs, HALO)
    gate_block = pl.BlockSpec((1, HS, 2 * HS), lambda h: (h, 0, 0))
    row_block = pl.BlockSpec((8, HS), lambda h: (0, h))
    return pl.pallas_call(
        mixer_backward_kernel,
        grid=(HEADS,),
        in_specs=[
            full,
            full,
            head_block(seqs, CHUNKS),
            full,
            small,
            full,
            full,
            small,
            shared_block((seqs, rows, HS)),
            gate_block,
            pl.BlockSpec((CONV, HS), lambda h: (0, h)),
            pl.BlockSpec((1, HS), lambda h: (0, h)),
        ],
        out_specs=[full, head_block(seqs, TAIL), small, gate_block, row_block, row_block],
        out_shape=[
            jax.ShapeDtypeStruct((seqs, rows, LRU), BF16),
            jax.ShapeDtypeStruct((seqs, TAIL, LRU), F32),
            jax.ShapeDtypeStruct((seqs, HALO, LRU), F32),
            jax.ShapeDtypeStruct((HEADS, HS, 2 * HS), F32),
            jax.ShapeDtypeStruct((8, LRU), F32),
            jax.ShapeDtypeStruct((8, LRU), F32),
        ],
        scratch_shapes=[
            pltpu.VMEM((rows, 2 * HS), F32),
            pltpu.VMEM((rows, 2 * HS), BF16),
            pltpu.VMEM((rows + BACK, HS), F32),
            pltpu.VMEM((rows + 8, HS), F32),
            pltpu.VMEM((rows + BACK, HS), F32),
            pltpu.VMEM((rows + BACK, HS), F32),
        ],
        compiler_params=PARAMS,
        name="mixer_backward",
    )(local, prod, carry, state, before, c, u, halo, dist, gates, taps, soft)


def rms_norm(x, gain, shards, core):
    rows = x.shape[0]
    block = min(rows, 256)
    return pl.pallas_call(
        functools.partial(norm_kernel, shards),
        grid=(rows // block,),
        in_specs=[
            pl.BlockSpec(memory_space=pltpu.SMEM),
            pl.BlockSpec((block, D), lambda n: (n, 0)),
            pl.BlockSpec((1, D), lambda n: (0, 0)),
        ],
        out_specs=[
            pl.BlockSpec((block, D), lambda n: (n, 0)),
            pl.BlockSpec((block, D // 2), lambda n: (n, 0)),
            pl.BlockSpec((block, D // 2), lambda n: (n, 0)),
            pl.BlockSpec((block, 128), lambda n: (n, 0)),
        ],
        out_shape=[
            jax.ShapeDtypeStruct((rows, D), BF16),
            jax.ShapeDtypeStruct((rows, D // 2), BF16),
            jax.ShapeDtypeStruct((rows, D // 2), BF16),
            jax.ShapeDtypeStruct((rows, 128), F32),
        ],
        compiler_params=PARAMS,
        name="rms_norm",
    )(core.reshape(1), x, gain.reshape(1, D))


FF_TILE = 512
GATHER_TILE = 768
DOT_TILE = 512


def ffn_forward(normed, proj_up):
    rows = normed.shape[0]
    steps = FF // FF_TILE
    return pl.pallas_call(
        ffn_forward_kernel,
        grid=(steps,),
        in_specs=[
            pl.BlockSpec((rows, D), lambda n: (0, 0)),
            pl.BlockSpec((D, FF_TILE), lambda n: (0, n)),
            pl.BlockSpec((D, FF_TILE), lambda n: (0, n + steps)),
        ],
        out_specs=[
            pl.BlockSpec((rows, FF_TILE), lambda n: (0, n)),
            pl.BlockSpec((2, rows, FF_TILE), lambda n: (0, 0, n)),
        ],
        out_shape=[
            jax.ShapeDtypeStruct((rows, FF), BF16),
            jax.ShapeDtypeStruct((2, rows, FF), BF16),
        ],
        compiler_params=PARAMS,
        name="ffn_forward",
    )(normed, proj_up, proj_up)


def ffn_backward(grad, proj_down, pull):
    rows = grad.shape[0]
    return pl.pallas_call(
        ffn_backward_kernel,
        grid=(FF // FF_TILE,),
        in_specs=[
            pl.BlockSpec((rows, D), lambda n: (0, 0)),
            pl.BlockSpec((FF_TILE, D), lambda n: (n, 0)),
            pl.BlockSpec((2, rows, FF_TILE), lambda n: (0, 0, n)),
        ],
        out_specs=pl.BlockSpec((2, rows, FF_TILE), lambda n: (0, 0, n)),
        out_shape=jax.ShapeDtypeStruct((2, rows, FF), BF16),
        compiler_params=PARAMS,
        name="ffn_backward",
    )(grad, proj_down, pull)


def gather_rows(shard):
    parts = lax.axis_size("grp")
    rows = shard.shape[0] // parts
    own = lax.dynamic_slice_in_dim(shard, lax.axis_index("grp") * rows, rows, 0)
    return lax.all_gather(own, ("seq", "grp"), axis=0, tiled=True)


def tie(value, *after):
    return lax.optimization_barrier((value, *after))[0]


def xor_pairs(axis, bit):
    return [(i, i ^ bit) for i in range(lax.axis_size(axis))]


def ring_pairs(steps):
    count = lax.axis_size("seq")
    return [(i, (i + steps) % count) for i in range(count)]


def same_cores():
    count = lax.axis_size("seq")
    return [list(range(core, count, 2)) for core in range(2)]


def dot_rows(a, b):
    return lax.dot_general(a, b, (((0,), (0,)), ((), ())), preferred_element_type=F32)


def reduce_rows(partial):
    part = lax.psum_scatter(partial, "seq", scatter_dimension=0, tiled=True)
    part = lax.psum_scatter(part, "grp", scatter_dimension=0, tiled=True)
    return lax.all_gather(part, "grp", axis=0, tiled=True).astype(F32)


def dot_far(a, b):
    return lax.dot_general(a, b, (((1,), (1,)), ((), ())), preferred_element_type=F32)


def by_position(a):
    seqs, rows = a.shape[:2]
    return a.reshape(seqs, CHUNKS, rows // CHUNKS, *a.shape[2:]).swapaxes(1, 2).reshape(a.shape)


def by_token(a):
    seqs, rows = a.shape[:2]
    return a.reshape(seqs, rows // CHUNKS, CHUNKS, *a.shape[2:]).swapaxes(1, 2).reshape(a.shape)


def fetch_columns(where_ref, pieces, start, target, sem):
    own, far = pieces[:6], pieces[6:]
    rows, columns = own[0].shape
    width, tile = columns // 4, target.shape[1]
    depth, half = own[1].shape[0], own[4].shape[0]
    chips = depth // rows + 1
    chip, core, group = where_ref[0], where_ref[1], where_ref[2]
    quarter = start // width
    offset = pl.multiple_of(start - quarter * width, 128)
    start = pl.multiple_of(start, 128)
    relation = lax.bitwise_xor(group, quarter)

    def copy(source, row, count):
        place = target.at[pl.ds(pl.multiple_of(row, 16), count), :]
        pltpu.make_async_copy(source, place, sem).start()

    for c, (shard, *parts) in enumerate((own, far)):
        other = lax.rem(core + c, 2)
        copy(shard.at[:, pl.ds(start, tile)], (chip * 2 + other) * rows, rows)
        for j in range(1, chips):
            row = (lax.rem(chip + j, chips) * 2 + other) * rows
            first = (j - 1) * rows
            for k in range(3):

                @pl.when(relation == k)
                def _():
                    copy(parts[k].at[pl.ds(first, rows), pl.ds(offset, tile)], row, rows)

            @pl.when(relation == 3)
            def _():
                for m in range(2):
                    low, high = max(first, m * half), min(first + rows, (m + 1) * half)
                    if low < high:
                        at = pl.ds(low - m * half, high - low)
                        source = parts[3 + m].at[at, pl.ds(offset, tile)]
                        copy(source, row + (low - first), high - low)


def gathered_tiles(fetch, held, sems):
    step, steps = pl.program_id(0), pl.num_programs(0)
    slot = lax.rem(step, 2)

    @pl.when(step == 0)
    def _():
        fetch(step, slot)

    @pl.when(step + 1 < steps)
    def _():
        fetch(step + 1, 1 - slot)

    for side in range(held.shape[1]):
        whole = held.at[slot, side]
        pltpu.make_async_copy(whole, whole, sems.at[slot, side]).wait()
    return slot


def gathered_ffn_kernel(where_ref, n_ref, *refs):
    pieces, (hidden_ref, pull_ref, gate_ref, up_ref, held, sems) = refs[:12], refs[12:]
    tile = hidden_ref.shape[1]

    def fetch(n, slot):
        for side in range(2):
            start = n * tile + side * (pieces[0].shape[1] // 2)
            fetch_columns(where_ref, pieces, start, held.at[slot, side], sems.at[slot, side])

    slot = gathered_tiles(fetch, held, sems)
    gate_ref[...] = held[slot, 0]
    up_ref[...] = held[slot, 1]
    ffn_forward_kernel(n_ref, gate_ref, up_ref, hidden_ref, pull_ref)


def gathered_dot_kernel(base, where_ref, n_ref, *refs):
    pieces, (out_ref, weight_ref, held, sems) = refs[:12], refs[12:]
    tile = out_ref.shape[1]

    def fetch(n, slot):
        start = base + n * tile
        fetch_columns(where_ref, pieces, start, held.at[slot, 0], sems.at[slot, 0])

    slot = gathered_tiles(fetch, held, sems)
    weight_ref[...] = held[slot, 0]
    out_ref[...] = jnp.dot(n_ref[...], weight_ref[...], preferred_element_type=F32).astype(
        out_ref.dtype
    )


class Gather:
    def __init__(self, shard, *after, offload=False):
        self.shard = shard
        self.chips = lax.axis_size("seq") // 2
        half = (self.chips - 1) * shard.shape[0] // 2
        self.simple = lax.axis_size("grp") != 4 or half % 16 != 0
        if self.simple:
            self.whole = gather_rows(shard)
            return
        group = lax.axis_index("grp")
        width = shard.shape[1] // 4
        own = lax.dynamic_slice_in_dim(shard, group * width, width, 1)
        if after:
            own = tie(own, *after)
        if offload:
            self.slabs = lax.all_gather(own, "seq", axis_index_groups=same_cores())
        else:
            self.slabs = [
                lax.ppermute(own, "seq", ring_pairs(-2 * j)) for j in range(1, self.chips)
            ]
        self.half = half

    def first(self, *after):
        if self.simple:
            return ()
        slabs = tie(self.slabs, *after) if after else self.slabs
        if not isinstance(slabs, list):
            chip = lax.axis_index("seq") // 2
            slabs = [
                lax.dynamic_index_in_dim(slabs, (chip + j) % self.chips, 0, False)
                for j in range(1, self.chips)
            ]
        self.near = jnp.concatenate(slabs, axis=0)
        self.from_x = lax.ppermute(self.near, "grp", xor_pairs("grp", 1))
        self.from_y = lax.ppermute(self.near, "grp", xor_pairs("grp", 2))
        return (self.near,)

    def second(self, *after):
        if self.simple:
            return ()
        if after:
            self.from_x, self.from_y = tie((self.from_x, self.from_y), *after)
        self.halves = (self.from_y[: self.half], self.from_x[self.half :])
        return self.halves

    def third(self):
        if self.simple:
            return
        diag_a = lax.ppermute(self.halves[0], "grp", xor_pairs("grp", 1))
        diag_b = lax.ppermute(self.halves[1], "grp", xor_pairs("grp", 2))
        own = (self.shard, self.near, self.from_x, self.from_y, diag_a, diag_b)
        far = tuple(lax.ppermute(piece, "seq", xor_pairs("seq", 1)) for piece in own)
        place = lax.axis_index("seq")
        where = jnp.stack([place // 2, place % 2, lax.axis_index("grp")]).astype(jnp.int32)
        self.pieces = (where, own, far)

    def call(self, kernel, normed, steps, tile, weights, out_specs, out_shape, name):
        where, own, far = self.pieces
        rows, depth = normed.shape
        return pl.pallas_call(
            kernel,
            grid=(steps,),
            in_specs=[
                pl.BlockSpec(memory_space=pltpu.SMEM),
                pl.BlockSpec((rows, depth), lambda n: (0, 0)),
            ]
            + [pl.BlockSpec(memory_space=pl.ANY)] * 12,
            out_specs=out_specs + [pl.BlockSpec((depth, tile), lambda n: (0, n))] * weights,
            out_shape=out_shape + [jax.ShapeDtypeStruct((depth, steps * tile), BF16)] * weights,
            scratch_shapes=[
                pltpu.VMEM((2, weights, depth, tile), BF16),
                pltpu.SemaphoreType.DMA((2, weights)),
            ],
            compiler_params=pltpu.CompilerParams(vmem_limit_bytes=56 * 1024 * 1024),
            name=name,
        )(where, normed, *own, *far)

    def dot(self, normed, half, dtype):
        columns = self.shard.shape[1] // 2
        base = half * columns
        if self.simple:
            weight = self.whole[:, base : base + columns]
            return jnp.dot(normed, weight, preferred_element_type=F32).astype(dtype), weight
        rows, tile = normed.shape[0], DOT_TILE
        return self.call(
            functools.partial(gathered_dot_kernel, base),
            normed,
            columns // tile,
            tile,
            1,
            [pl.BlockSpec((rows, tile), lambda n: (0, n))],
            [jax.ShapeDtypeStruct((rows, columns), dtype)],
            "gathered_dot",
        )

    def ffn_forward(self, normed):
        if self.simple:
            hidden, pull = ffn_forward(normed, self.whole)
            return hidden, pull, self.whole[:, :FF], self.whole[:, FF:]
        rows, tile = normed.shape[0], GATHER_TILE
        return self.call(
            gathered_ffn_kernel,
            normed,
            FF // tile,
            tile,
            2,
            [
                pl.BlockSpec((rows, tile), lambda n: (0, n)),
                pl.BlockSpec((2, rows, tile), lambda n: (0, 0, n)),
            ],
            [
                jax.ShapeDtypeStruct((rows, FF), BF16),
                jax.ShapeDtypeStruct((2, rows, FF), BF16),
            ],
            "gathered_ffn",
        )


class Reduction:
    def __init__(self, a_own, a_far, columns, width, paired=None):
        self.simple = lax.axis_size("grp") != 4
        count = lax.axis_size("seq")
        place = lax.axis_index("seq")
        self.chips = count // 2
        self.chip, core = place // 2, place % 2
        self.width = width
        full = a_own.shape[1]
        self.rows = full // self.chips
        self.half = full // 2
        self.a_own = a_own
        if self.simple:
            parts = [columns(k) for k in range(4)]
            own, far = (
                jnp.concatenate([dot_rows(a, part) for part in parts], axis=1)
                for a in (a_own, a_far)
            )
            cores = jnp.stack(
                [jnp.where(core == c, own, far).reshape(self.chips, self.rows, -1) for c in (0, 1)],
                axis=1,
            )
            self.product = cores.reshape(2 * full, 4 * width).astype(BF16)
            self.arrived = self.product
            self.sent = (self.product,)
            return
        self.group = lax.axis_index("grp")
        self.x, self.y = xor_pairs("grp", 1), xor_pairs("grp", 2)
        self.paired = paired
        self.columns = columns
        other = xor_pairs("seq", 1)
        half = self.half
        self.far = [None] * 4
        self.joint = None
        if paired is None:
            b_all = jnp.concatenate([columns(self.group ^ k) for k in range(4)], axis=1)
            far = lax.ppermute(dot_rows(a_far, b_all).astype(BF16), "seq", other)
            self.joint = (dot_rows(a_own, b_all) + far.astype(F32)).astype(BF16)
        else:
            for k in (3, 1, 2, 0):
                product = quarter_dot(a_far, 0, full, paired, self.group ^ k, [])
                self.far[k] = lax.ppermute(product, "seq", other)
        self.sent = (self.own(3, 0, half), self.own(3, half, full))
        self.diag_a = lax.ppermute(self.sent[0], "grp", self.x)
        self.diag_b = lax.ppermute(self.sent[1], "grp", self.y)

    def own(self, k, first, last, *adds):
        if self.joint is None:
            adds = [(place, add, 0, add.shape[0]) for place, add in adds]
            adds.append((0, self.far[k], first, last - first))
            return quarter_dot(self.a_own, first, last, self.paired, self.group ^ k, adds)
        left = k * self.width
        total = self.joint[first:last, left : left + self.width].astype(F32)
        for place, add in adds:
            after = last - first - place - add.shape[0]
            total = total + jnp.pad(add.astype(F32), ((place, after), (0, 0)))
        return total.astype(BF16)

    def second(self, *after):
        if self.simple:
            return ()
        full = 2 * self.half
        diag_a, diag_b = self.diag_a, self.diag_b
        if after:
            diag_a, diag_b = tie((diag_a, diag_b), *after)
        sent = (
            self.own(1, 0, full, (self.half, diag_b)),
            self.own(2, 0, full, (0, diag_a)),
        )
        self.from_x = lax.ppermute(sent[0], "grp", self.x)
        self.from_y = lax.ppermute(sent[1], "grp", self.y)
        return sent

    def mine(self, *after):
        from_x, from_y = self.from_x, self.from_y
        if after:
            from_x, from_y = tie((from_x, from_y), *after)
        return self.own(0, 0, 2 * self.half, (0, from_x), (0, from_y))

    def along_z(self, mine):
        mine = mine.reshape(self.chips, self.rows, -1)
        self.kept = lax.dynamic_index_in_dim(mine, self.chip, 0, False)
        sent = tuple(
            lax.dynamic_index_in_dim(mine, (self.chip + j) % self.chips, 0, False)
            for j in range(1, self.chips)
        )
        self.arrived = [
            lax.ppermute(part, "seq", ring_pairs(2 * j + 2)) for j, part in enumerate(sent)
        ]
        return sent

    def third(self, *after, offload=False):
        if self.simple:
            return ()
        mine = self.mine(*after)
        if not offload:
            return self.along_z(mine)
        self.kept = None
        self.arrived = lax.psum_scatter(
            mine, "seq", scatter_dimension=0, axis_index_groups=same_cores(), tiled=True
        )
        return (mine,)

    def total(self):
        if self.kept is None:
            return self.arrived
        total = self.kept.astype(F32)
        for part in self.arrived:
            total = total + part.astype(F32)
        return total

    def finish(self, *after):
        if self.simple:
            return reduce_rows(self.product)
        total = self.total()
        if after:
            total = tie(total, *after)
        parts = lax.all_gather(total.astype(BF16), "grp")
        return parts.transpose(1, 0, 2).reshape(self.rows, 4 * self.width).astype(F32)


def gather_parts(lines, one):
    if one.simple:
        return lax.psum(lines.astype(F32), "grp"), one.finish()
    total = one.total().astype(BF16)
    blocks = one.width // HS
    pieces = [lines] + [total[:, n * HS : (n + 1) * HS] for n in range(blocks)]
    parts = lax.all_gather(jnp.concatenate(pieces, axis=0), "grp")
    count = lines.shape[0]
    part = parts[:, count:].reshape(4, blocks, one.rows, HS).transpose(2, 0, 1, 3)
    found = part.reshape(one.rows, 4 * one.width).astype(F32)
    return jnp.sum(parts[:, :count].astype(F32), axis=0), found


def shard_carry(ends, prods, reverse):
    count = lax.axis_size("seq")
    place = lax.axis_index("seq")
    both = lax.all_gather(jnp.stack([ends, prods]), "seq")
    carry = jnp.zeros_like(ends)
    for step in range(count - 1):
        source = count - 1 - step if reverse else step
        ahead = source > place if reverse else source < place
        carry = jnp.where(ahead, both[source, 0] + both[source, 1] * carry, carry)
    return carry


def chunk_ends(chunks, reverse):
    state = jnp.zeros_like(chunks[:, 0, 0])
    prod = jnp.ones_like(state)
    order = range(CHUNKS - 1, -1, -1) if reverse else range(CHUNKS)
    for n in order:
        state = chunks[:, 0, n] + chunks[:, 1, n] * state
        prod = chunks[:, 1, n] * prod
    return state, prod


def chunk_carries(chunks, carry, reverse):
    order = range(CHUNKS - 1, -1, -1) if reverse else range(CHUNKS)
    found = [None] * CHUNKS
    for n in order:
        found[n] = carry
        carry = chunks[:, 0, n] + chunks[:, 1, n] * carry
    return jnp.stack(found, axis=1)


def norm_back(values, scale, gain, grad_normed):
    weighted = grad_normed * gain
    cubed = scale * scale * scale
    return scale * weighted - values * cubed * jnp.mean(weighted * values, axis=-1, keepdims=True)


def gain_grad(weight, grad_weight, gain):
    return jnp.sum(weight.astype(F32) * grad_weight, axis=1) / gain.astype(F32)


def body(
    tokens, seg_ids, cotangent, first_gain, in_proj, conv_taps, decay_param, gate_heads,
    out_proj, second_gain, up_proj, down_proj,
):
    seq_count, shard_len, _ = tokens.shape
    row_count = seq_count * shard_len
    edge_len = CONV - 1
    place = lax.axis_index("seq")
    last = lax.axis_size("seq") - 1

    small = jnp.concatenate(
        [first_gain, second_gain, decay_param, conv_taps.reshape(-1)]
    )
    small_all = lax.all_gather(small, "seq")
    n_gain, n_lru = first_gain.shape[0], decay_param.shape[0]
    gain_one = small_all[:, :n_gain].reshape(D).astype(F32)
    gain_two = small_all[:, n_gain : 2 * n_gain].reshape(D).astype(F32)
    decay_float = small_all[:, 2 * n_gain : 2 * n_gain + n_lru].reshape(LRU).astype(F32)
    taps_all = (
        small_all[:, 2 * n_gain + n_lru :].reshape(-1, CONV, n_lru).transpose(1, 0, 2)
    ).reshape(CONV, LRU).astype(F32)
    in_gather = Gather(in_proj)
    near = in_gather.first(small_all)
    in_gather.second()
    in_gather.third()
    gates_all = lax.all_gather(gate_heads, "seq", axis=0, tiled=True)
    up_gather = Gather(up_proj, gates_all, *near, offload=True)
    proj_out = gather_rows(out_proj)
    proj_down = gather_rows(down_proj)

    tokens = by_position(tokens)
    cotangent = by_position(cotangent)
    inputs = tokens.reshape(row_count, D).astype(F32)
    first_normed, first_own, first_far, first_scale = rms_norm(
        tokens.reshape(row_count, D), gain_one, last + 1, place % 2
    )
    first_scale = first_scale[:, :1]
    wide = (seq_count, shard_len, LRU)
    inner_low, in_value = in_gather.dot(first_normed, 0, BF16)
    inner_low = inner_low.reshape(wide)

    step = shard_len // CHUNKS
    final = inner_low.reshape(seq_count, step, CHUNKS, LRU)[:, step - HALO :, CHUNKS - 1]
    prev_inner = from_behind(final, "seq", 1)
    prev_ids = from_behind(seg_ids[:, shard_len - edge_len :], "seq", 1)
    prev_ids = jnp.where(place == 0, -1, prev_ids)
    ext_ids = jnp.concatenate([prev_ids, seg_ids], axis=1)
    dist = jnp.zeros((seq_count, shard_len), F32)
    for k in range(1, CONV):
        dist = dist + (ext_ids[:, edge_len - k : edge_len - k + shard_len] == seg_ids).astype(F32)
    dist = jnp.broadcast_to(by_position(dist)[:, :, None], (seq_count, shard_len, HS))
    soft = jax.nn.softplus(-decay_float).reshape(1, LRU)

    conv_low, keep, state_part, prod_part, chunks = mixer_forward(
        tie(inner_low, *up_gather.first(inner_low)), prev_inner, dist, gates_all, taps_all, soft
    )
    end_state, end_prod = chunk_ends(chunks, False)
    gate_pre, in_gate = in_gather.dot(first_normed, 1, F32)
    gate_pre = gate_pre.reshape(wide)
    carry_in = shard_carry(end_state, end_prod, False)
    carries = chunk_carries(chunks, carry_in, False)
    state, branch, branch_split = mixer_branch(
        tie(state_part, *up_gather.second(carries, gate_pre)), prod_part, carries, gate_pre, last + 1, place % 2
    )
    branch_split = branch_split.reshape(2, row_count, LRU // 2)
    resid = inputs + jnp.dot(
        branch.reshape(row_count, LRU), proj_out, preferred_element_type=F32
    )
    second_normed, second_own, second_far, second_scale = rms_norm(
        resid, gain_two, last + 1, place % 2
    )
    second_scale = second_scale[:, :1]
    up_gather.third()
    hidden, pull, proj_gate, proj_up = up_gather.ffn_forward(second_normed)

    grad_out = cotangent.reshape(row_count, D)
    grad_down = dot_rows(hidden, grad_out).astype(BF16)
    down_part = lax.psum_scatter(grad_down, ("seq", "grp"), scatter_dimension=0, tiled=True)
    grad_expanded = ffn_backward(tie(grad_out, grad_down), proj_down, pull)
    quarter = FF // 2

    def up_columns(n):
        part = lax.dynamic_slice(
            grad_expanded, (n // 2, 0, (n % 2) * quarter), (1, row_count, quarter)
        )
        return part[0]

    up_sum = Reduction(second_own, second_far, up_columns, quarter, grad_expanded)
    grad_expanded = tie(grad_expanded, *up_sum.sent)
    grad_second_normed = dot_far(grad_expanded[0], proj_gate) + dot_far(
        grad_expanded[1], proj_up
    )
    sent = up_sum.second(grad_second_normed)
    grad_second_normed = tie(grad_second_normed, *sent)
    grad_resid = grad_out.astype(F32) + norm_back(
        resid, second_scale, gain_two, grad_second_normed
    )
    grad_mixer = grad_resid.astype(BF16)
    grad_branch = dot_far(grad_mixer, proj_out)

    grad_gate, local, rev_prod, rev_chunks = mixer_reverse(
        grad_branch.reshape(wide), gate_pre, keep, state
    )
    down_sum = lax.all_gather(tie(down_part, rev_chunks), "grp", axis=0, tiled=True)
    head_pull, head_prod = chunk_ends(rev_chunks, True)
    grad_gate = grad_gate.reshape(row_count, LRU)
    width = LRU // 4
    rev_carry = shard_carry(head_pull, head_prod, True)
    rev_carries = chunk_carries(rev_chunks, rev_carry, True)
    grad_mixer, grad_gate = tie((grad_mixer, grad_gate), rev_carry)
    out_sum = Reduction(
        branch_split[0],
        branch_split[1],
        lambda n: lax.dynamic_slice_in_dim(grad_mixer, n * (D // 4), D // 4, 1),
        D // 4,
    )
    in_gate_sum = Reduction(
        first_own,
        first_far,
        lambda n: lax.dynamic_slice_in_dim(grad_gate, n * width, width, 1),
        width,
    )
    sent = (*out_sum.sent, *in_gate_sum.sent)
    sent = up_sum.third(down_sum, *sent, offload=True)
    local = tie(local, *sent)
    du, tail, edge, grad_gates, grad_taps, grad_decay = mixer_backward(
        local, rev_prod, rev_carries, state, carries, conv_low, inner_low,
        prev_inner, dist, gates_all, taps_all, soft,
    )
    returned = from_behind(edge[:, HALO - edge_len :].astype(BF16), "seq", -1).astype(F32)
    grad_gate = tie(grad_gate, *out_sum.second(edge), *in_gate_sum.second(edge))
    first_grad = dot_far(grad_gate, in_gate)
    groups = TAIL // CHUNKS
    padded = jnp.pad(
        returned[:, :, None, :], ((0, 0), (groups - edge_len, 0), (CHUNKS - 1, 0), (0, 0))
    ).reshape(seq_count, TAIL, LRU)
    grad_inner = lax.dynamic_update_slice(
        du, (tail + padded).astype(BF16), (0, shard_len - TAIL, 0)
    )
    grad_inner = tie(grad_inner, first_grad).reshape(row_count, LRU)
    in_value_sum = Reduction(
        first_own,
        first_far,
        lambda n: lax.dynamic_slice_in_dim(grad_inner, n * width, width, 1),
        width,
    )
    grad_inner = tie(grad_inner, *in_value_sum.sent)

    shards = last + 1
    grad_decay_row = grad_decay[0] * jax.nn.sigmoid(-decay_float)
    flat = jnp.concatenate(
        [
            grad_gates.reshape(shards, -1, HS),
            grad_taps[:CONV].reshape(CONV, shards, -1, HS).swapaxes(0, 1).reshape(shards, -1, HS),
            grad_decay_row.reshape(shards, -1, HS),
        ],
        axis=1,
    )
    lines = flat.shape[1]
    flat = jnp.pad(flat, ((0, 0), (0, -lines % 16), (0, 0))).astype(BF16).reshape(-1, HS)
    flat = tie(flat, up_sum.arrived)
    flat = lax.psum_scatter(flat, "seq", scatter_dimension=0, tiled=True)
    first_grad = first_grad + dot_far(grad_inner, in_value)
    sent = in_value_sum.second(first_grad)
    out_sum.third(*sent)
    up_total = up_sum.finish(edge)
    flat, out_total = gather_parts(tie(flat, up_total), out_sum)
    flat = flat[:lines].reshape(-1)
    n_gates = flat.shape[0] - (CONV + 1) * n_lru
    gates_total = flat[:n_gates].reshape(gate_heads.shape)
    taps_total = flat[n_gates : n_gates + CONV * n_lru].reshape(CONV, n_lru)
    decay_total = flat[n_gates + CONV * n_lru :]

    down_total = tie(down_sum, *sent).astype(F32)
    if in_value_sum.simple:
        in_total = jnp.concatenate([in_value_sum.finish(), in_gate_sum.finish()], axis=1)
    else:
        both = jnp.concatenate([in_value_sum.mine(), in_gate_sum.mine()], axis=1)
        in_value_sum.along_z(both)
        both = in_value_sum.total().astype(BF16)
        in_total = jnp.concatenate(
            [
                lax.all_gather(both[:, n * width : (n + 1) * width], "grp")
                .transpose(1, 0, 2)
                .reshape(-1, LRU)
                for n in range(2)
            ],
            axis=1,
        ).astype(F32)
    ffn_out = jnp.dot(tie(hidden, *sent), proj_down, preferred_element_type=F32)
    block_out = by_token((resid + ffn_out).astype(BF16).reshape(tokens.shape))
    grad_tokens = grad_resid + norm_back(inputs, first_scale, gain_one, first_grad)
    grad_tokens = by_token(grad_tokens.astype(BF16).reshape(tokens.shape))
    first_total = gain_grad(in_proj, in_total, first_gain)
    second_total = gain_grad(up_proj, up_total, second_gain)
    return (
        block_out, grad_tokens, first_total, in_total, taps_total, decay_total, gates_total,
        out_total, second_total, up_total, down_total,
    )


def solution(mesh):
    in_specs = (
        P("grp", "seq", None),
        P("grp", "seq"),
        P("grp", "seq", None),
        P("seq"),
        P("seq", None),
        P(None, "seq"),
        P("seq"),
        P("seq", None, None),
        P("seq", None),
        P("seq"),
        P("seq", None),
        P("seq", None),
    )
    out_specs = (
        P("grp", "seq", None),
        P("grp", "seq", None),
        P("seq"),
        P("seq", None),
        P(None, "seq"),
        P("seq"),
        P("seq", None, None),
        P("seq", None),
        P("seq"),
        P("seq", None),
        P("seq", None),
    )
    return jax.shard_map(body, mesh=mesh, in_specs=in_specs, out_specs=out_specs, check_vma=False)
```

```python
import functools

import jax
import jax.numpy as jnp
from jax import lax
from jax.experimental import pallas as pl
from jax.experimental.pallas import tpu as pltpu
from jax.sharding import PartitionSpec as P

D = 1536
HEADS = 16
HS = 128
LRU = 2048
FF = 4608
CONV = 4
CHUNKS = 8
HALO = 8
BACK = 8 * (CONV - 1)
TAIL = 32
F32 = jnp.float32
BF16 = jnp.bfloat16


def from_behind(value, axis, steps):
    count = lax.axis_size(axis)
    first, last = (max(0, -steps), min(count, count - steps))
    return lax.ppermute(value, axis, [(source, source + steps) for source in range(first, last)])


def gelu_parts(v):
    k = 0.7978845608028654
    square = v * v
    t = jnp.tanh(k * v * (1.0 + 0.044715 * square))
    half = 0.5 * (1.0 + t)
    slope = half + 0.5 * v * (1.0 - t * t) * (k * (1.0 + 3.0 * 0.044715 * square))
    return v * half, slope


def gelu_tanh(v):
    k = 0.7978845608028654
    return 0.5 * v * (1.0 + jnp.tanh(k * v * (1.0 + 0.044715 * v * v)))


def sigmoid(v):
    return 0.5 * jnp.tanh(0.5 * v) + 0.5


def drive_values(q_rate, q_input, soft):
    rate = sigmoid(q_rate)
    inp = sigmoid(q_input)
    decay = jnp.exp(-8.0 * rate * soft)
    square = 1.0 - decay * decay + 0.001
    inverse = lax.rsqrt(square)
    return rate, inp, decay, square * inverse, inverse


def shifted_group(group, step, fill):
    row = lax.broadcasted_iota(jnp.int32, group.shape, 0)
    edge = 0 if step == 1 else CHUNKS - 1
    moved = pltpu.roll(group, step % CHUNKS, 0)
    return jnp.where(row == edge, fill, moved)


def extend_back(ext_s, u_ref, halo_ref, b):
    rows = u_ref.shape[1]
    ext_s[pl.ds(BACK, rows), :] = u_ref[b].astype(F32)
    halo = halo_ref[b].astype(F32)
    for m in range(CONV - 1):
        group = ext_s[pl.ds(BACK + rows - BACK + 8 * m, 8), :]
        fill = halo[HALO - CONV + 1 + m : HALO - CONV + 2 + m, :]
        ext_s[pl.ds(8 * m, 8), :] = shifted_group(group, 1, fill)


def mixer_forward_kernel(
    u_ref, halo_ref, dist_ref, gates_ref, taps_ref, soft_ref,
    c_ref, keep_ref, state_ref, prod_ref, chunk_ref,
    ext_s, c_s, rate_s, inp_s,
):
    seqs, rows, _ = u_ref.shape
    soft = soft_ref[...]
    for b in range(seqs):
        extend_back(ext_s, u_ref, halo_ref, b)

        def conv_chunk(n, _):
            at = pl.multiple_of(n * 64, 64)
            far = dist_ref[b, pl.ds(at, 64), :]
            total = taps_ref[0:1, :] * ext_s[pl.ds(at + BACK, 64), :]
            for k in range(1, CONV):
                window = taps_ref[k : k + 1, :] * ext_s[pl.ds(at + BACK - 8 * k, 64), :]
                total = total + jnp.where(far >= float(k), window, 0.0)
            low = total.astype(BF16)
            c_ref[b, pl.ds(at, 64), :] = low
            c_s[b, pl.ds(at, 64), :] = low.astype(F32)
            return 0

        lax.fori_loop(0, rows // 64, conv_chunk, 0)
        both = jnp.dot(c_ref[b], gates_ref[0], preferred_element_type=F32)
        rate_s[b] = both[:, :HS]
        inp_s[b] = both[:, HS:]

    def scan_step(j, carry):
        new = []
        for b in range(seqs):
            at = pl.ds(pl.multiple_of(j * 8, 8), 8)
            state, prod = carry[b]
            _, inp, decay, root, _ = drive_values(rate_s[b, at, :], inp_s[b, at, :], soft)
            keep = jnp.where(dist_ref[b, at, :] >= 1.0, decay, 0.0)
            state = keep * state + root * inp * c_s[b, at, :]
            prod = keep * prod
            keep_ref[b, at, :] = keep
            state_ref[b, at, :] = state
            prod_ref[b, at, :] = prod
            new.append((state, prod))
        return tuple(new)

    zero, one = jnp.zeros((CHUNKS, HS), F32), jnp.ones((CHUNKS, HS), F32)
    ends = lax.fori_loop(0, rows // CHUNKS, scan_step, ((zero, one),) * seqs, unroll=8)
    for b in range(seqs):
        chunk_ref[b, 0] = ends[b][0]
        chunk_ref[b, 1] = ends[b][1]


def branch_kernel(core_ref, state_ref, prod_ref, carry_ref, gate_ref, out_ref, branch_ref, split_ref):
    del core_ref
    seqs, rows, _ = state_ref.shape
    for b in range(seqs):
        carry = jnp.concatenate([carry_ref[b]] * 4, axis=0)

        def point(n, _):
            at = pl.ds(pl.multiple_of(n * 32, 32), 32)
            state = state_ref[b, at, :] + prod_ref[b, at, :] * carry
            out_ref[b, at, :] = state
            low = (state * gelu_tanh(gate_ref[b, at, :])).astype(BF16)
            branch_ref[b, at, :] = low
            split_ref[0, b, at, :] = low
            return 0

        lax.fori_loop(0, rows // 32, point, 0, unroll=4)


def reverse_kernel(
    grad_ref, gate_ref, keep_ref, state_ref,
    dg_ref, local_ref, prod_ref, chunk_ref,
):
    seqs, rows, _ = grad_ref.shape
    pairs = rows // 16

    def scan_step(n, carry):
        first = pl.multiple_of((pairs - 1 - n) * 16, 16)
        at = pl.ds(first, 16)
        new = []
        for b in range(seqs):
            pull, prod = carry[b]
            act, slope = gelu_parts(gate_ref[b, at, :])
            grad = grad_ref[b, at, :]
            dg_ref[b, at, :] = (grad * state_ref[b, at, :] * slope).astype(BF16)
            dh = grad * act
            keep = keep_ref[b, at, :]
            late = dh[8:] + pull
            late_prod = prod
            pull, prod = keep[8:] * late, keep[8:] * prod
            early = dh[:8] + pull
            local_ref[b, at, :] = jnp.concatenate([early, late], axis=0)
            prod_ref[b, at, :] = jnp.concatenate([prod, late_prod], axis=0)
            new.append((keep[:8] * early, keep[:8] * prod))
        return tuple(new)

    zero, one = jnp.zeros((CHUNKS, HS), F32), jnp.ones((CHUNKS, HS), F32)
    ends = lax.fori_loop(0, pairs, scan_step, ((zero, one),) * seqs, unroll=4)
    for b in range(seqs):
        chunk_ref[b, 0] = ends[b][0]
        chunk_ref[b, 1] = ends[b][1]


def mixer_backward_kernel(
    local_ref, prod_ref, carry_ref, state_ref, before_ref, c_ref, u_ref, halo_ref, dist_ref,
    gates_ref, taps_ref, soft_ref,
    du_ref, tail_ref, edge_ref, ggate_ref, gtaps_ref, gdecay_ref,
    q_s, dq_s, dc_s, h_s, ext_s, dist_s,
):
    seqs, rows, _ = local_ref.shape
    soft = soft_ref[...]
    ggate = jnp.zeros((HS, 2 * HS), F32)
    decay_sum = jnp.zeros((8, HS), F32)
    taps_sum = [jnp.zeros((8, HS), F32) for _ in range(CONV)]

    def fold(value):
        return jnp.sum(value.reshape(value.shape[0] // 8, 8, HS), axis=0)

    for b in range(seqs):
        q_s[...] = jnp.dot(c_ref[b], gates_ref[0], preferred_element_type=F32)
        h_s[pl.ds(0, 8), :] = before_ref[b]
        h_s[pl.ds(8, rows), :] = state_ref[b]
        carry = jnp.concatenate([carry_ref[b]] * 4, axis=0)

        def point(n, total):
            first = pl.multiple_of(n * 32, 32)
            at = pl.ds(first, 32)
            lam = local_ref[b, at, :] + prod_ref[b, at, :] * carry
            rate, inp, decay, root, inverse = drive_values(q_s[at, :HS], q_s[at, HS:], soft)
            conv = c_ref[b, at, :].astype(F32)
            kept = jnp.where(dist_ref[b, at, :] >= 1.0, h_s[at, :], 0.0)
            lam_root = lam * root
            lam_inp = lam * inp
            grad_decay = lam * kept - lam_inp * conv * decay * inverse
            rated = grad_decay * decay * rate
            dq_s[at, :HS] = (-8.0 * soft * rated * (1.0 - rate)).astype(BF16)
            dq_s[at, HS:] = (lam_root * conv * inp * (1.0 - inp)).astype(BF16)
            dc_s[at, :] = lam_root * inp
            return total + fold(rated)

        decay_sum = lax.fori_loop(0, rows // 32, point, decay_sum, unroll=2)
        dc_s[pl.ds(0, rows), :] += lax.dot_general(
            dq_s[...], gates_ref[0], (((1,), (1,)), ((), ())), preferred_element_type=F32
        )
        ggate = ggate + lax.dot_general(
            c_ref[b], dq_s[...], (((0,), (0,)), ((), ())), preferred_element_type=F32
        )
        extend_back(ext_s, u_ref, halo_ref, b)
        dist_s[pl.ds(0, rows), :] = dist_ref[b]
        for m in range(CONV - 1):
            for held in (dc_s, dist_s):
                held[pl.ds(rows + 8 * m, 8), :] = shifted_group(held[pl.ds(8 * m, 8), :], -1, 0.0)

        def conv_chunk(n, totals):
            at = pl.multiple_of(n * 64, 64)
            grad = dc_s[pl.ds(at, 64), :]
            far = dist_s[pl.ds(at, 64), :]
            out = taps_ref[0:1, :] * grad
            totals = list(totals)
            totals[0] = totals[0] + fold(grad * ext_s[pl.ds(at + BACK, 64), :])
            for k in range(1, CONV):
                masked = jnp.where(far >= float(k), grad, 0.0)
                totals[k] = totals[k] + fold(masked * ext_s[pl.ds(at + BACK - 8 * k, 64), :])
                ahead = pl.ds(at + 8 * k, 64)
                value = taps_ref[k : k + 1, :] * dc_s[ahead, :]
                out = out + jnp.where(dist_s[ahead, :] >= float(k), value, 0.0)
            du_ref[b, pl.ds(at, 64), :] = out.astype(BF16)

            @pl.when(n == rows // 64 - 1)
            def _():
                tail_ref[b] = out[64 - TAIL :, :]

            return tuple(totals)

        taps_sum = list(lax.fori_loop(0, rows // 64, conv_chunk, tuple(taps_sum)))
        edges = [jnp.zeros((HALO - CONV + 1, HS), F32)]
        for m in range(CONV - 1, 0, -1):
            edge = jnp.zeros((1, HS), F32)
            for k in range(m, CONV):
                at = pl.ds(8 * (k - m), 1)
                masked = jnp.where(dist_s[at, :] >= float(k), dc_s[at, :], 0.0)
                edge = edge + taps_ref[k : k + 1, :] * masked
            edges.append(edge)
        edge_ref[b] = jnp.concatenate(edges, axis=0)
    ggate_ref[0] = ggate
    gdecay_ref[...] = jnp.broadcast_to(
        8.0 * jnp.sum(decay_sum, axis=0, keepdims=True), (8, HS)
    )
    gtaps_ref[...] = jnp.concatenate(
        [jnp.sum(t, axis=0, keepdims=True) for t in taps_sum] + [jnp.zeros((8 - CONV, HS), F32)],
        axis=0,
    )


def norm_kernel(shards, core_ref, x_ref, gain_ref, normed_ref, own_ref, far_ref, scale_ref):
    x = x_ref[...].astype(F32)
    scale = lax.rsqrt(jnp.mean(x * x, axis=-1, keepdims=True) + 1e-06)
    low = (x * scale * gain_ref[...]).astype(BF16)
    normed_ref[...] = low
    scale_ref[...] = jnp.broadcast_to(scale, scale_ref.shape)
    wide = low.astype(F32)
    size = D // shards
    even, odd = (
        jnp.concatenate([wide[:, n * size : (n + 1) * size] for n in range(c, shards, 2)], axis=1)
        for c in range(2)
    )
    first = core_ref[0] == 0
    own_ref[...] = jnp.where(first, even, odd).astype(BF16)
    far_ref[...] = jnp.where(first, odd, even).astype(BF16)


def ffn_forward_kernel(n_ref, gate_ref, up_ref, hidden_ref, pull_ref):
    for m in range(0, n_ref.shape[0], 256):
        at = pl.ds(m, 256)
        e1 = jnp.dot(n_ref[at, :], gate_ref[...], preferred_element_type=F32)
        e2 = jnp.dot(n_ref[at, :], up_ref[...], preferred_element_type=F32)
        act, slope = gelu_parts(e1)
        hidden_ref[at, :] = (act * e2).astype(BF16)
        pull_ref[0, at, :] = (slope * e2).astype(BF16)
        pull_ref[1, at, :] = act.astype(BF16)


def ffn_backward_kernel(grad_ref, down_ref, pull_ref, out_ref):
    for m in range(0, grad_ref.shape[0], 256):
        at = pl.ds(m, 256)
        dv = lax.dot_general(
            grad_ref[at, :], down_ref[...], (((1,), (1,)), ((), ())), preferred_element_type=F32
        )
        out_ref[0, at, :] = (dv * pull_ref[0, at, :].astype(F32)).astype(BF16)
        out_ref[1, at, :] = (dv * pull_ref[1, at, :].astype(F32)).astype(BF16)


def head_block(lead, rows):
    return pl.BlockSpec((lead, rows, HS), lambda h: (0, 0, h))


def shared_block(shape):
    return pl.BlockSpec(shape, lambda h: (0,) * len(shape))


def pair_block(seqs):
    return pl.BlockSpec((seqs, 2, CHUNKS, HS), lambda h: (0, 0, 0, h))


PARAMS = pltpu.CompilerParams(vmem_limit_bytes=40 * 1024 * 1024)


def mixer_forward(u, halo, dist, gates, taps, soft):
    seqs, rows, _ = u.shape
    full = head_block(seqs, rows)
    wide = jax.ShapeDtypeStruct((seqs, rows, LRU), F32)
    return pl.pallas_call(
        mixer_forward_kernel,
        grid=(HEADS,),
        in_specs=[
            full,
            head_block(seqs, HALO),
            shared_block((seqs, rows, HS)),
            pl.BlockSpec((1, HS, 2 * HS), lambda h: (h, 0, 0)),
            pl.BlockSpec((CONV, HS), lambda h: (0, h)),
            pl.BlockSpec((1, HS), lambda h: (0, h)),
        ],
        out_specs=[full, full, full, full, pair_block(seqs)],
        out_shape=[
            jax.ShapeDtypeStruct((seqs, rows, LRU), BF16),
            wide,
            wide,
            wide,
            jax.ShapeDtypeStruct((seqs, 2, CHUNKS, LRU), F32),
        ],
        scratch_shapes=[
            pltpu.VMEM((rows + BACK, HS), F32),
            pltpu.VMEM((seqs, rows, HS), F32),
            pltpu.VMEM((seqs, rows, HS), F32),
            pltpu.VMEM((seqs, rows, HS), F32),
        ],
        compiler_params=PARAMS,
        name="mixer_forward",
    )(u, halo, dist, gates, taps, soft)


def mixer_branch(state, prod, carry, gate, shards, core):
    seqs, rows, _ = state.shape
    per = HEADS // shards

    def at(h, core_ref):
        return (0, 0, h)

    def split_at(h, core_ref):
        shard = h // per
        return ((shard % 2 + core_ref[0]) % 2, 0, 0, (shard // 2) * per + h % per)

    full = pl.BlockSpec((seqs, rows, HS), at)
    return pl.pallas_call(
        branch_kernel,
        grid_spec=pltpu.PrefetchScalarGridSpec(
            num_scalar_prefetch=1,
            grid=(HEADS,),
            in_specs=[full, full, pl.BlockSpec((seqs, CHUNKS, HS), at), full],
            out_specs=[full, full, pl.BlockSpec((1, seqs, rows, HS), split_at)],
        ),
        out_shape=[
            jax.ShapeDtypeStruct((seqs, rows, LRU), F32),
            jax.ShapeDtypeStruct((seqs, rows, LRU), BF16),
            jax.ShapeDtypeStruct((2, seqs, rows, LRU // 2), BF16),
        ],
        compiler_params=PARAMS,
        name="mixer_branch",
    )(core.reshape(1), state, prod, carry, gate)


def mixer_reverse(grad, gate, keep, state):
    seqs, rows, _ = grad.shape
    full = head_block(seqs, rows)
    wide = jax.ShapeDtypeStruct((seqs, rows, LRU), F32)
    return pl.pallas_call(
        reverse_kernel,
        grid=(HEADS,),
        in_specs=[full, full, full, full],
        out_specs=[full, full, full, pair_block(seqs)],
        out_shape=[
            jax.ShapeDtypeStruct((seqs, rows, LRU), BF16),
            wide,
            wide,
            jax.ShapeDtypeStruct((seqs, 2, CHUNKS, LRU), F32),
        ],
        compiler_params=PARAMS,
        name="mixer_reverse",
    )(grad, gate, keep, state)


def mixer_backward(local, prod, carry, state, before, c, u, halo, dist, gates, taps, soft):
    seqs, rows, _ = local.shape
    full = head_block(seqs, rows)
    small = head_block(seqs, HALO)
    gate_block = pl.BlockSpec((1, HS, 2 * HS), lambda h: (h, 0, 0))
    row_block = pl.BlockSpec((8, HS), lambda h: (0, h))
    return pl.pallas_call(
        mixer_backward_kernel,
        grid=(HEADS,),
        in_specs=[
            full,
            full,
            head_block(seqs, CHUNKS),
            full,
            small,
            full,
            full,
            small,
            shared_block((seqs, rows, HS)),
            gate_block,
            pl.BlockSpec((CONV, HS), lambda h: (0, h)),
            pl.BlockSpec((1, HS), lambda h: (0, h)),
        ],
        out_specs=[full, head_block(seqs, TAIL), small, gate_block, row_block, row_block],
        out_shape=[
            jax.ShapeDtypeStruct((seqs, rows, LRU), BF16),
            jax.ShapeDtypeStruct((seqs, TAIL, LRU), F32),
            jax.ShapeDtypeStruct((seqs, HALO, LRU), F32),
            jax.ShapeDtypeStruct((HEADS, HS, 2 * HS), F32),
            jax.ShapeDtypeStruct((8, LRU), F32),
            jax.ShapeDtypeStruct((8, LRU), F32),
        ],
        scratch_shapes=[
            pltpu.VMEM((rows, 2 * HS), F32),
            pltpu.VMEM((rows, 2 * HS), BF16),
            pltpu.VMEM((rows + BACK, HS), F32),
            pltpu.VMEM((rows + 8, HS), F32),
            pltpu.VMEM((rows + BACK, HS), F32),
            pltpu.VMEM((rows + BACK, HS), F32),
        ],
        compiler_params=PARAMS,
        name="mixer_backward",
    )(local, prod, carry, state, before, c, u, halo, dist, gates, taps, soft)


def rms_norm(x, gain, shards, core):
    rows = x.shape[0]
    block = min(rows, 256)
    return pl.pallas_call(
        functools.partial(norm_kernel, shards),
        grid=(rows // block,),
        in_specs=[
            pl.BlockSpec(memory_space=pltpu.SMEM),
            pl.BlockSpec((block, D), lambda n: (n, 0)),
            pl.BlockSpec((1, D), lambda n: (0, 0)),
        ],
        out_specs=[
            pl.BlockSpec((block, D), lambda n: (n, 0)),
            pl.BlockSpec((block, D // 2), lambda n: (n, 0)),
            pl.BlockSpec((block, D // 2), lambda n: (n, 0)),
            pl.BlockSpec((block, 128), lambda n: (n, 0)),
        ],
        out_shape=[
            jax.ShapeDtypeStruct((rows, D), BF16),
            jax.ShapeDtypeStruct((rows, D // 2), BF16),
            jax.ShapeDtypeStruct((rows, D // 2), BF16),
            jax.ShapeDtypeStruct((rows, 128), F32),
        ],
        compiler_params=PARAMS,
        name="rms_norm",
    )(core.reshape(1), x, gain.reshape(1, D))


FF_TILE = 512
GATHER_TILE = 768
DOT_TILE = 512


def ffn_forward(normed, proj_up):
    rows = normed.shape[0]
    steps = FF // FF_TILE
    return pl.pallas_call(
        ffn_forward_kernel,
        grid=(steps,),
        in_specs=[
            pl.BlockSpec((rows, D), lambda n: (0, 0)),
            pl.BlockSpec((D, FF_TILE), lambda n: (0, n)),
            pl.BlockSpec((D, FF_TILE), lambda n: (0, n + steps)),
        ],
        out_specs=[
            pl.BlockSpec((rows, FF_TILE), lambda n: (0, n)),
            pl.BlockSpec((2, rows, FF_TILE), lambda n: (0, 0, n)),
        ],
        out_shape=[
            jax.ShapeDtypeStruct((rows, FF), BF16),
            jax.ShapeDtypeStruct((2, rows, FF), BF16),
        ],
        compiler_params=PARAMS,
        name="ffn_forward",
    )(normed, proj_up, proj_up)


def ffn_backward(grad, proj_down, pull):
    rows = grad.shape[0]
    return pl.pallas_call(
        ffn_backward_kernel,
        grid=(FF // FF_TILE,),
        in_specs=[
            pl.BlockSpec((rows, D), lambda n: (0, 0)),
            pl.BlockSpec((FF_TILE, D), lambda n: (n, 0)),
            pl.BlockSpec((2, rows, FF_TILE), lambda n: (0, 0, n)),
        ],
        out_specs=pl.BlockSpec((2, rows, FF_TILE), lambda n: (0, 0, n)),
        out_shape=jax.ShapeDtypeStruct((2, rows, FF), BF16),
        compiler_params=PARAMS,
        name="ffn_backward",
    )(grad, proj_down, pull)


def gather_rows(shard):
    parts = lax.axis_size("grp")
    rows = shard.shape[0] // parts
    own = lax.dynamic_slice_in_dim(shard, lax.axis_index("grp") * rows, rows, 0)
    return lax.all_gather(own, ("seq", "grp"), axis=0, tiled=True)


def tie(value, *after):
    return lax.optimization_barrier((value, *after))[0]


def xor_pairs(axis, bit):
    return [(i, i ^ bit) for i in range(lax.axis_size(axis))]


def ring_pairs(steps):
    count = lax.axis_size("seq")
    return [(i, (i + steps) % count) for i in range(count)]


def same_cores():
    count = lax.axis_size("seq")
    return [list(range(core, count, 2)) for core in range(2)]


def dot_rows(a, b):
    return lax.dot_general(a, b, (((0,), (0,)), ((), ())), preferred_element_type=F32)


def reduce_rows(partial):
    part = lax.psum_scatter(partial, "seq", scatter_dimension=0, tiled=True)
    part = lax.psum_scatter(part, "grp", scatter_dimension=0, tiled=True)
    return lax.all_gather(part, "grp", axis=0, tiled=True).astype(F32)


def dot_far(a, b):
    return lax.dot_general(a, b, (((1,), (1,)), ((), ())), preferred_element_type=F32)


def by_position(a):
    seqs, rows = a.shape[:2]
    return a.reshape(seqs, CHUNKS, rows // CHUNKS, *a.shape[2:]).swapaxes(1, 2).reshape(a.shape)


def by_token(a):
    seqs, rows = a.shape[:2]
    return a.reshape(seqs, rows // CHUNKS, CHUNKS, *a.shape[2:]).swapaxes(1, 2).reshape(a.shape)


def fetch_columns(where_ref, pieces, start, target, sem):
    own, far = pieces[:6], pieces[6:]
    rows, columns = own[0].shape
    width, tile = columns // 4, target.shape[1]
    depth, half = own[1].shape[0], own[4].shape[0]
    chips = depth // rows + 1
    chip, core, group = where_ref[0], where_ref[1], where_ref[2]
    quarter = start // width
    offset = pl.multiple_of(start - quarter * width, 128)
    start = pl.multiple_of(start, 128)
    relation = lax.bitwise_xor(group, quarter)

    def copy(source, row, count):
        place = target.at[pl.ds(pl.multiple_of(row, 16), count), :]
        pltpu.make_async_copy(source, place, sem).start()

    for c, (shard, *parts) in enumerate((own, far)):
        other = lax.rem(core + c, 2)
        copy(shard.at[:, pl.ds(start, tile)], (chip * 2 + other) * rows, rows)
        for j in range(1, chips):
            row = (lax.rem(chip + j, chips) * 2 + other) * rows
            first = (j - 1) * rows
            for k in range(3):

                @pl.when(relation == k)
                def _():
                    copy(parts[k].at[pl.ds(first, rows), pl.ds(offset, tile)], row, rows)

            @pl.when(relation == 3)
            def _():
                for m in range(2):
                    low, high = max(first, m * half), min(first + rows, (m + 1) * half)
                    if low < high:
                        at = pl.ds(low - m * half, high - low)
                        source = parts[3 + m].at[at, pl.ds(offset, tile)]
                        copy(source, row + (low - first), high - low)


def gathered_tiles(fetch, held, sems):
    step, steps = pl.program_id(0), pl.num_programs(0)
    slot = lax.rem(step, 2)

    @pl.when(step == 0)
    def _():
        fetch(step, slot)

    @pl.when(step + 1 < steps)
    def _():
        fetch(step + 1, 1 - slot)

    for side in range(held.shape[1]):
        whole = held.at[slot, side]
        pltpu.make_async_copy(whole, whole, sems.at[slot, side]).wait()
    return slot


def gathered_ffn_kernel(where_ref, n_ref, *refs):
    pieces, (hidden_ref, pull_ref, gate_ref, up_ref, held, sems) = refs[:12], refs[12:]
    tile = hidden_ref.shape[1]

    def fetch(n, slot):
        for side in range(2):
            start = n * tile + side * (pieces[0].shape[1] // 2)
            fetch_columns(where_ref, pieces, start, held.at[slot, side], sems.at[slot, side])

    slot = gathered_tiles(fetch, held, sems)
    gate_ref[...] = held[slot, 0]
    up_ref[...] = held[slot, 1]
    ffn_forward_kernel(n_ref, gate_ref, up_ref, hidden_ref, pull_ref)


def gathered_dot_kernel(base, where_ref, n_ref, *refs):
    pieces, (out_ref, weight_ref, held, sems) = refs[:12], refs[12:]
    tile = out_ref.shape[1]

    def fetch(n, slot):
        start = base + n * tile
        fetch_columns(where_ref, pieces, start, held.at[slot, 0], sems.at[slot, 0])

    slot = gathered_tiles(fetch, held, sems)
    weight_ref[...] = held[slot, 0]
    out_ref[...] = jnp.dot(n_ref[...], weight_ref[...], preferred_element_type=F32).astype(
        out_ref.dtype
    )


class Gather:
    def __init__(self, shard, *after, offload=False):
        self.shard = shard
        self.chips = lax.axis_size("seq") // 2
        half = (self.chips - 1) * shard.shape[0] // 2
        self.simple = lax.axis_size("grp") != 4 or half % 16 != 0
        if self.simple:
            self.whole = gather_rows(shard)
            return
        group = lax.axis_index("grp")
        width = shard.shape[1] // 4
        own = lax.dynamic_slice_in_dim(shard, group * width, width, 1)
        if after:
            own = tie(own, *after)
        if offload:
            self.slabs = lax.all_gather(own, "seq", axis_index_groups=same_cores())
        else:
            self.slabs = [
                lax.ppermute(own, "seq", ring_pairs(-2 * j)) for j in range(1, self.chips)
            ]
        self.half = half

    def first(self, *after):
        if self.simple:
            return ()
        slabs = tie(self.slabs, *after) if after else self.slabs
        if not isinstance(slabs, list):
            chip = lax.axis_index("seq") // 2
            slabs = [
                lax.dynamic_index_in_dim(slabs, (chip + j) % self.chips, 0, False)
                for j in range(1, self.chips)
            ]
        self.near = jnp.concatenate(slabs, axis=0)
        self.from_x = lax.ppermute(self.near, "grp", xor_pairs("grp", 1))
        self.from_y = lax.ppermute(self.near, "grp", xor_pairs("grp", 2))
        return (self.near,)

    def second(self, *after):
        if self.simple:
            return ()
        if after:
            self.from_x, self.from_y = tie((self.from_x, self.from_y), *after)
        self.halves = (self.from_y[: self.half], self.from_x[self.half :])
        return self.halves

    def third(self):
        if self.simple:
            return
        diag_a = lax.ppermute(self.halves[0], "grp", xor_pairs("grp", 1))
        diag_b = lax.ppermute(self.halves[1], "grp", xor_pairs("grp", 2))
        own = (self.shard, self.near, self.from_x, self.from_y, diag_a, diag_b)
        far = tuple(lax.ppermute(piece, "seq", xor_pairs("seq", 1)) for piece in own)
        place = lax.axis_index("seq")
        where = jnp.stack([place // 2, place % 2, lax.axis_index("grp")]).astype(jnp.int32)
        self.pieces = (where, own, far)

    def call(self, kernel, normed, steps, tile, weights, out_specs, out_shape, name):
        where, own, far = self.pieces
        rows, depth = normed.shape
        return pl.pallas_call(
            kernel,
            grid=(steps,),
            in_specs=[
                pl.BlockSpec(memory_space=pltpu.SMEM),
                pl.BlockSpec((rows, depth), lambda n: (0, 0)),
            ]
            + [pl.BlockSpec(memory_space=pl.ANY)] * 12,
            out_specs=out_specs + [pl.BlockSpec((depth, tile), lambda n: (0, n))] * weights,
            out_shape=out_shape + [jax.ShapeDtypeStruct((depth, steps * tile), BF16)] * weights,
            scratch_shapes=[
                pltpu.VMEM((2, weights, depth, tile), BF16),
                pltpu.SemaphoreType.DMA((2, weights)),
            ],
            compiler_params=pltpu.CompilerParams(vmem_limit_bytes=56 * 1024 * 1024),
            name=name,
        )(where, normed, *own, *far)

    def dot(self, normed, half, dtype):
        columns = self.shard.shape[1] // 2
        base = half * columns
        if self.simple:
            weight = self.whole[:, base : base + columns]
            return jnp.dot(normed, weight, preferred_element_type=F32).astype(dtype), weight
        rows, tile = normed.shape[0], DOT_TILE
        return self.call(
            functools.partial(gathered_dot_kernel, base),
            normed,
            columns // tile,
            tile,
            1,
            [pl.BlockSpec((rows, tile), lambda n: (0, n))],
            [jax.ShapeDtypeStruct((rows, columns), dtype)],
            "gathered_dot",
        )

    def ffn_forward(self, normed):
        if self.simple:
            hidden, pull = ffn_forward(normed, self.whole)
            return hidden, pull, self.whole[:, :FF], self.whole[:, FF:]
        rows, tile = normed.shape[0], GATHER_TILE
        return self.call(
            gathered_ffn_kernel,
            normed,
            FF // tile,
            tile,
            2,
            [
                pl.BlockSpec((rows, tile), lambda n: (0, n)),
                pl.BlockSpec((2, rows, tile), lambda n: (0, 0, n)),
            ],
            [
                jax.ShapeDtypeStruct((rows, FF), BF16),
                jax.ShapeDtypeStruct((2, rows, FF), BF16),
            ],
            "gathered_ffn",
        )


class Reduction:
    def __init__(self, a_own, a_far, columns, width, fused=False):
        self.simple = lax.axis_size("grp") != 4
        count = lax.axis_size("seq")
        place = lax.axis_index("seq")
        self.chips = count // 2
        self.chip, core = place // 2, place % 2
        self.width = width
        full = a_own.shape[1]
        self.rows = full // self.chips
        self.half = full // 2
        self.a_own = a_own
        if self.simple:
            parts = [columns(k) for k in range(4)]
            own, far = (
                jnp.concatenate([dot_rows(a, part) for part in parts], axis=1)
                for a in (a_own, a_far)
            )
            cores = jnp.stack(
                [jnp.where(core == c, own, far).reshape(self.chips, self.rows, -1) for c in (0, 1)],
                axis=1,
            )
            self.product = cores.reshape(2 * full, 4 * width).astype(BF16)
            self.arrived = self.product
            self.sent = (self.product,)
            return
        group = lax.axis_index("grp")
        self.x, self.y = xor_pairs("grp", 1), xor_pairs("grp", 2)
        self.b = [columns(group ^ k) for k in range(4)]
        self.far = [None] * 4
        self.product = None
        other = xor_pairs("seq", 1)
        if fused:
            b_all = jnp.concatenate(self.b, axis=1)
            far = lax.ppermute(dot_rows(a_far, b_all).astype(BF16), "seq", other)
            self.product = (dot_rows(a_own, b_all) + far.astype(F32)).astype(BF16)
        for k in () if fused else (3, 1, 2, 0):
            product = dot_rows(a_far, self.b[k]).astype(BF16)
            self.far[k] = lax.ppermute(product, "seq", other)
        half = self.half
        self.sent = (
            self.own(3, 0, half).astype(BF16),
            self.own(3, half, full).astype(BF16),
        )
        self.diag_a = lax.ppermute(self.sent[0], "grp", self.x)
        self.diag_b = lax.ppermute(self.sent[1], "grp", self.y)

    def own(self, k, first, last):
        if self.product is not None:
            left = k * self.width
            return self.product[first:last, left : left + self.width].astype(F32)
        product = dot_rows(self.a_own[:, first:last], self.b[k])
        return product + self.far[k][first:last].astype(F32)

    def second(self, *after):
        if self.simple:
            return ()
        full, none = 2 * self.half, ((0, self.half), (0, 0))
        diag_a, diag_b = self.diag_a, self.diag_b
        if after:
            diag_a, diag_b = tie((diag_a, diag_b), *after)
        sent = (
            (self.own(1, 0, full) + jnp.pad(diag_b.astype(F32), (none[0][::-1], (0, 0)))).astype(BF16),
            (self.own(2, 0, full) + jnp.pad(diag_a.astype(F32), none)).astype(BF16),
        )
        self.from_x = lax.ppermute(sent[0], "grp", self.x)
        self.from_y = lax.ppermute(sent[1], "grp", self.y)
        return sent

    def mine(self, *after):
        from_x, from_y = self.from_x, self.from_y
        if after:
            from_x, from_y = tie((from_x, from_y), *after)
        mine = self.own(0, 0, 2 * self.half) + from_x.astype(F32) + from_y.astype(F32)
        return mine.astype(BF16)

    def along_z(self, mine):
        mine = mine.reshape(self.chips, self.rows, -1)
        self.kept = lax.dynamic_index_in_dim(mine, self.chip, 0, False)
        sent = tuple(
            lax.dynamic_index_in_dim(mine, (self.chip + j) % self.chips, 0, False)
            for j in range(1, self.chips)
        )
        self.arrived = [
            lax.ppermute(part, "seq", ring_pairs(2 * j + 2)) for j, part in enumerate(sent)
        ]
        return sent

    def third(self, *after, offload=False):
        if self.simple:
            return ()
        mine = self.mine(*after)
        if not offload:
            return self.along_z(mine)
        self.kept = None
        self.arrived = lax.psum_scatter(
            mine, "seq", scatter_dimension=0, axis_index_groups=same_cores(), tiled=True
        )
        return (mine,)

    def total(self):
        if self.kept is None:
            return self.arrived
        total = self.kept.astype(F32)
        for part in self.arrived:
            total = total + part.astype(F32)
        return total

    def finish(self, *after):
        if self.simple:
            return reduce_rows(self.product)
        total = self.total()
        if after:
            total = tie(total, *after)
        parts = lax.all_gather(total.astype(BF16), "grp")
        return parts.transpose(1, 0, 2).reshape(self.rows, 4 * self.width).astype(F32)


def shard_carry(ends, prods, reverse):
    count = lax.axis_size("seq")
    place = lax.axis_index("seq")
    both = lax.all_gather(jnp.stack([ends, prods]), "seq")
    carry = jnp.zeros_like(ends)
    for step in range(count - 1):
        source = count - 1 - step if reverse else step
        ahead = source > place if reverse else source < place
        carry = jnp.where(ahead, both[source, 0] + both[source, 1] * carry, carry)
    return carry


def chunk_ends(chunks, reverse):
    state = jnp.zeros_like(chunks[:, 0, 0])
    prod = jnp.ones_like(state)
    order = range(CHUNKS - 1, -1, -1) if reverse else range(CHUNKS)
    for n in order:
        state = chunks[:, 0, n] + chunks[:, 1, n] * state
        prod = chunks[:, 1, n] * prod
    return state, prod


def chunk_carries(chunks, carry, reverse):
    order = range(CHUNKS - 1, -1, -1) if reverse else range(CHUNKS)
    found = [None] * CHUNKS
    for n in order:
        found[n] = carry
        carry = chunks[:, 0, n] + chunks[:, 1, n] * carry
    return jnp.stack(found, axis=1)


def norm_back(values, scale, gain, grad_normed):
    weighted = grad_normed * gain
    cubed = scale * scale * scale
    return scale * weighted - values * cubed * jnp.mean(weighted * values, axis=-1, keepdims=True)


def gain_grad(weight, grad_weight, gain):
    return jnp.sum(weight.astype(F32) * grad_weight, axis=1) / gain.astype(F32)


def body(
    tokens, seg_ids, cotangent, first_gain, in_proj, conv_taps, decay_param, gate_heads,
    out_proj, second_gain, up_proj, down_proj,
):
    seq_count, shard_len, _ = tokens.shape
    row_count = seq_count * shard_len
    edge_len = CONV - 1
    place = lax.axis_index("seq")
    last = lax.axis_size("seq") - 1

    small = jnp.concatenate(
        [first_gain, second_gain, decay_param, conv_taps.reshape(-1)]
    )
    small_all = lax.all_gather(small, "seq")
    n_gain, n_lru = first_gain.shape[0], decay_param.shape[0]
    gain_one = small_all[:, :n_gain].reshape(D).astype(F32)
    gain_two = small_all[:, n_gain : 2 * n_gain].reshape(D).astype(F32)
    decay_float = small_all[:, 2 * n_gain : 2 * n_gain + n_lru].reshape(LRU).astype(F32)
    taps_all = (
        small_all[:, 2 * n_gain + n_lru :].reshape(-1, CONV, n_lru).transpose(1, 0, 2)
    ).reshape(CONV, LRU).astype(F32)
    in_gather = Gather(in_proj)
    near = in_gather.first()
    in_gather.second()
    in_gather.third()
    gates_all = lax.all_gather(gate_heads, "seq", axis=0, tiled=True)
    up_gather = Gather(up_proj, gates_all, *near, offload=True)
    proj_out = gather_rows(out_proj)
    proj_down = gather_rows(down_proj)

    tokens = by_position(tokens)
    cotangent = by_position(cotangent)
    inputs = tokens.reshape(row_count, D).astype(F32)
    first_normed, first_own, first_far, first_scale = rms_norm(
        tokens.reshape(row_count, D), gain_one, last + 1, place % 2
    )
    first_scale = first_scale[:, :1]
    wide = (seq_count, shard_len, LRU)
    inner_low, in_value = in_gather.dot(first_normed, 0, BF16)
    inner_low = inner_low.reshape(wide)

    step = shard_len // CHUNKS
    final = inner_low.reshape(seq_count, step, CHUNKS, LRU)[:, step - HALO :, CHUNKS - 1]
    prev_inner = from_behind(final, "seq", 1)
    prev_ids = from_behind(seg_ids[:, shard_len - edge_len :], "seq", 1)
    prev_ids = jnp.where(place == 0, -1, prev_ids)
    ext_ids = jnp.concatenate([prev_ids, seg_ids], axis=1)
    dist = jnp.zeros((seq_count, shard_len), F32)
    for k in range(1, CONV):
        dist = dist + (ext_ids[:, edge_len - k : edge_len - k + shard_len] == seg_ids).astype(F32)
    dist = jnp.broadcast_to(by_position(dist)[:, :, None], (seq_count, shard_len, HS))
    soft = jax.nn.softplus(-decay_float).reshape(1, LRU)

    conv_low, keep, state_part, prod_part, chunks = mixer_forward(
        tie(inner_low, *up_gather.first(inner_low)), prev_inner, dist, gates_all, taps_all, soft
    )
    end_state, end_prod = chunk_ends(chunks, False)
    gate_pre, in_gate = in_gather.dot(first_normed, 1, F32)
    gate_pre = gate_pre.reshape(wide)
    carry_in = shard_carry(end_state, end_prod, False)
    carries = chunk_carries(chunks, carry_in, False)
    state, branch, branch_split = mixer_branch(
        tie(state_part, *up_gather.second(carries, gate_pre)), prod_part, carries, gate_pre, last + 1, place % 2
    )
    branch_split = branch_split.reshape(2, row_count, LRU // 2)
    resid = inputs + jnp.dot(
        branch.reshape(row_count, LRU), proj_out, preferred_element_type=F32
    )
    second_normed, second_own, second_far, second_scale = rms_norm(
        resid, gain_two, last + 1, place % 2
    )
    second_scale = second_scale[:, :1]
    up_gather.third()
    hidden, pull, proj_gate, proj_up = up_gather.ffn_forward(second_normed)

    grad_out = cotangent.reshape(row_count, D)
    grad_down = dot_rows(hidden, grad_out).astype(BF16)
    down_part = lax.psum_scatter(grad_down, ("seq", "grp"), scatter_dimension=0, tiled=True)
    grad_expanded = ffn_backward(tie(grad_out, grad_down), proj_down, pull)
    quarter = FF // 2

    def up_columns(n):
        part = lax.dynamic_slice(
            grad_expanded, (n // 2, 0, (n % 2) * quarter), (1, row_count, quarter)
        )
        return part[0]

    up_sum = Reduction(second_own, second_far, up_columns, quarter)
    grad_expanded = tie(grad_expanded, *up_sum.sent)
    grad_second_normed = dot_far(grad_expanded[0], proj_gate) + dot_far(
        grad_expanded[1], proj_up
    )
    sent = up_sum.second(grad_second_normed)
    grad_second_normed = tie(grad_second_normed, *sent)
    grad_resid = grad_out.astype(F32) + norm_back(
        resid, second_scale, gain_two, grad_second_normed
    )
    grad_mixer = grad_resid.astype(BF16)
    grad_branch = dot_far(grad_mixer, proj_out)

    grad_gate, local, rev_prod, rev_chunks = mixer_reverse(
        grad_branch.reshape(wide), gate_pre, keep, state
    )
    down_sum = lax.all_gather(tie(down_part, rev_chunks), "grp", axis=0, tiled=True)
    head_pull, head_prod = chunk_ends(rev_chunks, True)
    grad_gate = grad_gate.reshape(row_count, LRU)
    width = LRU // 4
    rev_carry = shard_carry(head_pull, head_prod, True)
    rev_carries = chunk_carries(rev_chunks, rev_carry, True)
    grad_mixer, grad_gate = tie((grad_mixer, grad_gate), rev_carry)
    out_sum = Reduction(
        branch_split[0],
        branch_split[1],
        lambda n: lax.dynamic_slice_in_dim(grad_mixer, n * (D // 4), D // 4, 1),
        D // 4,
        True,
    )
    in_gate_sum = Reduction(
        first_own,
        first_far,
        lambda n: lax.dynamic_slice_in_dim(grad_gate, n * width, width, 1),
        width,
        True,
    )
    sent = (*out_sum.sent, *in_gate_sum.sent)
    sent = up_sum.third(down_sum, *sent, offload=True)
    local = tie(local, *sent)
    du, tail, edge, grad_gates, grad_taps, grad_decay = mixer_backward(
        local, rev_prod, rev_carries, state, carries, conv_low, inner_low,
        prev_inner, dist, gates_all, taps_all, soft,
    )
    returned = from_behind(edge[:, HALO - edge_len :].astype(BF16), "seq", -1).astype(F32)
    grad_gate = tie(grad_gate, *out_sum.second(edge), *in_gate_sum.second(edge))
    first_grad = dot_far(grad_gate, in_gate)
    groups = TAIL // CHUNKS
    padded = jnp.pad(
        returned[:, :, None, :], ((0, 0), (groups - edge_len, 0), (CHUNKS - 1, 0), (0, 0))
    ).reshape(seq_count, TAIL, LRU)
    grad_inner = lax.dynamic_update_slice(
        du, (tail + padded).astype(BF16), (0, shard_len - TAIL, 0)
    )
    grad_inner = tie(grad_inner, first_grad).reshape(row_count, LRU)
    in_value_sum = Reduction(
        first_own,
        first_far,
        lambda n: lax.dynamic_slice_in_dim(grad_inner, n * width, width, 1),
        width,
        True,
    )
    grad_inner = tie(grad_inner, *in_value_sum.sent)

    shards = last + 1
    grad_decay_row = grad_decay[0] * jax.nn.sigmoid(-decay_float)
    flat = jnp.concatenate(
        [
            grad_gates.reshape(shards, -1, HS),
            grad_taps[:CONV].reshape(CONV, shards, -1, HS).swapaxes(0, 1).reshape(shards, -1, HS),
            grad_decay_row.reshape(shards, -1, HS),
        ],
        axis=1,
    )
    lines = flat.shape[1]
    flat = jnp.pad(flat, ((0, 0), (0, -lines % 16), (0, 0))).astype(BF16).reshape(-1, HS)
    flat = lax.psum_scatter(flat, "seq", scatter_dimension=0, tiled=True)
    first_grad = first_grad + dot_far(grad_inner, in_value)
    sent = in_value_sum.second(first_grad)
    out_sum.third(*sent)
    flat = lax.all_gather(tie(flat, *sent), "grp").astype(F32)
    flat = jnp.sum(flat, axis=0)[:lines].reshape(-1)
    n_gates = flat.shape[0] - (CONV + 1) * n_lru
    gates_total = flat[:n_gates].reshape(gate_heads.shape)
    taps_total = flat[n_gates : n_gates + CONV * n_lru].reshape(CONV, n_lru)
    decay_total = flat[n_gates + CONV * n_lru :]

    up_total = up_sum.finish(edge)
    down_total = tie(down_sum, *sent).astype(F32)
    if in_value_sum.simple:
        in_total = jnp.concatenate([in_value_sum.finish(), in_gate_sum.finish()], axis=1)
        last_sent = ()
    else:
        both = jnp.concatenate([in_value_sum.mine(), in_gate_sum.mine()], axis=1)
        last_sent = in_value_sum.along_z(both)
        both = in_value_sum.total().astype(BF16)
        in_total = jnp.concatenate(
            [
                lax.all_gather(both[:, n * width : (n + 1) * width], "grp")
                .transpose(1, 0, 2)
                .reshape(-1, LRU)
                for n in range(2)
            ],
            axis=1,
        ).astype(F32)
    out_total = out_sum.finish(*last_sent)
    ffn_out = jnp.dot(tie(hidden, *sent), proj_down, preferred_element_type=F32)
    block_out = by_token((resid + ffn_out).astype(BF16).reshape(tokens.shape))
    grad_tokens = grad_resid + norm_back(inputs, first_scale, gain_one, first_grad)
    grad_tokens = by_token(grad_tokens.astype(BF16).reshape(tokens.shape))
    first_total = gain_grad(in_proj, in_total, first_gain)
    second_total = gain_grad(up_proj, up_total, second_gain)
    return (
        block_out, grad_tokens, first_total, in_total, taps_total, decay_total, gates_total,
        out_total, second_total, up_total, down_total,
    )


def solution(mesh):
    in_specs = (
        P("grp", "seq", None),
        P("grp", "seq"),
        P("grp", "seq", None),
        P("seq"),
        P("seq", None),
        P(None, "seq"),
        P("seq"),
        P("seq", None, None),
        P("seq", None),
        P("seq"),
        P("seq", None),
        P("seq", None),
    )
    out_specs = (
        P("grp", "seq", None),
        P("grp", "seq", None),
        P("seq"),
        P("seq", None),
        P(None, "seq"),
        P("seq"),
        P("seq", None, None),
        P("seq", None),
        P("seq"),
        P("seq", None),
        P("seq", None),
    )
    return jax.shard_map(body, mesh=mesh, in_specs=in_specs, out_specs=out_specs, check_vma=False)
```

```python
import functools

import jax
import jax.numpy as jnp
from jax import lax
from jax.experimental import pallas as pl
from jax.experimental.pallas import tpu as pltpu
from jax.sharding import PartitionSpec as P

D = 1536
HEADS = 16
HS = 128
LRU = 2048
FF = 4608
CONV = 4
CHUNKS = 8
HALO = 8
BACK = 8 * (CONV - 1)
TAIL = 32
F32 = jnp.float32
BF16 = jnp.bfloat16


def from_behind(value, axis, steps):
    count = lax.axis_size(axis)
    first, last = (max(0, -steps), min(count, count - steps))
    return lax.ppermute(value, axis, [(source, source + steps) for source in range(first, last)])


def gelu_parts(v):
    k = 0.7978845608028654
    square = v * v
    t = jnp.tanh(k * v * (1.0 + 0.044715 * square))
    half = 0.5 * (1.0 + t)
    slope = half + 0.5 * v * (1.0 - t * t) * (k * (1.0 + 3.0 * 0.044715 * square))
    return v * half, slope


def gelu_tanh(v):
    k = 0.7978845608028654
    return 0.5 * v * (1.0 + jnp.tanh(k * v * (1.0 + 0.044715 * v * v)))


def sigmoid(v):
    return 0.5 * jnp.tanh(0.5 * v) + 0.5


def drive_values(q_rate, q_input, soft):
    rate = sigmoid(q_rate)
    inp = sigmoid(q_input)
    decay = jnp.exp(-8.0 * rate * soft)
    square = 1.0 - decay * decay + 0.001
    inverse = lax.rsqrt(square)
    return rate, inp, decay, square * inverse, inverse


def shifted_group(group, step, fill):
    row = lax.broadcasted_iota(jnp.int32, group.shape, 0)
    edge = 0 if step == 1 else CHUNKS - 1
    moved = pltpu.roll(group, step % CHUNKS, 0)
    return jnp.where(row == edge, fill, moved)


def extend_back(ext_s, u_ref, halo_ref, b):
    rows = u_ref.shape[1]
    ext_s[pl.ds(BACK, rows), :] = u_ref[b].astype(F32)
    halo = halo_ref[b].astype(F32)
    for m in range(CONV - 1):
        group = ext_s[pl.ds(BACK + rows - BACK + 8 * m, 8), :]
        fill = halo[HALO - CONV + 1 + m : HALO - CONV + 2 + m, :]
        ext_s[pl.ds(8 * m, 8), :] = shifted_group(group, 1, fill)


def mixer_forward_kernel(
    u_ref, halo_ref, dist_ref, gates_ref, taps_ref, soft_ref,
    c_ref, keep_ref, state_ref, prod_ref, chunk_ref,
    ext_s, c_s, rate_s, inp_s,
):
    seqs, rows, _ = u_ref.shape
    soft = soft_ref[...]
    for b in range(seqs):
        extend_back(ext_s, u_ref, halo_ref, b)

        def conv_chunk(n, _):
            at = pl.multiple_of(n * 64, 64)
            far = dist_ref[b, pl.ds(at, 64), :]
            total = taps_ref[0:1, :] * ext_s[pl.ds(at + BACK, 64), :]
            for k in range(1, CONV):
                window = taps_ref[k : k + 1, :] * ext_s[pl.ds(at + BACK - 8 * k, 64), :]
                total = total + jnp.where(far >= float(k), window, 0.0)
            low = total.astype(BF16)
            c_ref[b, pl.ds(at, 64), :] = low
            c_s[b, pl.ds(at, 64), :] = low.astype(F32)
            return 0

        lax.fori_loop(0, rows // 64, conv_chunk, 0)
        both = jnp.dot(c_ref[b], gates_ref[0], preferred_element_type=F32)
        rate_s[b] = both[:, :HS]
        inp_s[b] = both[:, HS:]

    def scan_step(j, carry):
        new = []
        for b in range(seqs):
            at = pl.ds(pl.multiple_of(j * 8, 8), 8)
            state, prod = carry[b]
            _, inp, decay, root, _ = drive_values(rate_s[b, at, :], inp_s[b, at, :], soft)
            keep = jnp.where(dist_ref[b, at, :] >= 1.0, decay, 0.0)
            state = keep * state + root * inp * c_s[b, at, :]
            prod = keep * prod
            keep_ref[b, at, :] = keep
            state_ref[b, at, :] = state
            prod_ref[b, at, :] = prod
            new.append((state, prod))
        return tuple(new)

    zero, one = jnp.zeros((CHUNKS, HS), F32), jnp.ones((CHUNKS, HS), F32)
    ends = lax.fori_loop(0, rows // CHUNKS, scan_step, ((zero, one),) * seqs, unroll=8)
    for b in range(seqs):
        chunk_ref[b, 0] = ends[b][0]
        chunk_ref[b, 1] = ends[b][1]


def branch_kernel(
    per, core_ref, state_ref, prod_ref, carry_ref, gate_ref, out_ref, branch_ref, own_ref, far_ref
):
    seqs, rows, _ = state_ref.shape
    for b in range(seqs):
        carry = jnp.concatenate([carry_ref[b]] * 4, axis=0)

        def point(n, _):
            at = pl.ds(pl.multiple_of(n * 32, 32), 32)
            state = state_ref[b, at, :] + prod_ref[b, at, :] * carry
            out_ref[b, at, :] = state
            low = (state * gelu_tanh(gate_ref[b, at, :])).astype(BF16)
            branch_ref[b, at, :] = low
            return 0

        lax.fori_loop(0, rows // 32, point, 0, unroll=4)
    own = (pl.program_id(0) // per) % 2 == core_ref[0]

    @pl.when(own)
    def _():
        own_ref[...] = branch_ref[...]

    @pl.when(jnp.logical_not(own))
    def _():
        far_ref[...] = branch_ref[...]


def reverse_kernel(
    grad_ref, gate_ref, keep_ref, state_ref,
    dg_ref, local_ref, prod_ref, chunk_ref,
):
    seqs, rows, _ = grad_ref.shape
    pairs = rows // 16

    def scan_step(n, carry):
        first = pl.multiple_of((pairs - 1 - n) * 16, 16)
        at = pl.ds(first, 16)
        new = []
        for b in range(seqs):
            pull, prod = carry[b]
            act, slope = gelu_parts(gate_ref[b, at, :])
            grad = grad_ref[b, at, :]
            dg_ref[b, at, :] = (grad * state_ref[b, at, :] * slope).astype(BF16)
            dh = grad * act
            keep = keep_ref[b, at, :]
            late = dh[8:] + pull
            late_prod = prod
            pull, prod = keep[8:] * late, keep[8:] * prod
            early = dh[:8] + pull
            local_ref[b, at, :] = jnp.concatenate([early, late], axis=0)
            prod_ref[b, at, :] = jnp.concatenate([prod, late_prod], axis=0)
            new.append((keep[:8] * early, keep[:8] * prod))
        return tuple(new)

    zero, one = jnp.zeros((CHUNKS, HS), F32), jnp.ones((CHUNKS, HS), F32)
    ends = lax.fori_loop(0, pairs, scan_step, ((zero, one),) * seqs, unroll=4)
    for b in range(seqs):
        chunk_ref[b, 0] = ends[b][0]
        chunk_ref[b, 1] = ends[b][1]


def mixer_backward_kernel(
    local_ref, prod_ref, carry_ref, state_ref, before_ref, c_ref, u_ref, halo_ref, dist_ref,
    gates_ref, taps_ref, soft_ref,
    du_ref, tail_ref, edge_ref, ggate_ref, gtaps_ref, gdecay_ref,
    q_s, dq_s, dc_s, h_s, ext_s, dist_s,
):
    seqs, rows, _ = local_ref.shape
    soft = soft_ref[...]
    ggate = jnp.zeros((HS, 2 * HS), F32)
    decay_sum = jnp.zeros((8, HS), F32)
    taps_sum = [jnp.zeros((8, HS), F32) for _ in range(CONV)]

    def fold(value):
        return jnp.sum(value.reshape(value.shape[0] // 8, 8, HS), axis=0)

    for b in range(seqs):
        q_s[...] = jnp.dot(c_ref[b], gates_ref[0], preferred_element_type=F32)
        h_s[pl.ds(0, 8), :] = before_ref[b]
        h_s[pl.ds(8, rows), :] = state_ref[b]
        carry = jnp.concatenate([carry_ref[b]] * 4, axis=0)

        def point(n, total):
            first = pl.multiple_of(n * 32, 32)
            at = pl.ds(first, 32)
            lam = local_ref[b, at, :] + prod_ref[b, at, :] * carry
            rate, inp, decay, root, inverse = drive_values(q_s[at, :HS], q_s[at, HS:], soft)
            conv = c_ref[b, at, :].astype(F32)
            kept = jnp.where(dist_ref[b, at, :] >= 1.0, h_s[at, :], 0.0)
            lam_root = lam * root
            lam_inp = lam * inp
            grad_decay = lam * kept - lam_inp * conv * decay * inverse
            rated = grad_decay * decay * rate
            dq_s[at, :HS] = (-8.0 * soft * rated * (1.0 - rate)).astype(BF16)
            dq_s[at, HS:] = (lam_root * conv * inp * (1.0 - inp)).astype(BF16)
            dc_s[at, :] = lam_root * inp
            return total + fold(rated)

        decay_sum = lax.fori_loop(0, rows // 32, point, decay_sum, unroll=2)
        dc_s[pl.ds(0, rows), :] += lax.dot_general(
            dq_s[...], gates_ref[0], (((1,), (1,)), ((), ())), preferred_element_type=F32
        )
        ggate = ggate + lax.dot_general(
            c_ref[b], dq_s[...], (((0,), (0,)), ((), ())), preferred_element_type=F32
        )
        extend_back(ext_s, u_ref, halo_ref, b)
        dist_s[pl.ds(0, rows), :] = dist_ref[b]
        for m in range(CONV - 1):
            for held in (dc_s, dist_s):
                held[pl.ds(rows + 8 * m, 8), :] = shifted_group(held[pl.ds(8 * m, 8), :], -1, 0.0)

        def conv_chunk(n, totals):
            at = pl.multiple_of(n * 64, 64)
            grad = dc_s[pl.ds(at, 64), :]
            far = dist_s[pl.ds(at, 64), :]
            out = taps_ref[0:1, :] * grad
            totals = list(totals)
            totals[0] = totals[0] + fold(grad * ext_s[pl.ds(at + BACK, 64), :])
            for k in range(1, CONV):
                masked = jnp.where(far >= float(k), grad, 0.0)
                totals[k] = totals[k] + fold(masked * ext_s[pl.ds(at + BACK - 8 * k, 64), :])
                ahead = pl.ds(at + 8 * k, 64)
                value = taps_ref[k : k + 1, :] * dc_s[ahead, :]
                out = out + jnp.where(dist_s[ahead, :] >= float(k), value, 0.0)
            du_ref[b, pl.ds(at, 64), :] = out.astype(BF16)

            @pl.when(n == rows // 64 - 1)
            def _():
                tail_ref[b] = out[64 - TAIL :, :]

            return tuple(totals)

        taps_sum = list(lax.fori_loop(0, rows // 64, conv_chunk, tuple(taps_sum)))
        edges = [jnp.zeros((HALO - CONV + 1, HS), F32)]
        for m in range(CONV - 1, 0, -1):
            edge = jnp.zeros((1, HS), F32)
            for k in range(m, CONV):
                at = pl.ds(8 * (k - m), 1)
                masked = jnp.where(dist_s[at, :] >= float(k), dc_s[at, :], 0.0)
                edge = edge + taps_ref[k : k + 1, :] * masked
            edges.append(edge)
        edge_ref[b] = jnp.concatenate(edges, axis=0)
    ggate_ref[0] = ggate
    gdecay_ref[...] = jnp.broadcast_to(
        8.0 * jnp.sum(decay_sum, axis=0, keepdims=True), (8, HS)
    )
    gtaps_ref[...] = jnp.concatenate(
        [jnp.sum(t, axis=0, keepdims=True) for t in taps_sum] + [jnp.zeros((8 - CONV, HS), F32)],
        axis=0,
    )


def norm_kernel(shards, core_ref, x_ref, gain_ref, normed_ref, own_ref, far_ref, scale_ref):
    x = x_ref[...].astype(F32)
    scale = lax.rsqrt(jnp.mean(x * x, axis=-1, keepdims=True) + 1e-06)
    low = (x * scale * gain_ref[...]).astype(BF16)
    normed_ref[...] = low
    scale_ref[...] = jnp.broadcast_to(scale, scale_ref.shape)
    wide = low.astype(F32)
    size = D // shards
    even, odd = (
        jnp.concatenate([wide[:, n * size : (n + 1) * size] for n in range(c, shards, 2)], axis=1)
        for c in range(2)
    )
    first = core_ref[0] == 0
    own_ref[...] = jnp.where(first, even, odd).astype(BF16)
    far_ref[...] = jnp.where(first, odd, even).astype(BF16)


def ffn_forward_kernel(n_ref, gate_ref, up_ref, hidden_ref, pull_ref):
    for m in range(0, n_ref.shape[0], 256):
        at = pl.ds(m, 256)
        e1 = jnp.dot(n_ref[at, :], gate_ref[...], preferred_element_type=F32)
        e2 = jnp.dot(n_ref[at, :], up_ref[...], preferred_element_type=F32)
        act, slope = gelu_parts(e1)
        hidden_ref[at, :] = (act * e2).astype(BF16)
        pull_ref[0, at, :] = (slope * e2).astype(BF16)
        pull_ref[1, at, :] = act.astype(BF16)


def ffn_backward_kernel(grad_ref, down_ref, pull_ref, out_ref):
    for m in range(0, grad_ref.shape[0], 256):
        at = pl.ds(m, 256)
        dv = lax.dot_general(
            grad_ref[at, :], down_ref[...], (((1,), (1,)), ((), ())), preferred_element_type=F32
        )
        out_ref[0, at, :] = (dv * pull_ref[0, at, :].astype(F32)).astype(BF16)
        out_ref[1, at, :] = (dv * pull_ref[1, at, :].astype(F32)).astype(BF16)


def head_block(lead, rows):
    return pl.BlockSpec((lead, rows, HS), lambda h: (0, 0, h))


def shared_block(shape):
    return pl.BlockSpec(shape, lambda h: (0,) * len(shape))


def pair_block(seqs):
    return pl.BlockSpec((seqs, 2, CHUNKS, HS), lambda h: (0, 0, 0, h))


VMEM_BYTES = 60 * 1024 * 1024
PARAMS = pltpu.CompilerParams(vmem_limit_bytes=VMEM_BYTES)


def mixer_forward(u, halo, dist, gates, taps, soft):
    seqs, rows, _ = u.shape
    full = head_block(seqs, rows)
    wide = jax.ShapeDtypeStruct((seqs, rows, LRU), F32)
    return pl.pallas_call(
        mixer_forward_kernel,
        grid=(HEADS,),
        in_specs=[
            full,
            head_block(seqs, HALO),
            shared_block((seqs, rows, HS)),
            pl.BlockSpec((1, HS, 2 * HS), lambda h: (h, 0, 0)),
            pl.BlockSpec((CONV, HS), lambda h: (0, h)),
            pl.BlockSpec((1, HS), lambda h: (0, h)),
        ],
        out_specs=[full, full, full, full, pair_block(seqs)],
        out_shape=[
            jax.ShapeDtypeStruct((seqs, rows, LRU), BF16),
            wide,
            wide,
            wide,
            jax.ShapeDtypeStruct((seqs, 2, CHUNKS, LRU), F32),
        ],
        scratch_shapes=[
            pltpu.VMEM((rows + BACK, HS), F32),
            pltpu.VMEM((seqs, rows, HS), F32),
            pltpu.VMEM((seqs, rows, HS), F32),
            pltpu.VMEM((seqs, rows, HS), F32),
        ],
        compiler_params=PARAMS,
        name="mixer_forward",
    )(u, halo, dist, gates, taps, soft)


def mixer_branch(state, prod, carry, gate, shards, core):
    seqs, rows, _ = state.shape
    per = HEADS // shards

    def at(h, core_ref):
        return (0, 0, h)

    def split_at(parity, h):
        shard = h // per
        count = jnp.where(parity == 0, shard // 2 * per + per, shard // 2 * per)
        count = jnp.where(shard % 2 == parity, shard // 2 * per + h % per + 1, count)
        return (0, 0, jnp.maximum(count - 1, 0))

    full = pl.BlockSpec((seqs, rows, HS), at)
    return pl.pallas_call(
        functools.partial(branch_kernel, per),
        grid_spec=pltpu.PrefetchScalarGridSpec(
            num_scalar_prefetch=1,
            grid=(HEADS,),
            in_specs=[full, full, pl.BlockSpec((seqs, CHUNKS, HS), at), full],
            out_specs=[
                full,
                full,
                pl.BlockSpec((seqs, rows, HS), lambda h, core_ref: split_at(core_ref[0], h)),
                pl.BlockSpec((seqs, rows, HS), lambda h, core_ref: split_at(1 - core_ref[0], h)),
            ],
        ),
        out_shape=[
            jax.ShapeDtypeStruct((seqs, rows, LRU), F32),
            jax.ShapeDtypeStruct((seqs, rows, LRU), BF16),
            jax.ShapeDtypeStruct((seqs, rows, LRU // 2), BF16),
            jax.ShapeDtypeStruct((seqs, rows, LRU // 2), BF16),
        ],
        compiler_params=PARAMS,
        name="mixer_branch",
    )(core.reshape(1), state, prod, carry, gate)


def mixer_reverse(grad, gate, keep, state):
    seqs, rows, _ = grad.shape
    full = head_block(seqs, rows)
    wide = jax.ShapeDtypeStruct((seqs, rows, LRU), F32)
    return pl.pallas_call(
        reverse_kernel,
        grid=(HEADS,),
        in_specs=[full, full, full, full],
        out_specs=[full, full, full, pair_block(seqs)],
        out_shape=[
            jax.ShapeDtypeStruct((seqs, rows, LRU), BF16),
            wide,
            wide,
            jax.ShapeDtypeStruct((seqs, 2, CHUNKS, LRU), F32),
        ],
        compiler_params=PARAMS,
        name="mixer_reverse",
    )(grad, gate, keep, state)


def mixer_backward(local, prod, carry, state, before, c, u, halo, dist, gates, taps, soft):
    seqs, rows, _ = local.shape
    full = head_block(seqs, rows)
    small = head_block(seqs, HALO)
    gate_block = pl.BlockSpec((1, HS, 2 * HS), lambda h: (h, 0, 0))
    row_block = pl.BlockSpec((8, HS), lambda h: (0, h))
    return pl.pallas_call(
        mixer_backward_kernel,
        grid=(HEADS,),
        in_specs=[
            full,
            full,
            head_block(seqs, CHUNKS),
            full,
            small,
            full,
            full,
            small,
            shared_block((seqs, rows, HS)),
            gate_block,
            pl.BlockSpec((CONV, HS), lambda h: (0, h)),
            pl.BlockSpec((1, HS), lambda h: (0, h)),
        ],
        out_specs=[full, head_block(seqs, TAIL), small, gate_block, row_block, row_block],
        out_shape=[
            jax.ShapeDtypeStruct((seqs, rows, LRU), BF16),
            jax.ShapeDtypeStruct((seqs, TAIL, LRU), F32),
            jax.ShapeDtypeStruct((seqs, HALO, LRU), F32),
            jax.ShapeDtypeStruct((HEADS, HS, 2 * HS), F32),
            jax.ShapeDtypeStruct((8, LRU), F32),
            jax.ShapeDtypeStruct((8, LRU), F32),
        ],
        scratch_shapes=[
            pltpu.VMEM((rows, 2 * HS), F32),
            pltpu.VMEM((rows, 2 * HS), BF16),
            pltpu.VMEM((rows + BACK, HS), F32),
            pltpu.VMEM((rows + 8, HS), F32),
            pltpu.VMEM((rows + BACK, HS), F32),
            pltpu.VMEM((rows + BACK, HS), F32),
        ],
        compiler_params=PARAMS,
        name="mixer_backward",
    )(local, prod, carry, state, before, c, u, halo, dist, gates, taps, soft)


def rms_norm(x, gain, shards, core):
    rows = x.shape[0]
    block = min(rows, 256)
    return pl.pallas_call(
        functools.partial(norm_kernel, shards),
        grid=(rows // block,),
        in_specs=[
            pl.BlockSpec(memory_space=pltpu.SMEM),
            pl.BlockSpec((block, D), lambda n: (n, 0)),
            pl.BlockSpec((1, D), lambda n: (0, 0)),
        ],
        out_specs=[
            pl.BlockSpec((block, D), lambda n: (n, 0)),
            pl.BlockSpec((block, D // 2), lambda n: (n, 0)),
            pl.BlockSpec((block, D // 2), lambda n: (n, 0)),
            pl.BlockSpec((block, 128), lambda n: (n, 0)),
        ],
        out_shape=[
            jax.ShapeDtypeStruct((rows, D), BF16),
            jax.ShapeDtypeStruct((rows, D // 2), BF16),
            jax.ShapeDtypeStruct((rows, D // 2), BF16),
            jax.ShapeDtypeStruct((rows, 128), F32),
        ],
        compiler_params=PARAMS,
        name="rms_norm",
    )(core.reshape(1), x, gain.reshape(1, D))


FF_TILE = 512
GATHER_TILE = 768
DOT_TILE = 512


def ffn_forward(normed, proj_up):
    rows = normed.shape[0]
    steps = FF // FF_TILE
    return pl.pallas_call(
        ffn_forward_kernel,
        grid=(steps,),
        in_specs=[
            pl.BlockSpec((rows, D), lambda n: (0, 0)),
            pl.BlockSpec((D, FF_TILE), lambda n: (0, n)),
            pl.BlockSpec((D, FF_TILE), lambda n: (0, n + steps)),
        ],
        out_specs=[
            pl.BlockSpec((rows, FF_TILE), lambda n: (0, n)),
            pl.BlockSpec((2, rows, FF_TILE), lambda n: (0, 0, n)),
        ],
        out_shape=[
            jax.ShapeDtypeStruct((rows, FF), BF16),
            jax.ShapeDtypeStruct((2, rows, FF), BF16),
        ],
        compiler_params=PARAMS,
        name="ffn_forward",
    )(normed, proj_up, proj_up)


def ffn_backward(grad, proj_down, pull):
    rows = grad.shape[0]
    return pl.pallas_call(
        ffn_backward_kernel,
        grid=(FF // FF_TILE,),
        in_specs=[
            pl.BlockSpec((rows, D), lambda n: (0, 0)),
            pl.BlockSpec((FF_TILE, D), lambda n: (n, 0)),
            pl.BlockSpec((2, rows, FF_TILE), lambda n: (0, 0, n)),
        ],
        out_specs=pl.BlockSpec((2, rows, FF_TILE), lambda n: (0, 0, n)),
        out_shape=jax.ShapeDtypeStruct((2, rows, FF), BF16),
        compiler_params=PARAMS,
        name="ffn_backward",
    )(grad, proj_down, pull)


def gather_rows(shard):
    parts = lax.axis_size("grp")
    rows = shard.shape[0] // parts
    own = lax.dynamic_slice_in_dim(shard, lax.axis_index("grp") * rows, rows, 0)
    return lax.all_gather(own, ("seq", "grp"), axis=0, tiled=True)


def tie(value, *after):
    return lax.optimization_barrier((value, *after))[0]


def xor_pairs(axis, bit):
    return [(i, i ^ bit) for i in range(lax.axis_size(axis))]


def ring_pairs(steps):
    count = lax.axis_size("seq")
    return [(i, (i + steps) % count) for i in range(count)]


def same_cores():
    count = lax.axis_size("seq")
    return [list(range(core, count, 2)) for core in range(2)]


def dot_rows(a, b):
    return lax.dot_general(a, b, (((0,), (0,)), ((), ())), preferred_element_type=F32)


def reduce_rows(partial):
    part = lax.psum_scatter(partial, "seq", scatter_dimension=0, tiled=True)
    part = lax.psum_scatter(part, "grp", scatter_dimension=0, tiled=True)
    return lax.all_gather(part, "grp", axis=0, tiled=True).astype(F32)


def dot_far(a, b):
    return lax.dot_general(a, b, (((1,), (1,)), ((), ())), preferred_element_type=F32)


def by_position(a):
    seqs, rows = a.shape[:2]
    return a.reshape(seqs, CHUNKS, rows // CHUNKS, *a.shape[2:]).swapaxes(1, 2).reshape(a.shape)


def by_token(a):
    seqs, rows = a.shape[:2]
    return a.reshape(seqs, rows // CHUNKS, CHUNKS, *a.shape[2:]).swapaxes(1, 2).reshape(a.shape)


def fetch_columns(where_ref, pieces, start, target, sem):
    own, far = pieces[:6], pieces[6:]
    rows, columns = own[0].shape
    width, tile = columns // 4, target.shape[1]
    depth, half = own[1].shape[0], own[4].shape[0]
    chips = depth // rows + 1
    chip, core, group = where_ref[0], where_ref[1], where_ref[2]
    quarter = start // width
    offset = pl.multiple_of(start - quarter * width, 128)
    start = pl.multiple_of(start, 128)
    relation = lax.bitwise_xor(group, quarter)

    def copy(source, row, count):
        place = target.at[pl.ds(pl.multiple_of(row, 16), count), :]
        pltpu.make_async_copy(source, place, sem).start()

    for c, (shard, *parts) in enumerate((own, far)):
        other = lax.rem(core + c, 2)
        copy(shard.at[:, pl.ds(start, tile)], (chip * 2 + other) * rows, rows)
        for j in range(1, chips):
            row = (lax.rem(chip + j, chips) * 2 + other) * rows
            first = (j - 1) * rows
            for k in range(3):

                @pl.when(relation == k)
                def _():
                    copy(parts[k].at[pl.ds(first, rows), pl.ds(offset, tile)], row, rows)

            @pl.when(relation == 3)
            def _():
                for m in range(2):
                    low, high = max(first, m * half), min(first + rows, (m + 1) * half)
                    if low < high:
                        at = pl.ds(low - m * half, high - low)
                        source = parts[3 + m].at[at, pl.ds(offset, tile)]
                        copy(source, row + (low - first), high - low)


def gathered_tiles(fetch, held, sems):
    step, steps = pl.program_id(0), pl.num_programs(0)
    slot = lax.rem(step, 2)

    @pl.when(step == 0)
    def _():
        fetch(step, slot)

    @pl.when(step + 1 < steps)
    def _():
        fetch(step + 1, 1 - slot)

    for side in range(held.shape[1]):
        whole = held.at[slot, side]
        pltpu.make_async_copy(whole, whole, sems.at[slot, side]).wait()
    return slot


def gathered_ffn_kernel(where_ref, n_ref, *refs):
    pieces, (hidden_ref, pull_ref, gate_ref, up_ref, held, sems) = refs[:12], refs[12:]
    tile = hidden_ref.shape[1]

    def fetch(n, slot):
        for side in range(2):
            start = n * tile + side * (pieces[0].shape[1] // 2)
            fetch_columns(where_ref, pieces, start, held.at[slot, side], sems.at[slot, side])

    slot = gathered_tiles(fetch, held, sems)
    gate_ref[...] = held[slot, 0]
    up_ref[...] = held[slot, 1]
    ffn_forward_kernel(n_ref, gate_ref, up_ref, hidden_ref, pull_ref)


def gathered_dot_kernel(base, where_ref, n_ref, *refs):
    pieces, (out_ref, weight_ref, held, sems) = refs[:12], refs[12:]
    tile = out_ref.shape[1]

    def fetch(n, slot):
        start = base + n * tile
        fetch_columns(where_ref, pieces, start, held.at[slot, 0], sems.at[slot, 0])

    slot = gathered_tiles(fetch, held, sems)
    weight_ref[...] = held[slot, 0]
    out_ref[...] = jnp.dot(n_ref[...], weight_ref[...], preferred_element_type=F32).astype(
        out_ref.dtype
    )


class Gather:
    def __init__(self, shard, *after, offload=False):
        self.shard = shard
        self.chips = lax.axis_size("seq") // 2
        half = (self.chips - 1) * shard.shape[0] // 2
        self.simple = lax.axis_size("grp") != 4 or half % 16 != 0
        if self.simple:
            self.whole = gather_rows(shard)
            return
        group = lax.axis_index("grp")
        width = shard.shape[1] // 4
        own = lax.dynamic_slice_in_dim(shard, group * width, width, 1)
        if after:
            own = tie(own, *after)
        if offload:
            self.slabs = lax.all_gather(own, "seq", axis_index_groups=same_cores())
        else:
            self.slabs = [
                lax.ppermute(own, "seq", ring_pairs(-2 * j)) for j in range(1, self.chips)
            ]
        self.half = half

    def first(self, *after):
        if self.simple:
            return ()
        slabs = tie(self.slabs, *after) if after else self.slabs
        if not isinstance(slabs, list):
            chip = lax.axis_index("seq") // 2
            slabs = [
                lax.dynamic_index_in_dim(slabs, (chip + j) % self.chips, 0, False)
                for j in range(1, self.chips)
            ]
        self.near = jnp.concatenate(slabs, axis=0)
        self.from_x = lax.ppermute(self.near, "grp", xor_pairs("grp", 1))
        self.from_y = lax.ppermute(self.near, "grp", xor_pairs("grp", 2))
        return (self.near,)

    def second(self, *after):
        if self.simple:
            return ()
        if after:
            self.from_x, self.from_y = tie((self.from_x, self.from_y), *after)
        self.halves = (self.from_y[: self.half], self.from_x[self.half :])
        return self.halves

    def third(self):
        if self.simple:
            return
        diag_a = lax.ppermute(self.halves[0], "grp", xor_pairs("grp", 1))
        diag_b = lax.ppermute(self.halves[1], "grp", xor_pairs("grp", 2))
        own = (self.shard, self.near, self.from_x, self.from_y, diag_a, diag_b)
        far = tuple(lax.ppermute(piece, "seq", xor_pairs("seq", 1)) for piece in own)
        place = lax.axis_index("seq")
        where = jnp.stack([place // 2, place % 2, lax.axis_index("grp")]).astype(jnp.int32)
        self.pieces = (where, own, far)

    def call(self, kernel, normed, steps, tile, weights, out_specs, out_shape, name):
        where, own, far = self.pieces
        rows, depth = normed.shape
        return pl.pallas_call(
            kernel,
            grid=(steps,),
            in_specs=[
                pl.BlockSpec(memory_space=pltpu.SMEM),
                pl.BlockSpec((rows, depth), lambda n: (0, 0)),
            ]
            + [pl.BlockSpec(memory_space=pl.ANY)] * 12,
            out_specs=out_specs + [pl.BlockSpec((depth, tile), lambda n: (0, n))] * weights,
            out_shape=out_shape + [jax.ShapeDtypeStruct((depth, steps * tile), BF16)] * weights,
            scratch_shapes=[
                pltpu.VMEM((2, weights, depth, tile), BF16),
                pltpu.SemaphoreType.DMA((2, weights)),
            ],
            compiler_params=PARAMS,
            name=name,
        )(where, normed, *own, *far)

    def dot(self, normed, half, dtype):
        columns = self.shard.shape[1] // 2
        base = half * columns
        if self.simple:
            weight = self.whole[:, base : base + columns]
            return jnp.dot(normed, weight, preferred_element_type=F32).astype(dtype), weight
        rows, tile = normed.shape[0], DOT_TILE
        return self.call(
            functools.partial(gathered_dot_kernel, base),
            normed,
            columns // tile,
            tile,
            1,
            [pl.BlockSpec((rows, tile), lambda n: (0, n))],
            [jax.ShapeDtypeStruct((rows, columns), dtype)],
            "gathered_dot",
        )

    def ffn_forward(self, normed):
        if self.simple:
            hidden, pull = ffn_forward(normed, self.whole)
            return hidden, pull, self.whole[:, :FF], self.whole[:, FF:]
        rows, tile = normed.shape[0], GATHER_TILE
        return self.call(
            gathered_ffn_kernel,
            normed,
            FF // tile,
            tile,
            2,
            [
                pl.BlockSpec((rows, tile), lambda n: (0, n)),
                pl.BlockSpec((2, rows, tile), lambda n: (0, 0, n)),
            ],
            [
                jax.ShapeDtypeStruct((rows, FF), BF16),
                jax.ShapeDtypeStruct((2, rows, FF), BF16),
            ],
            "gathered_ffn",
        )


class Reduction:
    def __init__(self, a_own, a_far, columns, width, fused=False):
        self.simple = lax.axis_size("grp") != 4
        count = lax.axis_size("seq")
        place = lax.axis_index("seq")
        self.chips = count // 2
        self.chip, core = place // 2, place % 2
        self.width = width
        full = a_own.shape[1]
        self.rows = full // self.chips
        self.half = full // 2
        self.a_own = a_own
        if self.simple:
            parts = [columns(k) for k in range(4)]
            own, far = (
                jnp.concatenate([dot_rows(a, part) for part in parts], axis=1)
                for a in (a_own, a_far)
            )
            cores = jnp.stack(
                [jnp.where(core == c, own, far).reshape(self.chips, self.rows, -1) for c in (0, 1)],
                axis=1,
            )
            self.product = cores.reshape(2 * full, 4 * width).astype(BF16)
            self.arrived = self.product
            self.sent = (self.product,)
            return
        group = lax.axis_index("grp")
        self.x, self.y = xor_pairs("grp", 1), xor_pairs("grp", 2)
        self.b = [columns(group ^ k) for k in range(4)]
        self.far = [None] * 4
        self.product = None
        other = xor_pairs("seq", 1)
        if fused:
            b_all = jnp.concatenate(self.b, axis=1)
            far = lax.ppermute(dot_rows(a_far, b_all).astype(BF16), "seq", other)
            self.product = (dot_rows(a_own, b_all) + far.astype(F32)).astype(BF16)
        for k in () if fused else (3, 1, 2, 0):
            product = dot_rows(a_far, self.b[k]).astype(BF16)
            self.far[k] = lax.ppermute(product, "seq", other)
        half = self.half
        self.sent = (
            self.own(3, 0, half).astype(BF16),
            self.own(3, half, full).astype(BF16),
        )
        self.diag_a = lax.ppermute(self.sent[0], "grp", self.x)
        self.diag_b = lax.ppermute(self.sent[1], "grp", self.y)

    def own(self, k, first, last):
        if self.product is not None:
            left = k * self.width
            return self.product[first:last, left : left + self.width].astype(F32)
        product = dot_rows(self.a_own[:, first:last], self.b[k])
        return product + self.far[k][first:last].astype(F32)

    def second(self, *after):
        if self.simple:
            return ()
        full, none = 2 * self.half, ((0, self.half), (0, 0))
        diag_a, diag_b = self.diag_a, self.diag_b
        if after:
            diag_a, diag_b = tie((diag_a, diag_b), *after)
        sent = (
            (self.own(1, 0, full) + jnp.pad(diag_b.astype(F32), (none[0][::-1], (0, 0)))).astype(BF16),
            (self.own(2, 0, full) + jnp.pad(diag_a.astype(F32), none)).astype(BF16),
        )
        self.from_x = lax.ppermute(sent[0], "grp", self.x)
        self.from_y = lax.ppermute(sent[1], "grp", self.y)
        return sent

    def mine(self, *after):
        from_x, from_y = self.from_x, self.from_y
        if after:
            from_x, from_y = tie((from_x, from_y), *after)
        mine = self.own(0, 0, 2 * self.half) + from_x.astype(F32) + from_y.astype(F32)
        return mine.astype(BF16)

    def along_z(self, mine):
        mine = mine.reshape(self.chips, self.rows, -1)
        self.kept = lax.dynamic_index_in_dim(mine, self.chip, 0, False)
        sent = tuple(
            lax.dynamic_index_in_dim(mine, (self.chip + j) % self.chips, 0, False)
            for j in range(1, self.chips)
        )
        self.arrived = [
            lax.ppermute(part, "seq", ring_pairs(2 * j + 2)) for j, part in enumerate(sent)
        ]
        return sent

    def third(self, *after, offload=False):
        if self.simple:
            return ()
        mine = self.mine(*after)
        if not offload:
            return self.along_z(mine)
        self.kept = None
        self.arrived = lax.psum_scatter(
            mine, "seq", scatter_dimension=0, axis_index_groups=same_cores(), tiled=True
        )
        return (mine,)

    def total(self):
        if self.kept is None:
            return self.arrived
        total = self.kept.astype(F32)
        for part in self.arrived:
            total = total + part.astype(F32)
        return total

    def finish(self, *after):
        if self.simple:
            return reduce_rows(self.product)
        total = self.total()
        if after:
            total = tie(total, *after)
        parts = lax.all_gather(total.astype(BF16), "grp")
        return parts.transpose(1, 0, 2).reshape(self.rows, 4 * self.width).astype(F32)


def shard_carry(ends, prods, reverse):
    count = lax.axis_size("seq")
    place = lax.axis_index("seq")
    both = lax.all_gather(jnp.stack([ends, prods]), "seq")
    carry = jnp.zeros_like(ends)
    for step in range(count - 1):
        source = count - 1 - step if reverse else step
        ahead = source > place if reverse else source < place
        carry = jnp.where(ahead, both[source, 0] + both[source, 1] * carry, carry)
    return carry


def chunk_ends(chunks, reverse):
    state = jnp.zeros_like(chunks[:, 0, 0])
    prod = jnp.ones_like(state)
    order = range(CHUNKS - 1, -1, -1) if reverse else range(CHUNKS)
    for n in order:
        state = chunks[:, 0, n] + chunks[:, 1, n] * state
        prod = chunks[:, 1, n] * prod
    return state, prod


def chunk_carries(chunks, carry, reverse):
    order = range(CHUNKS - 1, -1, -1) if reverse else range(CHUNKS)
    found = [None] * CHUNKS
    for n in order:
        found[n] = carry
        carry = chunks[:, 0, n] + chunks[:, 1, n] * carry
    return jnp.stack(found, axis=1)


def norm_back(values, scale, gain, grad_normed):
    weighted = grad_normed * gain
    cubed = scale * scale * scale
    return scale * weighted - values * cubed * jnp.mean(weighted * values, axis=-1, keepdims=True)


def gain_grad(weight, grad_weight, gain):
    return jnp.sum(weight.astype(F32) * grad_weight, axis=1) / gain.astype(F32)


def body(
    tokens, seg_ids, cotangent, first_gain, in_proj, conv_taps, decay_param, gate_heads,
    out_proj, second_gain, up_proj, down_proj,
):
    seq_count, shard_len, _ = tokens.shape
    row_count = seq_count * shard_len
    edge_len = CONV - 1
    place = lax.axis_index("seq")
    last = lax.axis_size("seq") - 1

    small = jnp.concatenate(
        [first_gain, second_gain, decay_param, conv_taps.reshape(-1)]
    )
    small_all = lax.all_gather(small, "seq")
    n_gain, n_lru = first_gain.shape[0], decay_param.shape[0]
    gain_one = small_all[:, :n_gain].reshape(D).astype(F32)
    gain_two = small_all[:, n_gain : 2 * n_gain].reshape(D).astype(F32)
    decay_float = small_all[:, 2 * n_gain : 2 * n_gain + n_lru].reshape(LRU).astype(F32)
    taps_all = (
        small_all[:, 2 * n_gain + n_lru :].reshape(-1, CONV, n_lru).transpose(1, 0, 2)
    ).reshape(CONV, LRU).astype(F32)
    in_gather = Gather(in_proj)
    near = in_gather.first()
    in_gather.second()
    in_gather.third()
    gates_all = lax.all_gather(gate_heads, "seq", axis=0, tiled=True)
    up_gather = Gather(up_proj, gates_all, *near, offload=True)
    proj_out = gather_rows(out_proj)
    proj_down = gather_rows(down_proj)

    tokens = by_position(tokens)
    cotangent = by_position(cotangent)
    inputs = tokens.reshape(row_count, D).astype(F32)
    first_normed, first_own, first_far, first_scale = rms_norm(
        tokens.reshape(row_count, D), gain_one, last + 1, place % 2
    )
    first_scale = first_scale[:, :1]
    wide = (seq_count, shard_len, LRU)
    inner_low, in_value = in_gather.dot(first_normed, 0, BF16)
    inner_low = inner_low.reshape(wide)

    step = shard_len // CHUNKS
    final = inner_low.reshape(seq_count, step, CHUNKS, LRU)[:, step - HALO :, CHUNKS - 1]
    prev_inner = from_behind(final, "seq", 1)
    prev_ids = from_behind(seg_ids[:, shard_len - edge_len :], "seq", 1)
    prev_ids = jnp.where(place == 0, -1, prev_ids)
    ext_ids = jnp.concatenate([prev_ids, seg_ids], axis=1)
    dist = jnp.zeros((seq_count, shard_len), F32)
    for k in range(1, CONV):
        dist = dist + (ext_ids[:, edge_len - k : edge_len - k + shard_len] == seg_ids).astype(F32)
    dist = jnp.broadcast_to(by_position(dist)[:, :, None], (seq_count, shard_len, HS))
    soft = jax.nn.softplus(-decay_float).reshape(1, LRU)

    conv_low, keep, state_part, prod_part, chunks = mixer_forward(
        tie(inner_low, *up_gather.first(inner_low)), prev_inner, dist, gates_all, taps_all, soft
    )
    end_state, end_prod = chunk_ends(chunks, False)
    gate_pre, in_gate = in_gather.dot(first_normed, 1, F32)
    gate_pre = gate_pre.reshape(wide)
    carry_in = shard_carry(end_state, end_prod, False)
    carries = chunk_carries(chunks, carry_in, False)
    state, branch, branch_own, branch_far = mixer_branch(
        tie(state_part, *up_gather.second(carries, gate_pre)), prod_part, carries, gate_pre, last + 1, place % 2
    )
    resid = inputs + jnp.dot(
        branch.reshape(row_count, LRU), proj_out, preferred_element_type=F32
    )
    second_normed, second_own, second_far, second_scale = rms_norm(
        resid, gain_two, last + 1, place % 2
    )
    second_scale = second_scale[:, :1]
    up_gather.third()
    hidden, pull, proj_gate, proj_up = up_gather.ffn_forward(second_normed)

    grad_out = cotangent.reshape(row_count, D)
    grad_down = dot_rows(hidden, grad_out).astype(BF16)
    down_part = lax.psum_scatter(grad_down, ("seq", "grp"), scatter_dimension=0, tiled=True)
    grad_expanded = ffn_backward(tie(grad_out, grad_down), proj_down, pull)
    quarter = FF // 2

    def up_columns(n):
        part = lax.dynamic_slice(
            grad_expanded, (n // 2, 0, (n % 2) * quarter), (1, row_count, quarter)
        )
        return part[0]

    up_sum = Reduction(second_own, second_far, up_columns, quarter)
    grad_expanded = tie(grad_expanded, *up_sum.sent)
    grad_second_normed = dot_far(grad_expanded[0], proj_gate) + dot_far(
        grad_expanded[1], proj_up
    )
    sent = up_sum.second(grad_second_normed)
    grad_second_normed = tie(grad_second_normed, *sent)
    grad_resid = grad_out.astype(F32) + norm_back(
        resid, second_scale, gain_two, grad_second_normed
    )
    grad_mixer = grad_resid.astype(BF16)
    grad_branch = dot_far(grad_mixer, proj_out)

    grad_gate, local, rev_prod, rev_chunks = mixer_reverse(
        grad_branch.reshape(wide), gate_pre, keep, state
    )
    down_sum = lax.all_gather(tie(down_part, rev_chunks), "grp", axis=0, tiled=True)
    head_pull, head_prod = chunk_ends(rev_chunks, True)
    grad_gate = grad_gate.reshape(row_count, LRU)
    width = LRU // 4
    rev_carry = shard_carry(head_pull, head_prod, True)
    rev_carries = chunk_carries(rev_chunks, rev_carry, True)
    grad_mixer, grad_gate = tie((grad_mixer, grad_gate), rev_carry)
    out_sum = Reduction(
        branch_own.reshape(row_count, LRU // 2),
        branch_far.reshape(row_count, LRU // 2),
        lambda n: lax.dynamic_slice_in_dim(grad_mixer, n * (D // 4), D // 4, 1),
        D // 4,
        True,
    )
    in_gate_sum = Reduction(
        first_own,
        first_far,
        lambda n: lax.dynamic_slice_in_dim(grad_gate, n * width, width, 1),
        width,
        True,
    )
    sent = (*out_sum.sent, *in_gate_sum.sent)
    sent = up_sum.third(down_sum, *sent, offload=True)
    local = tie(local, *sent)
    du, tail, edge, grad_gates, grad_taps, grad_decay = mixer_backward(
        local, rev_prod, rev_carries, state, carries, conv_low, inner_low,
        prev_inner, dist, gates_all, taps_all, soft,
    )
    returned = from_behind(edge[:, HALO - edge_len :].astype(BF16), "seq", -1).astype(F32)
    grad_gate = tie(grad_gate, *out_sum.second(edge), *in_gate_sum.second(edge))
    first_grad = dot_far(grad_gate, in_gate)
    groups = TAIL // CHUNKS
    padded = jnp.pad(
        returned[:, :, None, :], ((0, 0), (groups - edge_len, 0), (CHUNKS - 1, 0), (0, 0))
    ).reshape(seq_count, TAIL, LRU)
    grad_inner = lax.dynamic_update_slice(
        du, (tail + padded).astype(BF16), (0, shard_len - TAIL, 0)
    )
    grad_inner = tie(grad_inner, first_grad).reshape(row_count, LRU)
    in_value_sum = Reduction(
        first_own,
        first_far,
        lambda n: lax.dynamic_slice_in_dim(grad_inner, n * width, width, 1),
        width,
        True,
    )
    grad_inner = tie(grad_inner, *in_value_sum.sent)

    shards = last + 1
    grad_decay_row = grad_decay[0] * jax.nn.sigmoid(-decay_float)
    flat = jnp.concatenate(
        [
            grad_gates.reshape(shards, -1, HS),
            grad_taps[:CONV].reshape(CONV, shards, -1, HS).swapaxes(0, 1).reshape(shards, -1, HS),
            grad_decay_row.reshape(shards, -1, HS),
        ],
        axis=1,
    )
    lines = flat.shape[1]
    flat = jnp.pad(flat, ((0, 0), (0, -lines % 16), (0, 0))).astype(BF16).reshape(-1, HS)
    flat = lax.psum_scatter(flat, "seq", scatter_dimension=0, tiled=True)
    first_grad = first_grad + dot_far(grad_inner, in_value)
    sent = in_value_sum.second(first_grad)
    out_sum.third(*sent)
    flat = lax.all_gather(tie(flat, *sent), "grp").astype(F32)
    flat = jnp.sum(flat, axis=0)[:lines].reshape(-1)
    n_gates = flat.shape[0] - (CONV + 1) * n_lru
    gates_total = flat[:n_gates].reshape(gate_heads.shape)
    taps_total = flat[n_gates : n_gates + CONV * n_lru].reshape(CONV, n_lru)
    decay_total = flat[n_gates + CONV * n_lru :]

    up_total = up_sum.finish(edge)
    down_total = tie(down_sum, *sent).astype(F32)
    if in_value_sum.simple:
        in_total = jnp.concatenate([in_value_sum.finish(), in_gate_sum.finish()], axis=1)
        last_sent = ()
    else:
        both = jnp.concatenate([in_value_sum.mine(), in_gate_sum.mine()], axis=1)
        last_sent = in_value_sum.along_z(both)
        both = in_value_sum.total().astype(BF16)
        in_total = jnp.concatenate(
            [
                lax.all_gather(both[:, n * width : (n + 1) * width], "grp")
                .transpose(1, 0, 2)
                .reshape(-1, LRU)
                for n in range(2)
            ],
            axis=1,
        ).astype(F32)
    out_total = out_sum.finish(*last_sent)
    ffn_out = jnp.dot(tie(hidden, *sent), proj_down, preferred_element_type=F32)
    block_out = by_token((resid + ffn_out).astype(BF16).reshape(tokens.shape))
    grad_tokens = grad_resid + norm_back(inputs, first_scale, gain_one, first_grad)
    grad_tokens = by_token(grad_tokens.astype(BF16).reshape(tokens.shape))
    first_total = gain_grad(in_proj, in_total, first_gain)
    second_total = gain_grad(up_proj, up_total, second_gain)
    return (
        block_out, grad_tokens, first_total, in_total, taps_total, decay_total, gates_total,
        out_total, second_total, up_total, down_total,
    )


def solution(mesh):
    in_specs = (
        P("grp", "seq", None),
        P("grp", "seq"),
        P("grp", "seq", None),
        P("seq"),
        P("seq", None),
        P(None, "seq"),
        P("seq"),
        P("seq", None, None),
        P("seq", None),
        P("seq"),
        P("seq", None),
        P("seq", None),
    )
    out_specs = (
        P("grp", "seq", None),
        P("grp", "seq", None),
        P("seq"),
        P("seq", None),
        P(None, "seq"),
        P("seq"),
        P("seq", None, None),
        P("seq", None),
        P("seq"),
        P("seq", None),
        P("seq", None),
    )
    return jax.shard_map(body, mesh=mesh, in_specs=in_specs, out_specs=out_specs, check_vma=False)
```

```python
import functools

import jax
import jax.numpy as jnp
from jax import lax
from jax.experimental import pallas as pl
from jax.experimental.pallas import tpu as pltpu
from jax.sharding import PartitionSpec as P

D = 1536
HEADS = 16
HS = 128
LRU = 2048
FF = 4608
CONV = 4
CHUNKS = 8
HALO = 8
BACK = 8 * (CONV - 1)
TAIL = 32
F32 = jnp.float32
BF16 = jnp.bfloat16


def from_behind(value, axis, steps):
    count = lax.axis_size(axis)
    first, last = (max(0, -steps), min(count, count - steps))
    return lax.ppermute(value, axis, [(source, source + steps) for source in range(first, last)])


def gelu_parts(v):
    k = 0.7978845608028654
    square = v * v
    t = jnp.tanh(k * v * (1.0 + 0.044715 * square))
    half = 0.5 * (1.0 + t)
    slope = half + 0.5 * v * (1.0 - t * t) * (k * (1.0 + 3.0 * 0.044715 * square))
    return v * half, slope


def gelu_tanh(v):
    k = 0.7978845608028654
    return 0.5 * v * (1.0 + jnp.tanh(k * v * (1.0 + 0.044715 * v * v)))


def sigmoid(v):
    return 0.5 * jnp.tanh(0.5 * v) + 0.5


def drive_values(q_rate, q_input, soft):
    rate = sigmoid(q_rate)
    inp = sigmoid(q_input)
    decay = jnp.exp(-8.0 * rate * soft)
    square = 1.0 - decay * decay + 0.001
    inverse = lax.rsqrt(square)
    return rate, inp, decay, square * inverse, inverse


def shifted_group(group, step, fill):
    row = lax.broadcasted_iota(jnp.int32, group.shape, 0)
    edge = 0 if step == 1 else CHUNKS - 1
    moved = pltpu.roll(group, step % CHUNKS, 0)
    return jnp.where(row == edge, fill, moved)


def extend_back(ext_s, u_ref, halo_ref, b):
    rows = u_ref.shape[1]
    ext_s[pl.ds(BACK, rows), :] = u_ref[b].astype(F32)
    halo = halo_ref[b].astype(F32)
    for m in range(CONV - 1):
        group = ext_s[pl.ds(BACK + rows - BACK + 8 * m, 8), :]
        fill = halo[HALO - CONV + 1 + m : HALO - CONV + 2 + m, :]
        ext_s[pl.ds(8 * m, 8), :] = shifted_group(group, 1, fill)


def mixer_forward_kernel(
    u_ref, halo_ref, dist_ref, gates_ref, taps_ref, soft_ref,
    c_ref, keep_ref, state_ref, prod_ref, chunk_ref,
    ext_s, c_s, rate_s, inp_s,
):
    seqs, rows, _ = u_ref.shape
    soft = soft_ref[...]
    for b in range(seqs):
        extend_back(ext_s, u_ref, halo_ref, b)

        def conv_chunk(n, _):
            at = pl.multiple_of(n * 64, 64)
            far = dist_ref[b, pl.ds(at, 64), :]
            total = taps_ref[0:1, :] * ext_s[pl.ds(at + BACK, 64), :]
            for k in range(1, CONV):
                window = taps_ref[k : k + 1, :] * ext_s[pl.ds(at + BACK - 8 * k, 64), :]
                total = total + jnp.where(far >= float(k), window, 0.0)
            low = total.astype(BF16)
            c_ref[b, pl.ds(at, 64), :] = low
            c_s[b, pl.ds(at, 64), :] = low.astype(F32)
            return 0

        lax.fori_loop(0, rows // 64, conv_chunk, 0)
        both = jnp.dot(c_ref[b], gates_ref[0], preferred_element_type=F32)
        rate_s[b] = both[:, :HS]
        inp_s[b] = both[:, HS:]

    def scan_step(j, carry):
        new = []
        for b in range(seqs):
            at = pl.ds(pl.multiple_of(j * 8, 8), 8)
            state, prod = carry[b]
            _, inp, decay, root, _ = drive_values(rate_s[b, at, :], inp_s[b, at, :], soft)
            keep = jnp.where(dist_ref[b, at, :] >= 1.0, decay, 0.0)
            state = keep * state + root * inp * c_s[b, at, :]
            prod = keep * prod
            keep_ref[b, at, :] = keep
            state_ref[b, at, :] = state
            prod_ref[b, at, :] = prod
            new.append((state, prod))
        return tuple(new)

    zero, one = jnp.zeros((CHUNKS, HS), F32), jnp.ones((CHUNKS, HS), F32)
    ends = lax.fori_loop(0, rows // CHUNKS, scan_step, ((zero, one),) * seqs, unroll=8)
    for b in range(seqs):
        chunk_ref[b, 0] = ends[b][0]
        chunk_ref[b, 1] = ends[b][1]


def branch_kernel(core_ref, state_ref, prod_ref, carry_ref, gate_ref, out_ref, branch_ref, split_ref):
    del core_ref
    seqs, rows, _ = state_ref.shape
    for b in range(seqs):
        carry = jnp.concatenate([carry_ref[b]] * 4, axis=0)

        def point(n, _):
            at = pl.ds(pl.multiple_of(n * 32, 32), 32)
            state = state_ref[b, at, :] + prod_ref[b, at, :] * carry
            out_ref[b, at, :] = state
            low = (state * gelu_tanh(gate_ref[b, at, :])).astype(BF16)
            branch_ref[b, at, :] = low
            split_ref[0, b, at, :] = low
            return 0

        lax.fori_loop(0, rows // 32, point, 0, unroll=4)


def reverse_kernel(
    grad_ref, gate_ref, keep_ref, state_ref,
    dg_ref, local_ref, prod_ref, chunk_ref,
):
    seqs, rows, _ = grad_ref.shape
    pairs = rows // 16

    def scan_step(n, carry):
        first = pl.multiple_of((pairs - 1 - n) * 16, 16)
        at = pl.ds(first, 16)
        new = []
        for b in range(seqs):
            pull, prod = carry[b]
            act, slope = gelu_parts(gate_ref[b, at, :])
            grad = grad_ref[b, at, :]
            dg_ref[b, at, :] = (grad * state_ref[b, at, :] * slope).astype(BF16)
            dh = grad * act
            keep = keep_ref[b, at, :]
            late = dh[8:] + pull
            late_prod = prod
            pull, prod = keep[8:] * late, keep[8:] * prod
            early = dh[:8] + pull
            local_ref[b, at, :] = jnp.concatenate([early, late], axis=0)
            prod_ref[b, at, :] = jnp.concatenate([prod, late_prod], axis=0)
            new.append((keep[:8] * early, keep[:8] * prod))
        return tuple(new)

    zero, one = jnp.zeros((CHUNKS, HS), F32), jnp.ones((CHUNKS, HS), F32)
    ends = lax.fori_loop(0, pairs, scan_step, ((zero, one),) * seqs, unroll=4)
    for b in range(seqs):
        chunk_ref[b, 0] = ends[b][0]
        chunk_ref[b, 1] = ends[b][1]


def mixer_backward_kernel(
    local_ref, prod_ref, carry_ref, state_ref, before_ref, c_ref, u_ref, halo_ref, dist_ref,
    gates_ref, taps_ref, soft_ref,
    du_ref, tail_ref, edge_ref, ggate_ref, gtaps_ref, gdecay_ref,
    q_s, dq_s, dc_s, h_s, ext_s, dist_s, last_s,
):
    seqs, rows, _ = local_ref.shape
    soft = soft_ref[...]
    ggate = jnp.zeros((HS, 2 * HS), F32)
    decay_sum = jnp.zeros((8, HS), F32)
    taps_sum = [jnp.zeros((8, HS), F32) for _ in range(CONV)]

    def fold(value):
        return jnp.sum(value.reshape(value.shape[0] // 8, 8, HS), axis=0)

    for b in range(seqs):
        q_s[...] = jnp.dot(c_ref[b], gates_ref[0], preferred_element_type=F32)
        h_s[pl.ds(0, 8), :] = before_ref[b]
        h_s[pl.ds(8, rows), :] = state_ref[b]
        carry = jnp.concatenate([carry_ref[b]] * 4, axis=0)

        def point(n, total):
            first = pl.multiple_of(n * 32, 32)
            at = pl.ds(first, 32)
            lam = local_ref[b, at, :] + prod_ref[b, at, :] * carry
            rate, inp, decay, root, inverse = drive_values(q_s[at, :HS], q_s[at, HS:], soft)
            conv = c_ref[b, at, :].astype(F32)
            kept = jnp.where(dist_ref[b, at, :] >= 1.0, h_s[at, :], 0.0)
            lam_root = lam * root
            lam_inp = lam * inp
            grad_decay = lam * kept - lam_inp * conv * decay * inverse
            rated = grad_decay * decay * rate
            dq_s[at, :HS] = (-8.0 * soft * rated * (1.0 - rate)).astype(BF16)
            dq_s[at, HS:] = (lam_root * conv * inp * (1.0 - inp)).astype(BF16)
            dc_s[at, :] = lam_root * inp
            return total + fold(rated)

        decay_sum = lax.fori_loop(0, rows // 32, point, decay_sum, unroll=4)
        dc_s[pl.ds(0, rows), :] += lax.dot_general(
            dq_s[...], gates_ref[0], (((1,), (1,)), ((), ())), preferred_element_type=F32
        )
        ggate = ggate + lax.dot_general(
            c_ref[b], dq_s[...], (((0,), (0,)), ((), ())), preferred_element_type=F32
        )
        extend_back(ext_s, u_ref, halo_ref, b)
        dist_s[pl.ds(0, rows), :] = dist_ref[b]
        for m in range(CONV - 1):
            for held in (dc_s, dist_s):
                held[pl.ds(rows + 8 * m, 8), :] = shifted_group(held[pl.ds(8 * m, 8), :], -1, 0.0)

        def conv_chunk(n, totals):
            at = pl.multiple_of(n * 64, 64)
            grad = dc_s[pl.ds(at, 64), :]
            far = dist_s[pl.ds(at, 64), :]
            out = taps_ref[0:1, :] * grad
            totals = list(totals)
            totals[0] = totals[0] + fold(grad * ext_s[pl.ds(at + BACK, 64), :])
            for k in range(1, CONV):
                masked = jnp.where(far >= float(k), grad, 0.0)
                totals[k] = totals[k] + fold(masked * ext_s[pl.ds(at + BACK - 8 * k, 64), :])
                ahead = pl.ds(at + 8 * k, 64)
                value = taps_ref[k : k + 1, :] * dc_s[ahead, :]
                out = out + jnp.where(dist_s[ahead, :] >= float(k), value, 0.0)
            du_ref[b, pl.ds(at, 64), :] = out.astype(BF16)
            last_s[...] = out[64 - TAIL :, :]
            return tuple(totals)

        taps_sum = list(lax.fori_loop(0, rows // 64, conv_chunk, tuple(taps_sum), unroll=2))
        tail_ref[b] = last_s[...]
        edges = [jnp.zeros((HALO - CONV + 1, HS), F32)]
        for m in range(CONV - 1, 0, -1):
            edge = jnp.zeros((1, HS), F32)
            for k in range(m, CONV):
                at = pl.ds(8 * (k - m), 1)
                masked = jnp.where(dist_s[at, :] >= float(k), dc_s[at, :], 0.0)
                edge = edge + taps_ref[k : k + 1, :] * masked
            edges.append(edge)
        edge_ref[b] = jnp.concatenate(edges, axis=0)
    ggate_ref[0] = ggate
    gdecay_ref[...] = jnp.broadcast_to(
        8.0 * jnp.sum(decay_sum, axis=0, keepdims=True), (8, HS)
    )
    gtaps_ref[...] = jnp.concatenate(
        [jnp.sum(t, axis=0, keepdims=True) for t in taps_sum] + [jnp.zeros((8 - CONV, HS), F32)],
        axis=0,
    )


def norm_kernel(shards, core_ref, x_ref, gain_ref, normed_ref, own_ref, far_ref, scale_ref):
    x = x_ref[...].astype(F32)
    scale = lax.rsqrt(jnp.mean(x * x, axis=-1, keepdims=True) + 1e-06)
    low = (x * scale * gain_ref[...]).astype(BF16)
    normed_ref[...] = low
    scale_ref[...] = jnp.broadcast_to(scale, scale_ref.shape)
    wide = low.astype(F32)
    size = D // shards
    even, odd = (
        jnp.concatenate([wide[:, n * size : (n + 1) * size] for n in range(c, shards, 2)], axis=1)
        for c in range(2)
    )
    first = core_ref[0] == 0
    own_ref[...] = jnp.where(first, even, odd).astype(BF16)
    far_ref[...] = jnp.where(first, odd, even).astype(BF16)


def ffn_forward_kernel(n_ref, gate_ref, up_ref, hidden_ref, pull_ref):
    for m in range(0, n_ref.shape[0], 256):
        at = pl.ds(m, 256)
        e1 = jnp.dot(n_ref[at, :], gate_ref[...], preferred_element_type=F32)
        e2 = jnp.dot(n_ref[at, :], up_ref[...], preferred_element_type=F32)
        act, slope = gelu_parts(e1)
        hidden_ref[at, :] = (act * e2).astype(BF16)
        pull_ref[0, at, :] = (slope * e2).astype(BF16)
        pull_ref[1, at, :] = act.astype(BF16)


def ffn_backward_kernel(grad_ref, down_ref, pull_ref, out_ref):
    for m in range(0, grad_ref.shape[0], 512):
        at = pl.ds(m, 512)
        dv = lax.dot_general(
            grad_ref[at, :], down_ref[...], (((1,), (1,)), ((), ())), preferred_element_type=F32
        )
        out_ref[0, at, :] = (dv * pull_ref[0, at, :].astype(F32)).astype(BF16)
        out_ref[1, at, :] = (dv * pull_ref[1, at, :].astype(F32)).astype(BF16)


def head_block(lead, rows):
    return pl.BlockSpec((lead, rows, HS), lambda h: (0, 0, h))


def shared_block(shape):
    return pl.BlockSpec(shape, lambda h: (0,) * len(shape))


def pair_block(seqs):
    return pl.BlockSpec((seqs, 2, CHUNKS, HS), lambda h: (0, 0, 0, h))


PARAMS = pltpu.CompilerParams(vmem_limit_bytes=40 * 1024 * 1024)


def mixer_forward(u, halo, dist, gates, taps, soft):
    seqs, rows, _ = u.shape
    full = head_block(seqs, rows)
    wide = jax.ShapeDtypeStruct((seqs, rows, LRU), F32)
    return pl.pallas_call(
        mixer_forward_kernel,
        grid=(HEADS,),
        in_specs=[
            full,
            head_block(seqs, HALO),
            shared_block((seqs, rows, HS)),
            pl.BlockSpec((1, HS, 2 * HS), lambda h: (h, 0, 0)),
            pl.BlockSpec((CONV, HS), lambda h: (0, h)),
            pl.BlockSpec((1, HS), lambda h: (0, h)),
        ],
        out_specs=[full, full, full, full, pair_block(seqs)],
        out_shape=[
            jax.ShapeDtypeStruct((seqs, rows, LRU), BF16),
            wide,
            wide,
            wide,
            jax.ShapeDtypeStruct((seqs, 2, CHUNKS, LRU), F32),
        ],
        scratch_shapes=[
            pltpu.VMEM((rows + BACK, HS), F32),
            pltpu.VMEM((seqs, rows, HS), F32),
            pltpu.VMEM((seqs, rows, HS), F32),
            pltpu.VMEM((seqs, rows, HS), F32),
        ],
        compiler_params=PARAMS,
        name="mixer_forward",
    )(u, halo, dist, gates, taps, soft)


def mixer_branch(state, prod, carry, gate, shards, core):
    seqs, rows, _ = state.shape
    per = HEADS // shards

    def at(h, core_ref):
        return (0, 0, h)

    def split_at(h, core_ref):
        shard = h // per
        return ((shard % 2 + core_ref[0]) % 2, 0, 0, (shard // 2) * per + h % per)

    full = pl.BlockSpec((seqs, rows, HS), at)
    return pl.pallas_call(
        branch_kernel,
        grid_spec=pltpu.PrefetchScalarGridSpec(
            num_scalar_prefetch=1,
            grid=(HEADS,),
            in_specs=[full, full, pl.BlockSpec((seqs, CHUNKS, HS), at), full],
            out_specs=[full, full, pl.BlockSpec((1, seqs, rows, HS), split_at)],
        ),
        out_shape=[
            jax.ShapeDtypeStruct((seqs, rows, LRU), F32),
            jax.ShapeDtypeStruct((seqs, rows, LRU), BF16),
            jax.ShapeDtypeStruct((2, seqs, rows, LRU // 2), BF16),
        ],
        compiler_params=PARAMS,
        name="mixer_branch",
    )(core.reshape(1), state, prod, carry, gate)


def mixer_reverse(grad, gate, keep, state):
    seqs, rows, _ = grad.shape
    full = head_block(seqs, rows)
    wide = jax.ShapeDtypeStruct((seqs, rows, LRU), F32)
    return pl.pallas_call(
        reverse_kernel,
        grid=(HEADS,),
        in_specs=[full, full, full, full],
        out_specs=[full, full, full, pair_block(seqs)],
        out_shape=[
            jax.ShapeDtypeStruct((seqs, rows, LRU), BF16),
            wide,
            wide,
            jax.ShapeDtypeStruct((seqs, 2, CHUNKS, LRU), F32),
        ],
        compiler_params=PARAMS,
        name="mixer_reverse",
    )(grad, gate, keep, state)


def mixer_backward(local, prod, carry, state, before, c, u, halo, dist, gates, taps, soft):
    seqs, rows, _ = local.shape
    full = head_block(seqs, rows)
    small = head_block(seqs, HALO)
    gate_block = pl.BlockSpec((1, HS, 2 * HS), lambda h: (h, 0, 0))
    row_block = pl.BlockSpec((8, HS), lambda h: (0, h))
    return pl.pallas_call(
        mixer_backward_kernel,
        grid=(HEADS,),
        in_specs=[
            full,
            full,
            head_block(seqs, CHUNKS),
            full,
            small,
            full,
            full,
            small,
            shared_block((seqs, rows, HS)),
            gate_block,
            pl.BlockSpec((CONV, HS), lambda h: (0, h)),
            pl.BlockSpec((1, HS), lambda h: (0, h)),
        ],
        out_specs=[full, head_block(seqs, TAIL), small, gate_block, row_block, row_block],
        out_shape=[
            jax.ShapeDtypeStruct((seqs, rows, LRU), BF16),
            jax.ShapeDtypeStruct((seqs, TAIL, LRU), F32),
            jax.ShapeDtypeStruct((seqs, HALO, LRU), F32),
            jax.ShapeDtypeStruct((HEADS, HS, 2 * HS), F32),
            jax.ShapeDtypeStruct((8, LRU), F32),
            jax.ShapeDtypeStruct((8, LRU), F32),
        ],
        scratch_shapes=[
            pltpu.VMEM((rows, 2 * HS), F32),
            pltpu.VMEM((rows, 2 * HS), BF16),
            pltpu.VMEM((rows + BACK, HS), F32),
            pltpu.VMEM((rows + 8, HS), F32),
            pltpu.VMEM((rows + BACK, HS), F32),
            pltpu.VMEM((rows + BACK, HS), F32),
            pltpu.VMEM((TAIL, HS), F32),
        ],
        compiler_params=PARAMS,
        name="mixer_backward",
    )(local, prod, carry, state, before, c, u, halo, dist, gates, taps, soft)


def rms_norm(x, gain, shards, core):
    rows = x.shape[0]
    block = min(rows, 256)
    return pl.pallas_call(
        functools.partial(norm_kernel, shards),
        grid=(rows // block,),
        in_specs=[
            pl.BlockSpec(memory_space=pltpu.SMEM),
            pl.BlockSpec((block, D), lambda n: (n, 0)),
            pl.BlockSpec((1, D), lambda n: (0, 0)),
        ],
        out_specs=[
            pl.BlockSpec((block, D), lambda n: (n, 0)),
            pl.BlockSpec((block, D // 2), lambda n: (n, 0)),
            pl.BlockSpec((block, D // 2), lambda n: (n, 0)),
            pl.BlockSpec((block, 128), lambda n: (n, 0)),
        ],
        out_shape=[
            jax.ShapeDtypeStruct((rows, D), BF16),
            jax.ShapeDtypeStruct((rows, D // 2), BF16),
            jax.ShapeDtypeStruct((rows, D // 2), BF16),
            jax.ShapeDtypeStruct((rows, 128), F32),
        ],
        compiler_params=PARAMS,
        name="rms_norm",
    )(core.reshape(1), x, gain.reshape(1, D))


FF_TILE = 768
GATHER_TILE = 768
DOT_TILE = 512


def ffn_forward(normed, proj_up):
    rows = normed.shape[0]
    steps = FF // FF_TILE
    return pl.pallas_call(
        ffn_forward_kernel,
        grid=(steps,),
        in_specs=[
            pl.BlockSpec((rows, D), lambda n: (0, 0)),
            pl.BlockSpec((D, FF_TILE), lambda n: (0, n)),
            pl.BlockSpec((D, FF_TILE), lambda n: (0, n + steps)),
        ],
        out_specs=[
            pl.BlockSpec((rows, FF_TILE), lambda n: (0, n)),
            pl.BlockSpec((2, rows, FF_TILE), lambda n: (0, 0, n)),
        ],
        out_shape=[
            jax.ShapeDtypeStruct((rows, FF), BF16),
            jax.ShapeDtypeStruct((2, rows, FF), BF16),
        ],
        compiler_params=PARAMS,
        name="ffn_forward",
    )(normed, proj_up, proj_up)


def ffn_backward(grad, proj_down, pull):
    rows = grad.shape[0]
    return pl.pallas_call(
        ffn_backward_kernel,
        grid=(FF // FF_TILE,),
        in_specs=[
            pl.BlockSpec((rows, D), lambda n: (0, 0)),
            pl.BlockSpec((FF_TILE, D), lambda n: (n, 0)),
            pl.BlockSpec((2, rows, FF_TILE), lambda n: (0, 0, n)),
        ],
        out_specs=pl.BlockSpec((2, rows, FF_TILE), lambda n: (0, 0, n)),
        out_shape=jax.ShapeDtypeStruct((2, rows, FF), BF16),
        compiler_params=PARAMS,
        name="ffn_backward",
    )(grad, proj_down, pull)


def gather_rows(shard):
    parts = lax.axis_size("grp")
    rows = shard.shape[0] // parts
    own = lax.dynamic_slice_in_dim(shard, lax.axis_index("grp") * rows, rows, 0)
    return lax.all_gather(own, ("seq", "grp"), axis=0, tiled=True)


def tie(value, *after):
    return lax.optimization_barrier((value, *after))[0]


def xor_pairs(axis, bit):
    return [(i, i ^ bit) for i in range(lax.axis_size(axis))]


def ring_pairs(steps):
    count = lax.axis_size("seq")
    return [(i, (i + steps) % count) for i in range(count)]


def same_cores():
    count = lax.axis_size("seq")
    return [list(range(core, count, 2)) for core in range(2)]


def dot_rows(a, b):
    return lax.dot_general(a, b, (((0,), (0,)), ((), ())), preferred_element_type=F32)


def reduce_rows(partial):
    part = lax.psum_scatter(partial, "seq", scatter_dimension=0, tiled=True)
    part = lax.psum_scatter(part, "grp", scatter_dimension=0, tiled=True)
    return lax.all_gather(part, "grp", axis=0, tiled=True).astype(F32)


def dot_far(a, b):
    return lax.dot_general(a, b, (((1,), (1,)), ((), ())), preferred_element_type=F32)


def by_position(a):
    seqs, rows = a.shape[:2]
    return a.reshape(seqs, CHUNKS, rows // CHUNKS, *a.shape[2:]).swapaxes(1, 2).reshape(a.shape)


def by_token(a):
    seqs, rows = a.shape[:2]
    return a.reshape(seqs, rows // CHUNKS, CHUNKS, *a.shape[2:]).swapaxes(1, 2).reshape(a.shape)


def fetch_columns(where_ref, pieces, start, target, sem):
    own, far = pieces[:6], pieces[6:]
    rows, columns = own[0].shape
    width, tile = columns // 4, target.shape[1]
    depth, half = own[1].shape[0], own[4].shape[0]
    chips = depth // rows + 1
    chip, core, group = where_ref[0], where_ref[1], where_ref[2]
    quarter = start // width
    offset = pl.multiple_of(start - quarter * width, 128)
    start = pl.multiple_of(start, 128)
    relation = lax.bitwise_xor(group, quarter)

    def copy(source, row, count):
        place = target.at[pl.ds(pl.multiple_of(row, 16), count), :]
        pltpu.make_async_copy(source, place, sem).start()

    for c, (shard, *parts) in enumerate((own, far)):
        other = lax.rem(core + c, 2)
        copy(shard.at[:, pl.ds(start, tile)], (chip * 2 + other) * rows, rows)
        for j in range(1, chips):
            row = (lax.rem(chip + j, chips) * 2 + other) * rows
            first = (j - 1) * rows
            for k in range(3):

                @pl.when(relation == k)
                def _():
                    copy(parts[k].at[pl.ds(first, rows), pl.ds(offset, tile)], row, rows)

            @pl.when(relation == 3)
            def _():
                for m in range(2):
                    low, high = max(first, m * half), min(first + rows, (m + 1) * half)
                    if low < high:
                        at = pl.ds(low - m * half, high - low)
                        source = parts[3 + m].at[at, pl.ds(offset, tile)]
                        copy(source, row + (low - first), high - low)


def gathered_tiles(fetch, held, sems):
    step, steps = pl.program_id(0), pl.num_programs(0)
    slot = lax.rem(step, 2)

    @pl.when(step == 0)
    def _():
        fetch(step, slot)

    @pl.when(step + 1 < steps)
    def _():
        fetch(step + 1, 1 - slot)

    for side in range(held.shape[1]):
        whole = held.at[slot, side]
        pltpu.make_async_copy(whole, whole, sems.at[slot, side]).wait()
    return slot


def gathered_ffn_kernel(where_ref, n_ref, *refs):
    pieces, (hidden_ref, pull_ref, gate_ref, up_ref, held, sems) = refs[:12], refs[12:]
    tile = hidden_ref.shape[1]

    def fetch(n, slot):
        for side in range(2):
            start = n * tile + side * (pieces[0].shape[1] // 2)
            fetch_columns(where_ref, pieces, start, held.at[slot, side], sems.at[slot, side])

    slot = gathered_tiles(fetch, held, sems)
    gate_ref[...] = held[slot, 0]
    up_ref[...] = held[slot, 1]
    ffn_forward_kernel(n_ref, gate_ref, up_ref, hidden_ref, pull_ref)


def gathered_dot_kernel(base, where_ref, n_ref, *refs):
    pieces, (out_ref, weight_ref, held, sems) = refs[:12], refs[12:]
    tile = out_ref.shape[1]

    def fetch(n, slot):
        start = base + n * tile
        fetch_columns(where_ref, pieces, start, held.at[slot, 0], sems.at[slot, 0])

    slot = gathered_tiles(fetch, held, sems)
    weight_ref[...] = held[slot, 0]
    out_ref[...] = jnp.dot(n_ref[...], weight_ref[...], preferred_element_type=F32).astype(
        out_ref.dtype
    )


class Gather:
    def __init__(self, shard, *after, offload=False):
        self.shard = shard
        self.chips = lax.axis_size("seq") // 2
        half = (self.chips - 1) * shard.shape[0] // 2
        self.simple = lax.axis_size("grp") != 4 or half % 16 != 0
        if self.simple:
            self.whole = gather_rows(shard)
            return
        group = lax.axis_index("grp")
        width = shard.shape[1] // 4
        own = lax.dynamic_slice_in_dim(shard, group * width, width, 1)
        if after:
            own = tie(own, *after)
        if offload:
            self.slabs = lax.all_gather(own, "seq", axis_index_groups=same_cores())
        else:
            self.slabs = [
                lax.ppermute(own, "seq", ring_pairs(-2 * j)) for j in range(1, self.chips)
            ]
        self.half = half

    def first(self, *after):
        if self.simple:
            return ()
        slabs = tie(self.slabs, *after) if after else self.slabs
        if not isinstance(slabs, list):
            chip = lax.axis_index("seq") // 2
            slabs = [
                lax.dynamic_index_in_dim(slabs, (chip + j) % self.chips, 0, False)
                for j in range(1, self.chips)
            ]
        self.near = jnp.concatenate(slabs, axis=0)
        self.from_x = lax.ppermute(self.near, "grp", xor_pairs("grp", 1))
        self.from_y = lax.ppermute(self.near, "grp", xor_pairs("grp", 2))
        return (self.near,)

    def second(self, *after):
        if self.simple:
            return ()
        if after:
            self.from_x, self.from_y = tie((self.from_x, self.from_y), *after)
        self.halves = (self.from_y[: self.half], self.from_x[self.half :])
        return self.halves

    def third(self):
        if self.simple:
            return
        diag_a = lax.ppermute(self.halves[0], "grp", xor_pairs("grp", 1))
        diag_b = lax.ppermute(self.halves[1], "grp", xor_pairs("grp", 2))
        own = (self.shard, self.near, self.from_x, self.from_y, diag_a, diag_b)
        far = tuple(lax.ppermute(piece, "seq", xor_pairs("seq", 1)) for piece in own)
        place = lax.axis_index("seq")
        where = jnp.stack([place // 2, place % 2, lax.axis_index("grp")]).astype(jnp.int32)
        self.pieces = (where, own, far)

    def call(self, kernel, normed, steps, tile, weights, out_specs, out_shape, name):
        where, own, far = self.pieces
        rows, depth = normed.shape
        return pl.pallas_call(
            kernel,
            grid=(steps,),
            in_specs=[
                pl.BlockSpec(memory_space=pltpu.SMEM),
                pl.BlockSpec((rows, depth), lambda n: (0, 0)),
            ]
            + [pl.BlockSpec(memory_space=pl.ANY)] * 12,
            out_specs=out_specs + [pl.BlockSpec((depth, tile), lambda n: (0, n))] * weights,
            out_shape=out_shape + [jax.ShapeDtypeStruct((depth, steps * tile), BF16)] * weights,
            scratch_shapes=[
                pltpu.VMEM((2, weights, depth, tile), BF16),
                pltpu.SemaphoreType.DMA((2, weights)),
            ],
            compiler_params=pltpu.CompilerParams(vmem_limit_bytes=56 * 1024 * 1024),
            name=name,
        )(where, normed, *own, *far)

    def dot(self, normed, half, dtype):
        columns = self.shard.shape[1] // 2
        base = half * columns
        if self.simple:
            weight = self.whole[:, base : base + columns]
            return jnp.dot(normed, weight, preferred_element_type=F32).astype(dtype), weight
        rows, tile = normed.shape[0], DOT_TILE
        return self.call(
            functools.partial(gathered_dot_kernel, base),
            normed,
            columns // tile,
            tile,
            1,
            [pl.BlockSpec((rows, tile), lambda n: (0, n))],
            [jax.ShapeDtypeStruct((rows, columns), dtype)],
            "gathered_dot",
        )

    def ffn_forward(self, normed):
        if self.simple:
            hidden, pull = ffn_forward(normed, self.whole)
            return hidden, pull, self.whole[:, :FF], self.whole[:, FF:]
        rows, tile = normed.shape[0], GATHER_TILE
        return self.call(
            gathered_ffn_kernel,
            normed,
            FF // tile,
            tile,
            2,
            [
                pl.BlockSpec((rows, tile), lambda n: (0, n)),
                pl.BlockSpec((2, rows, tile), lambda n: (0, 0, n)),
            ],
            [
                jax.ShapeDtypeStruct((rows, FF), BF16),
                jax.ShapeDtypeStruct((2, rows, FF), BF16),
            ],
            "gathered_ffn",
        )


class Reduction:
    def __init__(self, a_own, a_far, columns, width, fused=False):
        self.simple = lax.axis_size("grp") != 4
        count = lax.axis_size("seq")
        place = lax.axis_index("seq")
        self.chips = count // 2
        self.chip, core = place // 2, place % 2
        self.width = width
        full = a_own.shape[1]
        self.rows = full // self.chips
        self.half = full // 2
        self.a_own = a_own
        if self.simple:
            parts = [columns(k) for k in range(4)]
            own, far = (
                jnp.concatenate([dot_rows(a, part) for part in parts], axis=1)
                for a in (a_own, a_far)
            )
            cores = jnp.stack(
                [jnp.where(core == c, own, far).reshape(self.chips, self.rows, -1) for c in (0, 1)],
                axis=1,
            )
            self.product = cores.reshape(2 * full, 4 * width).astype(BF16)
            self.arrived = self.product
            self.sent = (self.product,)
            return
        group = lax.axis_index("grp")
        self.x, self.y = xor_pairs("grp", 1), xor_pairs("grp", 2)
        self.b = [columns(group ^ k) for k in range(4)]
        self.far = [None] * 4
        self.product = None
        other = xor_pairs("seq", 1)
        if fused:
            b_all = jnp.concatenate(self.b, axis=1)
            far = lax.ppermute(dot_rows(a_far, b_all).astype(BF16), "seq", other)
            self.product = (dot_rows(a_own, b_all) + far.astype(F32)).astype(BF16)
        for k in () if fused else (3, 1, 2, 0):
            product = dot_rows(a_far, self.b[k]).astype(BF16)
            self.far[k] = lax.ppermute(product, "seq", other)
        half = self.half
        self.sent = (
            self.own(3, 0, half).astype(BF16),
            self.own(3, half, full).astype(BF16),
        )
        self.diag_a = lax.ppermute(self.sent[0], "grp", self.x)
        self.diag_b = lax.ppermute(self.sent[1], "grp", self.y)

    def own(self, k, first, last):
        if self.product is not None:
            left = k * self.width
            return self.product[first:last, left : left + self.width].astype(F32)
        product = dot_rows(self.a_own[:, first:last], self.b[k])
        return product + self.far[k][first:last].astype(F32)

    def second(self, *after):
        if self.simple:
            return ()
        full, none = 2 * self.half, ((0, self.half), (0, 0))
        diag_a, diag_b = self.diag_a, self.diag_b
        if after:
            diag_a, diag_b = tie((diag_a, diag_b), *after)
        sent = (
            (self.own(1, 0, full) + jnp.pad(diag_b.astype(F32), (none[0][::-1], (0, 0)))).astype(BF16),
            (self.own(2, 0, full) + jnp.pad(diag_a.astype(F32), none)).astype(BF16),
        )
        self.from_x = lax.ppermute(sent[0], "grp", self.x)
        self.from_y = lax.ppermute(sent[1], "grp", self.y)
        return sent

    def mine(self, *after):
        from_x, from_y = self.from_x, self.from_y
        if after:
            from_x, from_y = tie((from_x, from_y), *after)
        mine = self.own(0, 0, 2 * self.half) + from_x.astype(F32) + from_y.astype(F32)
        return mine.astype(BF16)

    def along_z(self, mine):
        mine = mine.reshape(self.chips, self.rows, -1)
        self.kept = lax.dynamic_index_in_dim(mine, self.chip, 0, False)
        sent = tuple(
            lax.dynamic_index_in_dim(mine, (self.chip + j) % self.chips, 0, False)
            for j in range(1, self.chips)
        )
        self.arrived = [
            lax.ppermute(part, "seq", ring_pairs(2 * j + 2)) for j, part in enumerate(sent)
        ]
        return sent

    def third(self, *after, offload=False):
        if self.simple:
            return ()
        mine = self.mine(*after)
        if not offload:
            return self.along_z(mine)
        self.kept = None
        self.arrived = lax.psum_scatter(
            mine, "seq", scatter_dimension=0, axis_index_groups=same_cores(), tiled=True
        )
        return (mine,)

    def total(self):
        if self.kept is None:
            return self.arrived
        total = self.kept.astype(F32)
        for part in self.arrived:
            total = total + part.astype(F32)
        return total

    def finish(self, *after):
        if self.simple:
            return reduce_rows(self.product)
        total = self.total()
        if after:
            total = tie(total, *after)
        parts = lax.all_gather(total.astype(BF16), "grp")
        return parts.transpose(1, 0, 2).reshape(self.rows, 4 * self.width).astype(F32)


def shard_carry(ends, prods, reverse):
    count = lax.axis_size("seq")
    place = lax.axis_index("seq")
    both = lax.all_gather(jnp.stack([ends, prods]), "seq")
    carry = jnp.zeros_like(ends)
    for step in range(count - 1):
        source = count - 1 - step if reverse else step
        ahead = source > place if reverse else source < place
        carry = jnp.where(ahead, both[source, 0] + both[source, 1] * carry, carry)
    return carry


def chunk_ends(chunks, reverse):
    state = jnp.zeros_like(chunks[:, 0, 0])
    prod = jnp.ones_like(state)
    order = range(CHUNKS - 1, -1, -1) if reverse else range(CHUNKS)
    for n in order:
        state = chunks[:, 0, n] + chunks[:, 1, n] * state
        prod = chunks[:, 1, n] * prod
    return state, prod


def chunk_carries(chunks, carry, reverse):
    order = range(CHUNKS - 1, -1, -1) if reverse else range(CHUNKS)
    found = [None] * CHUNKS
    for n in order:
        found[n] = carry
        carry = chunks[:, 0, n] + chunks[:, 1, n] * carry
    return jnp.stack(found, axis=1)


def norm_back(values, scale, gain, grad_normed):
    weighted = grad_normed * gain
    cubed = scale * scale * scale
    return scale * weighted - values * cubed * jnp.mean(weighted * values, axis=-1, keepdims=True)


def gain_grad(weight, grad_weight, gain):
    return jnp.sum(weight.astype(F32) * grad_weight, axis=1) / gain.astype(F32)


def body(
    tokens, seg_ids, cotangent, first_gain, in_proj, conv_taps, decay_param, gate_heads,
    out_proj, second_gain, up_proj, down_proj,
):
    seq_count, shard_len, _ = tokens.shape
    row_count = seq_count * shard_len
    edge_len = CONV - 1
    place = lax.axis_index("seq")
    last = lax.axis_size("seq") - 1

    small = jnp.concatenate(
        [first_gain, second_gain, decay_param, conv_taps.reshape(-1)]
    )
    small_all = lax.all_gather(small, "seq")
    n_gain, n_lru = first_gain.shape[0], decay_param.shape[0]
    gain_one = small_all[:, :n_gain].reshape(D).astype(F32)
    gain_two = small_all[:, n_gain : 2 * n_gain].reshape(D).astype(F32)
    decay_float = small_all[:, 2 * n_gain : 2 * n_gain + n_lru].reshape(LRU).astype(F32)
    taps_all = (
        small_all[:, 2 * n_gain + n_lru :].reshape(-1, CONV, n_lru).transpose(1, 0, 2)
    ).reshape(CONV, LRU).astype(F32)
    in_gather = Gather(in_proj)
    near = in_gather.first()
    in_gather.second()
    in_gather.third()
    gates_all = lax.all_gather(gate_heads, "seq", axis=0, tiled=True)
    up_gather = Gather(up_proj, gates_all, *near, offload=True)
    proj_out = gather_rows(out_proj)
    proj_down = gather_rows(down_proj)

    tokens = by_position(tokens)
    cotangent = by_position(cotangent)
    inputs = tokens.reshape(row_count, D).astype(F32)
    first_normed, first_own, first_far, first_scale = rms_norm(
        tokens.reshape(row_count, D), gain_one, last + 1, place % 2
    )
    first_scale = first_scale[:, :1]
    wide = (seq_count, shard_len, LRU)
    inner_low, in_value = in_gather.dot(first_normed, 0, BF16)
    inner_low = inner_low.reshape(wide)

    step = shard_len // CHUNKS
    final = inner_low.reshape(seq_count, step, CHUNKS, LRU)[:, step - HALO :, CHUNKS - 1]
    prev_inner = from_behind(final, "seq", 1)
    prev_ids = from_behind(seg_ids[:, shard_len - edge_len :], "seq", 1)
    prev_ids = jnp.where(place == 0, -1, prev_ids)
    ext_ids = jnp.concatenate([prev_ids, seg_ids], axis=1)
    dist = jnp.zeros((seq_count, shard_len), F32)
    for k in range(1, CONV):
        dist = dist + (ext_ids[:, edge_len - k : edge_len - k + shard_len] == seg_ids).astype(F32)
    dist = jnp.broadcast_to(by_position(dist)[:, :, None], (seq_count, shard_len, HS))
    soft = jax.nn.softplus(-decay_float).reshape(1, LRU)

    conv_low, keep, state_part, prod_part, chunks = mixer_forward(
        tie(inner_low, *up_gather.first(inner_low)), prev_inner, dist, gates_all, taps_all, soft
    )
    end_state, end_prod = chunk_ends(chunks, False)
    gate_pre, in_gate = in_gather.dot(first_normed, 1, F32)
    gate_pre = gate_pre.reshape(wide)
    carry_in = shard_carry(end_state, end_prod, False)
    carries = chunk_carries(chunks, carry_in, False)
    state, branch, branch_split = mixer_branch(
        tie(state_part, *up_gather.second(carries, gate_pre)), prod_part, carries, gate_pre, last + 1, place % 2
    )
    branch_split = branch_split.reshape(2, row_count, LRU // 2)
    resid = inputs + jnp.dot(
        branch.reshape(row_count, LRU), proj_out, preferred_element_type=F32
    )
    second_normed, second_own, second_far, second_scale = rms_norm(
        resid, gain_two, last + 1, place % 2
    )
    second_scale = second_scale[:, :1]
    up_gather.third()
    hidden, pull, proj_gate, proj_up = up_gather.ffn_forward(second_normed)

    grad_out = cotangent.reshape(row_count, D)
    grad_down = dot_rows(hidden, grad_out).astype(BF16)
    down_part = lax.psum_scatter(grad_down, ("seq", "grp"), scatter_dimension=0, tiled=True)
    grad_expanded = ffn_backward(tie(grad_out, grad_down), proj_down, pull)
    quarter = FF // 2

    def up_columns(n):
        part = lax.dynamic_slice(
            grad_expanded, (n // 2, 0, (n % 2) * quarter), (1, row_count, quarter)
        )
        return part[0]

    up_sum = Reduction(second_own, second_far, up_columns, quarter)
    grad_expanded = tie(grad_expanded, *up_sum.sent)
    grad_second_normed = dot_far(grad_expanded[0], proj_gate) + dot_far(
        grad_expanded[1], proj_up
    )
    sent = up_sum.second(grad_second_normed)
    grad_second_normed = tie(grad_second_normed, *sent)
    grad_resid = grad_out.astype(F32) + norm_back(
        resid, second_scale, gain_two, grad_second_normed
    )
    grad_mixer = grad_resid.astype(BF16)
    grad_branch = dot_far(grad_mixer, proj_out)

    grad_gate, local, rev_prod, rev_chunks = mixer_reverse(
        grad_branch.reshape(wide), gate_pre, keep, state
    )
    down_sum = lax.all_gather(tie(down_part, rev_chunks), "grp", axis=0, tiled=True)
    head_pull, head_prod = chunk_ends(rev_chunks, True)
    grad_gate = grad_gate.reshape(row_count, LRU)
    width = LRU // 4
    rev_carry = shard_carry(head_pull, head_prod, True)
    rev_carries = chunk_carries(rev_chunks, rev_carry, True)
    grad_mixer, grad_gate = tie((grad_mixer, grad_gate), rev_carry)
    out_sum = Reduction(
        branch_split[0],
        branch_split[1],
        lambda n: lax.dynamic_slice_in_dim(grad_mixer, n * (D // 4), D // 4, 1),
        D // 4,
        True,
    )
    in_gate_sum = Reduction(
        first_own,
        first_far,
        lambda n: lax.dynamic_slice_in_dim(grad_gate, n * width, width, 1),
        width,
        True,
    )
    sent = (*out_sum.sent, *in_gate_sum.sent)
    sent = up_sum.third(down_sum, *sent, offload=True)
    local = tie(local, *sent)
    du, tail, edge, grad_gates, grad_taps, grad_decay = mixer_backward(
        local, rev_prod, rev_carries, state, carries, conv_low, inner_low,
        prev_inner, dist, gates_all, taps_all, soft,
    )
    returned = from_behind(edge[:, HALO - edge_len :].astype(BF16), "seq", -1).astype(F32)
    grad_gate = tie(grad_gate, *out_sum.second(edge), *in_gate_sum.second(edge))
    first_grad = dot_far(grad_gate, in_gate)
    groups = TAIL // CHUNKS
    padded = jnp.pad(
        returned[:, :, None, :], ((0, 0), (groups - edge_len, 0), (CHUNKS - 1, 0), (0, 0))
    ).reshape(seq_count, TAIL, LRU)
    grad_inner = lax.dynamic_update_slice(
        du, (tail + padded).astype(BF16), (0, shard_len - TAIL, 0)
    )
    grad_inner = tie(grad_inner, first_grad).reshape(row_count, LRU)
    in_value_sum = Reduction(
        first_own,
        first_far,
        lambda n: lax.dynamic_slice_in_dim(grad_inner, n * width, width, 1),
        width,
        True,
    )
    grad_inner = tie(grad_inner, *in_value_sum.sent)

    shards = last + 1
    grad_decay_row = grad_decay[0] * jax.nn.sigmoid(-decay_float)
    flat = jnp.concatenate(
        [
            grad_gates.reshape(shards, -1, HS),
            grad_taps[:CONV].reshape(CONV, shards, -1, HS).swapaxes(0, 1).reshape(shards, -1, HS),
            grad_decay_row.reshape(shards, -1, HS),
        ],
        axis=1,
    )
    lines = flat.shape[1]
    flat = jnp.pad(flat, ((0, 0), (0, -lines % 16), (0, 0))).astype(BF16).reshape(-1, HS)
    flat = lax.psum_scatter(flat, "seq", scatter_dimension=0, tiled=True)
    first_grad = first_grad + dot_far(grad_inner, in_value)
    sent = in_value_sum.second(first_grad)
    out_sum.third(*sent)
    flat = lax.all_gather(tie(flat, *sent), "grp").astype(F32)
    flat = jnp.sum(flat, axis=0)[:lines].reshape(-1)
    n_gates = flat.shape[0] - (CONV + 1) * n_lru
    gates_total = flat[:n_gates].reshape(gate_heads.shape)
    taps_total = flat[n_gates : n_gates + CONV * n_lru].reshape(CONV, n_lru)
    decay_total = flat[n_gates + CONV * n_lru :]

    up_total = up_sum.finish(edge)
    down_total = tie(down_sum, *sent).astype(F32)
    if in_value_sum.simple:
        in_total = jnp.concatenate([in_value_sum.finish(), in_gate_sum.finish()], axis=1)
        last_sent = ()
    else:
        both = jnp.concatenate([in_value_sum.mine(), in_gate_sum.mine()], axis=1)
        last_sent = in_value_sum.along_z(both)
        both = in_value_sum.total().astype(BF16)
        in_total = jnp.concatenate(
            [
                lax.all_gather(both[:, n * width : (n + 1) * width], "grp")
                .transpose(1, 0, 2)
                .reshape(-1, LRU)
                for n in range(2)
            ],
            axis=1,
        ).astype(F32)
    out_total = out_sum.finish(*last_sent)
    ffn_out = jnp.dot(tie(hidden, *sent), proj_down, preferred_element_type=F32)
    block_out = by_token((resid + ffn_out).astype(BF16).reshape(tokens.shape))
    grad_tokens = grad_resid + norm_back(inputs, first_scale, gain_one, first_grad)
    grad_tokens = by_token(grad_tokens.astype(BF16).reshape(tokens.shape))
    first_total = gain_grad(in_proj, in_total, first_gain)
    second_total = gain_grad(up_proj, up_total, second_gain)
    return (
        block_out, grad_tokens, first_total, in_total, taps_total, decay_total, gates_total,
        out_total, second_total, up_total, down_total,
    )


def solution(mesh):
    in_specs = (
        P("grp", "seq", None),
        P("grp", "seq"),
        P("grp", "seq", None),
        P("seq"),
        P("seq", None),
        P(None, "seq"),
        P("seq"),
        P("seq", None, None),
        P("seq", None),
        P("seq"),
        P("seq", None),
        P("seq", None),
    )
    out_specs = (
        P("grp", "seq", None),
        P("grp", "seq", None),
        P("seq"),
        P("seq", None),
        P(None, "seq"),
        P("seq"),
        P("seq", None, None),
        P("seq", None),
        P("seq"),
        P("seq", None),
        P("seq", None),
    )
    return jax.shard_map(body, mesh=mesh, in_specs=in_specs, out_specs=out_specs, check_vma=False)
```
